32 devices in a mesh: section: 2 (over core), dp: 16 (over z, y, x).
Axes of the slice: x: 2, y: 2, z: 4, core: 2. Of those that a mesh axis runs over, the one named last changes fastest.
Arguments:
- frames: bfloat16 [2, 1024, 84, 336], P(None, 'dp'), may hold values from -4 to 4
- options: int32 [2, 1024, 3], P(None, 'dp'), may hold values from 0 to 17
- legal: int32 [2, 1024, 18], P(None, 'dp'), may hold values from 0 to 1, as said below
- games: int32 [2, 1024], P(None, 'dp'), may hold values from 0 to 7
- valid: int32 [2, 1024, 3], P(None, 'dp'), may hold values from 0 to 1, as said below
- rewards: float32 [2, 1024, 3], P(None, 'dp'), may hold values from -5 to 5
- returns: float32 [2, 1024, 4], P(None, 'dp'), may hold values from -5 to 5
- conv_kernels: float32 [256, 48], P('dp'), may hold values from -0.375 to 0.375
- enc_linear: float32 [2592, 128], P(None, 'dp'), may hold values from -0.125 to 0.125
- plan_mats: float32 [3, 128, 128], P(None, None, 'dp'), may hold values from -0.5 to 0.5
- option_emb: float32 [18, 128], P(None, 'dp'), may hold values from -3 to 3
- heads: float32 [3, 8, 128], P(None, None, 'dp'), may hold values from -0.5 to 0.5
- biases: float32 [304], replicated, may hold values from -0.5 to 0.5
- conv_moment: float32 [256, 48], P('dp'), may hold values from 1.5668244e-09 to 6.267298e-09
- lin_rows: float32 [2592], replicated, may hold values from 1.5668244e-09 to 6.267298e-09
- lin_cols: float32 [128], P('dp'), may hold values from 1.5668244e-09 to 6.267298e-09
- mats_rows: float32 [3, 128], replicated, may hold values from 1.5668244e-09 to 6.267298e-09
- mats_cols: float32 [3, 128], P(None, 'dp'), may hold values from 1.5668244e-09 to 6.267298e-09
- emb_moment: float32 [18, 128], P(None, 'dp'), may hold values from 1.5668244e-09 to 6.267298e-09
- head_moment: float32 [3, 8, 128], P(None, None, 'dp'), may hold values from 1.5668244e-09 to 6.267298e-09
- bias_moment: float32 [304], replicated, may hold values from 1.5668244e-09 to 6.267298e-09
Outputs:
- conv_new: float32 [256, 48], P('dp')
- conv_grad: float32 [256, 48], P('dp')
- conv_moment_new: float32 [256, 48], P('dp')
- lin_new: float32 [2592, 128], P(None, 'dp')
- lin_grad: float32 [2592, 128], P(None, 'dp')
- lin_rows_new: float32 [2592], replicated
- lin_cols_new: float32 [128], P('dp')
- mats_new: float32 [3, 128, 128], P(None, None, 'dp')
- mats_grad: float32 [3, 128, 128], P(None, None, 'dp')
- mats_rows_new: float32 [3, 128], replicated
- mats_cols_new: float32 [3, 128], P(None, 'dp')
- emb_new: float32 [18, 128], P(None, 'dp')
- emb_grad: float32 [18, 128], P(None, 'dp')
- emb_moment_new: float32 [18, 128], P(None, 'dp')
- heads_new: float32 [3, 8, 128], P(None, None, 'dp')
- heads_grad: float32 [3, 8, 128], P(None, None, 'dp')
- head_moment_new: float32 [3, 8, 128], P(None, None, 'dp')
- bias_new: float32 [304], replicated
- bias_grad: float32 [304], replicated
- bias_moment_new: float32 [304], replicated
- grad_norm: float32 [], replicated
- loss: float32 [], replicated
- conv_low: bfloat16 [256, 48], P('dp')
- lin_low: bfloat16 [2592, 128], P(None, 'dp')
The draws below stay inside these ranges and needn't reach their ends.
Inputs may be any that keep to these rules, and one draw needn't show every extreme that they name: Option 0 is legal in every row. In every row the first step is valid and the valid steps come first.
All inputs are finite; a program needn't handle non-finite values.
Results may differ from the reference program's by a relative error of at most 0.0075.
Values may be sent and summed in bfloat16 or wider, within the bound.
A program may use at most 320 MiB of HBM per device.

```python
import math
import jax
import jax.numpy as jnp
from jax import lax

D = 128
C1 = 16
C2 = 32
OPTS = 18
KERN = 256
SIDE = 84
DEPTH = 3
GAMES = 8
MB = 2
BATCH = 1024
FEAT = 2592
BIAS = 304


def draw_legal(key, part):
    key = jax.random.fold_in(key, 11)
    picked = jax.random.randint(key, (MB, BATCH, OPTS), 0, 2)
    always = (jnp.arange(OPTS) == 0)[None, None, :]
    return jnp.where(always, 1, picked).astype(jnp.int32)


def draw_valid(key, part):
    key = jax.random.fold_in(key, 23)
    endings = jax.random.randint(key, (MB, BATCH, 1), 1, DEPTH + 1)
    return (jnp.arange(DEPTH)[None, None, :] < endings).astype(jnp.int32)


def with_ends(drawn, key, low, high):
    shape = drawn.shape
    place = [jax.random.randint(jax.random.fold_in(key, axis), (), 0, shape[axis]) for axis in range(len(shape))]
    drawn = drawn.at[tuple(place)].set(low)
    longest = shape.index(max(shape))
    place[longest] = (place[longest] + 1) % shape[longest]
    return drawn.at[tuple(place)].set(high)


def steps_of(own_key, dims, pieces, low, high):
    def one(position, parts):
        steps = jax.random.uniform(jax.random.fold_in(jax.random.fold_in(own_key, 6), position), (parts,), jnp.float32, low / len(pieces), high / len(pieces))
        return jnp.repeat(jnp.exp(steps), dims[position] // parts).reshape((-1,) + (1,) * (len(dims) - position - 1))

    loudness = one(*pieces[0])
    for cut in pieces[1:]:
        loudness = loudness * one(*cut)
    return loudness


def bell_draw(rng, dims, deviation, reach, cuts=(), kind=jnp.bfloat16):
    entries = jax.random.normal(rng, dims, jnp.float32) * deviation
    if len(cuts) > 0:
        entries = steps_of(rng, dims, cuts, -0.22, 0.18) * entries
    return jnp.clip(entries, min=-reach, max=reach).astype(kind)


def setup_inputs(seed: int = 0) -> dict:
    key_of = jax.random.split(jax.random.key(seed), 22)
    return {
        "frames": bell_draw(key_of[0], (MB, BATCH, SIDE, SIDE * 4), 1.0, 4.0, ((1, 16),)),
        "options": with_ends(jax.random.randint(key_of[1], (MB, BATCH, DEPTH), 0, OPTS), jax.random.fold_in(key_of[1], 1), 0, OPTS - 1).astype(jnp.int32),
        "legal": draw_legal(jax.random.fold_in(key_of[21], 71), 0),
        "games": with_ends(jax.random.randint(key_of[3], (MB, BATCH), 0, GAMES), jax.random.fold_in(key_of[3], 1), 0, GAMES - 1).astype(jnp.int32),
        "valid": draw_valid(jax.random.fold_in(key_of[21], 71), 0),
        "rewards": bell_draw(key_of[5], (MB, BATCH, DEPTH), 1.0, 5.0, ((1, 16),), jnp.float32),
        "returns": bell_draw(key_of[6], (MB, BATCH, DEPTH + 1), 1.0, 5.0, ((1, 16),), jnp.float32),
        "conv_kernels": bell_draw(key_of[7], (KERN, C1 + C2), KERN ** -0.5, 0.375, ((0, 16),), jnp.float32),
        "enc_linear": bell_draw(key_of[8], (FEAT, D), FEAT ** -0.5, 0.125, ((1, 16),), jnp.float32),
        "plan_mats": bell_draw(key_of[9], (3, D, D), D ** -0.5, 0.5, ((2, 16),), jnp.float32),
        "option_emb": bell_draw(key_of[10], (OPTS, D), 0.5, 3.0, ((1, 16),), jnp.float32),
        "heads": bell_draw(key_of[11], (3, GAMES, D), D ** -0.5, 0.5, ((2, 16),), jnp.float32),
        "biases": bell_draw(key_of[12], (BIAS,), 0.1, 0.5, (), jnp.float32),
        "conv_moment": jnp.clip(jnp.exp(math.log(6.267297791850979e-09) - 1.3862944 * jax.random.uniform(key_of[13], (KERN, C1 + C2), jnp.float32) ** steps_of(key_of[13], (KERN, C1 + C2), ((0, 16),), -0.2, 0.2)), 1.5668244479627447e-09, 6.267297791850979e-09),
        "lin_rows": jnp.clip(jnp.exp(jax.random.uniform(key_of[14], (FEAT,), jnp.float32, math.log(1.5668244479627447e-09), math.log(6.267297791850979e-09))), 1.5668244479627447e-09, 6.267297791850979e-09),
        "lin_cols": jnp.clip(jnp.exp(math.log(6.267297791850979e-09) - 1.3862944 * jax.random.uniform(key_of[15], (D,), jnp.float32) ** steps_of(key_of[15], (D,), ((0, 16),), -0.2, 0.2)), 1.5668244479627447e-09, 6.267297791850979e-09),
        "mats_rows": jnp.clip(jnp.exp(jax.random.uniform(key_of[16], (3, D), jnp.float32, math.log(1.5668244479627447e-09), math.log(6.267297791850979e-09))), 1.5668244479627447e-09, 6.267297791850979e-09),
        "mats_cols": jnp.clip(jnp.exp(math.log(6.267297791850979e-09) - 1.3862944 * jax.random.uniform(key_of[17], (3, D), jnp.float32) ** steps_of(key_of[17], (3, D), ((1, 16),), -0.2, 0.2)), 1.5668244479627447e-09, 6.267297791850979e-09),
        "emb_moment": jnp.clip(jnp.exp(math.log(6.267297791850979e-09) - 1.3862944 * jax.random.uniform(key_of[18], (OPTS, D), jnp.float32) ** steps_of(key_of[18], (OPTS, D), ((1, 16),), -0.2, 0.2)), 1.5668244479627447e-09, 6.267297791850979e-09),
        "head_moment": jnp.clip(jnp.exp(math.log(6.267297791850979e-09) - 1.3862944 * jax.random.uniform(key_of[19], (3, GAMES, D), jnp.float32) ** steps_of(key_of[19], (3, GAMES, D), ((2, 16),), -0.2, 0.2)), 1.5668244479627447e-09, 6.267297791850979e-09),
        "bias_moment": jnp.clip(jnp.exp(jax.random.uniform(key_of[20], (BIAS,), jnp.float32, math.log(1.5668244479627447e-09), math.log(6.267297791850979e-09))), 1.5668244479627447e-09, 6.267297791850979e-09),
    }


CLIP_LIMIT = 0.05
DECAY_RATE = 0.8
STEP_RATE = 0.5
FLOOR_ONE = 1e-30
FLOOR_TWO = 0.001
PRECISE = lax.Precision.HIGHEST

@jax.custom_vjp
def low(v):
    return lax.optimization_barrier(v.astype(jnp.bfloat16)).astype(jnp.float32)

@jax.custom_vjp
def low_back(v):
    return v

def low_keep(v):
    return (low(v), None)

def low_pass(kept, grad):
    return (grad,)

def back_keep(v):
    return (v, None)

def back_low(kept, grad):
    return (low(grad),)
low.defvjp(low_keep, low_pass)
low_back.defvjp(back_keep, back_low)

def matmul_high(operand, matrix):
    return jnp.dot(operand, matrix, precision=PRECISE, preferred_element_type=jnp.float32)

def plan_loss(states, matrices, option_table, head_table, value_bias, options, legal, games, valid, rewards, returns):
    row_count = states.shape[0]
    feature_count = states.shape[1]
    option_count = option_table.shape[0]
    trans_in = matrices[0]
    trans_out = matrices[1]
    value_in = matrices[2]
    game_pick = jax.nn.one_hot(games, head_table.shape[1], dtype=jnp.float32)
    head_rows = jnp.einsum('bg,kgd->kbd', game_pick, head_table, precision=PRECISE)
    reward_head = head_rows[0]
    discount_head = head_rows[1]
    value_head = head_rows[2]
    valid_float = valid.astype(jnp.float32)
    pre_all = low_back(matmul_high(states, trans_in)[:, None, :] + option_table[None, :, :])
    hidden_all = jax.nn.silu(pre_all)
    change_all = low_back(matmul_high(low(hidden_all).reshape(row_count * option_count, feature_count), trans_out))
    after_all = states[:, None, :] + change_all.reshape(row_count, option_count, feature_count)
    after_low = low(after_all)
    judged_all = jax.nn.silu(low_back(matmul_high(after_low.reshape(row_count * option_count, feature_count), value_in) + value_bias))
    judged_all = judged_all.reshape(row_count, option_count, feature_count)
    value_all = lax.optimization_barrier(jnp.sum(judged_all * value_head[:, None, :], axis=2))
    reward_all = lax.optimization_barrier(jnp.sum(hidden_all * reward_head[:, None, :], axis=2))
    discount_all = jax.nn.sigmoid(lax.optimization_barrier(jnp.sum(hidden_all * discount_head[:, None, :], axis=2)))
    backed_up = reward_all + discount_all * value_all
    allowed = legal > 0
    highest = lax.optimization_barrier(jnp.max(jnp.where(allowed, backed_up, -1e+30), axis=1, keepdims=True))
    shares = jnp.where(allowed, jnp.exp(jnp.where(allowed, backed_up - highest, -60.0)), 0.0)
    planned = lax.optimization_barrier(jnp.sum(shares * backed_up, axis=1)) / lax.optimization_barrier(jnp.sum(shares, axis=1))
    choose = jax.nn.one_hot(options[:, 0], option_count, dtype=jnp.float32)
    rollout = lax.optimization_barrier(jnp.sum(choose[:, :, None] * after_all, axis=1))
    rollout_low = lax.optimization_barrier(jnp.sum(choose[:, :, None] * after_low, axis=1))
    plan_miss = planned - returns[:, 0]
    reward_miss = lax.optimization_barrier(jnp.sum(choose * reward_all, axis=1)) - rewards[:, 0]
    value_miss = lax.optimization_barrier(jnp.sum(choose * value_all, axis=1)) - returns[:, 1]
    errors = valid_float[:, 0] * (plan_miss * plan_miss + reward_miss * reward_miss + value_miss * value_miss)
    for depth_k in range(1, options.shape[1]):
        option_bias = matmul_high(jax.nn.one_hot(options[:, depth_k], option_count, dtype=jnp.float32), option_table)
        hidden_k = jax.nn.silu(low_back(matmul_high(rollout_low, trans_in) + option_bias))
        rollout = rollout + low_back(matmul_high(low(hidden_k), trans_out))
        rollout_low = low(rollout)
        judged_k = jax.nn.silu(low_back(matmul_high(rollout_low, value_in) + value_bias))
        reward_miss = lax.optimization_barrier(jnp.sum(hidden_k * reward_head, axis=1)) - rewards[:, depth_k]
        value_miss = lax.optimization_barrier(jnp.sum(judged_k * value_head, axis=1)) - returns[:, depth_k + 1]
        errors = errors + valid_float[:, depth_k] * (reward_miss * reward_miss + value_miss * value_miss)
    return jnp.sum(errors)

def encode_frames(frame_block, kernels, linear, bias_enc):
    frame_count = frame_block.shape[0]
    frame_side = frame_block.shape[1]
    image = frame_block.reshape(frame_count, frame_side, frame_side, 4)
    layout = ('NHWC', 'HWIO', 'NHWC')
    kernel_one = kernels[:, :C1].reshape(8, 8, 4, C1)
    z_one = lax.conv_general_dilated(image, kernel_one, (4, 4), 'VALID', dimension_numbers=layout, precision=PRECISE)
    a_one = low(jax.nn.silu(low_back(z_one + bias_enc[:C1])))
    kernel_two = kernels[:, C1:].reshape(4, 4, C1, C2)
    z_two = lax.conv_general_dilated(a_one, kernel_two, (2, 2), 'VALID', dimension_numbers=layout, precision=PRECISE)
    a_two = low(jax.nn.silu(low_back(z_two + bias_enc[C1:C1 + C2])))
    flat = a_two.reshape(frame_count, -1)
    return low(low_back(matmul_high(flat, linear) + bias_enc[C1 + C2:]))

def relative(weight):
    return jnp.maximum(FLOOR_TWO, jnp.sqrt(jnp.mean(weight * weight)))

def unfactored(weight, grad, moment):
    moment_new = DECAY_RATE * moment + (1.0 - DECAY_RATE) * (grad * grad + FLOOR_ONE)
    return (weight - STEP_RATE * relative(weight) * grad * lax.rsqrt(moment_new), moment_new)

def factored(weight, grad, rows_old, cols_old):
    rows_new = DECAY_RATE * rows_old + (1.0 - DECAY_RATE) * lax.optimization_barrier(jnp.mean(grad * grad + FLOOR_ONE, axis=-1))
    cols_new = DECAY_RATE * cols_old + (1.0 - DECAY_RATE) * lax.optimization_barrier(jnp.mean(grad * grad + FLOOR_ONE, axis=-2))
    second = rows_new[..., :, None] * cols_new[..., None, :] / lax.optimization_barrier(jnp.mean(rows_new, axis=-1))[..., None, None]
    return (weight - STEP_RATE * relative(weight) * grad * lax.rsqrt(second), rows_new, cols_new)

def reference(frames, options, legal, games, valid, rewards, returns, conv_kernels, enc_linear, plan_mats, option_emb, heads, biases, conv_moment, lin_rows, lin_cols, mats_rows, mats_cols, emb_moment, head_moment, bias_moment):
    count = jnp.sum(valid.astype(jnp.float32))
    pixels = frames.astype(jnp.float32)

    def total(kernels, linear, matrices, option_table, head_table, bias_all):
        kernels_low = low(kernels)
        linear_low = low(linear)
        matrices_low = low(matrices)
        table_low = low(option_table)
        heads_low = low(head_table)
        summed = jnp.zeros((), jnp.float32)
        for which_batch in range(MB):
            states = encode_frames(pixels[which_batch], kernels_low, linear_low, bias_all[:C1 + C2 + D])
            summed = summed + plan_loss(states, matrices_low, table_low, heads_low, bias_all[C1 + C2 + D:], options[which_batch], legal[which_batch], games[which_batch], valid[which_batch], rewards[which_batch], returns[which_batch])
        return summed / count
    loss_value, pullback = jax.vjp(total, conv_kernels, enc_linear, plan_mats, option_emb, heads, biases)
    gradients = pullback(jnp.ones((), jnp.float32))
    squares = jnp.zeros((), jnp.float32)
    for gradient in gradients:
        squares = squares + jnp.sum(gradient * gradient)
    grad_norm = jnp.sqrt(squares)
    factor = jnp.minimum(1.0, CLIP_LIMIT / grad_norm)
    g_conv, g_lin, g_mats, g_emb, g_heads, g_bias = [factor * gradient for gradient in gradients]
    conv_new, conv_moment_new = unfactored(conv_kernels, g_conv, conv_moment)
    lin_new, lin_rows_new, lin_cols_new = factored(enc_linear, g_lin, lin_rows, lin_cols)
    mats_new, mats_rows_new, mats_cols_new = factored(plan_mats, g_mats, mats_rows, mats_cols)
    emb_new, emb_moment_new = unfactored(option_emb, g_emb, emb_moment)
    heads_new, head_moment_new = unfactored(heads, g_heads, head_moment)
    bias_new, bias_moment_new = unfactored(biases, g_bias, bias_moment)
    return (conv_new, g_conv, conv_moment_new, lin_new, g_lin, lin_rows_new, lin_cols_new, mats_new, g_mats, mats_rows_new, mats_cols_new, emb_new, g_emb, emb_moment_new, heads_new, g_heads, head_moment_new, bias_new, g_bias, bias_moment_new, grad_norm, loss_value, conv_new.astype(jnp.bfloat16), lin_new.astype(jnp.bfloat16))
```

```python
import functools

import jax
import jax.numpy as jnp
from jax import lax
from jax.experimental import pallas as pl
from jax.experimental.pallas import tpu as pltpu
from jax.sharding import PartitionSpec as P

D = 128
C1 = 16
C2 = 32
OPTS = 18
KERN = 256
GAMES = 8
FEAT = 2592
BIAS = 304

OUT1 = 20
OUT2 = 9
WIDE = 384
FEATS_ROW = OUT2 * C2

CLIP_LIMIT = 0.05
DECAY_RATE = 0.8
STEP_RATE = 0.5
FLOOR_ONE = 1e-30
FLOOR_TWO = 0.001

HIGH = lax.Precision.HIGHEST
BF = jnp.bfloat16
F32 = jnp.float32


def dot(left, right, over_left=1, over_right=0, precision=None):
    return lax.dot_general(
        left,
        right,
        (((over_left,), (over_right,)), ((), ())),
        precision=precision,
        preferred_element_type=F32,
    )


def sigmoid(value):
    return 0.5 * jnp.tanh(0.5 * value) + 0.5


def slope(value, sigma):
    return sigma * (1.0 + value * (1.0 - sigma))


def iota(shape, axis):
    return lax.broadcasted_iota(jnp.int32, shape, axis)


def turn(value, steps):
    return pltpu.roll(value, steps, 1)


def fold(value, width):
    step = 64
    while step >= width:
        value = value + turn(value, step)
        step //= 2
    return value


def row_of(column):
    square = jnp.broadcast_to(column, (128, 128))
    return jnp.sum(jnp.where(iota((128, 128), 0) == iota((128, 128), 1), square, 0.0), axis=0, keepdims=True)


def load_frames(frames_hbm, section, frame_buf, sems, chunk):
    copies = []
    for which in range(frame_buf.shape[0] // chunk):
        rows = pl.ds(which * chunk, chunk)
        copies.append(
            pltpu.make_async_copy(
                frames_hbm.at[section, rows], frame_buf.at[rows], sems.at[which]
            )
        )
    return copies


def place_frames(frame_buf, pixels, first, chunk, frames):
    for row in range(first, first + chunk):
        block, part = row // 4, row % 4
        pixels[block * frames : (block + 1) * frames, part * WIDE : part * WIDE + 336] = frame_buf[row]


def build_bands(kernels, band_one, band_two):
    rows48 = iota((48, WIDE), 0)
    lanes48 = iota((48, WIDE), 1)
    pick_one = jnp.where((lanes48 % C1 == rows48) & (lanes48 < OUT1 * C1), 1.0, 0.0).astype(BF)
    pick_two = jnp.where(
        (lanes48 % C2 + C1 == rows48) & (lanes48 < OUT2 * C2), 1.0, 0.0
    ).astype(BF)
    wide_one = dot(kernels, pick_one)
    wide_two = dot(kernels, pick_two)
    group = iota((16, WIDE), 1) // C1
    for tap in range(8):
        left = wide_one[tap * 32 : tap * 32 + 16]
        right = wide_one[tap * 32 + 16 : tap * 32 + 32]
        for block in range(24):
            rows = tap * WIDE + block * 16
            if block > OUT1:
                band_one[rows : rows + 16] = jnp.zeros((16, WIDE), BF)
            else:
                band_one[rows : rows + 16] = jnp.where(
                    group == block, left, jnp.where(group == block - 1, right, 0.0)
                ).astype(BF)
    group = iota((32, WIDE), 1) // C2
    for tap in range(4):
        left = wide_two[tap * 64 : tap * 64 + 32]
        right = wide_two[tap * 64 + 32 : tap * 64 + 64]
        for block in range(12):
            rows = tap * WIDE + block * 32
            if block > OUT2:
                band_two[rows : rows + 32] = jnp.zeros((32, WIDE), BF)
            else:
                band_two[rows : rows + 32] = jnp.where(
                    group == block, left, jnp.where(group == block - 1, right, 0.0)
                ).astype(BF)


def wide_biases(bias_row):
    bias8 = jnp.broadcast_to(bias_row, (8, BIAS))
    rows = iota((BIAS, WIDE), 0)
    lanes = iota((BIAS, WIDE), 1)
    one = jnp.where((lanes % C1 == rows) & (lanes < OUT1 * C1), 1.0, 0.0)
    two = jnp.where((lanes % C2 + C1 == rows) & (lanes < OUT2 * C2), 1.0, 0.0)
    rows = iota((D, BIAS), 0)
    lanes = iota((D, BIAS), 1)
    three = jnp.where(lanes == rows + C1 + C2, 1.0, 0.0)
    four = jnp.where(lanes == rows + C1 + C2 + D, 1.0, 0.0)
    return (
        dot(bias8, one, precision=HIGH)[0:1],
        dot(bias8, two, precision=HIGH)[0:1],
        dot(three, bias8, 1, 1, precision=HIGH)[:, 0:1],
        dot(four, bias8, 1, 1, precision=HIGH)[:, 0:1],
    )


def encode_one(pixels, band_one, bias, z_one, act_one, frames, chunk):
    half = 4 * WIDE
    rows = chunk * frames
    for first in range(0, OUT1, chunk):
        low = first * frames
        z = dot(pixels[low : low + rows, :], band_one[0:half, :]) + dot(
            pixels[low + frames : low + frames + rows, :], band_one[half : 2 * half, :]
        )
        z = z + bias
        act = (z * sigmoid(z)).astype(BF)
        for step in range(chunk):
            at, part = divmod(first + step, 2)
            spot = (slice(at * frames, (at + 1) * frames), slice(part * WIDE, (part + 1) * WIDE))
            z_one[spot] = z[step * frames : (step + 1) * frames]
            act_one[spot] = act[step * frames : (step + 1) * frames]


def encode_two(act_one, band_two, bias, z_two, act_two, frames, chunk):
    half = 2 * WIDE
    rows = chunk * frames
    for first in range(0, OUT2, chunk):
        low = first * frames
        z = dot(act_one[low : low + rows, :], band_two[0:half, :]) + dot(
            act_one[low + frames : low + frames + rows, :], band_two[half : 2 * half, :]
        )
        z = z + bias
        z_two[low : low + rows] = z
        act = (z * sigmoid(z)).astype(BF)
        for step in range(chunk):
            at = (first + step) * FEATS_ROW
            act_two[:, at : at + FEATS_ROW] = act[step * frames : (step + 1) * frames, :FEATS_ROW]


def back_two(dstate_t, linear_t, act_two, z_two, dz_two, grad_linear, frames):
    grad_linear(dot(dstate_t, act_two[...]))
    dact = dot(dstate_t, linear_t, 0, 0)
    dz_two[0:frames] = jnp.zeros((frames, WIDE), BF)
    dz_two[(OUT2 + 1) * frames : (OUT2 + 2) * frames] = jnp.zeros((frames, WIDE), BF)
    blank = jnp.zeros((frames, WIDE - FEATS_ROW), F32)
    for at in range(OUT2):
        z = z_two[at * frames : (at + 1) * frames]
        part = jnp.concatenate([dact[:, at * FEATS_ROW : (at + 1) * FEATS_ROW], blank], axis=1)
        dz_two[(at + 1) * frames : (at + 2) * frames] = (part * slope(z, sigmoid(z))).astype(BF)


def back_one(dz_two, band_two, z_one, dz_one, frames, chunk):
    half = 2 * WIDE
    rows = chunk * frames
    for first in range(0, OUT1 // 2, chunk):
        low = first * frames
        dact = dot(dz_two[low + frames : low + frames + rows], band_two[0:half], 1, 1) + dot(
            dz_two[low : low + rows], band_two[half : 2 * half], 1, 1
        )
        z = z_one[low : low + rows]
        dz = (dact * slope(z, sigmoid(z))).astype(BF)
        for step in range(chunk):
            for part in range(2):
                at = (2 * (first + step) + part) * frames
                dz_one[at : at + frames] = dz[
                    step * frames : (step + 1) * frames, part * WIDE : (part + 1) * WIDE
                ]


def band_sums(full, base, outputs, width):
    per_tile = 128 // width
    lane = iota((width, 128), 1) // width
    sums = []
    for shift in range(2):
        total = None
        for spot in range(per_tile):
            part = None
            for position in range(outputs):
                tile, inside = divmod(position + shift, per_tile)
                if inside != spot:
                    continue
                term = full[
                    position * width : (position + 1) * width,
                    base + tile * 128 : base + (tile + 1) * 128,
                ]
                part = term if part is None else part + term
            if part is None:
                continue
            part = jnp.where(lane == spot, part, 0.0)
            total = part if total is None else total + part
        sums.append(fold(total, width))
    return sums


def kernel_grad(full_pairs, outputs, width, taps_per):
    tiles = []
    lane = iota((width, 128), 1) // width
    pieces = []
    for full in full_pairs:
        for tap in range(taps_per):
            pieces.extend(band_sums(full, tap * WIDE, outputs, width))
    per_tile = 128 // width
    for tile in range(2):
        total = jnp.zeros((width, 128), F32)
        for spot in range(per_tile):
            total = jnp.where(lane == spot, pieces[tile * per_tile + spot], total)
        tiles.append(total)
    return jnp.concatenate(tiles, axis=1)


def tiled(tile, count):
    return jnp.concatenate([tile] * count, axis=1)


def twice(row):
    return jnp.concatenate([row, row], axis=1)


def plan(states, mats_t, emb_t, heads_t, bias_col, options, legal, games, valid, rewards, returns):
    frames = states.shape[1]
    pairs = OPTS // 2
    lanes = OPTS * frames
    trans_in, trans_out, value_in = mats_t
    low_half = iota((1, 128), 1) < frames
    upper = iota((1, 128), 1) // frames

    valid_f = [twice(v.astype(F32)) for v in valid]
    rewards = [twice(r) for r in rewards]
    returns = [twice(r) for r in returns]
    chosen = [twice(o) for o in options]
    game = twice(games)

    game_rows = iota((24, WIDE), 0)
    game_pick = jnp.where(
        game_rows == tiled(game, 3) + GAMES * (iota((24, WIDE), 1) // 128), 1.0, 0.0
    ).astype(BF)
    head_rows = dot(heads_t, game_pick)
    hr, hd, hv = (head_rows[:, k * 128 : (k + 1) * 128] for k in range(3))

    option_rows = jnp.where(
        iota((32, lanes), 0) == iota((32, lanes), 1) // frames, 1.0, 0.0
    ).astype(BF)
    s_low = twice(states)
    s_f = s_low.astype(F32)
    base = dot(trans_in, s_low)
    pre = tiled(base, pairs) + dot(emb_t, option_rows)
    sig_h = sigmoid(pre)
    hid = pre * sig_h
    hid_low = hid.astype(BF)
    after = tiled(s_f, pairs) + dot(trans_out, hid_low)
    after_low = after.astype(BF)
    judge_pre = dot(value_in, after_low) + bias_col
    sig_j = sigmoid(judge_pre)
    judged = judge_pre * sig_j

    def tile_of(value, k):
        return value[:, k * 128 : (k + 1) * 128]

    def over(value):
        return jnp.sum(value, axis=0, keepdims=True)

    reward = [over(tile_of(hid, k) * hr) for k in range(pairs)]
    gamma = [sigmoid(over(tile_of(hid, k) * hd)) for k in range(pairs)]
    value = [over(tile_of(judged, k) * hv) for k in range(pairs)]
    backed = [reward[k] + gamma[k] * value[k] for k in range(pairs)]
    allowed = [
        jnp.concatenate([legal[2 * k], legal[2 * k + 1]], axis=1) > 0 for k in range(pairs)
    ]
    highest = functools.reduce(
        jnp.maximum, [jnp.where(allowed[k], backed[k], -1e30) for k in range(pairs)]
    )
    highest = jnp.maximum(highest, turn(highest, frames))
    shares = [
        jnp.where(allowed[k], jnp.exp(jnp.where(allowed[k], backed[k] - highest, -60.0)), 0.0)
        for k in range(pairs)
    ]

    def halves(total):
        return total + turn(total, frames)

    share_sum = halves(sum(shares))
    planned = halves(sum(shares[k] * backed[k] for k in range(pairs))) / share_sum
    choose = [chosen[0] == 2 * k + upper for k in range(pairs)]

    def chosen_of(parts):
        return halves(sum(jnp.where(choose[k], parts[k], 0.0) for k in range(pairs)))

    roll_f = [chosen_of([tile_of(after, k) for k in range(pairs)])]
    roll_low = [roll_f[0].astype(BF)]
    plan_miss = planned - returns[0]
    reward_miss = [chosen_of(reward) - rewards[0]]
    value_miss = [chosen_of(value) - returns[1]]
    steps = len(options)
    picks, pre_k, sig_k, hid_k, hid_k_low, judge_k, sig_jk, judged_k = ([None] for _ in range(8))
    for k in range(1, steps):
        picks.append(jnp.where(iota((32, 128), 0) == chosen[k], 1.0, 0.0).astype(BF))
        pre_k.append(dot(trans_in, roll_low[k - 1]) + dot(emb_t, picks[k]))
        sig_k.append(sigmoid(pre_k[k]))
        hid_k.append(pre_k[k] * sig_k[k])
        hid_k_low.append(hid_k[k].astype(BF))
        roll_f.append(roll_f[k - 1] + dot(trans_out, hid_k_low[k]))
        roll_low.append(roll_f[k].astype(BF))
        judge_k.append(dot(value_in, roll_low[k]) + bias_col)
        sig_jk.append(sigmoid(judge_k[k]))
        judged_k.append(judge_k[k] * sig_jk[k])
        reward_miss.append(over(hid_k[k] * hr) - rewards[k])
        value_miss.append(over(judged_k[k] * hv) - returns[k + 1])
    errors = valid_f[0] * plan_miss * plan_miss
    for k in range(steps):
        errors = errors + valid_f[k] * (
            reward_miss[k] * reward_miss[k] + value_miss[k] * value_miss[k]
        )
    errors = jnp.where(low_half, errors, 0.0)

    half = jnp.where(low_half, 1.0, 0.0)
    d_plan = 2.0 * valid_f[0] * plan_miss / share_sum
    d_reward_k = [2.0 * valid_f[k] * reward_miss[k] for k in range(steps)]
    d_value_k = [2.0 * valid_f[k] * value_miss[k] for k in range(steps)]

    def through(matrix_t, grad):
        return dot(matrix_t, grad, 0, 0)

    d_roll = None
    d_judge_low, d_step_low, d_pre_low = ([None] * steps for _ in range(3))
    d_hr = jnp.zeros((D, 128), F32)
    d_hd = jnp.zeros((D, 128), F32)
    d_hv = jnp.zeros((D, 128), F32)
    for k in range(steps - 1, 0, -1):
        d_judge_low[k] = (d_value_k[k] * hv * slope(judge_k[k], sig_jk[k])).astype(BF)
        term = through(value_in, d_judge_low[k])
        d_roll = term if d_roll is None else d_roll + term
        d_step_low[k] = d_roll.astype(BF)
        d_hid = through(trans_out, d_step_low[k]) + d_reward_k[k] * hr
        d_pre_low[k] = (d_hid * slope(pre_k[k], sig_k[k])).astype(BF)
        d_roll = d_roll + through(trans_in, d_pre_low[k])
        d_hr = d_hr + (half * d_reward_k[k]) * hid_k[k]
        d_hv = d_hv + (half * d_value_k[k]) * judged_k[k]

    d_backed = [d_plan * shares[k] * (1.0 + backed[k] - planned) for k in range(pairs)]
    d_reward = [
        d_backed[k] + jnp.where(choose[k], d_reward_k[0], 0.0) for k in range(pairs)
    ]
    d_value = [
        d_backed[k] * gamma[k] + jnp.where(choose[k], d_value_k[0], 0.0) for k in range(pairs)
    ]
    d_gamma = [d_backed[k] * value[k] * gamma[k] * (1.0 - gamma[k]) for k in range(pairs)]
    d_judge = [
        (d_value[k] * hv * slope(tile_of(judge_pre, k), tile_of(sig_j, k))).astype(BF)
        for k in range(pairs)
    ]
    d_judge_all = jnp.concatenate(d_judge, axis=1)
    d_after = through(value_in, d_judge_all)
    d_after = [
        tile_of(d_after, k) + jnp.where(choose[k], d_roll, 0.0) for k in range(pairs)
    ]
    d_after_low = jnp.concatenate([d.astype(BF) for d in d_after], axis=1)
    d_hid_all = through(trans_out, d_after_low)
    d_pre = [
        (
            (tile_of(d_hid_all, k) + d_reward[k] * hr + d_gamma[k] * hd)
            * slope(tile_of(pre, k), tile_of(sig_h, k))
        ).astype(BF)
        for k in range(pairs)
    ]
    d_pre_all = jnp.concatenate(d_pre, axis=1)
    d_base = through(trans_in, d_pre_all)
    d_state = halves(sum(d_after[k] + tile_of(d_base, k) for k in range(pairs)))
    for k in range(pairs):
        d_hr = d_hr + d_reward[k] * tile_of(hid, k)
        d_hd = d_hd + d_gamma[k] * tile_of(hid, k)
        d_hv = d_hv + d_value[k] * tile_of(judged, k)

    def both(parts):
        joined = [jnp.where(low_half, parts[k].astype(F32), parts[k + 1].astype(F32)) for k in range(1, steps, 2)]
        return [part.astype(BF) for part in joined]

    def with_steps(wide, parts):
        return jnp.concatenate([wide] + both(parts), axis=1)

    before_low = [None] + roll_low[:-1]
    d_pre_cat = with_steps(d_pre_all, d_pre_low)
    d_judge_cat = with_steps(d_judge_all, d_judge_low)
    grad_in = dot(d_pre_cat, with_steps(tiled(s_low, pairs), before_low), 1, 1)
    grad_out = dot(
        with_steps(d_after_low, d_step_low), with_steps(hid_low, hid_k_low), 1, 1
    )
    grad_value = dot(d_judge_cat, with_steps(after_low, roll_low), 1, 1)
    grad_emb = dot(d_pre_cat, with_steps(option_rows, picks), 1, 1)
    grad_heads = dot(
        jnp.concatenate([d_hr, d_hd, d_hv], axis=1), game_pick.astype(F32), 1, 1, precision=HIGH
    )
    grad_bias = jnp.sum(d_judge_cat.astype(F32), axis=1, keepdims=True)
    return (
        d_state[:, :frames],
        (grad_in, grad_out, grad_value),
        grad_emb,
        grad_heads,
        grad_bias,
        errors,
    )


def local_kernel(
    frames_hbm,
    kernels_ref,
    linear_ref,
    mats_ref,
    emb_ref,
    heads_ref,
    bias_ref,
    options_ref,
    legal_ref,
    games_ref,
    valid_ref,
    rewards_ref,
    returns_ref,
    lin_out,
    mats_out,
    emb_out,
    heads_out,
    conv_out,
    small_out,
    frame_buf,
    pixels,
    band_one,
    band_two,
    z_one,
    act_one,
    z_two,
    act_two,
    dz_two,
    dz_one,
    sems,
):
    section = lax.axis_index("section")
    frames = frame_buf.shape[1]
    side = frame_buf.shape[0]
    chunk = 12
    copies = load_frames(frames_hbm, section, frame_buf, sems, chunk)
    for copy in copies:
        copy.start()
    build_bands(kernels_ref[...], band_one, band_two)
    bias_one, bias_two, bias_three, bias_four = wide_biases(bias_ref[...])
    tail = jnp.zeros((pixels.shape[0], WIDE - 336), BF)
    for part in range(4):
        pixels[:, part * WIDE + 336 : (part + 1) * WIDE] = tail
    for which, copy in enumerate(copies):
        copy.wait()
        place_frames(frame_buf, pixels, which * chunk, chunk, frames)
    encode_one(pixels, band_one, bias_one, z_one, act_one, frames, 4)
    encode_two(act_one, band_two, bias_two, z_two, act_two, frames, 3)
    linear_t = linear_ref[...]
    states = (dot(linear_t, act_two[...], 1, 1) + bias_three).astype(BF)

    def row(ref, k):
        return ref[k, pl.ds(section, 1), :]

    depth = options_ref.shape[0]
    d_state, grad_mats, grad_emb, grad_heads, grad_bias, errors = plan(
        states,
        tuple(mats_ref[k] for k in range(3)),
        emb_ref[:, 0:32],
        heads_ref[:, 0:24],
        bias_four,
        [row(options_ref, k) for k in range(depth)],
        [row(legal_ref, k) for k in range(OPTS)],
        games_ref[pl.ds(section, 1), :],
        [row(valid_ref, k) for k in range(depth)],
        [row(rewards_ref, k) for k in range(depth)],
        [returns_ref[section, k : k + 1, :] for k in range(depth + 1)],
    )
    for k in range(3):
        mats_out[k] = grad_mats[k]
    emb_out[...] = jnp.concatenate([grad_emb, jnp.zeros((D, 96), F32)], axis=1)
    heads_out[...] = jnp.concatenate([grad_heads, jnp.zeros((D, 104), F32)], axis=1)
    d_state_low = d_state.astype(BF)
    grad_three = jnp.sum(d_state_low.astype(F32), axis=1, keepdims=True)

    def keep_linear(grad):
        lin_out[...] = grad

    back_two(d_state_low, linear_t, act_two, z_two, dz_two, keep_linear, frames)
    d_two = dz_two[frames : (OUT2 + 1) * frames]
    rows_two = OUT2 * frames
    grad_two = kernel_grad(
        [
            dot(d_two, act_one[0:rows_two], 0, 0),
            dot(d_two, act_one[frames : frames + rows_two], 0, 0),
        ],
        OUT2,
        C2,
        2,
    )
    bias_two_grad = fold(tiles_sum(dot(jnp.ones((8, rows_two), BF), d_two)), C2)
    back_one(dz_two, band_two, z_one, dz_one, frames, 5)
    d_one = dz_one[...]
    rows_one = OUT1 * frames
    grad_one = kernel_grad(
        [
            dot(d_one, pixels[0:rows_one], 0, 0),
            dot(d_one, pixels[frames : frames + rows_one], 0, 0),
        ],
        OUT1,
        C1,
        4,
    )
    bias_one_grad = fold(tiles_sum(dot(jnp.ones((8, rows_one), BF), d_one)), C1)
    conv_t = jnp.concatenate(
        [grad_one, grad_two, jnp.zeros((128 - C1 - C2, KERN), F32)], axis=0
    )
    conv_out[...] = conv_t.T
    lane = iota((8, 128), 1)
    line = iota((8, 128), 0)
    row_zero = jnp.where(
        lane < C1, bias_one_grad, jnp.where(lane < C1 + C2, turn(bias_two_grad, C1), 0.0)
    )
    count = sum(row(valid_ref, k).astype(F32) for k in range(depth))
    count = jnp.where(iota((1, 128), 1) < frames, twice(count), 0.0)
    small = jnp.where(line == 0, row_zero, 0.0)
    small = jnp.where(line == 1, row_of(grad_three), small)
    small = jnp.where(line == 2, row_of(grad_bias), small)
    small = jnp.where(line == 3, errors, small)
    small = jnp.where(line == 4, count, small)
    small_out[...] = small


def tiles_sum(value):
    return sum(value[:, k * 128 : (k + 1) * 128] for k in range(value.shape[1] // 128))


VMEM_SPEC = pl.BlockSpec(memory_space=pltpu.VMEM)
ANY_SPEC = pl.BlockSpec(memory_space=pl.ANY)


def local_scratch(frames, side):
    return [
        pltpu.VMEM((side, frames, 336), BF),
        pltpu.VMEM(((OUT1 + 1) * frames, 4 * WIDE), BF),
        pltpu.VMEM((8 * WIDE, WIDE), BF),
        pltpu.VMEM((4 * WIDE, WIDE), BF),
        pltpu.VMEM((OUT1 // 2 * frames, 2 * WIDE), F32),
        pltpu.VMEM((OUT1 // 2 * frames, 2 * WIDE), BF),
        pltpu.VMEM((OUT2 * frames, WIDE), F32),
        pltpu.VMEM((frames, FEAT), BF),
        pltpu.VMEM(((OUT2 + 2) * frames, WIDE), BF),
        pltpu.VMEM((OUT1 * frames, WIDE), BF),
        pltpu.SemaphoreType.DMA((side // 12,)),
    ]


def local_step(frames, kernels, linear_t, mats_t, emb_t, heads_t, biases, options, legal, games, valid, rewards, returns):
    count = frames.shape[1]
    side = frames.shape[2]
    shapes = [(D, FEAT), (3, D, D), (D, 128), (D, 128), (KERN, 128), (8, 128)]
    return pl.pallas_call(
        local_kernel,
        out_shape=[jax.ShapeDtypeStruct(shape, F32) for shape in shapes],
        in_specs=[ANY_SPEC] + [VMEM_SPEC] * 12,
        out_specs=[VMEM_SPEC] * len(shapes),
        scratch_shapes=local_scratch(count, side),
        compiler_params=pltpu.CompilerParams(vmem_limit_bytes=56 * 1024 * 1024),
    )(
        frames.transpose(0, 2, 1, 3),
        kernels,
        linear_t,
        mats_t,
        emb_t,
        heads_t,
        biases.reshape(1, BIAS),
        options.transpose(2, 0, 1),
        legal.transpose(2, 0, 1),
        games,
        valid.transpose(2, 0, 1),
        rewards.transpose(2, 0, 1),
        returns.transpose(0, 2, 1),
    )


def gather_rows(shard):
    return lax.all_gather(shard, "dp", axis=0, tiled=True)


def relative(square_total, entries):
    return jnp.maximum(FLOOR_TWO, jnp.sqrt(square_total / entries))


def unfactored(weight, grad, moment, scale):
    moment_new = DECAY_RATE * moment + (1.0 - DECAY_RATE) * (grad * grad + FLOOR_ONE)
    return (weight - STEP_RATE * scale * grad * lax.rsqrt(moment_new), moment_new)


def per_device(
    frames,
    options,
    legal,
    games,
    valid,
    rewards,
    returns,
    conv_kernels,
    enc_linear,
    plan_mats,
    option_emb,
    heads,
    biases,
    conv_moment,
    lin_rows,
    lin_cols,
    mats_rows,
    mats_cols,
    emb_moment,
    head_moment,
    bias_moment,
):
    weight_squares = lax.psum(
        (
            jnp.sum(conv_kernels * conv_kernels),
            jnp.sum(enc_linear * enc_linear),
            jnp.sum(plan_mats * plan_mats),
            jnp.sum(option_emb * option_emb),
            jnp.sum(heads * heads),
        ),
        "dp",
    )
    width = enc_linear.shape[1]
    kernels = gather_rows(conv_kernels.astype(BF))
    linear_t = gather_rows(enc_linear.astype(BF).T)
    mats_t = gather_rows(plan_mats.astype(BF).transpose(2, 0, 1)).transpose(1, 0, 2)
    emb_t = gather_rows(option_emb.astype(BF).T)
    heads_t = gather_rows(heads.astype(BF).reshape(3 * GAMES, width).T)
    emb_t = jnp.pad(emb_t, ((0, 0), (0, 128 - OPTS)))
    heads_t = jnp.pad(heads_t, ((0, 0), (0, 128 - 3 * GAMES)))
    lin, mats, emb, hds, conv, small = local_step(
        frames,
        kernels,
        linear_t,
        mats_t,
        emb_t,
        heads_t,
        biases,
        options,
        legal,
        games,
        valid,
        rewards,
        returns,
    )
    rows = jnp.concatenate(
        [lin, mats[0], mats[1], mats[2], emb[:, :OPTS], hds[:, : 3 * GAMES]], axis=1
    )
    rows = lax.psum(lax.psum_scatter(rows, "dp", scatter_dimension=0, tiled=True), "section")
    conv = lax.psum(
        lax.psum_scatter(conv[:, : C1 + C2], "dp", scatter_dimension=0, tiled=True), "section"
    )
    small = lax.psum(small, ("section", "dp"))
    inverse_count = 1.0 / jnp.sum(small[4])
    loss_value = jnp.sum(small[3]) * inverse_count
    bias_raw = (
        jnp.concatenate([small[0, : C1 + C2], small[1], small[2]]) * inverse_count
    )
    rows = rows * inverse_count
    g_conv = conv * inverse_count
    g_lin = rows[:, :FEAT].T
    g_mats = rows[:, FEAT : FEAT + 3 * D].reshape(width, 3, D).transpose(1, 2, 0)
    g_emb = rows[:, FEAT + 3 * D : FEAT + 3 * D + OPTS].T
    g_heads = rows[:, FEAT + 3 * D + OPTS :].T.reshape(3, GAMES, width)
    partial_squares = (
        jnp.sum(g_conv * g_conv)
        + jnp.sum(g_lin * g_lin)
        + jnp.sum(g_mats * g_mats)
        + jnp.sum(g_emb * g_emb)
        + jnp.sum(g_heads * g_heads)
    )
    reduced = lax.psum(
        (partial_squares, jnp.sum(g_lin * g_lin, axis=1), jnp.sum(g_mats * g_mats, axis=2)), "dp"
    )
    grad_norm = jnp.sqrt(reduced[0] + jnp.sum(bias_raw * bias_raw))
    factor = jnp.minimum(1.0, CLIP_LIMIT / grad_norm)
    conv_grad = factor * g_conv
    lin_grad = factor * g_lin
    mats_grad = factor * g_mats
    emb_grad = factor * g_emb
    heads_grad = factor * g_heads
    bias_grad = factor * bias_raw
    conv_new, conv_moment_new = unfactored(
        conv_kernels, conv_grad, conv_moment, relative(weight_squares[0], KERN * (C1 + C2))
    )
    emb_new, emb_moment_new = unfactored(
        option_emb, emb_grad, emb_moment, relative(weight_squares[3], OPTS * D)
    )
    heads_new, head_moment_new = unfactored(
        heads, heads_grad, head_moment, relative(weight_squares[4], 3 * GAMES * D)
    )
    bias_new, bias_moment_new = unfactored(
        biases, bias_grad, bias_moment, relative(jnp.sum(biases * biases), BIAS)
    )
    lin_rows_new = DECAY_RATE * lin_rows + (1.0 - DECAY_RATE) * (
        factor * factor * reduced[1] / D + FLOOR_ONE
    )
    lin_cols_new = DECAY_RATE * lin_cols + (1.0 - DECAY_RATE) * jnp.mean(
        lin_grad * lin_grad + FLOOR_ONE, axis=0
    )
    lin_second = lin_rows_new[:, None] * lin_cols_new[None, :] / jnp.mean(lin_rows_new)
    lin_new = enc_linear - STEP_RATE * relative(weight_squares[1], FEAT * D) * lin_grad * lax.rsqrt(
        lin_second
    )
    mats_rows_new = DECAY_RATE * mats_rows + (1.0 - DECAY_RATE) * (
        factor * factor * reduced[2] / D + FLOOR_ONE
    )
    mats_cols_new = DECAY_RATE * mats_cols + (1.0 - DECAY_RATE) * jnp.mean(
        mats_grad * mats_grad + FLOOR_ONE, axis=1
    )
    mats_second = (
        mats_rows_new[:, :, None]
        * mats_cols_new[:, None, :]
        / jnp.mean(mats_rows_new, axis=1)[:, None, None]
    )
    mats_new = plan_mats - STEP_RATE * relative(weight_squares[2], 3 * D * D) * mats_grad * lax.rsqrt(
        mats_second
    )
    return (
        conv_new,
        conv_grad,
        conv_moment_new,
        lin_new,
        lin_grad,
        lin_rows_new,
        lin_cols_new,
        mats_new,
        mats_grad,
        mats_rows_new,
        mats_cols_new,
        emb_new,
        emb_grad,
        emb_moment_new,
        heads_new,
        heads_grad,
        head_moment_new,
        bias_new,
        bias_grad,
        bias_moment_new,
        grad_norm,
        loss_value,
        conv_new.astype(BF),
        lin_new.astype(BF),
    )


def solution(mesh):
    return jax.shard_map(
        per_device,
        mesh=mesh,
        in_specs=(
            P(None, "dp", None, None),
            P(None, "dp", None),
            P(None, "dp", None),
            P(None, "dp"),
            P(None, "dp", None),
            P(None, "dp", None),
            P(None, "dp", None),
            P("dp", None),
            P(None, "dp"),
            P(None, None, "dp"),
            P(None, "dp"),
            P(None, None, "dp"),
            P(),
            P("dp", None),
            P(),
            P("dp"),
            P(),
            P(None, "dp"),
            P(None, "dp"),
            P(None, None, "dp"),
            P(),
        ),
        out_specs=(
            P("dp", None),
            P("dp", None),
            P("dp", None),
            P(None, "dp"),
            P(None, "dp"),
            P(),
            P("dp"),
            P(None, None, "dp"),
            P(None, None, "dp"),
            P(),
            P(None, "dp"),
            P(None, "dp"),
            P(None, "dp"),
            P(None, "dp"),
            P(None, None, "dp"),
            P(None, None, "dp"),
            P(None, None, "dp"),
            P(),
            P(),
            P(),
            P(),
            P(),
            P("dp", None),
            P(None, "dp"),
        ),
        check_vma=False,
    )
```

```python
import functools

import jax
import jax.numpy as jnp
from jax import lax
from jax.experimental import pallas as pl
from jax.experimental.pallas import tpu as pltpu
from jax.sharding import PartitionSpec as P

D = 128
C1 = 16
C2 = 32
OPTS = 18
KERN = 256
GAMES = 8
FEAT = 2592
BIAS = 304

OUT1 = 20
OUT2 = 9
WIDE = 384
CHUNK = 12
FEATS_ROW = OUT2 * C2

CLIP_LIMIT = 0.05
DECAY_RATE = 0.8
STEP_RATE = 0.5
FLOOR_ONE = 1e-30
FLOOR_TWO = 0.001

HIGH = lax.Precision.HIGHEST
BF = jnp.bfloat16
F32 = jnp.float32


def dot(left, right, over_left=1, over_right=0, precision=None):
    return lax.dot_general(
        left,
        right,
        (((over_left,), (over_right,)), ((), ())),
        precision=precision,
        preferred_element_type=F32,
    )


def sigmoid(value):
    return 0.5 * jnp.tanh(0.5 * value) + 0.5


def slope(value, sigma):
    return sigma * (1.0 + value * (1.0 - sigma))


def iota(shape, axis):
    return lax.broadcasted_iota(jnp.int32, shape, axis)


def turn(value, steps):
    return pltpu.roll(value, steps, 1)


def fold(value, width):
    step = 64
    while step >= width:
        value = value + turn(value, step)
        step //= 2
    return value


def row_of(column):
    square = jnp.broadcast_to(column, (128, 128))
    return jnp.sum(jnp.where(iota((128, 128), 0) == iota((128, 128), 1), square, 0.0), axis=0, keepdims=True)


def load_frames(frames_hbm, section, frame_buf, sems, chunk):
    copies = []
    for which in range(frame_buf.shape[0] // chunk):
        rows = pl.ds(which * chunk, chunk)
        copies.append(
            pltpu.make_async_copy(
                frames_hbm.at[section, rows], frame_buf.at[rows], sems.at[which]
            )
        )
    return copies


def place_frames(frame_buf, pixels, first, chunk, frames):
    for row in range(first, first + chunk):
        block, part = row // 4, row % 4
        pixels[block * frames : (block + 1) * frames, part * WIDE : part * WIDE + 336] = frame_buf[row]


def build_bands(kernels, band_one, band_two):
    held = kernels.shape[1]
    rows48 = iota((held, WIDE), 0)
    lanes48 = iota((held, WIDE), 1)
    pick_one = jnp.where((lanes48 % C1 == rows48) & (lanes48 < OUT1 * C1), 1.0, 0.0).astype(BF)
    pick_two = jnp.where(
        (lanes48 % C2 + C1 == rows48) & (lanes48 < OUT2 * C2), 1.0, 0.0
    ).astype(BF)
    wide_one = dot(kernels, pick_one)
    wide_two = dot(kernels, pick_two)
    group = iota((16, WIDE), 1) // C1
    for tap in range(8):
        left = wide_one[tap * 32 : tap * 32 + 16]
        right = wide_one[tap * 32 + 16 : tap * 32 + 32]
        for block in range(24):
            rows = tap * WIDE + block * 16
            if block > OUT1:
                band_one[rows : rows + 16] = jnp.zeros((16, WIDE), BF)
            else:
                band_one[rows : rows + 16] = jnp.where(
                    group == block, left, jnp.where(group == block - 1, right, 0.0)
                ).astype(BF)
    group = iota((32, WIDE), 1) // C2
    for tap in range(4):
        left = wide_two[tap * 64 : tap * 64 + 32]
        right = wide_two[tap * 64 + 32 : tap * 64 + 64]
        for block in range(12):
            rows = tap * WIDE + block * 32
            if block > OUT2:
                band_two[rows : rows + 32] = jnp.zeros((32, WIDE), BF)
            else:
                band_two[rows : rows + 32] = jnp.where(
                    group == block, left, jnp.where(group == block - 1, right, 0.0)
                ).astype(BF)


def wide_biases(bias_row):
    bias8 = jnp.broadcast_to(bias_row, (8, BIAS))
    rows = iota((BIAS, WIDE), 0)
    lanes = iota((BIAS, WIDE), 1)
    one = jnp.where((lanes % C1 == rows) & (lanes < OUT1 * C1), 1.0, 0.0)
    two = jnp.where((lanes % C2 + C1 == rows) & (lanes < OUT2 * C2), 1.0, 0.0)
    rows = iota((D, BIAS), 0)
    lanes = iota((D, BIAS), 1)
    three = jnp.where(lanes == rows + C1 + C2, 1.0, 0.0)
    four = jnp.where(lanes == rows + C1 + C2 + D, 1.0, 0.0)
    return (
        dot(bias8, one, precision=HIGH)[0:1],
        dot(bias8, two, precision=HIGH)[0:1],
        dot(three, bias8, 1, 1, precision=HIGH)[:, 0:1],
        dot(four, bias8, 1, 1, precision=HIGH)[:, 0:1],
    )


def encode_one(pixels, band_one, bias, z_one, act_one, frames, chunk):
    half = 4 * WIDE
    rows = chunk * frames
    for first in range(0, OUT1, chunk):
        low = first * frames
        z = dot(pixels[low : low + rows, :], band_one[0:half, :]) + dot(
            pixels[low + frames : low + frames + rows, :], band_one[half : 2 * half, :]
        )
        z = z + bias
        act = (z * sigmoid(z)).astype(BF)
        for step in range(chunk):
            at, part = divmod(first + step, 2)
            spot = (slice(at * frames, (at + 1) * frames), slice(part * WIDE, (part + 1) * WIDE))
            z_one[spot] = z[step * frames : (step + 1) * frames]
            act_one[spot] = act[step * frames : (step + 1) * frames]


def encode_two(act_one, band_two, bias, z_two, act_two, frames, chunk):
    half = 2 * WIDE
    rows = chunk * frames
    for first in range(0, OUT2, chunk):
        low = first * frames
        z = dot(act_one[low : low + rows, :], band_two[0:half, :]) + dot(
            act_one[low + frames : low + frames + rows, :], band_two[half : 2 * half, :]
        )
        z = z + bias
        z_two[low : low + rows] = z
        act = (z * sigmoid(z)).astype(BF)
        for step in range(chunk):
            at = (first + step) * FEATS_ROW
            act_two[:, at : at + FEATS_ROW] = act[step * frames : (step + 1) * frames, :FEATS_ROW]


def back_two(dstate_t, linear_t, z_two, dz_two, frames):
    dact = dot(dstate_t, linear_t, 0, 0)
    dz_two[0:frames] = jnp.zeros((frames, WIDE), BF)
    dz_two[(OUT2 + 1) * frames : (OUT2 + 2) * frames] = jnp.zeros((frames, WIDE), BF)
    blank = jnp.zeros((frames, WIDE - FEATS_ROW), F32)
    for at in range(OUT2):
        z = z_two[at * frames : (at + 1) * frames]
        part = jnp.concatenate([dact[:, at * FEATS_ROW : (at + 1) * FEATS_ROW], blank], axis=1)
        dz_two[(at + 1) * frames : (at + 2) * frames] = (part * slope(z, sigmoid(z))).astype(BF)


def back_one(dz_two, band_two, z_one, dz_one, frames, chunk):
    half = 2 * WIDE
    rows = chunk * frames
    for first in range(0, OUT1 // 2, chunk):
        low = first * frames
        dact = dot(dz_two[low + frames : low + frames + rows], band_two[0:half], 1, 1) + dot(
            dz_two[low : low + rows], band_two[half : 2 * half], 1, 1
        )
        z = z_one[low : low + rows]
        dz = (dact * slope(z, sigmoid(z))).astype(BF)
        for step in range(chunk):
            for part in range(2):
                at = (2 * (first + step) + part) * frames
                dz_one[at : at + frames] = dz[
                    step * frames : (step + 1) * frames, part * WIDE : (part + 1) * WIDE
                ]


def band_sums(full, base, outputs, width):
    per_tile = 128 // width
    lane = iota((width, 128), 1) // width
    sums = []
    for shift in range(2):
        total = None
        for spot in range(per_tile):
            part = None
            for position in range(outputs):
                tile, inside = divmod(position + shift, per_tile)
                if inside != spot:
                    continue
                term = full[
                    position * width : (position + 1) * width,
                    base + tile * 128 : base + (tile + 1) * 128,
                ]
                part = term if part is None else part + term
            if part is None:
                continue
            part = jnp.where(lane == spot, part, 0.0)
            total = part if total is None else total + part
        sums.append(fold(total, width))
    return sums


def kernel_grad(full_pairs, outputs, width, taps_per):
    tiles = []
    lane = iota((width, 128), 1) // width
    pieces = []
    for full in full_pairs:
        for tap in range(taps_per):
            pieces.extend(band_sums(full, tap * WIDE, outputs, width))
    per_tile = 128 // width
    for tile in range(2):
        total = jnp.zeros((width, 128), F32)
        for spot in range(per_tile):
            total = jnp.where(lane == spot, pieces[tile * per_tile + spot], total)
        tiles.append(total)
    return jnp.concatenate(tiles, axis=1)


def tiled(tile, count):
    return jnp.concatenate([tile] * count, axis=1)


def twice(row):
    return jnp.concatenate([row, row], axis=1)


def plan(states, mats_t, emb_t, heads_t, bias_col, options, legal, games, valid, rewards, returns, scale):
    frames = states.shape[1]
    pairs = OPTS // 2
    lanes = OPTS * frames
    trans_in, trans_out, value_in = mats_t
    low_half = iota((1, 128), 1) < frames
    upper = iota((1, 128), 1) // frames

    valid_f = [twice(v.astype(F32)) for v in valid]
    rewards = [twice(r) for r in rewards]
    returns = [twice(r) for r in returns]
    chosen = [twice(o) for o in options]
    game = twice(games)

    game_rows = iota((24, WIDE), 0)
    game_pick = jnp.where(
        game_rows == tiled(game, 3) + GAMES * (iota((24, WIDE), 1) // 128), 1.0, 0.0
    ).astype(BF)
    head_rows = dot(heads_t, game_pick)
    hr, hd, hv = (head_rows[:, k * 128 : (k + 1) * 128] for k in range(3))

    option_rows = jnp.where(
        iota((32, lanes), 0) == iota((32, lanes), 1) // frames, 1.0, 0.0
    ).astype(BF)
    s_low = twice(states)
    s_f = s_low.astype(F32)
    base = dot(trans_in, s_low)
    pre = tiled(base, pairs) + dot(emb_t, option_rows)
    sig_h = sigmoid(pre)
    hid = pre * sig_h
    hid_low = hid.astype(BF)
    after = tiled(s_f, pairs) + dot(trans_out, hid_low)
    after_low = after.astype(BF)
    judge_pre = dot(value_in, after_low) + bias_col
    sig_j = sigmoid(judge_pre)
    judged = judge_pre * sig_j

    def tile_of(value, k):
        return value[:, k * 128 : (k + 1) * 128]

    def over(value):
        return jnp.sum(value, axis=0, keepdims=True)

    reward = [over(tile_of(hid, k) * hr) for k in range(pairs)]
    gamma = [sigmoid(over(tile_of(hid, k) * hd)) for k in range(pairs)]
    value = [over(tile_of(judged, k) * hv) for k in range(pairs)]
    backed = [reward[k] + gamma[k] * value[k] for k in range(pairs)]
    allowed = [
        jnp.concatenate([legal[2 * k], legal[2 * k + 1]], axis=1) > 0 for k in range(pairs)
    ]
    highest = functools.reduce(
        jnp.maximum, [jnp.where(allowed[k], backed[k], -1e30) for k in range(pairs)]
    )
    highest = jnp.maximum(highest, turn(highest, frames))
    shares = [
        jnp.where(allowed[k], jnp.exp(jnp.where(allowed[k], backed[k] - highest, -60.0)), 0.0)
        for k in range(pairs)
    ]

    def halves(total):
        return total + turn(total, frames)

    share_sum = halves(sum(shares))
    planned = halves(sum(shares[k] * backed[k] for k in range(pairs))) / share_sum
    choose = [chosen[0] == 2 * k + upper for k in range(pairs)]

    def chosen_of(parts):
        return halves(sum(jnp.where(choose[k], parts[k], 0.0) for k in range(pairs)))

    roll_f = [chosen_of([tile_of(after, k) for k in range(pairs)])]
    roll_low = [roll_f[0].astype(BF)]
    plan_miss = planned - returns[0]
    reward_miss = [chosen_of(reward) - rewards[0]]
    value_miss = [chosen_of(value) - returns[1]]
    steps = len(options)
    picks, pre_k, sig_k, hid_k, hid_k_low, judge_k, sig_jk, judged_k = ([None] for _ in range(8))
    for k in range(1, steps):
        picks.append(jnp.where(iota((32, 128), 0) == chosen[k], 1.0, 0.0).astype(BF))
        pre_k.append(dot(trans_in, roll_low[k - 1]) + dot(emb_t, picks[k]))
        sig_k.append(sigmoid(pre_k[k]))
        hid_k.append(pre_k[k] * sig_k[k])
        hid_k_low.append(hid_k[k].astype(BF))
        roll_f.append(roll_f[k - 1] + dot(trans_out, hid_k_low[k]))
        roll_low.append(roll_f[k].astype(BF))
        judge_k.append(dot(value_in, roll_low[k]) + bias_col)
        sig_jk.append(sigmoid(judge_k[k]))
        judged_k.append(judge_k[k] * sig_jk[k])
        reward_miss.append(over(hid_k[k] * hr) - rewards[k])
        value_miss.append(over(judged_k[k] * hv) - returns[k + 1])
    errors = valid_f[0] * plan_miss * plan_miss
    for k in range(steps):
        errors = errors + valid_f[k] * (
            reward_miss[k] * reward_miss[k] + value_miss[k] * value_miss[k]
        )
    errors = jnp.where(low_half, errors * scale, 0.0)

    half = jnp.where(low_half, 1.0, 0.0)
    double = 2.0 * scale
    d_plan = double * valid_f[0] * plan_miss / share_sum
    d_reward_k = [double * valid_f[k] * reward_miss[k] for k in range(steps)]
    d_value_k = [double * valid_f[k] * value_miss[k] for k in range(steps)]

    def through(matrix_t, grad):
        return dot(matrix_t, grad, 0, 0)

    d_roll = None
    d_judge_low, d_step_low, d_pre_low = ([None] * steps for _ in range(3))
    d_hr = jnp.zeros((D, 128), F32)
    d_hd = jnp.zeros((D, 128), F32)
    d_hv = jnp.zeros((D, 128), F32)
    for k in range(steps - 1, 0, -1):
        d_judge_low[k] = (d_value_k[k] * hv * slope(judge_k[k], sig_jk[k])).astype(BF)
        term = through(value_in, d_judge_low[k])
        d_roll = term if d_roll is None else d_roll + term
        d_step_low[k] = d_roll.astype(BF)
        d_hid = through(trans_out, d_step_low[k]) + d_reward_k[k] * hr
        d_pre_low[k] = (d_hid * slope(pre_k[k], sig_k[k])).astype(BF)
        d_roll = d_roll + through(trans_in, d_pre_low[k])
        d_hr = d_hr + (half * d_reward_k[k]) * hid_k[k]
        d_hv = d_hv + (half * d_value_k[k]) * judged_k[k]

    d_backed = [d_plan * shares[k] * (1.0 + backed[k] - planned) for k in range(pairs)]
    d_reward = [
        d_backed[k] + jnp.where(choose[k], d_reward_k[0], 0.0) for k in range(pairs)
    ]
    d_value = [
        d_backed[k] * gamma[k] + jnp.where(choose[k], d_value_k[0], 0.0) for k in range(pairs)
    ]
    d_gamma = [d_backed[k] * value[k] * gamma[k] * (1.0 - gamma[k]) for k in range(pairs)]
    d_judge = [
        (d_value[k] * hv * slope(tile_of(judge_pre, k), tile_of(sig_j, k))).astype(BF)
        for k in range(pairs)
    ]
    d_judge_all = jnp.concatenate(d_judge, axis=1)
    d_after = through(value_in, d_judge_all)
    d_after = [
        tile_of(d_after, k) + jnp.where(choose[k], d_roll, 0.0) for k in range(pairs)
    ]
    d_after_low = jnp.concatenate([d.astype(BF) for d in d_after], axis=1)
    d_hid_all = through(trans_out, d_after_low)
    d_pre = [
        (
            (tile_of(d_hid_all, k) + d_reward[k] * hr + d_gamma[k] * hd)
            * slope(tile_of(pre, k), tile_of(sig_h, k))
        ).astype(BF)
        for k in range(pairs)
    ]
    d_pre_all = jnp.concatenate(d_pre, axis=1)
    d_base = through(trans_in, d_pre_all)
    d_state = halves(sum(d_after[k] + tile_of(d_base, k) for k in range(pairs)))
    for k in range(pairs):
        d_hr = d_hr + d_reward[k] * tile_of(hid, k)
        d_hd = d_hd + d_gamma[k] * tile_of(hid, k)
        d_hv = d_hv + d_value[k] * tile_of(judged, k)

    def both(parts):
        joined = [jnp.where(low_half, parts[k].astype(F32), parts[k + 1].astype(F32)) for k in range(1, steps, 2)]
        return [part.astype(BF) for part in joined]

    def with_steps(wide, parts):
        return jnp.concatenate([wide] + both(parts), axis=1)

    before_low = [None] + roll_low[:-1]
    d_pre_cat = with_steps(d_pre_all, d_pre_low)
    d_judge_cat = with_steps(d_judge_all, d_judge_low)
    grad_in = dot(d_pre_cat, with_steps(tiled(s_low, pairs), before_low), 1, 1)
    grad_out = dot(
        with_steps(d_after_low, d_step_low), with_steps(hid_low, hid_k_low), 1, 1
    )
    grad_value = dot(d_judge_cat, with_steps(after_low, roll_low), 1, 1)
    grad_emb = dot(d_pre_cat, with_steps(option_rows, picks), 1, 1)
    grad_heads = dot(
        jnp.concatenate([d_hr, d_hd, d_hv], axis=1), game_pick.astype(F32), 1, 1, precision=HIGH
    )
    grad_bias = jnp.sum(d_judge_cat.astype(F32), axis=1, keepdims=True)
    return (
        d_state[:, :frames],
        (grad_in, grad_out, grad_value),
        grad_emb,
        grad_heads,
        grad_bias,
        errors,
    )


def frame_rows(section, refs):
    options_ref, legal_ref, games_ref, valid_ref, rewards_ref, returns_ref = refs

    def row(ref, k):
        return ref[k, pl.ds(section, 1), :]

    depth = options_ref.shape[0]
    return (
        [row(options_ref, k) for k in range(depth)],
        [row(legal_ref, k) for k in range(OPTS)],
        games_ref[pl.ds(section, 1), :],
        [row(valid_ref, k) for k in range(depth)],
        [row(rewards_ref, k) for k in range(depth)],
        [returns_ref[section, k : k + 1, :] for k in range(depth + 1)],
    )


def clear_tails(pixels):
    tail = jnp.zeros((pixels.shape[0], WIDE - 336), BF)
    for part in range(4):
        pixels[:, part * WIDE + 336 : (part + 1) * WIDE] = tail


def grad_kernel_two(act_one, dz_two, frames):
    rows = OUT2 * frames
    d_two = dz_two[frames : frames + rows]
    grad = kernel_grad(
        [dot(d_two, act_one[0:rows], 0, 0), dot(d_two, act_one[frames : frames + rows], 0, 0)],
        OUT2,
        C2,
        2,
    )
    return grad, fold(tiles_sum(dot(jnp.ones((8, rows), BF), d_two)), C2)


def grad_kernel_one(pixels, dz_one, frames):
    rows = OUT1 * frames
    d_one = dz_one[...]
    grad = kernel_grad(
        [dot(d_one, pixels[0:rows], 0, 0), dot(d_one, pixels[frames : frames + rows], 0, 0)],
        OUT1,
        C1,
        4,
    )
    return grad, fold(tiles_sum(dot(jnp.ones((8, rows), BF), d_one)), C1)


def local_kernel(
    frames_hbm,
    kernels_ref,
    linear_ref,
    mats_ref,
    emb_ref,
    heads_ref,
    bias_ref,
    options_ref,
    legal_ref,
    games_ref,
    valid_ref,
    rewards_ref,
    returns_ref,
    lin_out,
    mats_out,
    emb_out,
    heads_out,
    conv_out,
    small_out,
    frame_buf,
    pixels,
    band_one,
    band_two,
    z_one,
    act_one,
    z_two,
    act_two,
    dz_two,
    dz_one,
    sems,
):
    section = lax.axis_index("section")
    frames = frame_buf.shape[1]
    copies = load_frames(frames_hbm, section, frame_buf, sems, CHUNK)
    for copy in copies:
        copy.start()
    build_bands(kernels_ref[...], band_one, band_two)
    bias_one, bias_two, bias_three, bias_four = wide_biases(bias_ref[...])
    clear_tails(pixels)
    for which, copy in enumerate(copies):
        copy.wait()
        place_frames(frame_buf, pixels, which * CHUNK, CHUNK, frames)
    encode_one(pixels, band_one, bias_one, z_one, act_one, frames, 4)
    encode_two(act_one, band_two, bias_two, z_two, act_two, frames, 3)
    linear_t = linear_ref[...]
    states = (dot(linear_t, act_two[...], 1, 1) + bias_three).astype(BF)
    d_state, grad_mats, grad_emb, grad_heads, grad_bias, errors = plan(
        states,
        tuple(mats_ref[k] for k in range(3)),
        emb_ref[:, 0:32],
        heads_ref[:, 0:24],
        bias_four,
        *frame_rows(
            section, (options_ref, legal_ref, games_ref, valid_ref, rewards_ref, returns_ref)
        ),
        1.0,
    )
    for k in range(3):
        mats_out[k] = grad_mats[k]
    emb_out[...] = jnp.concatenate([grad_emb, jnp.zeros((D, 96), F32)], axis=1)
    heads_out[...] = jnp.concatenate([grad_heads, jnp.zeros((D, 104), F32)], axis=1)
    d_state_low = d_state.astype(BF)
    lin_out[...] = dot(d_state_low, act_two[...])
    back_two(d_state_low, linear_t, z_two, dz_two, frames)
    grad_two, bias_two_grad = grad_kernel_two(act_one, dz_two, frames)
    back_one(dz_two, band_two, z_one, dz_one, frames, 5)
    grad_one, bias_one_grad = grad_kernel_one(pixels, dz_one, frames)
    conv_out[...] = stack_kernels(grad_one, grad_two)
    lane = iota((8, 128), 1)
    line = iota((8, 128), 0)
    row_zero = jnp.where(
        lane < C1, bias_one_grad, jnp.where(lane < C1 + C2, turn(bias_two_grad, C1), 0.0)
    )
    count = sum(
        valid_ref[k, pl.ds(section, 1), :].astype(F32) for k in range(valid_ref.shape[0])
    )
    count = jnp.where(iota((1, 128), 1) < frames, twice(count), 0.0)
    small = jnp.where(line == 0, row_zero, 0.0)
    small = jnp.where(line == 1, row_of(lane_sum(d_state_low)), small)
    small = jnp.where(line == 2, row_of(grad_bias), small)
    small = jnp.where(line == 3, errors, small)
    small = jnp.where(line == 4, count, small)
    small_out[...] = small


def lane_sum(value):
    return jnp.sum(value.astype(F32), axis=1, keepdims=True)


def stack_kernels(grad_one, grad_two):
    rows = jnp.concatenate([grad_one, grad_two, jnp.zeros((128 - C1 - C2, KERN), F32)], axis=0)
    return rows.T


def tiles_sum(value):
    return sum(value[:, k * 128 : (k + 1) * 128] for k in range(value.shape[1] // 128))


VMEM_SPEC = pl.BlockSpec(memory_space=pltpu.VMEM)
ANY_SPEC = pl.BlockSpec(memory_space=pl.ANY)


def local_scratch(frames, side):
    return [
        pltpu.VMEM((side, frames, 336), BF),
        pltpu.VMEM(((OUT1 + 1) * frames, 4 * WIDE), BF),
        pltpu.VMEM((8 * WIDE, WIDE), BF),
        pltpu.VMEM((4 * WIDE, WIDE), BF),
        pltpu.VMEM((OUT1 // 2 * frames, 2 * WIDE), F32),
        pltpu.VMEM((OUT1 // 2 * frames, 2 * WIDE), BF),
        pltpu.VMEM((OUT2 * frames, WIDE), F32),
        pltpu.VMEM((frames, FEAT), BF),
        pltpu.VMEM(((OUT2 + 2) * frames, WIDE), BF),
        pltpu.VMEM((OUT1 * frames, WIDE), BF),
        pltpu.SemaphoreType.DMA((side // CHUNK,)),
    ]


def local_step(frames, kernels, linear_t, mats_t, emb_t, heads_t, biases, options, legal, games, valid, rewards, returns):
    count = frames.shape[1]
    side = frames.shape[2]
    shapes = [(D, FEAT), (3, D, D), (D, 128), (D, 128), (KERN, 128), (8, 128)]
    return pl.pallas_call(
        local_kernel,
        out_shape=[jax.ShapeDtypeStruct(shape, F32) for shape in shapes],
        in_specs=[ANY_SPEC] + [VMEM_SPEC] * 12,
        out_specs=[VMEM_SPEC] * len(shapes),
        scratch_shapes=local_scratch(count, side),
        compiler_params=pltpu.CompilerParams(vmem_limit_bytes=56 * 1024 * 1024),
    )(
        frames.transpose(0, 2, 1, 3),
        kernels,
        linear_t,
        mats_t,
        emb_t,
        heads_t,
        biases.reshape(1, BIAS),
        options.transpose(2, 0, 1),
        legal.transpose(2, 0, 1),
        games,
        valid.transpose(2, 0, 1),
        rewards.transpose(2, 0, 1),
        returns.transpose(0, 2, 1),
    )


MESH = pl.DeviceIdType.MESH
LIN_PAD = 2688
QUARTER = 896
HALF = 2 * QUARTER
AT_MATS = LIN_PAD
AT_EMB = AT_MATS + 3 * D
AT_HEADS = AT_EMB + 128
AT_END = AT_HEADS + 128


def fused_kernel(
    peers,
    frames_hbm,
    conv_ref,
    lin_ref,
    mats_ref,
    emb_ref,
    heads_ref,
    bias_ref,
    options_ref,
    legal_ref,
    games_ref,
    valid_ref,
    rewards_ref,
    returns_ref,
    main_out,
    conv_out,
    tile_out,
    stats_out,
    frame_buf,
    pixels,
    band_one,
    band_two,
    z_one,
    act_one,
    z_two,
    act_two,
    dz_two,
    dz_one,
    frame_sems,
    stage,
    kernel_msg,
    weight_msg,
    weights,
    grad_own,
    grad_mate,
    grad_msg,
    grad_in,
    tile_msg,
    tile_in,
    stats_in,
    half_in,
    conv_half_in,
    send_sems,
    recv_sems,
    all_send,
    all_recv,
    mate_send,
    mate_recv,
):
    section = lax.axis_index("section")
    place = lax.axis_index("dp")
    mate = 1 - section
    frames = frame_buf.shape[1]
    everyone = 2 * peers

    barrier = pltpu.get_barrier_semaphore()

    def other(step):
        flat = lax.rem(section * peers + place + step, everyone)
        return flat // peers, lax.rem(flat, peers)

    def greet(step, carry):
        to_section, to_place = other(step)
        pl.semaphore_signal(barrier, inc=1, device_id=(to_section, to_place), device_id_type=MESH)
        return carry

    lax.fori_loop(1, everyone, greet, 0)
    copies = load_frames(frames_hbm, section, frame_buf, frame_sems, CHUNK)
    for copy in copies:
        copy.start()

    def to_peer(phase, step, source, target):
        peer = lax.rem(place + step, peers)
        return pltpu.make_async_remote_copy(
            src_ref=source(peer),
            dst_ref=target.at[place],
            send_sem=send_sems.at[phase, step],
            recv_sem=recv_sems.at[phase, place],
            device_id=(section, peer),
            device_id_type=MESH,
        )

    def from_peer(phase, step, target):
        peer = lax.rem(place + step, peers)
        return pltpu.make_async_remote_copy(
            src_ref=target.at[peer],
            dst_ref=target.at[peer],
            send_sem=send_sems.at[phase, step],
            recv_sem=recv_sems.at[phase, peer],
            device_id=(section, peer),
            device_id_type=MESH,
        )

    def each_peer(act):
        def body(step, carry):
            act(step)
            return carry

        lax.fori_loop(1, peers, body, 0)

    def to_other(phase, step, source, target):
        to_section, to_place = other(step)
        return pltpu.make_async_remote_copy(
            src_ref=source(to_section, to_place),
            dst_ref=target.at[section, place],
            send_sem=all_send.at[phase, step],
            recv_sem=all_recv.at[phase, section, place],
            device_id=(to_section, to_place),
            device_id_type=MESH,
        )

    def from_other(phase, step, target):
        its_section, its_place = other(step)
        return pltpu.make_async_remote_copy(
            src_ref=target.at[its_section, its_place],
            dst_ref=target.at[its_section, its_place],
            send_sem=all_send.at[phase, step],
            recv_sem=all_recv.at[phase, its_section, its_place],
            device_id=(its_section, its_place),
            device_id_type=MESH,
        )

    def each_other(act):
        def body(step, carry):
            act(step)
            return carry

        lax.fori_loop(1, everyone, body, 0)

    def to_mate(which, source, target):
        return pltpu.make_async_remote_copy(
            src_ref=source,
            dst_ref=target,
            send_sem=mate_send.at[which],
            recv_sem=mate_recv.at[which],
            device_id=(mate, place),
            device_id_type=MESH,
        )

    upper_lanes = iota((16, 128), 1) >= 64
    counts = sum(
        valid_ref[k, m : m + 1, :].astype(F32)
        for k in range(valid_ref.shape[0])
        for m in range(valid_ref.shape[1])
    )
    conv_pad = jnp.concatenate([conv_ref[...], jnp.zeros((16, 80), F32)], axis=1)
    kernel_msg[place] = jnp.where(
        upper_lanes & (iota((16, 128), 0) == 0), jnp.broadcast_to(twice(counts), (16, 128)), conv_pad
    ).astype(BF)
    heads_pad = jnp.concatenate([heads_ref[...], jnp.zeros((24, 120), F32)], axis=1)
    heads_pad = jnp.concatenate([heads_pad, jnp.zeros((104, 128), F32)], axis=0).T
    stage[:, 0:FEAT] = lin_ref[...]
    stage[:, FEAT:LIN_PAD] = jnp.zeros((8, LIN_PAD - FEAT), F32)
    for k in range(3):
        stage[:, AT_MATS + k * D : AT_MATS + (k + 1) * D] = mats_ref[k]
    stage[:, AT_EMB:AT_HEADS] = jnp.concatenate(
        [emb_ref[...], jnp.zeros((8, 128 - OPTS), F32)], axis=1
    )
    stage[:, AT_HEADS:AT_END] = heads_pad[0:8]
    stage[:, AT_END : 2 * HALF] = jnp.zeros((8, 2 * HALF - AT_END), F32)
    first = stage[:, pl.ds(pl.multiple_of(section * HALF, 128), QUARTER)]
    second = stage[:, pl.ds(pl.multiple_of(section * HALF + QUARTER, 128), QUARTER)]
    weight_msg[section, place] = jnp.concatenate([first, second], axis=0).astype(BF)

    pl.semaphore_wait(barrier, everyone - 1)
    own_kernel = lambda peer: kernel_msg.at[place]
    own_weight = lambda peer: weight_msg.at[section, place]
    each_peer(lambda step: to_peer(0, step, own_kernel, kernel_msg).start())
    each_peer(lambda step: to_peer(1, step, own_weight, weight_msg.at[section]).start())

    bias_one, bias_two, bias_three, bias_four = wide_biases(bias_ref[...])
    clear_tails(pixels)
    act_two[:, FEAT:LIN_PAD] = jnp.zeros((frames, LIN_PAD - FEAT), BF)
    for which, copy in enumerate(copies):
        copy.wait()
        place_frames(frame_buf, pixels, which * CHUNK, CHUNK, frames)
    each_peer(lambda step: from_peer(0, step, kernel_msg).wait_recv())
    kernels = kernel_msg[...].reshape(KERN, 128)
    counted = jnp.where(iota((KERN, 128), 1) >= 64, kernels.astype(F32), 0.0)
    count = jnp.sum(jnp.sum(counted, axis=0, keepdims=True), axis=1, keepdims=True)
    scale = 1.0 / count
    build_bands(kernels, band_one, band_two)
    encode_one(pixels, band_one, bias_one, z_one, act_one, frames, 4)
    each_peer(lambda step: from_peer(1, step, weight_msg.at[section]).wait_recv())
    pass_weights = to_mate(0, weight_msg.at[section], weight_msg.at[section])
    pass_weights.start()
    encode_two(act_one, band_two, bias_two, z_two, act_two, frames, 3)
    to_mate(0, weight_msg.at[section], weight_msg.at[mate]).wait_recv()
    for half in range(2):
        block = weight_msg[half].astype(F32)
        for part in range(2):
            lane = (2 * half + part) * QUARTER
            weights[:, lane : lane + QUARTER] = (
                block[:, part * 8 : (part + 1) * 8].reshape(D, QUARTER).astype(BF)
            )
    linear_t = weights[:, 0:LIN_PAD]
    states = (dot(linear_t, act_two[...], 1, 1) + bias_three).astype(BF)
    d_state, grad_mats, grad_emb, grad_heads, grad_bias, errors = plan(
        states,
        tuple(weights[:, AT_MATS + k * D : AT_MATS + (k + 1) * D] for k in range(3)),
        weights[:, AT_EMB : AT_EMB + 32],
        weights[:, AT_HEADS : AT_HEADS + 24],
        bias_four,
        *frame_rows(
            section, (options_ref, legal_ref, games_ref, valid_ref, rewards_ref, returns_ref)
        ),
        scale,
    )

    d_state_low = d_state.astype(BF)
    grad_linear = dot(d_state_low, act_two[...])
    grad_own[0] = grad_linear[:, 0:HALF].reshape(peers, 8, HALF)
    grad_own[1, :, :, 0 : LIN_PAD - HALF] = grad_linear[:, HALF:LIN_PAD].reshape(
        peers, 8, LIN_PAD - HALF
    )
    for k in range(3):
        lane = AT_MATS - HALF + k * D
        grad_own[1, :, :, lane : lane + D] = grad_mats[k].reshape(peers, 8, D)
    lane = AT_EMB - HALF
    grad_own[1, :, :, lane : lane + 128] = jnp.concatenate(
        [grad_emb, jnp.zeros((D, 96), F32)], axis=1
    ).reshape(peers, 8, 128)
    grad_own[1, :, :, lane + 128 : lane + 256] = jnp.concatenate(
        [grad_heads, jnp.zeros((D, 104), F32)], axis=1
    ).reshape(peers, 8, 128)
    grad_own[1, :, :, lane + 256 : HALF] = jnp.zeros((peers, 8, 2 * HALF - AT_END), F32)
    pass_grads = to_mate(1, grad_own.at[mate], grad_mate)
    pass_grads.start()
    back_two(d_state_low, linear_t, z_two, dz_two, frames)
    grad_two, bias_two_grad = grad_kernel_two(act_one, dz_two, frames)
    pass_grads.wait_recv()
    paired = grad_own[section] + grad_mate[...]
    grad_msg[...] = jnp.concatenate(
        [paired[:, :, 0:QUARTER], paired[:, :, QUARTER:HALF]], axis=1
    ).astype(BF)
    each_peer(lambda step: to_peer(2, step, lambda peer: grad_msg.at[peer], grad_in).start())
    grad_in[place] = grad_msg[place]
    back_one(dz_two, band_two, z_one, dz_one, frames, 5)
    grad_one, bias_one_grad = grad_kernel_one(pixels, dz_one, frames)

    conv_rows = stack_kernels(grad_one, grad_two).reshape(everyone, 8, 128)
    lane = iota((8, 128), 1)
    line = iota((8, 128), 0)
    row_three = row_of(lane_sum(d_state_low))
    row_four = row_of(grad_bias)
    row_first = jnp.where(
        lane < C1, bias_one_grad, jnp.where(lane < C1 + C2, turn(bias_two_grad, C1), 0.0)
    )
    rows = [turn(row_three, 64), row_three, turn(row_four, 64), row_four, turn(row_first, 64)[0:1], turn(errors, 64)]
    extra = jnp.zeros((8, 128), F32)
    for which, row in enumerate(rows):
        extra = jnp.where(line == which, row, extra)
    tiles = jnp.where(iota((everyone, 8, 128), 2) >= 64, extra[None], conv_rows)
    tile_msg[...] = tiles.reshape(peers, 2, 8, 128)
    each_other(
        lambda step: to_other(0, step, lambda s, d: tile_msg.at[d, s], tile_in).start()
    )
    tile_in[section, place] = tile_msg[place, section]
    each_peer(lambda step: from_peer(2, step, grad_in).wait_recv())
    total = jnp.sum(grad_in[...].astype(F32), axis=0)
    squares = total * total
    stat = jnp.zeros((16, 128), F32)
    stat_line = iota((16, 128), 0)
    for part in range(2):
        sums = jnp.sum(squares[part * 8 : (part + 1) * 8], axis=0, keepdims=True)
        for tile in range(7):
            stat = jnp.where(
                stat_line == part * 7 + tile, sums[:, tile * 128 : (tile + 1) * 128], stat
            )
    each_other(lambda step: from_other(0, step, tile_in).wait_recv())
    tile_total = jnp.sum(tile_in[...].reshape(everyone, 8, 128), axis=0)
    conv_squares = jnp.where(lane < C1 + C2, tile_total * tile_total, 0.0)
    stat = jnp.where(stat_line == 14, jnp.sum(conv_squares, axis=0, keepdims=True), stat)

    def square_sum(value):
        return jnp.sum(jnp.sum(value * value, axis=0, keepdims=True), axis=1, keepdims=True)

    weight_squares = [
        square_sum(conv_pad),
        square_sum(lin_ref[...]),
        sum(square_sum(mats_ref[k]) for k in range(3)),
        square_sum(emb_ref[...]),
        square_sum(heads_ref[...]),
    ]
    for which, value in enumerate(weight_squares):
        stat = jnp.where((stat_line == 15) & (iota((16, 128), 1) == which), value, stat)
    stats_in[section, place] = stat
    own_half = jnp.concatenate([total[0:8], total[8:16]], axis=1)
    half_in[section] = own_half
    conv_half_in[section] = tile_total
    each_other(
        lambda step: to_other(
            1, step, lambda s, d: stats_in.at[section, place], stats_in
        ).start()
    )
    pass_half = to_mate(2, half_in.at[section], half_in.at[section])
    pass_half.start()
    pass_conv = to_mate(3, conv_half_in.at[section], conv_half_in.at[section])
    pass_conv.start()
    tile_out[...] = tile_total
    to_mate(2, half_in.at[section], half_in.at[mate]).wait_recv()
    to_mate(3, conv_half_in.at[section], conv_half_in.at[mate]).wait_recv()
    for half in range(2):
        main_out[:, half * HALF : (half + 1) * HALF] = half_in[half]
        conv_out[half * 8 : (half + 1) * 8] = conv_half_in[half]
    each_other(lambda step: from_other(1, step, stats_in).wait_recv())
    stats_out[...] = jnp.sum(stats_in[...], axis=1)

    each_peer(lambda step: to_peer(0, step, own_kernel, kernel_msg).wait_send())
    each_peer(lambda step: to_peer(1, step, own_weight, weight_msg.at[section]).wait_send())
    each_peer(lambda step: to_peer(2, step, lambda peer: grad_msg.at[peer], grad_in).wait_send())
    each_other(
        lambda step: to_other(0, step, lambda s, d: tile_msg.at[d, s], tile_in).wait_send()
    )
    each_other(
        lambda step: to_other(
            1, step, lambda s, d: stats_in.at[section, place], stats_in
        ).wait_send()
    )
    for copy in (pass_weights, pass_grads, pass_half, pass_conv):
        copy.wait_send()


def fused_step(peers, frames, shards, biases, rows):
    count = frames.shape[1]
    side = frames.shape[2]
    scratch = local_scratch(count, side)
    scratch[7] = pltpu.VMEM((count, LIN_PAD), BF)
    scratch += [
        pltpu.VMEM((8, 2 * HALF), F32),
        pltpu.VMEM((peers, 16, 128), BF),
        pltpu.VMEM((2, peers, 16, QUARTER), BF),
        pltpu.VMEM((D, 2 * HALF), BF),
        pltpu.VMEM((2, peers, 8, HALF), F32),
        pltpu.VMEM((peers, 8, HALF), F32),
        pltpu.VMEM((peers, 16, QUARTER), BF),
        pltpu.VMEM((peers, 16, QUARTER), BF),
        pltpu.VMEM((peers, 2, 8, 128), F32),
        pltpu.VMEM((2, peers, 8, 128), F32),
        pltpu.VMEM((2, peers, 16, 128), F32),
        pltpu.VMEM((2, 8, HALF), F32),
        pltpu.VMEM((2, 8, 128), F32),
        pltpu.SemaphoreType.DMA((3, peers)),
        pltpu.SemaphoreType.DMA((3, peers)),
        pltpu.SemaphoreType.DMA((2, 2 * peers)),
        pltpu.SemaphoreType.DMA((2, 2, peers)),
        pltpu.SemaphoreType.DMA((4,)),
        pltpu.SemaphoreType.DMA((4,)),
    ]
    shapes = [(8, 2 * HALF), (16, 128), (8, 128), (2, 16, 128)]
    operands = [frames.transpose(0, 2, 1, 3), *shards, biases.reshape(1, BIAS), *rows]
    return pl.pallas_call(
        functools.partial(fused_kernel, peers),
        out_shape=[jax.ShapeDtypeStruct(shape, F32) for shape in shapes],
        in_specs=[ANY_SPEC] + [VMEM_SPEC] * (len(operands) - 1),
        out_specs=[VMEM_SPEC] * len(shapes),
        scratch_shapes=scratch,
        compiler_params=pltpu.CompilerParams(
            vmem_limit_bytes=56 * 1024 * 1024, collective_id=0, has_side_effects=True
        ),
    )(*operands)


def column_of(row):
    square = jnp.broadcast_to(row, (8, 8))
    return jnp.sum(jnp.where(iota((8, 8), 0) == iota((8, 8), 1), square, 0.0), axis=1, keepdims=True)


def row_back(column):
    square = jnp.broadcast_to(column, (8, 8))
    return jnp.sum(jnp.where(iota((8, 8), 0) == iota((8, 8), 1), square, 0.0), axis=0, keepdims=True)


def total_of(value):
    return jnp.sum(jnp.sum(value, axis=0, keepdims=True), axis=1, keepdims=True)


def update_kernel(
    main_ref,
    convg_ref,
    tile_ref,
    stats_ref,
    conv_ref,
    lin_ref,
    mats_ref,
    emb_ref,
    heads_ref,
    bias_ref,
    conv_moment,
    lin_rows,
    lin_cols,
    mats_rows,
    mats_cols,
    emb_moment,
    head_moment,
    bias_moment,
    conv_new,
    conv_grad,
    conv_moment_new,
    lin_new,
    lin_grad,
    lin_rows_new,
    lin_cols_new,
    mats_new,
    mats_grad,
    mats_rows_new,
    mats_cols_new,
    emb_new,
    emb_grad,
    emb_moment_new,
    heads_new,
    heads_grad,
    head_moment_new,
    bias_new,
    bias_grad,
    bias_moment_new,
    norm_out,
    loss_out,
    conv_low,
    lin_low,
):
    stats = stats_ref[...]
    tile = tile_ref[...]
    squares = jnp.where(iota((2, 16, 128), 1) < 15, stats, 0.0)
    squares = total_of(squares[0] + squares[1])
    scales = 0.5 * (stats[0] + stats[1])[15:16]
    bias_raw = jnp.concatenate(
        [tile[4:5, 64 : 64 + C1 + C2]] + [tile[k : k + 1, 64:128] for k in range(4)], axis=1
    )
    norm = jnp.sqrt(squares + total_of(bias_raw * bias_raw))
    factor = jnp.minimum(1.0, CLIP_LIMIT / norm)
    norm_out[...] = norm
    loss_out[...] = total_of(tile[5:6, 64:128])

    def simple(weight, grad, moment, square_total, outs):
        new, moment_new = unfactored(
            weight, grad, moment, relative(square_total, weight.size * outs[3])
        )
        outs[0][...] = new
        outs[1][...] = grad
        outs[2][...] = moment_new
        return new

    peers = D // lin_ref.shape[0]
    conv = simple(
        conv_ref[...],
        factor * convg_ref[:, 0 : C1 + C2],
        conv_moment[...],
        scales[:, 0:1],
        (conv_new, conv_grad, conv_moment_new, peers),
    )
    conv_low[...] = conv.astype(BF)
    simple(
        emb_ref[...],
        factor * main_ref[:, AT_EMB : AT_EMB + OPTS],
        emb_moment[...],
        scales[:, 3:4],
        (emb_new, emb_grad, emb_moment_new, peers),
    )
    heads_t = jnp.concatenate([main_ref[:, AT_HEADS:AT_END], jnp.zeros((120, 128), F32)], axis=0).T
    simple(
        heads_ref[...],
        factor * heads_t[0 : 3 * GAMES, 0:8],
        head_moment[...],
        scales[:, 4:5],
        (heads_new, heads_grad, head_moment_new, peers),
    )
    bias = bias_ref[...]
    simple(
        bias,
        factor * bias_raw,
        bias_moment[...],
        total_of(bias * bias),
        (bias_new, bias_grad, bias_moment_new, 1),
    )
    row_sums = [stats[t // 14, t % 14 : t % 14 + 1] for t in range(24)]

    def factored(weight, grad, rows_old, cols_old, row_sum, square_total, entries):
        rows = DECAY_RATE * rows_old + (1.0 - DECAY_RATE) * (
            factor * factor * row_sum / D + FLOOR_ONE
        )
        wide = grad.shape[1]
        cols = DECAY_RATE * cols_old + (1.0 - DECAY_RATE) * (
            jnp.sum(grad * grad + FLOOR_ONE, axis=1, keepdims=True) / wide
        )
        mean = jnp.sum(rows, axis=1, keepdims=True) / wide
        second = rows * cols / mean
        new = weight - STEP_RATE * relative(square_total, entries) * grad * lax.rsqrt(second)
        return new, rows, cols

    grad = factor * main_ref[:, 0:FEAT]
    new, rows, cols = factored(
        lin_ref[...],
        grad,
        lin_rows[...],
        column_of(lin_cols[...]),
        jnp.concatenate(row_sums[:21], axis=1)[:, 0:FEAT],
        scales[:, 1:2],
        FEAT * D,
    )
    lin_new[...] = new
    lin_grad[...] = grad
    lin_rows_new[...] = rows
    lin_cols_new[...] = row_back(cols)
    lin_low[...] = new.astype(BF)
    for k in range(3):
        grad = factor * main_ref[:, AT_MATS + k * D : AT_MATS + (k + 1) * D]
        new, rows, cols = factored(
            mats_ref[k],
            grad,
            mats_rows[k : k + 1],
            column_of(mats_cols[k : k + 1]),
            row_sums[21 + k],
            scales[:, 2:3],
            3 * D * D,
        )
        mats_new[k] = new
        mats_grad[k] = grad
        mats_rows_new[k : k + 1] = rows
        mats_cols_new[k : k + 1] = row_back(cols)


def fused_device(
    frames,
    options,
    legal,
    games,
    valid,
    rewards,
    returns,
    conv_kernels,
    enc_linear,
    plan_mats,
    option_emb,
    heads,
    biases,
    conv_moment,
    lin_rows,
    lin_cols,
    mats_rows,
    mats_cols,
    emb_moment,
    head_moment,
    bias_moment,
):
    width = enc_linear.shape[1]
    peers = D // width
    shards = (
        conv_kernels,
        enc_linear.T,
        plan_mats.transpose(0, 2, 1),
        option_emb.T,
        heads.reshape(3 * GAMES, width),
    )
    summed = fused_step(
        peers,
        frames,
        shards,
        biases,
        (
            options.transpose(2, 0, 1),
            legal.transpose(2, 0, 1),
            games,
            valid.transpose(2, 0, 1),
            rewards.transpose(2, 0, 1),
            returns.transpose(0, 2, 1),
        ),
    )
    shapes = [(16, 48)] * 3 + [(8, FEAT)] * 2 + [(1, FEAT), (1, 8)] + [(3, 8, D)] * 2 + [(3, D), (3, 8)]
    shapes += [(8, OPTS)] * 3 + [(24, 8)] * 3 + [(1, BIAS)] * 3 + [(1, 1)] * 2
    outs = [jax.ShapeDtypeStruct(shape, F32) for shape in shapes]
    outs += [jax.ShapeDtypeStruct((16, 48), BF), jax.ShapeDtypeStruct((8, FEAT), BF)]
    operands = [
        *summed,
        *shards,
        biases.reshape(1, BIAS),
        conv_moment,
        lin_rows.reshape(1, FEAT),
        lin_cols.reshape(1, width),
        mats_rows,
        mats_cols,
        emb_moment.T,
        head_moment.reshape(3 * GAMES, width),
        bias_moment.reshape(1, BIAS),
    ]
    o = pl.pallas_call(
        update_kernel,
        out_shape=outs,
        in_specs=[VMEM_SPEC] * len(operands),
        out_specs=[VMEM_SPEC] * len(outs),
    )(*operands)
    flat_heads = [h.reshape(3, GAMES, width) for h in o[14:17]]
    return (
        *o[0:3],
        o[3].T,
        o[4].T,
        o[5].reshape(FEAT),
        o[6].reshape(width),
        o[7].transpose(0, 2, 1),
        o[8].transpose(0, 2, 1),
        o[9],
        o[10],
        o[11].T,
        o[12].T,
        o[13].T,
        *flat_heads,
        *[b.reshape(BIAS) for b in o[17:20]],
        o[20].reshape(()),
        o[21].reshape(()),
        o[22],
        o[23].T,
    )


def gather_rows(shard):
    return lax.all_gather(shard, "dp", axis=0, tiled=True)


def relative(square_total, entries):
    return jnp.maximum(FLOOR_TWO, jnp.sqrt(square_total / entries))


def unfactored(weight, grad, moment, scale):
    moment_new = DECAY_RATE * moment + (1.0 - DECAY_RATE) * (grad * grad + FLOOR_ONE)
    return (weight - STEP_RATE * scale * grad * lax.rsqrt(moment_new), moment_new)


def per_device(
    frames,
    options,
    legal,
    games,
    valid,
    rewards,
    returns,
    conv_kernels,
    enc_linear,
    plan_mats,
    option_emb,
    heads,
    biases,
    conv_moment,
    lin_rows,
    lin_cols,
    mats_rows,
    mats_cols,
    emb_moment,
    head_moment,
    bias_moment,
):
    weight_squares = lax.psum(
        (
            jnp.sum(conv_kernels * conv_kernels),
            jnp.sum(enc_linear * enc_linear),
            jnp.sum(plan_mats * plan_mats),
            jnp.sum(option_emb * option_emb),
            jnp.sum(heads * heads),
        ),
        "dp",
    )
    width = enc_linear.shape[1]
    kernels = gather_rows(conv_kernels.astype(BF))
    linear_t = gather_rows(enc_linear.astype(BF).T)
    mats_t = gather_rows(plan_mats.astype(BF).transpose(2, 0, 1)).transpose(1, 0, 2)
    emb_t = gather_rows(option_emb.astype(BF).T)
    heads_t = gather_rows(heads.astype(BF).reshape(3 * GAMES, width).T)
    emb_t = jnp.pad(emb_t, ((0, 0), (0, 128 - OPTS)))
    heads_t = jnp.pad(heads_t, ((0, 0), (0, 128 - 3 * GAMES)))
    lin, mats, emb, hds, conv, small = local_step(
        frames,
        kernels,
        linear_t,
        mats_t,
        emb_t,
        heads_t,
        biases,
        options,
        legal,
        games,
        valid,
        rewards,
        returns,
    )
    rows = jnp.concatenate(
        [lin, mats[0], mats[1], mats[2], emb[:, :OPTS], hds[:, : 3 * GAMES]], axis=1
    )
    rows = lax.psum(lax.psum_scatter(rows, "dp", scatter_dimension=0, tiled=True), "section")
    conv = lax.psum(
        lax.psum_scatter(conv[:, : C1 + C2], "dp", scatter_dimension=0, tiled=True), "section"
    )
    small = lax.psum(small, ("section", "dp"))
    inverse_count = 1.0 / jnp.sum(small[4])
    loss_value = jnp.sum(small[3]) * inverse_count
    bias_raw = (
        jnp.concatenate([small[0, : C1 + C2], small[1], small[2]]) * inverse_count
    )
    rows = rows * inverse_count
    g_conv = conv * inverse_count
    g_lin = rows[:, :FEAT].T
    g_mats = rows[:, FEAT : FEAT + 3 * D].reshape(width, 3, D).transpose(1, 2, 0)
    g_emb = rows[:, FEAT + 3 * D : FEAT + 3 * D + OPTS].T
    g_heads = rows[:, FEAT + 3 * D + OPTS :].T.reshape(3, GAMES, width)
    partial_squares = (
        jnp.sum(g_conv * g_conv)
        + jnp.sum(g_lin * g_lin)
        + jnp.sum(g_mats * g_mats)
        + jnp.sum(g_emb * g_emb)
        + jnp.sum(g_heads * g_heads)
    )
    reduced = lax.psum(
        (partial_squares, jnp.sum(g_lin * g_lin, axis=1), jnp.sum(g_mats * g_mats, axis=2)), "dp"
    )
    grad_norm = jnp.sqrt(reduced[0] + jnp.sum(bias_raw * bias_raw))
    factor = jnp.minimum(1.0, CLIP_LIMIT / grad_norm)
    conv_grad = factor * g_conv
    lin_grad = factor * g_lin
    mats_grad = factor * g_mats
    emb_grad = factor * g_emb
    heads_grad = factor * g_heads
    bias_grad = factor * bias_raw
    conv_new, conv_moment_new = unfactored(
        conv_kernels, conv_grad, conv_moment, relative(weight_squares[0], KERN * (C1 + C2))
    )
    emb_new, emb_moment_new = unfactored(
        option_emb, emb_grad, emb_moment, relative(weight_squares[3], OPTS * D)
    )
    heads_new, head_moment_new = unfactored(
        heads, heads_grad, head_moment, relative(weight_squares[4], 3 * GAMES * D)
    )
    bias_new, bias_moment_new = unfactored(
        biases, bias_grad, bias_moment, relative(jnp.sum(biases * biases), BIAS)
    )
    lin_rows_new = DECAY_RATE * lin_rows + (1.0 - DECAY_RATE) * (
        factor * factor * reduced[1] / D + FLOOR_ONE
    )
    lin_cols_new = DECAY_RATE * lin_cols + (1.0 - DECAY_RATE) * jnp.mean(
        lin_grad * lin_grad + FLOOR_ONE, axis=0
    )
    lin_second = lin_rows_new[:, None] * lin_cols_new[None, :] / jnp.mean(lin_rows_new)
    lin_new = enc_linear - STEP_RATE * relative(weight_squares[1], FEAT * D) * lin_grad * lax.rsqrt(
        lin_second
    )
    mats_rows_new = DECAY_RATE * mats_rows + (1.0 - DECAY_RATE) * (
        factor * factor * reduced[2] / D + FLOOR_ONE
    )
    mats_cols_new = DECAY_RATE * mats_cols + (1.0 - DECAY_RATE) * jnp.mean(
        mats_grad * mats_grad + FLOOR_ONE, axis=1
    )
    mats_second = (
        mats_rows_new[:, :, None]
        * mats_cols_new[:, None, :]
        / jnp.mean(mats_rows_new, axis=1)[:, None, None]
    )
    mats_new = plan_mats - STEP_RATE * relative(weight_squares[2], 3 * D * D) * mats_grad * lax.rsqrt(
        mats_second
    )
    return (
        conv_new,
        conv_grad,
        conv_moment_new,
        lin_new,
        lin_grad,
        lin_rows_new,
        lin_cols_new,
        mats_new,
        mats_grad,
        mats_rows_new,
        mats_cols_new,
        emb_new,
        emb_grad,
        emb_moment_new,
        heads_new,
        heads_grad,
        head_moment_new,
        bias_new,
        bias_grad,
        bias_moment_new,
        grad_norm,
        loss_value,
        conv_new.astype(BF),
        lin_new.astype(BF),
    )


def solution(mesh):
    return jax.shard_map(
        fused_device if mesh.shape["dp"] * 8 == D else per_device,
        mesh=mesh,
        in_specs=(
            P(None, "dp", None, None),
            P(None, "dp", None),
            P(None, "dp", None),
            P(None, "dp"),
            P(None, "dp", None),
            P(None, "dp", None),
            P(None, "dp", None),
            P("dp", None),
            P(None, "dp"),
            P(None, None, "dp"),
            P(None, "dp"),
            P(None, None, "dp"),
            P(),
            P("dp", None),
            P(),
            P("dp"),
            P(),
            P(None, "dp"),
            P(None, "dp"),
            P(None, None, "dp"),
            P(),
        ),
        out_specs=(
            P("dp", None),
            P("dp", None),
            P("dp", None),
            P(None, "dp"),
            P(None, "dp"),
            P(),
            P("dp"),
            P(None, None, "dp"),
            P(None, None, "dp"),
            P(),
            P(None, "dp"),
            P(None, "dp"),
            P(None, "dp"),
            P(None, "dp"),
            P(None, None, "dp"),
            P(None, None, "dp"),
            P(None, None, "dp"),
            P(),
            P(),
            P(),
            P(),
            P(),
            P("dp", None),
            P(None, "dp"),
        ),
        check_vma=False,
    )
```

```python
import functools

import jax
import jax.numpy as jnp
from jax import lax
from jax.experimental import pallas as pl
from jax.experimental.pallas import tpu as pltpu
from jax.sharding import PartitionSpec as P

D = 128
C1 = 16
C2 = 32
OPTS = 18
KERN = 256
GAMES = 8
FEAT = 2592
BIAS = 304

OUT1 = 20
OUT2 = 9
WIDE = 384
LIN_PAD = 2688
EMB_LANE = FEAT % 128
HEAD_LANE = EMB_LANE + OPTS
CHUNK = 12
FEATS_ROW = OUT2 * C2

CLIP_LIMIT = 0.05
DECAY_RATE = 0.8
STEP_RATE = 0.5
FLOOR_ONE = 1e-30
FLOOR_TWO = 0.001

HIGH = lax.Precision.HIGHEST
BF = jnp.bfloat16
F32 = jnp.float32


def dot(left, right, over_left=1, over_right=0, precision=None):
    return lax.dot_general(
        left,
        right,
        (((over_left,), (over_right,)), ((), ())),
        precision=precision,
        preferred_element_type=F32,
    )


def sigmoid(value):
    return 0.5 * jnp.tanh(0.5 * value) + 0.5


def slope(value, sigma):
    return sigma * (1.0 + value * (1.0 - sigma))


def iota(shape, axis):
    return lax.broadcasted_iota(jnp.int32, shape, axis)


def turn(value, steps):
    return pltpu.roll(value, steps, 1)


def fold(value, width):
    step = 64
    while step >= width:
        value = value + turn(value, step)
        step //= 2
    return value


def row_of(column):
    square = jnp.broadcast_to(column, (128, 128))
    return jnp.sum(jnp.where(iota((128, 128), 0) == iota((128, 128), 1), square, 0.0), axis=0, keepdims=True)


def load_frames(frames_hbm, section, frame_buf, sems, chunk):
    copies = []
    for which in range(frame_buf.shape[0] // chunk):
        rows = pl.ds(which * chunk, chunk)
        copies.append(
            pltpu.make_async_copy(
                frames_hbm.at[section, rows], frame_buf.at[rows], sems.at[which]
            )
        )
    return copies


def place_frames(frame_buf, pixels, first, chunk, frames):
    for row in range(first, first + chunk):
        block, part = row // 4, row % 4
        pixels[block * frames : (block + 1) * frames, part * WIDE : part * WIDE + 336] = frame_buf[row]


def build_bands(kernels, band_one, band_two):
    held = kernels.shape[1]
    rows48 = iota((held, WIDE), 0)
    lanes48 = iota((held, WIDE), 1)
    pick_one = jnp.where((lanes48 % C1 == rows48) & (lanes48 < OUT1 * C1), 1.0, 0.0).astype(BF)
    pick_two = jnp.where(
        (lanes48 % C2 + C1 == rows48) & (lanes48 < OUT2 * C2), 1.0, 0.0
    ).astype(BF)
    wide_one = dot(kernels, pick_one)
    wide_two = dot(kernels, pick_two)
    for wide, band, width, taps, blocks in (
        (wide_one, band_one, C1, 8, OUT1),
        (wide_two, band_two, C2, 4, OUT2),
    ):
        per_tile = 128 // width
        group = iota((width, 128), 1) // width
        for tap in range(taps):
            base = 2 * tap * width
            for block in range(blocks + 1):
                rows = tap * WIDE + block * width
                tile, spot = divmod(block, per_tile)
                lanes = slice(tile * 128, (tile + 1) * 128)
                left = jnp.where(group == spot, wide[base : base + width, lanes], 0.0)
                right = wide[base + width : base + 2 * width]
                if spot > 0:
                    left = jnp.where(group == spot - 1, right[:, lanes], left)
                elif block > 0:
                    before = slice((tile - 1) * 128, tile * 128)
                    band[rows : rows + width, before] = jnp.where(
                        group == per_tile - 1, right[:, before], 0.0
                    ).astype(BF)
                band[rows : rows + width, lanes] = left.astype(BF)


def clear_bands(band_one, band_two):
    band_one[...] = jnp.zeros(band_one.shape, BF)
    band_two[...] = jnp.zeros(band_two.shape, BF)


def wide_biases(bias_row):
    bias8 = jnp.broadcast_to(bias_row, (8, BIAS))
    rows = iota((BIAS, WIDE), 0)
    lanes = iota((BIAS, WIDE), 1)
    one = jnp.where((lanes % C1 == rows) & (lanes < OUT1 * C1), 1.0, 0.0)
    two = jnp.where((lanes % C2 + C1 == rows) & (lanes < OUT2 * C2), 1.0, 0.0)
    rows = iota((D, BIAS), 0)
    lanes = iota((D, BIAS), 1)
    three = jnp.where(lanes == rows + C1 + C2, 1.0, 0.0)
    four = jnp.where(lanes == rows + C1 + C2 + D, 1.0, 0.0)
    return (
        dot(bias8, one, precision=HIGH)[0:1],
        dot(bias8, two, precision=HIGH)[0:1],
        dot(three, bias8, 1, 1, precision=HIGH)[:, 0:1],
        dot(four, bias8, 1, 1, precision=HIGH)[:, 0:1],
    )


def encode_one(pixels, band_one, bias, z_one, act_one, frames, chunk):
    half = 4 * WIDE
    rows = chunk * frames
    for first in range(0, OUT1, chunk):
        low = first * frames
        z = dot(pixels[low : low + rows, :], band_one[0:half, :]) + dot(
            pixels[low + frames : low + frames + rows, :], band_one[half : 2 * half, :]
        )
        z = z + bias
        act = (z * sigmoid(z)).astype(BF)
        for step in range(chunk):
            at, part = divmod(first + step, 2)
            spot = (slice(at * frames, (at + 1) * frames), slice(part * WIDE, (part + 1) * WIDE))
            z_one[spot] = z[step * frames : (step + 1) * frames]
            act_one[spot] = act[step * frames : (step + 1) * frames]


def encode_two(act_one, band_two, bias, z_two, act_two, frames, chunk):
    half = 2 * WIDE
    rows = chunk * frames
    for first in range(0, OUT2, chunk):
        low = first * frames
        z = dot(act_one[low : low + rows, :], band_two[0:half, :]) + dot(
            act_one[low + frames : low + frames + rows, :], band_two[half : 2 * half, :]
        )
        z = z + bias
        z_two[low : low + rows] = z
        act = (z * sigmoid(z)).astype(BF)
        for step in range(chunk):
            at = (first + step) * FEATS_ROW
            act_two[:, at : at + FEATS_ROW] = act[step * frames : (step + 1) * frames, :FEATS_ROW]


def back_two(dstate_t, linear_t, z_two, dz_two, frames):
    dact = dot(dstate_t, linear_t, 0, 0)
    dz_two[0:frames] = jnp.zeros((frames, WIDE), BF)
    dz_two[(OUT2 + 1) * frames : (OUT2 + 2) * frames] = jnp.zeros((frames, WIDE), BF)
    blank = jnp.zeros((frames, WIDE - FEATS_ROW), F32)
    for at in range(OUT2):
        z = z_two[at * frames : (at + 1) * frames]
        part = jnp.concatenate([dact[:, at * FEATS_ROW : (at + 1) * FEATS_ROW], blank], axis=1)
        dz_two[(at + 1) * frames : (at + 2) * frames] = (part * slope(z, sigmoid(z))).astype(BF)


def back_one(dz_two, band_two, z_one, dz_one, frames, chunk):
    half = 2 * WIDE
    rows = chunk * frames
    for first in range(0, OUT1 // 2, chunk):
        low = first * frames
        dact = dot(dz_two[low + frames : low + frames + rows], band_two[0:half], 1, 1) + dot(
            dz_two[low : low + rows], band_two[half : 2 * half], 1, 1
        )
        z = z_one[low : low + rows]
        dz = (dact * slope(z, sigmoid(z))).astype(BF)
        for step in range(chunk):
            for part in range(2):
                at = (2 * (first + step) + part) * frames
                dz_one[at : at + frames] = dz[
                    step * frames : (step + 1) * frames, part * WIDE : (part + 1) * WIDE
                ]


def band_sums(term, outputs, width):
    per_tile = 128 // width
    lane = iota((width, 128), 1) // width
    sums = []
    for shift in range(2):
        total = None
        for spot in range(per_tile):
            part = None
            for position in range(outputs):
                tile, inside = divmod(position + shift, per_tile)
                if inside != spot:
                    continue
                one = term(position, tile)
                part = one if part is None else part + one
            if part is None:
                continue
            part = jnp.where(lane == spot, part, 0.0)
            total = part if total is None else total + part
        sums.append(fold(total, width))
    return sums


def kernel_grad(terms, outputs, width):
    tiles = []
    lane = iota((width, 128), 1) // width
    pieces = []
    for term in terms:
        pieces.extend(band_sums(term, outputs, width))
    per_tile = 128 // width
    for tile in range(2):
        total = jnp.zeros((width, 128), F32)
        for spot in range(per_tile):
            total = jnp.where(lane == spot, pieces[tile * per_tile + spot], total)
        tiles.append(total)
    return jnp.concatenate(tiles, axis=1)


def tiled(tile, count):
    return jnp.concatenate([tile] * count, axis=1)


def twice(row):
    return jnp.concatenate([row, row], axis=1)


def plan(states, mats_t, table, bias_col, options, legal, games, valid, rewards, returns, scale):
    frames = states.shape[1]
    pairs = OPTS // 2
    lanes = OPTS * frames
    trans_in, trans_out, value_in = mats_t
    low_half = iota((1, 128), 1) < frames
    upper = iota((1, 128), 1) // frames

    valid_f = [twice(v.astype(F32)) for v in valid]
    rewards = [twice(r) for r in rewards]
    returns = [twice(r) for r in returns]
    chosen = [twice(o) for o in options]
    game = twice(games)

    game_rows = iota((128, WIDE), 0) - HEAD_LANE
    game_pick = jnp.where(
        game_rows == tiled(game, 3) + GAMES * (iota((128, WIDE), 1) // 128), 1.0, 0.0
    )
    head_rows = dot(table, game_pick.astype(BF))
    hr, hd, hv = (head_rows[:, k * 128 : (k + 1) * 128] for k in range(3))

    option_rows = jnp.where(
        iota((128, lanes), 0) - EMB_LANE == iota((128, lanes), 1) // frames, 1.0, 0.0
    ).astype(BF)
    s_low = twice(states)
    s_f = s_low.astype(F32)
    base = dot(trans_in, s_low)
    pre = tiled(base, pairs) + dot(table, option_rows)
    sig_h = sigmoid(pre)
    hid = pre * sig_h
    hid_low = hid.astype(BF)
    after = tiled(s_f, pairs) + dot(trans_out, hid_low)
    after_low = after.astype(BF)
    judge_pre = dot(value_in, after_low) + bias_col
    sig_j = sigmoid(judge_pre)
    judged = judge_pre * sig_j

    def tile_of(value, k):
        return value[:, k * 128 : (k + 1) * 128]

    def over(value):
        return jnp.sum(value, axis=0, keepdims=True)

    reward = [over(tile_of(hid, k) * hr) for k in range(pairs)]
    gamma = [sigmoid(over(tile_of(hid, k) * hd)) for k in range(pairs)]
    value = [over(tile_of(judged, k) * hv) for k in range(pairs)]
    backed = [reward[k] + gamma[k] * value[k] for k in range(pairs)]
    allowed = [
        jnp.concatenate([legal[2 * k], legal[2 * k + 1]], axis=1) > 0 for k in range(pairs)
    ]
    highest = functools.reduce(
        jnp.maximum, [jnp.where(allowed[k], backed[k], -1e30) for k in range(pairs)]
    )
    highest = jnp.maximum(highest, turn(highest, frames))
    shares = [
        jnp.where(allowed[k], jnp.exp(jnp.where(allowed[k], backed[k] - highest, -60.0)), 0.0)
        for k in range(pairs)
    ]

    def halves(total):
        return total + turn(total, frames)

    share_sum = halves(sum(shares))
    planned = halves(sum(shares[k] * backed[k] for k in range(pairs))) / share_sum
    choose = [chosen[0] == 2 * k + upper for k in range(pairs)]

    def chosen_of(parts):
        return halves(sum(jnp.where(choose[k], parts[k], 0.0) for k in range(pairs)))

    roll_f = [chosen_of([tile_of(after, k) for k in range(pairs)])]
    roll_low = [roll_f[0].astype(BF)]
    plan_miss = planned - returns[0]
    reward_miss = [chosen_of(reward) - rewards[0]]
    value_miss = [chosen_of(value) - returns[1]]
    steps = len(options)
    picks, pre_k, sig_k, hid_k, hid_k_low, judge_k, sig_jk, judged_k = ([None] for _ in range(8))
    for k in range(1, steps):
        picks.append(jnp.where(iota((128, 128), 0) - EMB_LANE == chosen[k], 1.0, 0.0).astype(BF))
        pre_k.append(dot(trans_in, roll_low[k - 1]) + dot(table, picks[k]))
        sig_k.append(sigmoid(pre_k[k]))
        hid_k.append(pre_k[k] * sig_k[k])
        hid_k_low.append(hid_k[k].astype(BF))
        roll_f.append(roll_f[k - 1] + dot(trans_out, hid_k_low[k]))
        roll_low.append(roll_f[k].astype(BF))
        judge_k.append(dot(value_in, roll_low[k]) + bias_col)
        sig_jk.append(sigmoid(judge_k[k]))
        judged_k.append(judge_k[k] * sig_jk[k])
        reward_miss.append(over(hid_k[k] * hr) - rewards[k])
        value_miss.append(over(judged_k[k] * hv) - returns[k + 1])
    errors = valid_f[0] * plan_miss * plan_miss
    for k in range(steps):
        errors = errors + valid_f[k] * (
            reward_miss[k] * reward_miss[k] + value_miss[k] * value_miss[k]
        )
    errors = jnp.where(low_half, errors * scale, 0.0)

    half = jnp.where(low_half, 1.0, 0.0)
    double = 2.0 * scale
    d_plan = double * valid_f[0] * plan_miss / share_sum
    d_reward_k = [double * valid_f[k] * reward_miss[k] for k in range(steps)]
    d_value_k = [double * valid_f[k] * value_miss[k] for k in range(steps)]

    def through(matrix_t, grad):
        return dot(matrix_t, grad, 0, 0)

    d_roll = None
    d_judge_low, d_step_low, d_pre_low = ([None] * steps for _ in range(3))
    d_hr = jnp.zeros((D, 128), F32)
    d_hd = jnp.zeros((D, 128), F32)
    d_hv = jnp.zeros((D, 128), F32)
    for k in range(steps - 1, 0, -1):
        d_judge_low[k] = (d_value_k[k] * hv * slope(judge_k[k], sig_jk[k])).astype(BF)
        term = through(value_in, d_judge_low[k])
        d_roll = term if d_roll is None else d_roll + term
        d_step_low[k] = d_roll.astype(BF)
        d_hid = through(trans_out, d_step_low[k]) + d_reward_k[k] * hr
        d_pre_low[k] = (d_hid * slope(pre_k[k], sig_k[k])).astype(BF)
        d_roll = d_roll + through(trans_in, d_pre_low[k])
        d_hr = d_hr + (half * d_reward_k[k]) * hid_k[k]
        d_hv = d_hv + (half * d_value_k[k]) * judged_k[k]

    d_backed = [d_plan * shares[k] * (1.0 + backed[k] - planned) for k in range(pairs)]
    d_reward = [
        d_backed[k] + jnp.where(choose[k], d_reward_k[0], 0.0) for k in range(pairs)
    ]
    d_value = [
        d_backed[k] * gamma[k] + jnp.where(choose[k], d_value_k[0], 0.0) for k in range(pairs)
    ]
    d_gamma = [d_backed[k] * value[k] * gamma[k] * (1.0 - gamma[k]) for k in range(pairs)]
    d_judge = [
        (d_value[k] * hv * slope(tile_of(judge_pre, k), tile_of(sig_j, k))).astype(BF)
        for k in range(pairs)
    ]
    d_judge_all = jnp.concatenate(d_judge, axis=1)
    d_after = through(value_in, d_judge_all)
    d_after = [
        tile_of(d_after, k) + jnp.where(choose[k], d_roll, 0.0) for k in range(pairs)
    ]
    d_after_low = jnp.concatenate([d.astype(BF) for d in d_after], axis=1)
    d_hid_all = through(trans_out, d_after_low)
    d_pre = [
        (
            (tile_of(d_hid_all, k) + d_reward[k] * hr + d_gamma[k] * hd)
            * slope(tile_of(pre, k), tile_of(sig_h, k))
        ).astype(BF)
        for k in range(pairs)
    ]
    d_pre_all = jnp.concatenate(d_pre, axis=1)
    d_base = through(trans_in, d_pre_all)
    d_state = halves(sum(d_after[k] + tile_of(d_base, k) for k in range(pairs)))
    for k in range(pairs):
        d_hr = d_hr + d_reward[k] * tile_of(hid, k)
        d_hd = d_hd + d_gamma[k] * tile_of(hid, k)
        d_hv = d_hv + d_value[k] * tile_of(judged, k)

    def both(parts):
        joined = [jnp.where(low_half, parts[k].astype(F32), parts[k + 1].astype(F32)) for k in range(1, steps, 2)]
        return [part.astype(BF) for part in joined]

    def with_steps(wide, parts):
        return jnp.concatenate([wide] + both(parts), axis=1)

    before_low = [None] + roll_low[:-1]
    d_pre_cat = with_steps(d_pre_all, d_pre_low)
    d_judge_cat = with_steps(d_judge_all, d_judge_low)
    grad_in = dot(d_pre_cat, with_steps(tiled(s_low, pairs), before_low), 1, 1)
    grad_out = dot(
        with_steps(d_after_low, d_step_low), with_steps(hid_low, hid_k_low), 1, 1
    )
    grad_value = dot(d_judge_cat, with_steps(after_low, roll_low), 1, 1)
    grad_table = dot(d_pre_cat, with_steps(option_rows, picks), 1, 1) + dot(
        jnp.concatenate([d_hr, d_hd, d_hv], axis=1), game_pick, 1, 1, precision=HIGH
    )
    grad_bias = jnp.sum(d_judge_cat.astype(F32), axis=1, keepdims=True)
    return (
        d_state[:, :frames],
        (grad_in, grad_out, grad_value),
        grad_table,
        grad_bias,
        errors,
    )


def frame_rows(section, refs):
    options_ref, legal_ref, games_ref, valid_ref, rewards_ref, returns_ref = refs

    def row(ref, k):
        return ref[k, pl.ds(section, 1), :]

    depth = options_ref.shape[0]
    return (
        [row(options_ref, k) for k in range(depth)],
        [row(legal_ref, k) for k in range(OPTS)],
        games_ref[pl.ds(section, 1), :],
        [row(valid_ref, k) for k in range(depth)],
        [row(rewards_ref, k) for k in range(depth)],
        [returns_ref[section, k : k + 1, :] for k in range(depth + 1)],
    )


def clear_tails(pixels):
    tail = jnp.zeros((pixels.shape[0], WIDE - 336), BF)
    for part in range(4):
        pixels[:, part * WIDE + 336 : (part + 1) * WIDE] = tail


def grad_kernel_two(act_one, dz_two, frames):
    rows = OUT2 * frames
    d_two = dz_two[frames : frames + rows]
    full = [dot(d_two, act_one[0:rows], 0, 0), dot(d_two, act_one[frames : frames + rows], 0, 0)]

    def term_of(tap):
        def term(position, tile):
            lane = (tap % 2) * WIDE + tile * 128
            return full[tap // 2][position * C2 : (position + 1) * C2, lane : lane + 128]

        return term

    grad = kernel_grad([term_of(tap) for tap in range(4)], OUT2, C2)
    return grad, fold(tiles_sum(dot(jnp.ones((8, rows), BF), d_two)), C2)


def grad_kernel_one(pixels, dz_one, frames):
    rows = OUT1 * frames
    d_one = dz_one[...]
    turned = d_one.T

    def term_of(tap):
        first = (tap // 4) * frames
        base = (tap % 4) * WIDE
        blocks = []
        for group, (low, high) in enumerate(((0, 256), (128, 384), (256, 384))):
            left = turned[group * 128 : min((group + 1) * 128, OUT1 * C1)]
            blocks.append(dot(left, pixels[first : first + rows, base + low : base + high]))

        def term(position, tile):
            group, inside = divmod(position, 8)
            lane = (tile - group) * 128
            return blocks[group][inside * C1 : (inside + 1) * C1, lane : lane + 128]

        return term

    grad = kernel_grad([term_of(tap) for tap in range(8)], OUT1, C1)
    return grad, fold(tiles_sum(dot(jnp.ones((8, rows), BF), d_one)), C1)


def local_kernel(
    frames_hbm,
    kernels_ref,
    linear_ref,
    mats_ref,
    table_ref,
    bias_ref,
    options_ref,
    legal_ref,
    games_ref,
    valid_ref,
    rewards_ref,
    returns_ref,
    lin_out,
    mats_out,
    table_out,
    conv_out,
    small_out,
    frame_buf,
    pixels,
    band_one,
    band_two,
    z_one,
    act_one,
    z_two,
    act_two,
    dz_two,
    dz_one,
    sems,
):
    section = lax.axis_index("section")
    frames = frame_buf.shape[1]
    copies = load_frames(frames_hbm, section, frame_buf, sems, CHUNK)
    for copy in copies:
        copy.start()
    clear_bands(band_one, band_two)
    build_bands(kernels_ref[...], band_one, band_two)
    bias_one, bias_two, bias_three, bias_four = wide_biases(bias_ref[...])
    clear_tails(pixels)
    for which, copy in enumerate(copies):
        copy.wait()
        place_frames(frame_buf, pixels, which * CHUNK, CHUNK, frames)
    encode_one(pixels, band_one, bias_one, z_one, act_one, frames, 4)
    encode_two(act_one, band_two, bias_two, z_two, act_two, frames, 3)
    linear_t = linear_ref[...]
    states = (dot(linear_t, act_two[...], 1, 1) + bias_three).astype(BF)
    d_state, grad_mats, grad_table, grad_bias, errors = plan(
        states,
        tuple(mats_ref[k] for k in range(3)),
        table_ref[...],
        bias_four,
        *frame_rows(
            section, (options_ref, legal_ref, games_ref, valid_ref, rewards_ref, returns_ref)
        ),
        1.0,
    )
    for k in range(3):
        mats_out[k] = grad_mats[k]
    table_out[...] = grad_table
    d_state_low = d_state.astype(BF)
    lin_out[...] = dot(d_state_low, act_two[...])
    back_two(d_state_low, linear_t, z_two, dz_two, frames)
    grad_two, bias_two_grad = grad_kernel_two(act_one, dz_two, frames)
    back_one(dz_two, band_two, z_one, dz_one, frames, 5)
    grad_one, bias_one_grad = grad_kernel_one(pixels, dz_one, frames)
    conv_out[...] = stack_kernels(grad_one, grad_two)
    lane = iota((8, 128), 1)
    line = iota((8, 128), 0)
    row_zero = jnp.where(
        lane < C1, bias_one_grad, jnp.where(lane < C1 + C2, turn(bias_two_grad, C1), 0.0)
    )
    count = sum(
        valid_ref[k, pl.ds(section, 1), :].astype(F32) for k in range(valid_ref.shape[0])
    )
    count = jnp.where(iota((1, 128), 1) < frames, twice(count), 0.0)
    small = jnp.where(line == 0, row_zero, 0.0)
    small = jnp.where(line == 1, row_of(lane_sum(d_state_low)), small)
    small = jnp.where(line == 2, row_of(grad_bias), small)
    small = jnp.where(line == 3, errors, small)
    small = jnp.where(line == 4, count, small)
    small_out[...] = small


def lane_sum(value):
    return jnp.sum(value.astype(F32), axis=1, keepdims=True)


def stack_kernels(grad_one, grad_two):
    rows = jnp.concatenate([grad_one, grad_two, jnp.zeros((128 - C1 - C2, KERN), F32)], axis=0)
    return rows.T


def tiles_sum(value):
    return sum(value[:, k * 128 : (k + 1) * 128] for k in range(value.shape[1] // 128))


VMEM_SPEC = pl.BlockSpec(memory_space=pltpu.VMEM)
ANY_SPEC = pl.BlockSpec(memory_space=pl.ANY)


def local_scratch(frames, side):
    return [
        pltpu.VMEM((side, frames, 336), BF),
        pltpu.VMEM(((OUT1 + 1) * frames, 4 * WIDE), BF),
        pltpu.VMEM((8 * WIDE, WIDE), BF),
        pltpu.VMEM((4 * WIDE, WIDE), BF),
        pltpu.VMEM((OUT1 // 2 * frames, 2 * WIDE), F32),
        pltpu.VMEM((OUT1 // 2 * frames, 2 * WIDE), BF),
        pltpu.VMEM((OUT2 * frames, WIDE), F32),
        pltpu.VMEM((frames, FEAT), BF),
        pltpu.VMEM(((OUT2 + 2) * frames, WIDE), BF),
        pltpu.VMEM((OUT1 * frames, WIDE), BF),
        pltpu.SemaphoreType.DMA((side // CHUNK,)),
    ]


def local_step(frames, kernels, linear_t, mats_t, table, biases, options, legal, games, valid, rewards, returns):
    count = frames.shape[1]
    side = frames.shape[2]
    shapes = [(D, FEAT), (3, D, D), (D, 128), (KERN, 128), (8, 128)]
    return pl.pallas_call(
        local_kernel,
        out_shape=[jax.ShapeDtypeStruct(shape, F32) for shape in shapes],
        in_specs=[ANY_SPEC] + [VMEM_SPEC] * 11,
        out_specs=[VMEM_SPEC] * len(shapes),
        scratch_shapes=local_scratch(count, side),
        compiler_params=pltpu.CompilerParams(vmem_limit_bytes=56 * 1024 * 1024),
    )(
        frames.transpose(0, 2, 1, 3),
        kernels,
        linear_t,
        mats_t,
        table,
        biases.reshape(1, BIAS),
        options.transpose(2, 0, 1),
        legal.transpose(2, 0, 1),
        games,
        valid.transpose(2, 0, 1),
        rewards.transpose(2, 0, 1),
        returns.transpose(0, 2, 1),
    )


MESH = pl.DeviceIdType.MESH


def packed(value):
    axis = value.ndim - 2
    return jnp.concatenate([value[..., 0:QUARTER], value[..., QUARTER:HALF]], axis=axis)


QUARTER = 768
HALF = 2 * QUARTER
AT_EMB = FEAT
AT_HEADS = AT_EMB + OPTS
AT_MATS = LIN_PAD
TILES = HALF // 128
NEAR = 8
FOUR = 4


def fused_kernel(
    peers,
    frames_hbm,
    conv_ref,
    lin_ref,
    mats_ref,
    emb_ref,
    heads_ref,
    bias_ref,
    options_ref,
    legal_ref,
    games_ref,
    valid_ref,
    rewards_ref,
    returns_ref,
    main_out,
    conv_out,
    tile_out,
    stats_out,
    frame_buf,
    pixels,
    band_one,
    band_two,
    z_one,
    act_one,
    z_two,
    act_two,
    dz_two,
    dz_one,
    frame_sems,
    stage,
    kernel_msg,
    weight_msg,
    weights,
    grad_own,
    mate_msg,
    mate_in,
    grad_msg,
    near_in,
    cross_in,
    cross_msg,
    far_in,
    tile_own,
    tile_mate,
    tile_msg,
    tile_in,
    stats_in,
    stats_both,
    stats_base,
    half_in,
    send_sems,
    recv_sems,
    mate_send,
    mate_recv,
):
    section = lax.axis_index("section")
    place = lax.axis_index("dp")
    mate = 1 - section
    frames = frame_buf.shape[1]

    barrier = pltpu.get_barrier_semaphore()

    def greet(step, carry):
        peer = lax.rem(place + step, peers)
        pl.semaphore_signal(barrier, inc=1, device_id=(section, peer), device_id_type=MESH)
        return carry

    pl.semaphore_signal(barrier, inc=1, device_id=(mate, place), device_id_type=MESH)
    lax.fori_loop(1, peers, greet, 0)
    copies = load_frames(frames_hbm, section, frame_buf, frame_sems, CHUNK)
    wait_frames = lambda: [copy.wait() for copy in copies]
    for copy in copies:
        copy.start()

    sends = []

    side, spot = place // NEAR, lax.rem(place, NEAR)
    row, column = spot // FOUR, lax.rem(spot, FOUR)

    def near(step):
        return side * NEAR + lax.rem(spot + step, NEAR)

    def beyond(step):
        return (1 - side) * NEAR + lax.rem(spot + step, NEAR)

    def beside(step):
        return place - column + lax.rem(column + step, FOUR)

    def across(step, where):
        return (1 - side) * NEAR + lax.rem(row + step, 2) * FOUR + where

    def send(sems, peer, source, target):
        pltpu.make_async_remote_copy(
            src_ref=source,
            dst_ref=target,
            send_sem=send_sems.at[sems],
            recv_sem=recv_sems.at[sems],
            device_id=(section, peer),
            device_id_type=MESH,
        ).start()

    def loop(low, high, act):
        def body(step, carry):
            act(step)
            return carry

        lax.fori_loop(low, high, body, 0)

    def settle(sems, blocks):
        whole = pltpu.make_async_remote_copy(
            src_ref=blocks,
            dst_ref=blocks,
            send_sem=send_sems.at[sems],
            recv_sem=recv_sems.at[sems],
            device_id=(mate, place),
            device_id_type=MESH,
        )
        sends.append(whole.wait_send)
        return whole.wait_recv

    def send_peers(sems, source, target):
        loop(0, NEAR, lambda step: send(sems, beyond(step), source, target.at[place]))
        loop(1, NEAR, lambda step: send(sems, near(step), source, target.at[place]))
        return settle(sems, target.at[pl.ds(0, peers - 1)])

    def send_mate(which, source, target, landing):
        def copy(into):
            return pltpu.make_async_remote_copy(
                src_ref=source,
                dst_ref=into,
                send_sem=mate_send.at[which],
                recv_sem=mate_recv.at[which],
                device_id=(mate, place),
                device_id_type=MESH,
            )

        copy(target).start()
        sends.append(lambda: copy(target).wait_send())
        return lambda: copy(landing).wait_recv()

    upper_lanes = iota((16, 128), 1) >= 64
    counts = sum(
        valid_ref[k, m : m + 1, :].astype(F32)
        for k in range(valid_ref.shape[0])
        for m in range(valid_ref.shape[1])
    )
    conv_pad = jnp.concatenate([conv_ref[...], jnp.zeros((16, 80), F32)], axis=1)
    kernel_msg[place] = jnp.where(
        upper_lanes & (iota((16, 128), 0) == 0), jnp.broadcast_to(twice(counts), (16, 128)), conv_pad
    ).astype(BF)
    heads_pad = jnp.concatenate([heads_ref[...], jnp.zeros((24, 120), F32)], axis=1)
    heads_pad = jnp.concatenate([heads_pad, jnp.zeros((104, 128), F32)], axis=0).T
    last = FEAT - EMB_LANE
    stage[:, 0:last] = lin_ref[:, 0:last]
    stage[:, last:LIN_PAD] = jnp.concatenate(
        [
            lin_ref[:, last:FEAT],
            emb_ref[...],
            heads_pad[0:8, 0 : 3 * GAMES],
            jnp.zeros((8, 128 - HEAD_LANE - 3 * GAMES), F32),
        ],
        axis=1,
    )
    for k in range(3):
        stage[:, AT_MATS + k * D : AT_MATS + (k + 1) * D] = mats_ref[k]
    first = stage[:, pl.ds(pl.multiple_of(section * HALF, 128), QUARTER)]
    second = stage[:, pl.ds(pl.multiple_of(section * HALF + QUARTER, 128), QUARTER)]
    weight_msg[section, place] = jnp.concatenate([first, second], axis=0).astype(BF)

    def square_sum(value):
        return jnp.sum(jnp.sum(value * value, axis=0, keepdims=True), axis=1, keepdims=True)

    weight_squares = [
        square_sum(conv_pad),
        square_sum(lin_ref[...]),
        square_sum(mats_ref[...].reshape(24, D)),
        square_sum(emb_ref[...]),
        square_sum(heads_ref[...]),
    ]
    stat_line = iota((16, 128), 0)
    stat = jnp.zeros((16, 128), F32)
    for which, value in enumerate(weight_squares):
        at = iota((16, 128), 1) == which
        rough = value.astype(BF).astype(F32)
        stat = jnp.where(at & (stat_line == TILES + 1), rough, stat)
        stat = jnp.where(at & (stat_line == TILES + 2), value - rough, stat)
    stats_base[...] = stat
    pl.semaphore_wait(barrier, peers)
    wait_kernels = send_peers(0, kernel_msg.at[place], kernel_msg)
    half_msg = weight_msg.at[section]
    loop(0, 2, lambda step: send(1, across(step, column), half_msg.at[place], half_msg.at[place]))
    wait_across = settle(1, half_msg.at[pl.ds(0, 2)])
    loop(1, NEAR, lambda step: send(2, near(step), half_msg.at[place], half_msg.at[place]))
    wait_near = settle(2, half_msg.at[pl.ds(0, NEAR - 1)])

    clear_bands(band_one, band_two)
    bias_one, bias_two, bias_three, bias_four = wide_biases(bias_ref[...].reshape(1, BIAS))
    clear_tails(pixels)
    act_two[:, FEAT:LIN_PAD] = jnp.zeros((frames, LIN_PAD - FEAT), BF)
    for which, copy in enumerate(copies):
        copy.wait()
        place_frames(frame_buf, pixels, which * CHUNK, CHUNK, frames)
    wait_kernels()
    wait_across()
    for which in range(2):
        block = half_msg.at[across(which, column)]
        loop(1, FOUR, lambda step: send(3, beside(step), block, block))
    wait_beside = settle(3, half_msg.at[pl.ds(0, 2 * (FOUR - 1))])
    kernels = kernel_msg[...].reshape(KERN, 128)
    counted = jnp.where(iota((KERN, 128), 1) >= 64, kernels.astype(F32), 0.0)
    count = jnp.sum(jnp.sum(counted, axis=0, keepdims=True), axis=1, keepdims=True)
    scale = 1.0 / count
    build_bands(kernels, band_one, band_two)
    encode_one(pixels, band_one, bias_one, z_one, act_one, frames, 4)
    encode_two(act_one, band_two, bias_two, z_two, act_two, frames, 3)
    wait_near()
    wait_beside()
    wait_half = send_mate(0, weight_msg.at[section], weight_msg.at[section], weight_msg.at[mate])
    wait_half()
    for half in range(2):
        block = weight_msg[half].astype(F32)
        for part in range(2):
            lane = (2 * half + part) * QUARTER
            weights[:, lane : lane + QUARTER] = (
                block[:, part * 8 : (part + 1) * 8].reshape(D, QUARTER).astype(BF)
            )
    linear_t = weights[:, 0:LIN_PAD]
    states = (dot(linear_t, act_two[...], 1, 1) + bias_three).astype(BF)
    d_state, grad_mats, grad_table, grad_bias, errors = plan(
        states,
        tuple(weights[:, AT_MATS + k * D : AT_MATS + (k + 1) * D] for k in range(3)),
        weights[:, LIN_PAD - 128 : LIN_PAD],
        bias_four,
        *frame_rows(
            section, (options_ref, legal_ref, games_ref, valid_ref, rewards_ref, returns_ref)
        ),
        scale,
    )

    d_state_low = d_state.astype(BF)
    grad_linear = dot(d_state_low, act_two[...])
    grad_own[0] = grad_linear[:, 0:HALF].reshape(peers, 8, HALF)
    grad_own[1, :, :, 0 : LIN_PAD - 128 - HALF] = grad_linear[:, HALF : LIN_PAD - 128].reshape(
        peers, 8, LIN_PAD - 128 - HALF
    )
    rest = [grad_linear[:, LIN_PAD - 128 : LIN_PAD] + grad_table, *grad_mats]
    for k in range(4):
        lane = LIN_PAD - 128 - HALF + k * D
        grad_own[1, :, :, lane : lane + D] = rest[k].reshape(peers, 8, D)
    mate_msg[...] = packed(grad_own[mate]).astype(BF)
    wait_mate = send_mate(1, mate_msg, mate_in, mate_in)
    back_two(d_state_low, linear_t, z_two, dz_two, frames)
    grad_two, bias_two_grad = grad_kernel_two(act_one, dz_two, frames)
    wait_mate()
    grad_msg[...] = (packed(grad_own[section]) + mate_in[...].astype(F32)).astype(BF)
    for which in range(2):

        def collect(step):
            peer = beside(step)
            owner = across(which, lax.rem(peer, FOUR))
            send(4, peer, grad_msg.at[owner], cross_in.at[which, column])

        loop(1, FOUR, collect)
        cross_in[which, column] = grad_msg[across(which, column)]
    wait_cross = settle(4, grad_msg.at[pl.ds(0, 2 * (FOUR - 1))])
    loop(1, NEAR, lambda step: send(5, near(step), grad_msg.at[near(step)], near_in.at[spot]))
    wait_grads = settle(5, near_in.at[pl.ds(0, NEAR - 1)])
    near_in[spot] = grad_msg[place]
    lane = iota((8, 128), 1)
    line = iota((8, 128), 0)
    row_three = row_of(lane_sum(d_state_low))
    row_four = row_of(grad_bias)
    extra_rows = jnp.zeros((8, 128), F32)
    for which, entry in (
        (0, turn(row_three, 64)),
        (1, row_three),
        (2, turn(row_four, 64)),
        (3, row_four),
        (5, turn(errors, 64)),
    ):
        extra_rows = jnp.where(line == which, entry, extra_rows)
    back_one(dz_two, band_two, z_one, dz_one, frames, 5)
    grad_one, bias_one_grad = grad_kernel_one(pixels, dz_one, frames)
    wait_cross()
    cross_msg[...] = jnp.sum(cross_in[...].astype(F32), axis=1).astype(BF)
    loop(0, 2, lambda step: send(6, across(step, column), cross_msg.at[step], far_in.at[row]))
    wait_far = settle(6, far_in)

    conv_rows = stack_kernels(grad_one, grad_two).reshape(2 * peers, 8, 128)
    row_first = jnp.where(
        lane < C1, bias_one_grad, jnp.where(lane < C1 + C2, turn(bias_two_grad, C1), 0.0)
    )
    extra = jnp.where(line == 4, turn(row_first, 64), extra_rows)
    tiles = jnp.where(iota((2 * peers, 8, 128), 2) >= 64, extra[None], conv_rows)
    tile_own[0] = tiles.reshape(peers, 2, 8, 128)[:, 0]
    tile_own[1] = tiles.reshape(peers, 2, 8, 128)[:, 1]
    wait_pair = send_mate(2, tile_own.at[mate], tile_mate, tile_mate)
    wait_pair()
    tile_msg[...] = tile_own[section] + tile_mate[...]
    loop(
        0, NEAR, lambda step: send(7, beyond(step), tile_msg.at[beyond(step)], tile_in.at[place])
    )
    loop(1, NEAR, lambda step: send(7, near(step), tile_msg.at[near(step)], tile_in.at[place]))
    wait_tiles = settle(7, tile_in.at[pl.ds(0, peers - 1)])
    tile_in[place] = tile_msg[place]
    wait_grads()
    wait_far()
    total = jnp.sum(near_in[...].astype(F32), axis=0) + jnp.sum(far_in[...].astype(F32), axis=0)
    squares = total * total
    stat = stats_base[...]
    for part in range(2):
        sums = jnp.sum(squares[part * 8 : (part + 1) * 8], axis=0, keepdims=True)
        for tile in range(TILES // 2):
            stat = jnp.where(
                stat_line == part * (TILES // 2) + tile, sums[:, tile * 128 : (tile + 1) * 128], stat
            )
    wait_tiles()
    tile_total = jnp.sum(tile_in[...], axis=0)
    conv_squares = jnp.where(lane < C1 + C2, tile_total * tile_total, 0.0)
    stat = jnp.where(stat_line == TILES, jnp.sum(conv_squares, axis=0, keepdims=True), stat)

    stats_in[place] = stat.astype(BF)
    half_in[section, :, 0:QUARTER] = total[0:8]
    half_in[section, :, QUARTER:HALF] = total[8:16]
    half_in[section, :, HALF : HALF + 128] = tile_total
    wait_stats = send_peers(8, stats_in.at[place], stats_in)
    wait_half_grads = send_mate(3, half_in.at[section], half_in.at[section], half_in.at[mate])
    tile_out[...] = tile_total
    wait_stats()
    stats_both[section] = jnp.sum(stats_in[...].astype(F32), axis=0)
    wait_half_stats = send_mate(
        4, stats_both.at[section], stats_both.at[section], stats_both.at[mate]
    )
    wait_half_grads()
    for half in range(2):
        main_out[:, half * HALF : (half + 1) * HALF] = half_in[half, :, 0:HALF]
        conv_out[half * 8 : (half + 1) * 8] = half_in[half, :, HALF : HALF + 128]
    wait_half_stats()
    stats_out[...] = stats_both[...]

    for wait in sends:
        wait()


def fused_step(peers, frames, shards, biases, rows):
    count = frames.shape[1]
    side = frames.shape[2]
    scratch = local_scratch(count, side)
    scratch[7] = pltpu.VMEM((count, LIN_PAD), BF)
    scratch += [
        pltpu.VMEM((8, 2 * HALF), F32),
        pltpu.VMEM((peers, 16, 128), BF),
        pltpu.VMEM((2, peers, 16, QUARTER), BF),
        pltpu.VMEM((D, 2 * HALF), BF),
        pltpu.VMEM((2, peers, 8, HALF), F32),
        pltpu.VMEM((peers, 16, QUARTER), BF),
        pltpu.VMEM((peers, 16, QUARTER), BF),
        pltpu.VMEM((peers, 16, QUARTER), BF),
        pltpu.VMEM((NEAR, 16, QUARTER), BF),
        pltpu.VMEM((2, FOUR, 16, QUARTER), BF),
        pltpu.VMEM((2, 16, QUARTER), BF),
        pltpu.VMEM((2, 16, QUARTER), BF),
        pltpu.VMEM((2, peers, 8, 128), F32),
        pltpu.VMEM((peers, 8, 128), F32),
        pltpu.VMEM((peers, 8, 128), F32),
        pltpu.VMEM((peers, 8, 128), F32),
        pltpu.VMEM((peers, 16, 128), BF),
        pltpu.VMEM((2, 16, 128), F32),
        pltpu.VMEM((16, 128), F32),
        pltpu.VMEM((2, 8, HALF + 128), F32),
        pltpu.SemaphoreType.DMA((9,)),
        pltpu.SemaphoreType.DMA((9,)),
        pltpu.SemaphoreType.DMA((5,)),
        pltpu.SemaphoreType.DMA((5,)),
    ]
    shapes = [(8, 2 * HALF), (16, 128), (8, 128), (2, 16, 128)]
    operands = [frames.transpose(0, 2, 1, 3), *shards, biases, *rows]
    return pl.pallas_call(
        functools.partial(fused_kernel, peers),
        out_shape=[jax.ShapeDtypeStruct(shape, F32) for shape in shapes],
        in_specs=[ANY_SPEC] + [VMEM_SPEC] * (len(operands) - 1),
        out_specs=[VMEM_SPEC] * len(shapes),
        scratch_shapes=scratch,
        compiler_params=pltpu.CompilerParams(
            vmem_limit_bytes=56 * 1024 * 1024, collective_id=0, has_side_effects=True
        ),
    )(*operands)


def column_of(row):
    square = jnp.broadcast_to(row, (8, 8))
    return jnp.sum(jnp.where(iota((8, 8), 0) == iota((8, 8), 1), square, 0.0), axis=1, keepdims=True)


def row_back(column):
    square = jnp.broadcast_to(column, (8, 8))
    return jnp.sum(jnp.where(iota((8, 8), 0) == iota((8, 8), 1), square, 0.0), axis=0, keepdims=True)


def total_of(value):
    return jnp.sum(jnp.sum(value, axis=0, keepdims=True), axis=1, keepdims=True)


def update_kernel(
    main_ref,
    convg_ref,
    tile_ref,
    stats_ref,
    conv_ref,
    lin_ref,
    mats_ref,
    emb_ref,
    heads_ref,
    bias_ref,
    conv_moment,
    lin_rows,
    lin_cols,
    mats_rows,
    mats_cols,
    emb_moment,
    head_moment,
    bias_moment,
    conv_new,
    conv_grad,
    conv_moment_new,
    lin_new,
    lin_grad,
    lin_rows_new,
    lin_cols_new,
    mats_new,
    mats_grad,
    mats_rows_new,
    mats_cols_new,
    emb_new,
    emb_grad,
    emb_moment_new,
    heads_new,
    heads_grad,
    head_moment_new,
    bias_new,
    bias_grad,
    bias_moment_new,
    norm_out,
    loss_out,
    conv_low,
    lin_low,
):
    stats = stats_ref[...]
    tile = tile_ref[...]
    squares = jnp.where(iota((2, 16, 128), 1) <= TILES, stats, 0.0)
    squares = total_of(squares[0] + squares[1])
    scales = stats[0, TILES + 1 : TILES + 2] + stats[0, TILES + 2 : TILES + 3]
    bias_raw = jnp.concatenate(
        [tile[4:5, 64 : 64 + C1 + C2]] + [tile[k : k + 1, 64:128] for k in range(4)], axis=1
    )
    norm = jnp.sqrt(squares + total_of(bias_raw * bias_raw))
    factor = jnp.minimum(1.0, CLIP_LIMIT / norm)
    norm_out[...] = norm
    loss_out[...] = total_of(tile[5:6, 64:128])

    def simple(weight, grad, moment, square_total, outs):
        new, moment_new = unfactored(
            weight, grad, moment, relative(square_total, weight.size * outs[3])
        )
        for out, value in zip(outs, (new, grad, moment_new)):
            out[...] = value.reshape(out.shape)
        return new

    peers = D // lin_ref.shape[0]
    conv = simple(
        conv_ref[...],
        factor * convg_ref[:, 0 : C1 + C2],
        conv_moment[...],
        scales[:, 0:1],
        (conv_new, conv_grad, conv_moment_new, peers),
    )
    conv_low[...] = conv.astype(BF)
    simple(
        emb_ref[...],
        factor * main_ref[:, AT_EMB:AT_HEADS],
        emb_moment[...],
        scales[:, 3:4],
        (emb_new, emb_grad, emb_moment_new, peers),
    )
    heads_t = jnp.concatenate(
        [main_ref[:, LIN_PAD - 128 : LIN_PAD], jnp.zeros((120, 128), F32)], axis=0
    ).T
    simple(
        heads_ref[...],
        factor * heads_t[HEAD_LANE : HEAD_LANE + 3 * GAMES, 0:8],
        head_moment[...],
        scales[:, 4:5],
        (heads_new, heads_grad, head_moment_new, peers),
    )
    bias = bias_ref[...].reshape(1, BIAS)
    simple(
        bias,
        factor * bias_raw,
        bias_moment[...].reshape(1, BIAS),
        total_of(bias * bias),
        (bias_new, bias_grad, bias_moment_new, 1),
    )
    row_sums = [stats[t // TILES, t % TILES : t % TILES + 1] for t in range(24)]

    def factored(weight, grad, rows_old, cols_old, row_sum, square_total, entries):
        rows = DECAY_RATE * rows_old + (1.0 - DECAY_RATE) * (
            factor * factor * row_sum / D + FLOOR_ONE
        )
        wide = grad.shape[1]
        cols = DECAY_RATE * cols_old + (1.0 - DECAY_RATE) * (
            jnp.sum(grad * grad + FLOOR_ONE, axis=1, keepdims=True) / wide
        )
        mean = jnp.sum(rows, axis=1, keepdims=True) / wide
        second = rows * cols / mean
        new = weight - STEP_RATE * relative(square_total, entries) * grad * lax.rsqrt(second)
        return new, rows, cols

    grad = factor * main_ref[:, 0:FEAT]
    new, rows, cols = factored(
        lin_ref[...],
        grad,
        lin_rows[...].reshape(1, FEAT),
        column_of(lin_cols[...]),
        jnp.concatenate(row_sums[:21], axis=1)[:, 0:FEAT],
        scales[:, 1:2],
        FEAT * D,
    )
    lin_new[...] = new
    lin_grad[...] = grad
    lin_rows_new[...] = rows.reshape(FEAT)
    lin_cols_new[...] = row_back(cols)
    lin_low[...] = new.astype(BF)
    for k in range(3):
        grad = factor * main_ref[:, AT_MATS + k * D : AT_MATS + (k + 1) * D]
        new, rows, cols = factored(
            mats_ref[k],
            grad,
            mats_rows[k : k + 1],
            column_of(mats_cols[k : k + 1]),
            row_sums[21 + k],
            scales[:, 2:3],
            3 * D * D,
        )
        mats_new[k] = new
        mats_grad[k] = grad
        mats_rows_new[k : k + 1] = rows
        mats_cols_new[k : k + 1] = row_back(cols)


def fused_device(
    frames,
    options,
    legal,
    games,
    valid,
    rewards,
    returns,
    conv_kernels,
    enc_linear,
    plan_mats,
    option_emb,
    heads,
    biases,
    conv_moment,
    lin_rows,
    lin_cols,
    mats_rows,
    mats_cols,
    emb_moment,
    head_moment,
    bias_moment,
):
    width = enc_linear.shape[1]
    peers = D // width
    shards = (
        conv_kernels,
        enc_linear.T,
        plan_mats.transpose(0, 2, 1),
        option_emb.T,
        heads.reshape(3 * GAMES, width),
    )
    summed = fused_step(
        peers,
        frames,
        shards,
        biases,
        (
            options.transpose(2, 0, 1),
            legal.transpose(2, 0, 1),
            games,
            valid.transpose(2, 0, 1),
            rewards.transpose(2, 0, 1),
            returns.transpose(0, 2, 1),
        ),
    )
    shapes = [(16, 48)] * 3 + [(8, FEAT)] * 2 + [(FEAT,), (1, 8)] + [(3, 8, D)] * 2 + [(3, D), (3, 8)]
    shapes += [(8, OPTS)] * 3 + [(24, 8)] * 3 + [(BIAS,)] * 3 + [(1, 1)] * 2
    outs = [jax.ShapeDtypeStruct(shape, F32) for shape in shapes]
    outs += [jax.ShapeDtypeStruct((16, 48), BF), jax.ShapeDtypeStruct((8, FEAT), BF)]
    operands = [
        *summed,
        *shards,
        biases,
        conv_moment,
        lin_rows,
        lin_cols.reshape(1, width),
        mats_rows,
        mats_cols,
        emb_moment.T,
        head_moment.reshape(3 * GAMES, width),
        bias_moment,
    ]
    o = pl.pallas_call(
        update_kernel,
        out_shape=outs,
        in_specs=[VMEM_SPEC] * len(operands),
        out_specs=[VMEM_SPEC] * len(outs),
    )(*operands)
    flat_heads = [h.reshape(3, GAMES, width) for h in o[14:17]]
    return (
        *o[0:3],
        o[3].T,
        o[4].T,
        o[5],
        o[6].reshape(width),
        o[7].transpose(0, 2, 1),
        o[8].transpose(0, 2, 1),
        o[9],
        o[10],
        o[11].T,
        o[12].T,
        o[13].T,
        *flat_heads,
        *o[17:20],
        o[20].reshape(()),
        o[21].reshape(()),
        o[22],
        o[23].T,
    )


def gather_rows(shard):
    return lax.all_gather(shard, "dp", axis=0, tiled=True)


def relative(square_total, entries):
    return jnp.maximum(FLOOR_TWO, jnp.sqrt(square_total / entries))


def unfactored(weight, grad, moment, scale):
    moment_new = DECAY_RATE * moment + (1.0 - DECAY_RATE) * (grad * grad + FLOOR_ONE)
    return (weight - STEP_RATE * scale * grad * lax.rsqrt(moment_new), moment_new)


def per_device(
    frames,
    options,
    legal,
    games,
    valid,
    rewards,
    returns,
    conv_kernels,
    enc_linear,
    plan_mats,
    option_emb,
    heads,
    biases,
    conv_moment,
    lin_rows,
    lin_cols,
    mats_rows,
    mats_cols,
    emb_moment,
    head_moment,
    bias_moment,
):
    weight_squares = lax.psum(
        (
            jnp.sum(conv_kernels * conv_kernels),
            jnp.sum(enc_linear * enc_linear),
            jnp.sum(plan_mats * plan_mats),
            jnp.sum(option_emb * option_emb),
            jnp.sum(heads * heads),
        ),
        "dp",
    )
    width = enc_linear.shape[1]
    kernels = gather_rows(conv_kernels.astype(BF))
    linear_t = gather_rows(enc_linear.astype(BF).T)
    mats_t = gather_rows(plan_mats.astype(BF).transpose(2, 0, 1)).transpose(1, 0, 2)
    emb_t = gather_rows(option_emb.astype(BF).T)
    heads_t = gather_rows(heads.astype(BF).reshape(3 * GAMES, width).T)
    table = jnp.pad(
        jnp.concatenate([emb_t, heads_t], axis=1),
        ((0, 0), (EMB_LANE, 128 - HEAD_LANE - 3 * GAMES)),
    )
    lin, mats, table_grad, conv, small = local_step(
        frames,
        kernels,
        linear_t,
        mats_t,
        table,
        biases,
        options,
        legal,
        games,
        valid,
        rewards,
        returns,
    )
    rows = jnp.concatenate(
        [lin, mats[0], mats[1], mats[2], table_grad[:, EMB_LANE : HEAD_LANE + 3 * GAMES]], axis=1
    )
    rows = lax.psum(lax.psum_scatter(rows, "dp", scatter_dimension=0, tiled=True), "section")
    conv = lax.psum(
        lax.psum_scatter(conv[:, : C1 + C2], "dp", scatter_dimension=0, tiled=True), "section"
    )
    small = lax.psum(small, ("section", "dp"))
    inverse_count = 1.0 / jnp.sum(small[4])
    loss_value = jnp.sum(small[3]) * inverse_count
    bias_raw = (
        jnp.concatenate([small[0, : C1 + C2], small[1], small[2]]) * inverse_count
    )
    rows = rows * inverse_count
    g_conv = conv * inverse_count
    g_lin = rows[:, :FEAT].T
    g_mats = rows[:, FEAT : FEAT + 3 * D].reshape(width, 3, D).transpose(1, 2, 0)
    g_emb = rows[:, FEAT + 3 * D : FEAT + 3 * D + OPTS].T
    g_heads = rows[:, FEAT + 3 * D + OPTS :].T.reshape(3, GAMES, width)
    partial_squares = (
        jnp.sum(g_conv * g_conv)
        + jnp.sum(g_lin * g_lin)
        + jnp.sum(g_mats * g_mats)
        + jnp.sum(g_emb * g_emb)
        + jnp.sum(g_heads * g_heads)
    )
    reduced = lax.psum(
        (partial_squares, jnp.sum(g_lin * g_lin, axis=1), jnp.sum(g_mats * g_mats, axis=2)), "dp"
    )
    grad_norm = jnp.sqrt(reduced[0] + jnp.sum(bias_raw * bias_raw))
    factor = jnp.minimum(1.0, CLIP_LIMIT / grad_norm)
    conv_grad = factor * g_conv
    lin_grad = factor * g_lin
    mats_grad = factor * g_mats
    emb_grad = factor * g_emb
    heads_grad = factor * g_heads
    bias_grad = factor * bias_raw
    conv_new, conv_moment_new = unfactored(
        conv_kernels, conv_grad, conv_moment, relative(weight_squares[0], KERN * (C1 + C2))
    )
    emb_new, emb_moment_new = unfactored(
        option_emb, emb_grad, emb_moment, relative(weight_squares[3], OPTS * D)
    )
    heads_new, head_moment_new = unfactored(
        heads, heads_grad, head_moment, relative(weight_squares[4], 3 * GAMES * D)
    )
    bias_new, bias_moment_new = unfactored(
        biases, bias_grad, bias_moment, relative(jnp.sum(biases * biases), BIAS)
    )
    lin_rows_new = DECAY_RATE * lin_rows + (1.0 - DECAY_RATE) * (
        factor * factor * reduced[1] / D + FLOOR_ONE
    )
    lin_cols_new = DECAY_RATE * lin_cols + (1.0 - DECAY_RATE) * jnp.mean(
        lin_grad * lin_grad + FLOOR_ONE, axis=0
    )
    lin_second = lin_rows_new[:, None] * lin_cols_new[None, :] / jnp.mean(lin_rows_new)
    lin_new = enc_linear - STEP_RATE * relative(weight_squares[1], FEAT * D) * lin_grad * lax.rsqrt(
        lin_second
    )
    mats_rows_new = DECAY_RATE * mats_rows + (1.0 - DECAY_RATE) * (
        factor * factor * reduced[2] / D + FLOOR_ONE
    )
    mats_cols_new = DECAY_RATE * mats_cols + (1.0 - DECAY_RATE) * jnp.mean(
        mats_grad * mats_grad + FLOOR_ONE, axis=1
    )
    mats_second = (
        mats_rows_new[:, :, None]
        * mats_cols_new[:, None, :]
        / jnp.mean(mats_rows_new, axis=1)[:, None, None]
    )
    mats_new = plan_mats - STEP_RATE * relative(weight_squares[2], 3 * D * D) * mats_grad * lax.rsqrt(
        mats_second
    )
    return (
        conv_new,
        conv_grad,
        conv_moment_new,
        lin_new,
        lin_grad,
        lin_rows_new,
        lin_cols_new,
        mats_new,
        mats_grad,
        mats_rows_new,
        mats_cols_new,
        emb_new,
        emb_grad,
        emb_moment_new,
        heads_new,
        heads_grad,
        head_moment_new,
        bias_new,
        bias_grad,
        bias_moment_new,
        grad_norm,
        loss_value,
        conv_new.astype(BF),
        lin_new.astype(BF),
    )


def solution(mesh):
    return jax.shard_map(
        fused_device if mesh.shape["dp"] * 8 == D else per_device,
        mesh=mesh,
        in_specs=(
            P(None, "dp", None, None),
            P(None, "dp", None),
            P(None, "dp", None),
            P(None, "dp"),
            P(None, "dp", None),
            P(None, "dp", None),
            P(None, "dp", None),
            P("dp", None),
            P(None, "dp"),
            P(None, None, "dp"),
            P(None, "dp"),
            P(None, None, "dp"),
            P(),
            P("dp", None),
            P(),
            P("dp"),
            P(),
            P(None, "dp"),
            P(None, "dp"),
            P(None, None, "dp"),
            P(),
        ),
        out_specs=(
            P("dp", None),
            P("dp", None),
            P("dp", None),
            P(None, "dp"),
            P(None, "dp"),
            P(),
            P("dp"),
            P(None, None, "dp"),
            P(None, None, "dp"),
            P(),
            P(None, "dp"),
            P(None, "dp"),
            P(None, "dp"),
            P(None, "dp"),
            P(None, None, "dp"),
            P(None, None, "dp"),
            P(None, None, "dp"),
            P(),
            P(),
            P(),
            P(),
            P(),
            P("dp", None),
            P(None, "dp"),
        ),
        check_vma=False,
    )
```

```python
import functools

import jax
import jax.numpy as jnp
from jax import lax
from jax.experimental import pallas as pl
from jax.experimental.pallas import tpu as pltpu
from jax.sharding import PartitionSpec as P

D = 128
C1 = 16
C2 = 32
OPTS = 18
KERN = 256
GAMES = 8
FEAT = 2592
BIAS = 304

OUT1 = 20
OUT2 = 9
WIDE = 384
LIN_PAD = 2688
EMB_LANE = FEAT % 128
HEAD_LANE = EMB_LANE + OPTS
CHUNK = 12
LATE_POSITIONS = 12
FEATS_ROW = OUT2 * C2

CLIP_LIMIT = 0.05
DECAY_RATE = 0.8
STEP_RATE = 0.5
FLOOR_ONE = 1e-30
FLOOR_TWO = 0.001

HIGH = lax.Precision.HIGHEST
BF = jnp.bfloat16
F32 = jnp.float32


def dot(left, right, over_left=1, over_right=0, precision=None):
    return lax.dot_general(
        left,
        right,
        (((over_left,), (over_right,)), ((), ())),
        precision=precision,
        preferred_element_type=F32,
    )


def sigmoid(value):
    return 0.5 * jnp.tanh(0.5 * value) + 0.5


def slope(value, sigma):
    return sigma * (1.0 + value * (1.0 - sigma))


def iota(shape, axis):
    return lax.broadcasted_iota(jnp.int32, shape, axis)


def turn(value, steps):
    return pltpu.roll(value, steps, 1)


def fold(value, width):
    step = 64
    while step >= width:
        value = value + turn(value, step)
        step //= 2
    return value


def row_of(column):
    square = jnp.broadcast_to(column, (128, 128))
    return jnp.sum(jnp.where(iota((128, 128), 0) == iota((128, 128), 1), square, 0.0), axis=0, keepdims=True)


def load_frames(frames_hbm, section, frame_buf, sems, chunk):
    copies = []
    for which in range(frame_buf.shape[0] // chunk):
        rows = pl.ds(which * chunk, chunk)
        copies.append(
            pltpu.make_async_copy(
                frames_hbm.at[section, rows], frame_buf.at[rows], sems.at[which]
            )
        )
    return copies


def place_frames(frame_buf, pixels, first, chunk, frames):
    for row in range(first, first + chunk):
        block, part = row // 4, row % 4
        pixels[block * frames : (block + 1) * frames, part * WIDE : part * WIDE + 336] = frame_buf[row]


def fill_band(wide, put, width, taps, blocks):
    per_tile = 128 // width
    group = iota((width, 128), 1) // width
    for tap in range(taps):
        base = 2 * tap * width
        for block in range(blocks + 1):
            tile, spot = divmod(block, per_tile)
            lanes = slice(tile * 128, (tile + 1) * 128)
            left = jnp.where(group == spot, wide[base : base + width, lanes], 0.0)
            right = wide[base + width : base + 2 * width]
            if spot > 0:
                left = jnp.where(group == spot - 1, right[:, lanes], left)
            elif block > 0:
                before = slice((tile - 1) * 128, tile * 128)
                put(tap, block, before, jnp.where(group == per_tile - 1, right[:, before], 0.0).astype(BF))
            put(tap, block, lanes, left.astype(BF))


def repeat_kernels(kernels, first, width, positions, lanes):
    held = kernels.shape[1]
    rows = iota((held, lanes), 0)
    cols = iota((held, lanes), 1)
    pick = jnp.where((cols % width + first == rows) & (cols < positions * width), 1.0, 0.0)
    return dot(kernels, pick.astype(BF))


def build_one(kernels, band):
    wide = repeat_kernels(kernels, 0, C1, LATE_POSITIONS, 256)

    def put(tap, block, lanes, value):
        rows = tap * 256 + block * C1
        band[rows : rows + C1, lanes] = value

    fill_band(wide, put, C1, 4, LATE_POSITIONS)


def build_two(kernels, band):
    wide = repeat_kernels(kernels, C1, C2, OUT2, WIDE)

    def put(tap, block, lanes, value):
        rows = tap * WIDE + block * C2
        band[rows : rows + C2, lanes] = value

    fill_band(wide, put, C2, 4, OUT2)


def clear_bands(band_one, band_two):
    band_one[...] = jnp.zeros(band_one.shape, BF)
    band_two[...] = jnp.zeros(band_two.shape, BF)


def wide_biases(bias_row):
    bias8 = jnp.broadcast_to(bias_row, (8, BIAS))
    rows = iota((BIAS, WIDE), 0)
    lanes = iota((BIAS, WIDE), 1)
    one = jnp.where((lanes % C1 == rows) & (lanes < OUT1 * C1), 1.0, 0.0)
    two = jnp.where((lanes % C2 + C1 == rows) & (lanes < OUT2 * C2), 1.0, 0.0)
    rows = iota((D, BIAS), 0)
    lanes = iota((D, BIAS), 1)
    three = jnp.where(lanes == rows + C1 + C2, 1.0, 0.0)
    four = jnp.where(lanes == rows + C1 + C2 + D, 1.0, 0.0)
    return (
        dot(bias8, one, precision=HIGH)[0:1],
        dot(bias8, two, precision=HIGH)[0:1],
        dot(three, bias8, 1, 1, precision=HIGH)[:, 0:1],
        dot(four, bias8, 1, 1, precision=HIGH)[:, 0:1],
    )


def encode_one(pixels, band_one, half, more, bias, z_one, act_one, frames, chunk):
    rows = chunk * frames
    band = band_one[half]
    for first in range(0, OUT1, chunk):
        block = pixels[pl.ds(pl.multiple_of((half + first) * frames, frames), rows), :]
        parts = []
        for low, wide in ((0, 128), (128, 256)):
            window = jnp.concatenate(
                [block[:, tap * WIDE + low : tap * WIDE + low + 256] for tap in range(4)], axis=1
            )
            parts.append(dot(window, band[:, 0:wide]))
        z = jnp.concatenate(parts, axis=1)
        for step in range(chunk):
            at, part = divmod(first + step, 2)
            spot = (slice(at * frames, (at + 1) * frames), slice(part * WIDE, (part + 1) * WIDE))
            z_step = z[step * frames : (step + 1) * frames]
            if more:
                z_one[spot] = z_step
            else:
                z_step = z_step + z_one[spot] + bias
                z_one[spot] = z_step
                act_one[spot] = (z_step * sigmoid(z_step)).astype(BF)


def encode_two(act_one, band_two, bias, z_two, act_two, frames, chunk):
    half = 2 * WIDE
    rows = chunk * frames
    for first in range(0, OUT2, chunk):
        low = first * frames
        z = dot(act_one[low : low + rows, :], band_two[0:half, :]) + dot(
            act_one[low + frames : low + frames + rows, :], band_two[half : 2 * half, :]
        )
        z = z + bias
        z_two[low : low + rows] = z
        act = (z * sigmoid(z)).astype(BF)
        for step in range(chunk):
            at = (first + step) * FEATS_ROW
            act_two[:, at : at + FEATS_ROW] = act[step * frames : (step + 1) * frames, :FEATS_ROW]


def back_two(dstate_t, linear_t, z_two, dz_two, frames):
    dact = dot(dstate_t, linear_t, 0, 0)
    dz_two[0:frames] = jnp.zeros((frames, WIDE), BF)
    dz_two[(OUT2 + 1) * frames : (OUT2 + 2) * frames] = jnp.zeros((frames, WIDE), BF)
    blank = jnp.zeros((frames, WIDE - FEATS_ROW), F32)
    for at in range(OUT2):
        z = z_two[at * frames : (at + 1) * frames]
        part = jnp.concatenate([dact[:, at * FEATS_ROW : (at + 1) * FEATS_ROW], blank], axis=1)
        dz_two[(at + 1) * frames : (at + 2) * frames] = (part * slope(z, sigmoid(z))).astype(BF)


def back_one(dz_two, band_two, z_one, dz_one, frames, chunk):
    half = 2 * WIDE
    rows = chunk * frames
    for first in range(0, OUT1 // 2, chunk):
        low = first * frames
        dact = dot(dz_two[low + frames : low + frames + rows], band_two[0:half], 1, 1) + dot(
            dz_two[low : low + rows], band_two[half : 2 * half], 1, 1
        )
        z = z_one[low : low + rows]
        dz = (dact * slope(z, sigmoid(z))).astype(BF)
        for step in range(chunk):
            for part in range(2):
                at = (2 * (first + step) + part) * frames
                dz_one[at : at + frames] = dz[
                    step * frames : (step + 1) * frames, part * WIDE : (part + 1) * WIDE
                ]


def band_sums(term, outputs, width):
    per_tile = 128 // width
    lane = iota((width, 128), 1) // width
    sums = []
    for shift in range(2):
        total = None
        for spot in range(per_tile):
            part = None
            for position in range(outputs):
                tile, inside = divmod(position + shift, per_tile)
                if inside != spot:
                    continue
                one = term(position, tile)
                part = one if part is None else part + one
            if part is None:
                continue
            part = jnp.where(lane == spot, part, 0.0)
            total = part if total is None else total + part
        sums.append(fold(total, width))
    return sums


def kernel_grad(terms, outputs, width):
    tiles = []
    lane = iota((width, 128), 1) // width
    pieces = []
    for term in terms:
        pieces.extend(band_sums(term, outputs, width))
    per_tile = 128 // width
    for tile in range(2):
        total = jnp.zeros((width, 128), F32)
        for spot in range(per_tile):
            total = jnp.where(lane == spot, pieces[tile * per_tile + spot], total)
        tiles.append(total)
    return jnp.concatenate(tiles, axis=1)


def tiled(tile, count):
    return jnp.concatenate([tile] * count, axis=1)


def twice(row):
    return jnp.concatenate([row, row], axis=1)


def plan(states, mats_t, table, bias_col, options, legal, games, valid, rewards, returns, scale):
    frames = states.shape[1]
    pairs = OPTS // 2
    lanes = OPTS * frames
    trans_in, trans_out, value_in = mats_t
    low_half = iota((1, 128), 1) < frames
    upper = iota((1, 128), 1) // frames

    valid_f = [twice(v.astype(F32)) for v in valid]
    rewards = [twice(r) for r in rewards]
    returns = [twice(r) for r in returns]
    chosen = [twice(o) for o in options]
    game = twice(games)

    game_rows = iota((128, WIDE), 0) - HEAD_LANE
    game_pick = jnp.where(
        game_rows == tiled(game, 3) + GAMES * (iota((128, WIDE), 1) // 128), 1.0, 0.0
    )
    head_rows = dot(table, game_pick.astype(BF))
    hr, hd, hv = (head_rows[:, k * 128 : (k + 1) * 128] for k in range(3))

    option_rows = jnp.where(
        iota((128, lanes), 0) - EMB_LANE == iota((128, lanes), 1) // frames, 1.0, 0.0
    ).astype(BF)
    s_low = twice(states)
    s_f = s_low.astype(F32)
    base = dot(trans_in, s_low)
    pre = tiled(base, pairs) + dot(table, option_rows)
    sig_h = sigmoid(pre)
    hid = pre * sig_h
    hid_low = hid.astype(BF)
    after = tiled(s_f, pairs) + dot(trans_out, hid_low)
    after_low = after.astype(BF)
    judge_pre = dot(value_in, after_low) + bias_col
    sig_j = sigmoid(judge_pre)
    judged = judge_pre * sig_j

    def tile_of(value, k):
        return value[:, k * 128 : (k + 1) * 128]

    def over(value):
        return jnp.sum(value, axis=0, keepdims=True)

    reward = [over(tile_of(hid, k) * hr) for k in range(pairs)]
    gamma = [sigmoid(over(tile_of(hid, k) * hd)) for k in range(pairs)]
    value = [over(tile_of(judged, k) * hv) for k in range(pairs)]
    backed = [reward[k] + gamma[k] * value[k] for k in range(pairs)]
    allowed = [
        jnp.concatenate([legal[2 * k], legal[2 * k + 1]], axis=1) > 0 for k in range(pairs)
    ]
    highest = functools.reduce(
        jnp.maximum, [jnp.where(allowed[k], backed[k], -1e30) for k in range(pairs)]
    )
    highest = jnp.maximum(highest, turn(highest, frames))
    shares = [
        jnp.where(allowed[k], jnp.exp(jnp.where(allowed[k], backed[k] - highest, -60.0)), 0.0)
        for k in range(pairs)
    ]

    def halves(total):
        return total + turn(total, frames)

    share_sum = halves(sum(shares))
    planned = halves(sum(shares[k] * backed[k] for k in range(pairs))) / share_sum
    choose = [chosen[0] == 2 * k + upper for k in range(pairs)]

    def chosen_of(parts):
        return halves(sum(jnp.where(choose[k], parts[k], 0.0) for k in range(pairs)))

    roll_f = [chosen_of([tile_of(after, k) for k in range(pairs)])]
    roll_low = [roll_f[0].astype(BF)]
    plan_miss = planned - returns[0]
    reward_miss = [chosen_of(reward) - rewards[0]]
    value_miss = [chosen_of(value) - returns[1]]
    steps = len(options)
    picks, pre_k, sig_k, hid_k, hid_k_low, judge_k, sig_jk, judged_k = ([None] for _ in range(8))
    for k in range(1, steps):
        picks.append(jnp.where(iota((128, 128), 0) - EMB_LANE == chosen[k], 1.0, 0.0).astype(BF))
        pre_k.append(dot(trans_in, roll_low[k - 1]) + dot(table, picks[k]))
        sig_k.append(sigmoid(pre_k[k]))
        hid_k.append(pre_k[k] * sig_k[k])
        hid_k_low.append(hid_k[k].astype(BF))
        roll_f.append(roll_f[k - 1] + dot(trans_out, hid_k_low[k]))
        roll_low.append(roll_f[k].astype(BF))
        judge_k.append(dot(value_in, roll_low[k]) + bias_col)
        sig_jk.append(sigmoid(judge_k[k]))
        judged_k.append(judge_k[k] * sig_jk[k])
        reward_miss.append(over(hid_k[k] * hr) - rewards[k])
        value_miss.append(over(judged_k[k] * hv) - returns[k + 1])
    errors = valid_f[0] * plan_miss * plan_miss
    for k in range(steps):
        errors = errors + valid_f[k] * (
            reward_miss[k] * reward_miss[k] + value_miss[k] * value_miss[k]
        )
    errors = jnp.where(low_half, errors * scale, 0.0)

    half = jnp.where(low_half, 1.0, 0.0)
    double = 2.0 * scale
    d_plan = double * valid_f[0] * plan_miss / share_sum
    d_reward_k = [double * valid_f[k] * reward_miss[k] for k in range(steps)]
    d_value_k = [double * valid_f[k] * value_miss[k] for k in range(steps)]

    def through(matrix_t, grad):
        return dot(matrix_t, grad, 0, 0)

    d_roll = None
    d_judge_low, d_step_low, d_pre_low = ([None] * steps for _ in range(3))
    d_hr = jnp.zeros((D, 128), F32)
    d_hd = jnp.zeros((D, 128), F32)
    d_hv = jnp.zeros((D, 128), F32)
    for k in range(steps - 1, 0, -1):
        d_judge_low[k] = (d_value_k[k] * hv * slope(judge_k[k], sig_jk[k])).astype(BF)
        term = through(value_in, d_judge_low[k])
        d_roll = term if d_roll is None else d_roll + term
        d_step_low[k] = d_roll.astype(BF)
        d_hid = through(trans_out, d_step_low[k]) + d_reward_k[k] * hr
        d_pre_low[k] = (d_hid * slope(pre_k[k], sig_k[k])).astype(BF)
        d_roll = d_roll + through(trans_in, d_pre_low[k])
        d_hr = d_hr + (half * d_reward_k[k]) * hid_k[k]
        d_hv = d_hv + (half * d_value_k[k]) * judged_k[k]

    d_backed = [d_plan * shares[k] * (1.0 + backed[k] - planned) for k in range(pairs)]
    d_reward = [
        d_backed[k] + jnp.where(choose[k], d_reward_k[0], 0.0) for k in range(pairs)
    ]
    d_value = [
        d_backed[k] * gamma[k] + jnp.where(choose[k], d_value_k[0], 0.0) for k in range(pairs)
    ]
    d_gamma = [d_backed[k] * value[k] * gamma[k] * (1.0 - gamma[k]) for k in range(pairs)]
    d_judge = [
        (d_value[k] * hv * slope(tile_of(judge_pre, k), tile_of(sig_j, k))).astype(BF)
        for k in range(pairs)
    ]
    d_judge_all = jnp.concatenate(d_judge, axis=1)
    d_after = through(value_in, d_judge_all)
    d_after = [
        tile_of(d_after, k) + jnp.where(choose[k], d_roll, 0.0) for k in range(pairs)
    ]
    d_after_low = jnp.concatenate([d.astype(BF) for d in d_after], axis=1)
    d_hid_all = through(trans_out, d_after_low)
    d_pre = [
        (
            (tile_of(d_hid_all, k) + d_reward[k] * hr + d_gamma[k] * hd)
            * slope(tile_of(pre, k), tile_of(sig_h, k))
        ).astype(BF)
        for k in range(pairs)
    ]
    d_pre_all = jnp.concatenate(d_pre, axis=1)
    d_base = through(trans_in, d_pre_all)
    d_state = halves(sum(d_after[k] + tile_of(d_base, k) for k in range(pairs)))
    for k in range(pairs):
        d_hr = d_hr + d_reward[k] * tile_of(hid, k)
        d_hd = d_hd + d_gamma[k] * tile_of(hid, k)
        d_hv = d_hv + d_value[k] * tile_of(judged, k)

    def both(parts):
        joined = [jnp.where(low_half, parts[k].astype(F32), parts[k + 1].astype(F32)) for k in range(1, steps, 2)]
        return [part.astype(BF) for part in joined]

    def with_steps(wide, parts):
        return jnp.concatenate([wide] + both(parts), axis=1)

    before_low = [None] + roll_low[:-1]
    d_pre_cat = with_steps(d_pre_all, d_pre_low)
    d_judge_cat = with_steps(d_judge_all, d_judge_low)
    grad_in = dot(d_pre_cat, with_steps(tiled(s_low, pairs), before_low), 1, 1)
    grad_out = dot(
        with_steps(d_after_low, d_step_low), with_steps(hid_low, hid_k_low), 1, 1
    )
    grad_value = dot(d_judge_cat, with_steps(after_low, roll_low), 1, 1)
    grad_table = dot(d_pre_cat, with_steps(option_rows, picks), 1, 1) + dot(
        jnp.concatenate([d_hr, d_hd, d_hv], axis=1), game_pick, 1, 1, precision=HIGH
    )
    grad_bias = jnp.sum(d_judge_cat.astype(F32), axis=1, keepdims=True)
    return (
        d_state[:, :frames],
        (grad_in, grad_out, grad_value),
        grad_table,
        grad_bias,
        errors,
    )


def frame_rows(section, refs):
    options_ref, legal_ref, games_ref, valid_ref, rewards_ref, returns_ref = refs

    def row(ref, k):
        return ref[k, pl.ds(section, 1), :]

    depth = options_ref.shape[0]
    return (
        [row(options_ref, k) for k in range(depth)],
        [row(legal_ref, k) for k in range(OPTS)],
        games_ref[pl.ds(section, 1), :],
        [row(valid_ref, k) for k in range(depth)],
        [row(rewards_ref, k) for k in range(depth)],
        [returns_ref[section, k : k + 1, :] for k in range(depth + 1)],
    )


def clear_tails(pixels):
    tail = jnp.zeros((pixels.shape[0], WIDE - 336), BF)
    for part in range(4):
        pixels[:, part * WIDE + 336 : (part + 1) * WIDE] = tail


def grad_kernel_two(act_one, dz_two, frames):
    rows = OUT2 * frames
    d_two = dz_two[frames : frames + rows]
    full = [dot(d_two, act_one[0:rows], 0, 0), dot(d_two, act_one[frames : frames + rows], 0, 0)]

    def term_of(tap):
        def term(position, tile):
            lane = (tap % 2) * WIDE + tile * 128
            return full[tap // 2][position * C2 : (position + 1) * C2, lane : lane + 128]

        return term

    grad = kernel_grad([term_of(tap) for tap in range(4)], OUT2, C2)
    return grad, fold(tiles_sum(dot(jnp.ones((8, rows), BF), d_two)), C2)


def grad_kernel_one(pixels, dz_one, frames):
    rows = OUT1 * frames
    d_one = dz_one[...]
    turned = d_one.T

    def term_of(tap):
        first = (tap // 4) * frames
        base = (tap % 4) * WIDE
        blocks = []
        for low, high in ((0, 128), (128, OUT1 * C1)):
            blocks.append(
                dot(turned[low:high], pixels[first : first + rows, base + low : base + low + 256])
            )

        def term(position, tile):
            group = min(position // 8, 1)
            inside, lane = position - 8 * group, (tile - group) * 128
            return blocks[group][inside * C1 : (inside + 1) * C1, lane : lane + 128]

        return term

    grad = kernel_grad([term_of(tap) for tap in range(8)], OUT1, C1)
    return grad, fold(tiles_sum(dot(jnp.ones((8, rows), BF), d_one)), C1)


def local_kernel(
    frames_hbm,
    kernels_ref,
    linear_ref,
    mats_ref,
    table_ref,
    bias_ref,
    options_ref,
    legal_ref,
    games_ref,
    valid_ref,
    rewards_ref,
    returns_ref,
    lin_out,
    mats_out,
    table_out,
    conv_out,
    small_out,
    frame_buf,
    pixels,
    band_one,
    band_two,
    z_one,
    act_one,
    z_two,
    act_two,
    dz_two,
    dz_one,
    sems,
):
    section = lax.axis_index("section")
    frames = frame_buf.shape[1]
    copies = load_frames(frames_hbm, section, frame_buf, sems, CHUNK)
    for copy in copies:
        copy.start()
    clear_bands(band_one, band_two)
    kernels = kernels_ref[...]
    build_one(kernels[0 : KERN // 2], band_one.at[0])
    build_one(kernels[KERN // 2 : KERN], band_one.at[1])
    build_two(kernels, band_two)
    bias_one, bias_two, bias_three, bias_four = wide_biases(bias_ref[...])
    clear_tails(pixels)
    for which, copy in enumerate(copies):
        copy.wait()
        place_frames(frame_buf, pixels, which * CHUNK, CHUNK, frames)
    encode_one(pixels, band_one, 0, True, bias_one, z_one, act_one, frames, 4)
    encode_one(pixels, band_one, 1, False, bias_one, z_one, act_one, frames, 4)
    encode_two(act_one, band_two, bias_two, z_two, act_two, frames, 3)
    linear_t = linear_ref[...]
    states = (dot(linear_t, act_two[...], 1, 1) + bias_three).astype(BF)
    d_state, grad_mats, grad_table, grad_bias, errors = plan(
        states,
        tuple(mats_ref[k] for k in range(3)),
        table_ref[...],
        bias_four,
        *frame_rows(
            section, (options_ref, legal_ref, games_ref, valid_ref, rewards_ref, returns_ref)
        ),
        1.0,
    )
    for k in range(3):
        mats_out[k] = grad_mats[k]
    table_out[...] = grad_table
    d_state_low = d_state.astype(BF)
    lin_out[...] = dot(d_state_low, act_two[...])
    back_two(d_state_low, linear_t, z_two, dz_two, frames)
    grad_two, bias_two_grad = grad_kernel_two(act_one, dz_two, frames)
    back_one(dz_two, band_two, z_one, dz_one, frames, 5)
    grad_one, bias_one_grad = grad_kernel_one(pixels, dz_one, frames)
    conv_out[...] = stack_kernels(grad_one, grad_two)
    lane = iota((8, 128), 1)
    line = iota((8, 128), 0)
    row_zero = jnp.where(
        lane < C1, bias_one_grad, jnp.where(lane < C1 + C2, turn(bias_two_grad, C1), 0.0)
    )
    count = sum(
        valid_ref[k, pl.ds(section, 1), :].astype(F32) for k in range(valid_ref.shape[0])
    )
    count = jnp.where(iota((1, 128), 1) < frames, twice(count), 0.0)
    small = jnp.where(line == 0, row_zero, 0.0)
    small = jnp.where(line == 1, row_of(lane_sum(d_state_low)), small)
    small = jnp.where(line == 2, row_of(grad_bias), small)
    small = jnp.where(line == 3, errors, small)
    small = jnp.where(line == 4, count, small)
    small_out[...] = small


def lane_sum(value):
    return jnp.sum(value.astype(F32), axis=1, keepdims=True)


def stack_kernels(grad_one, grad_two):
    rows = jnp.concatenate([grad_one, grad_two, jnp.zeros((128 - C1 - C2, KERN), F32)], axis=0)
    return rows.T


def tiles_sum(value):
    return sum(value[:, k * 128 : (k + 1) * 128] for k in range(value.shape[1] // 128))


VMEM_SPEC = pl.BlockSpec(memory_space=pltpu.VMEM)
ANY_SPEC = pl.BlockSpec(memory_space=pl.ANY)


def local_scratch(frames, side):
    return [
        pltpu.VMEM((side, frames, 336), BF),
        pltpu.VMEM(((OUT1 + 1) * frames, 4 * WIDE), BF),
        pltpu.VMEM((2, 4 * 256, 256), BF),
        pltpu.VMEM((4 * WIDE, WIDE), BF),
        pltpu.VMEM((OUT1 // 2 * frames, 2 * WIDE), F32),
        pltpu.VMEM((OUT1 // 2 * frames, 2 * WIDE), BF),
        pltpu.VMEM((OUT2 * frames, WIDE), F32),
        pltpu.VMEM((frames, FEAT), BF),
        pltpu.VMEM(((OUT2 + 2) * frames, WIDE), BF),
        pltpu.VMEM((OUT1 * frames, WIDE), BF),
        pltpu.SemaphoreType.DMA((side // CHUNK,)),
    ]


def local_step(frames, kernels, linear_t, mats_t, table, biases, options, legal, games, valid, rewards, returns):
    count = frames.shape[1]
    side = frames.shape[2]
    shapes = [(D, FEAT), (3, D, D), (D, 128), (KERN, 128), (8, 128)]
    return pl.pallas_call(
        local_kernel,
        out_shape=[jax.ShapeDtypeStruct(shape, F32) for shape in shapes],
        in_specs=[ANY_SPEC] + [VMEM_SPEC] * 11,
        out_specs=[VMEM_SPEC] * len(shapes),
        scratch_shapes=local_scratch(count, side),
        compiler_params=pltpu.CompilerParams(vmem_limit_bytes=56 * 1024 * 1024),
    )(
        frames.transpose(0, 2, 1, 3),
        kernels,
        linear_t,
        mats_t,
        table,
        biases.reshape(1, BIAS),
        options.transpose(2, 0, 1),
        legal.transpose(2, 0, 1),
        games,
        valid.transpose(2, 0, 1),
        rewards.transpose(2, 0, 1),
        returns.transpose(0, 2, 1),
    )


MESH = pl.DeviceIdType.MESH


def packed(value):
    axis = value.ndim - 2
    return jnp.concatenate([value[..., 0:QUARTER], value[..., QUARTER:HALF]], axis=axis)


QUARTER = 768
HALF = 2 * QUARTER
AT_EMB = FEAT
AT_HEADS = AT_EMB + OPTS
AT_MATS = LIN_PAD
TILES = HALF // 128
NEAR = 8
FOUR = 4


def fused_kernel(
    peers,
    frames_hbm,
    conv_hbm,
    lin_hbm,
    mats_hbm,
    emb_hbm,
    heads_hbm,
    bias_hbm,
    options_hbm,
    legal_hbm,
    games_hbm,
    valid_hbm,
    rewards_hbm,
    returns_hbm,
    main_out,
    conv_out,
    tile_out,
    stats_out,
    frame_buf,
    pixels,
    band_one,
    band_two,
    z_one,
    act_one,
    z_two,
    act_two,
    dz_two,
    dz_one,
    frame_sems,
    stage,
    kernel_msg,
    weight_msg,
    weights,
    grad_own,
    mate_msg,
    mate_in,
    grad_msg,
    near_in,
    cross_in,
    cross_msg,
    far_in,
    tile_own,
    tile_mate,
    tile_msg,
    tile_in,
    stats_in,
    stats_both,
    stats_base,
    half_in,
    send_sems,
    recv_sems,
    mate_send,
    mate_recv,
    conv_ref,
    lin_ref,
    mats_ref,
    emb_ref,
    heads_ref,
    bias_ref,
    options_ref,
    legal_ref,
    games_ref,
    valid_ref,
    rewards_ref,
    returns_ref,
    operand_sems,
):
    section = lax.axis_index("section")
    place = lax.axis_index("dp")
    mate = 1 - section
    frames = frame_buf.shape[1]

    barrier = pltpu.get_barrier_semaphore()

    def greet(step, carry):
        peer = lax.rem(place + step, peers)
        pl.semaphore_signal(barrier, inc=1, device_id=(section, peer), device_id_type=MESH)
        return carry

    pl.semaphore_signal(barrier, inc=1, device_id=(mate, place), device_id_type=MESH)
    lax.fori_loop(1, peers, greet, 0)
    loads = [
        pltpu.make_async_copy(source, target, operand_sems.at[which])
        for which, (source, target) in enumerate(
            (
                (conv_hbm, conv_ref),
                (lin_hbm, lin_ref),
                (mats_hbm, mats_ref),
                (emb_hbm, emb_ref),
                (heads_hbm, heads_ref),
                (bias_hbm, bias_ref),
                (options_hbm, options_ref),
                (legal_hbm, legal_ref),
                (games_hbm, games_ref),
                (valid_hbm, valid_ref),
                (rewards_hbm, rewards_ref),
                (returns_hbm, returns_ref),
            )
        )
    ]
    for load in loads:
        load.start()
    copies = load_frames(frames_hbm, section, frame_buf, frame_sems, CHUNK)
    wait_frames = lambda: [copy.wait() for copy in copies]
    for copy in copies:
        copy.start()

    sends = []

    side, spot = place // NEAR, lax.rem(place, NEAR)
    row, column = spot // FOUR, lax.rem(spot, FOUR)

    def near(step):
        return side * NEAR + lax.rem(spot + step, NEAR)

    def beyond(step):
        return (1 - side) * NEAR + lax.rem(spot + step, NEAR)

    def beside(step):
        return place - column + lax.rem(column + step, FOUR)

    def across(step, where):
        return (1 - side) * NEAR + lax.rem(row + step, 2) * FOUR + where

    def send(sems, peer, source, target):
        pltpu.make_async_remote_copy(
            src_ref=source,
            dst_ref=target,
            send_sem=send_sems.at[sems],
            recv_sem=recv_sems.at[sems],
            device_id=(section, peer),
            device_id_type=MESH,
        ).start()

    def loop(low, high, act):
        def body(step, carry):
            act(step)
            return carry

        lax.fori_loop(low, high, body, 0)

    def settle(sems, blocks):
        whole = pltpu.make_async_remote_copy(
            src_ref=blocks,
            dst_ref=blocks,
            send_sem=send_sems.at[sems],
            recv_sem=recv_sems.at[sems],
            device_id=(mate, place),
            device_id_type=MESH,
        )
        sends.append(whole.wait_send)
        return whole.wait_recv

    def send_peers(sems, source, target):
        loop(0, NEAR, lambda step: send(sems, beyond(step), source, target.at[place]))
        loop(1, NEAR, lambda step: send(sems, near(step), source, target.at[place]))
        return settle(sems, target.at[pl.ds(0, peers - 1)])

    def send_mate(which, source, target, landing):
        def copy(into):
            return pltpu.make_async_remote_copy(
                src_ref=source,
                dst_ref=into,
                send_sem=mate_send.at[which],
                recv_sem=mate_recv.at[which],
                device_id=(mate, place),
                device_id_type=MESH,
            )

        copy(target).start()
        sends.append(lambda: copy(target).wait_send())
        return lambda: copy(landing).wait_recv()

    for load in loads:
        load.wait()
    upper_lanes = iota((16, 128), 1) >= 64
    counts = sum(
        valid_ref[k, m : m + 1, :].astype(F32)
        for k in range(valid_ref.shape[0])
        for m in range(valid_ref.shape[1])
    )
    conv_pad = jnp.concatenate([conv_ref[...], jnp.zeros((16, 80), F32)], axis=1)
    kernel_msg[place] = jnp.where(
        upper_lanes & (iota((16, 128), 0) == 0), jnp.broadcast_to(twice(counts), (16, 128)), conv_pad
    ).astype(BF)
    heads_pad = jnp.concatenate([heads_ref[...], jnp.zeros((24, 120), F32)], axis=1)
    heads_pad = jnp.concatenate([heads_pad, jnp.zeros((104, 128), F32)], axis=0).T
    last = FEAT - EMB_LANE
    stage[:, 0:last] = lin_ref[:, 0:last]
    stage[:, last:LIN_PAD] = jnp.concatenate(
        [
            lin_ref[:, last:FEAT],
            emb_ref[...],
            heads_pad[0:8, 0 : 3 * GAMES],
            jnp.zeros((8, 128 - HEAD_LANE - 3 * GAMES), F32),
        ],
        axis=1,
    )
    for k in range(3):
        stage[:, AT_MATS + k * D : AT_MATS + (k + 1) * D] = mats_ref[k]
    first = stage[:, pl.ds(pl.multiple_of(section * HALF, 128), QUARTER)]
    second = stage[:, pl.ds(pl.multiple_of(section * HALF + QUARTER, 128), QUARTER)]
    weight_msg[section, place] = jnp.concatenate([first, second], axis=0).astype(BF)

    def square_sum(value):
        return jnp.sum(jnp.sum(value * value, axis=0, keepdims=True), axis=1, keepdims=True)

    weight_squares = [
        square_sum(conv_pad),
        square_sum(lin_ref[...]),
        square_sum(mats_ref[...].reshape(24, D)),
        square_sum(emb_ref[...]),
        square_sum(heads_ref[...]),
    ]
    stat_line = iota((16, 128), 0)
    stat = jnp.zeros((16, 128), F32)
    for which, value in enumerate(weight_squares):
        at = iota((16, 128), 1) == which
        rough = value.astype(BF).astype(F32)
        stat = jnp.where(at & (stat_line == TILES + 1), rough, stat)
        stat = jnp.where(at & (stat_line == TILES + 2), value - rough, stat)
    stats_base[...] = stat
    pl.semaphore_wait(barrier, peers)
    half_msg = weight_msg.at[section]

    def spread_own(sems, blocks):
        own = blocks.at[place]
        loop(0, 2, lambda step: send(sems, across(step, column), own, own))
        wait_across = settle(sems, blocks.at[pl.ds(0, 2)])
        loop(1, NEAR, lambda step: send(sems + 1, near(step), own, own))
        return wait_across, settle(sems + 1, blocks.at[pl.ds(0, NEAR - 1)])

    def pass_on(sems, blocks):
        for which in range(2):
            block = blocks.at[across(which, column)]
            loop(1, FOUR, lambda step: send(sems, beside(step), block, block))
        return settle(sems, blocks.at[pl.ds(0, 2 * (FOUR - 1))])

    wait_kernel_across, wait_kernel_near = spread_own(0, kernel_msg)
    wait_across, wait_near = spread_own(3, half_msg)

    clear_bands(band_one, band_two)
    bias_one, bias_two, bias_three, bias_four = wide_biases(bias_ref[...].reshape(1, BIAS))
    clear_tails(pixels)
    act_two[:, FEAT:LIN_PAD] = jnp.zeros((frames, LIN_PAD - FEAT), BF)
    for which, copy in enumerate(copies):
        copy.wait()
        place_frames(frame_buf, pixels, which * CHUNK, CHUNK, frames)
    wait_kernel_across()
    wait_kernel_beside = pass_on(2, kernel_msg)
    wait_kernel_near()

    def side_kernels(which):
        return kernel_msg[pl.ds(which * NEAR, NEAR)].reshape(KERN // 2, 128)

    build_one(side_kernels(side), band_one.at[side])
    wait_across()
    wait_beside = pass_on(5, half_msg)
    encode_one(pixels, band_one, side, True, bias_one, z_one, act_one, frames, 4)
    wait_kernel_beside()
    build_one(side_kernels(1 - side), band_one.at[1 - side])
    kernels = kernel_msg[...].reshape(KERN, 128)
    build_two(kernels, band_two)
    counted = jnp.where(iota((KERN, 128), 1) >= 64, kernels.astype(F32), 0.0)
    count = jnp.sum(jnp.sum(counted, axis=0, keepdims=True), axis=1, keepdims=True)
    scale = 1.0 / count
    encode_one(pixels, band_one, 1 - side, False, bias_one, z_one, act_one, frames, 4)
    wait_near()
    own_side, far_side = pl.ds(side * NEAR, NEAR), pl.ds((1 - side) * NEAR, NEAR)
    wait_own_side = send_mate(
        0, half_msg.at[own_side], half_msg.at[own_side], weight_msg.at[mate, own_side]
    )
    encode_two(act_one, band_two, bias_two, z_two, act_two, frames, 3)
    wait_beside()
    wait_far_side = send_mate(
        5, half_msg.at[far_side], half_msg.at[far_side], weight_msg.at[mate, far_side]
    )
    wait_own_side()
    wait_far_side()
    for half in range(2):
        block = weight_msg[half].astype(F32)
        for part in range(2):
            lane = (2 * half + part) * QUARTER
            weights[:, lane : lane + QUARTER] = (
                block[:, part * 8 : (part + 1) * 8].reshape(D, QUARTER).astype(BF)
            )
    linear_t = weights[:, 0:LIN_PAD]
    states = (dot(linear_t, act_two[...], 1, 1) + bias_three).astype(BF)
    d_state, grad_mats, grad_table, grad_bias, errors = plan(
        states,
        tuple(weights[:, AT_MATS + k * D : AT_MATS + (k + 1) * D] for k in range(3)),
        weights[:, LIN_PAD - 128 : LIN_PAD],
        bias_four,
        *frame_rows(
            section, (options_ref, legal_ref, games_ref, valid_ref, rewards_ref, returns_ref)
        ),
        scale,
    )

    d_state_low = d_state.astype(BF)
    grad_linear = dot(d_state_low, act_two[...])
    grad_own[0] = grad_linear[:, 0:HALF].reshape(peers, 8, HALF)
    grad_own[1, :, :, 0 : LIN_PAD - 128 - HALF] = grad_linear[:, HALF : LIN_PAD - 128].reshape(
        peers, 8, LIN_PAD - 128 - HALF
    )
    rest = [grad_linear[:, LIN_PAD - 128 : LIN_PAD] + grad_table, *grad_mats]
    for k in range(4):
        lane = LIN_PAD - 128 - HALF + k * D
        grad_own[1, :, :, lane : lane + D] = rest[k].reshape(peers, 8, D)
    mate_msg[...] = packed(grad_own[mate]).astype(BF)
    wait_mate = send_mate(1, mate_msg, mate_in, mate_in)
    back_two(d_state_low, linear_t, z_two, dz_two, frames)
    wait_mate()
    grad_msg[...] = (packed(grad_own[section]) + mate_in[...].astype(F32)).astype(BF)
    for which in range(2):

        def collect(step):
            peer = beside(step)
            owner = across(which, lax.rem(peer, FOUR))
            send(6, peer, grad_msg.at[owner], cross_in.at[which, column])

        loop(1, FOUR, collect)
        cross_in[which, column] = grad_msg[across(which, column)]
    wait_cross = settle(6, grad_msg.at[pl.ds(0, 2 * (FOUR - 1))])
    loop(1, NEAR, lambda step: send(7, near(step), grad_msg.at[near(step)], near_in.at[spot]))
    wait_grads = settle(7, near_in.at[pl.ds(0, NEAR - 1)])
    near_in[spot] = grad_msg[place]
    lane = iota((8, 128), 1)
    line = iota((8, 128), 0)
    row_three = row_of(lane_sum(d_state_low))
    row_four = row_of(grad_bias)
    extra_rows = jnp.zeros((8, 128), F32)
    for which, entry in (
        (0, turn(row_three, 64)),
        (1, row_three),
        (2, turn(row_four, 64)),
        (3, row_four),
        (5, turn(errors, 64)),
    ):
        extra_rows = jnp.where(line == which, entry, extra_rows)
    grad_two, bias_two_grad = grad_kernel_two(act_one, dz_two, frames)
    back_one(dz_two, band_two, z_one, dz_one, frames, 5)
    grad_one, bias_one_grad = grad_kernel_one(pixels, dz_one, frames)

    conv_rows = stack_kernels(grad_one, grad_two).reshape(2 * peers, 8, 128)
    row_first = jnp.where(
        lane < C1, bias_one_grad, jnp.where(lane < C1 + C2, turn(bias_two_grad, C1), 0.0)
    )
    extra = jnp.where(line == 4, turn(row_first, 64), extra_rows)
    tiles = jnp.where(iota((2 * peers, 8, 128), 2) >= 64, extra[None], conv_rows)
    tile_own[0] = tiles.reshape(peers, 2, 8, 128)[:, 0]
    tile_own[1] = tiles.reshape(peers, 2, 8, 128)[:, 1]
    wait_pair = send_mate(2, tile_own.at[mate], tile_mate, tile_mate)
    wait_cross()
    cross_msg[...] = jnp.sum(cross_in[...].astype(F32), axis=1).astype(BF)
    loop(0, 2, lambda step: send(8, across(step, column), cross_msg.at[step], far_in.at[row]))
    wait_far = settle(8, far_in)
    wait_pair()
    tile_msg[...] = tile_own[section] + tile_mate[...]
    loop(
        0, NEAR, lambda step: send(9, beyond(step), tile_msg.at[beyond(step)], tile_in.at[place])
    )
    loop(1, NEAR, lambda step: send(9, near(step), tile_msg.at[near(step)], tile_in.at[place]))
    wait_tiles = settle(9, tile_in.at[pl.ds(0, peers - 1)])
    tile_in[place] = tile_msg[place]
    wait_grads()
    wait_far()
    total = jnp.sum(near_in[...].astype(F32), axis=0) + jnp.sum(far_in[...].astype(F32), axis=0)
    squares = total * total
    stat = stats_base[...]
    for part in range(2):
        sums = jnp.sum(squares[part * 8 : (part + 1) * 8], axis=0, keepdims=True)
        for tile in range(TILES // 2):
            stat = jnp.where(
                stat_line == part * (TILES // 2) + tile, sums[:, tile * 128 : (tile + 1) * 128], stat
            )
    wait_tiles()
    tile_total = jnp.sum(tile_in[...], axis=0)
    conv_squares = jnp.where(lane < C1 + C2, tile_total * tile_total, 0.0)
    stat = jnp.where(stat_line == TILES, jnp.sum(conv_squares, axis=0, keepdims=True), stat)

    stats_in[place] = stat.astype(BF)
    half_in[section, :, 0:QUARTER] = total[0:8]
    half_in[section, :, QUARTER:HALF] = total[8:16]
    half_in[section, :, HALF : HALF + 128] = tile_total
    wait_stats = send_peers(10, stats_in.at[place], stats_in)
    wait_half_grads = send_mate(3, half_in.at[section], half_in.at[section], half_in.at[mate])
    tile_out[...] = tile_total
    wait_stats()
    stats_both[section] = jnp.sum(stats_in[...].astype(F32), axis=0)
    wait_half_stats = send_mate(
        4, stats_both.at[section], stats_both.at[section], stats_both.at[mate]
    )
    wait_half_grads()
    for half in range(2):
        main_out[:, half * HALF : (half + 1) * HALF] = half_in[half, :, 0:HALF]
        conv_out[half * 8 : (half + 1) * 8] = half_in[half, :, HALF : HALF + 128]
    wait_half_stats()
    stats_out[...] = stats_both[...]

    for wait in sends:
        wait()


def fused_step(peers, frames, shards, biases, rows):
    count = frames.shape[1]
    side = frames.shape[2]
    scratch = local_scratch(count, side)
    scratch[7] = pltpu.VMEM((count, LIN_PAD), BF)
    scratch += [
        pltpu.VMEM((8, 2 * HALF), F32),
        pltpu.VMEM((peers, 16, 128), BF),
        pltpu.VMEM((2, peers, 16, QUARTER), BF),
        pltpu.VMEM((D, 2 * HALF), BF),
        pltpu.VMEM((2, peers, 8, HALF), F32),
        pltpu.VMEM((peers, 16, QUARTER), BF),
        pltpu.VMEM((peers, 16, QUARTER), BF),
        pltpu.VMEM((peers, 16, QUARTER), BF),
        pltpu.VMEM((NEAR, 16, QUARTER), BF),
        pltpu.VMEM((2, FOUR, 16, QUARTER), BF),
        pltpu.VMEM((2, 16, QUARTER), BF),
        pltpu.VMEM((2, 16, QUARTER), BF),
        pltpu.VMEM((2, peers, 8, 128), F32),
        pltpu.VMEM((peers, 8, 128), F32),
        pltpu.VMEM((peers, 8, 128), F32),
        pltpu.VMEM((peers, 8, 128), F32),
        pltpu.VMEM((peers, 16, 128), BF),
        pltpu.VMEM((2, 16, 128), F32),
        pltpu.VMEM((16, 128), F32),
        pltpu.VMEM((2, 8, HALF + 128), F32),
        pltpu.SemaphoreType.DMA((11,)),
        pltpu.SemaphoreType.DMA((11,)),
        pltpu.SemaphoreType.DMA((6,)),
        pltpu.SemaphoreType.DMA((6,)),
    ]
    shapes = [(8, 2 * HALF), (16, 128), (8, 128), (2, 16, 128)]
    operands = [frames.transpose(0, 2, 1, 3), *shards, biases, *rows]
    scratch += [pltpu.VMEM(operand.shape, operand.dtype) for operand in operands[1:]]
    scratch += [pltpu.SemaphoreType.DMA((len(operands) - 1,))]
    return pl.pallas_call(
        functools.partial(fused_kernel, peers),
        out_shape=[jax.ShapeDtypeStruct(shape, F32) for shape in shapes],
        in_specs=[ANY_SPEC] * len(operands),
        out_specs=[VMEM_SPEC] * len(shapes),
        scratch_shapes=scratch,
        compiler_params=pltpu.CompilerParams(
            vmem_limit_bytes=56 * 1024 * 1024, collective_id=0, has_side_effects=True
        ),
    )(*operands)


def column_of(row):
    square = jnp.broadcast_to(row, (8, 8))
    return jnp.sum(jnp.where(iota((8, 8), 0) == iota((8, 8), 1), square, 0.0), axis=1, keepdims=True)


def row_back(column):
    square = jnp.broadcast_to(column, (8, 8))
    return jnp.sum(jnp.where(iota((8, 8), 0) == iota((8, 8), 1), square, 0.0), axis=0, keepdims=True)


def total_of(value):
    return jnp.sum(jnp.sum(value, axis=0, keepdims=True), axis=1, keepdims=True)


def update_kernel(
    main_ref,
    convg_ref,
    tile_ref,
    stats_ref,
    conv_ref,
    lin_ref,
    mats_ref,
    emb_ref,
    heads_ref,
    bias_ref,
    conv_moment,
    lin_rows,
    lin_cols,
    mats_rows,
    mats_cols,
    emb_moment,
    head_moment,
    bias_moment,
    conv_new,
    conv_grad,
    conv_moment_new,
    lin_new,
    lin_grad,
    lin_rows_new,
    lin_cols_new,
    mats_new,
    mats_grad,
    mats_rows_new,
    mats_cols_new,
    emb_new,
    emb_grad,
    emb_moment_new,
    heads_new,
    heads_grad,
    head_moment_new,
    bias_new,
    bias_grad,
    bias_moment_new,
    norm_out,
    loss_out,
    conv_low,
    lin_low,
):
    stats = stats_ref[...]
    tile = tile_ref[...]
    squares = jnp.where(iota((2, 16, 128), 1) <= TILES, stats, 0.0)
    squares = total_of(squares[0] + squares[1])
    scales = stats[0, TILES + 1 : TILES + 2] + stats[0, TILES + 2 : TILES + 3]
    bias_raw = jnp.concatenate(
        [tile[4:5, 64 : 64 + C1 + C2]] + [tile[k : k + 1, 64:128] for k in range(4)], axis=1
    )
    norm = jnp.sqrt(squares + total_of(bias_raw * bias_raw))
    factor = jnp.minimum(1.0, CLIP_LIMIT / norm)
    norm_out[...] = norm
    loss_out[...] = total_of(tile[5:6, 64:128])

    def simple(weight, grad, moment, square_total, outs):
        new, moment_new = unfactored(
            weight, grad, moment, relative(square_total, weight.size * outs[3])
        )
        for out, value in zip(outs, (new, grad, moment_new)):
            out[...] = value.reshape(out.shape)
        return new

    peers = D // lin_ref.shape[0]
    conv = simple(
        conv_ref[...],
        factor * convg_ref[:, 0 : C1 + C2],
        conv_moment[...],
        scales[:, 0:1],
        (conv_new, conv_grad, conv_moment_new, peers),
    )
    conv_low[...] = conv.astype(BF)
    simple(
        emb_ref[...],
        factor * main_ref[:, AT_EMB:AT_HEADS],
        emb_moment[...],
        scales[:, 3:4],
        (emb_new, emb_grad, emb_moment_new, peers),
    )
    heads_t = jnp.concatenate(
        [main_ref[:, LIN_PAD - 128 : LIN_PAD], jnp.zeros((120, 128), F32)], axis=0
    ).T
    simple(
        heads_ref[...],
        factor * heads_t[HEAD_LANE : HEAD_LANE + 3 * GAMES, 0:8],
        head_moment[...],
        scales[:, 4:5],
        (heads_new, heads_grad, head_moment_new, peers),
    )
    bias = bias_ref[...].reshape(1, BIAS)
    simple(
        bias,
        factor * bias_raw,
        bias_moment[...].reshape(1, BIAS),
        total_of(bias * bias),
        (bias_new, bias_grad, bias_moment_new, 1),
    )
    row_sums = [stats[t // TILES, t % TILES : t % TILES + 1] for t in range(24)]

    def factored(weight, grad, rows_old, cols_old, row_sum, square_total, entries):
        rows = DECAY_RATE * rows_old + (1.0 - DECAY_RATE) * (
            factor * factor * row_sum / D + FLOOR_ONE
        )
        wide = grad.shape[1]
        cols = DECAY_RATE * cols_old + (1.0 - DECAY_RATE) * (
            jnp.sum(grad * grad + FLOOR_ONE, axis=1, keepdims=True) / wide
        )
        mean = jnp.sum(rows, axis=1, keepdims=True) / wide
        second = rows * cols / mean
        new = weight - STEP_RATE * relative(square_total, entries) * grad * lax.rsqrt(second)
        return new, rows, cols

    grad = factor * main_ref[:, 0:FEAT]
    new, rows, cols = factored(
        lin_ref[...],
        grad,
        lin_rows[...].reshape(1, FEAT),
        column_of(lin_cols[...]),
        jnp.concatenate(row_sums[:21], axis=1)[:, 0:FEAT],
        scales[:, 1:2],
        FEAT * D,
    )
    lin_new[...] = new
    lin_grad[...] = grad
    lin_rows_new[...] = rows.reshape(FEAT)
    lin_cols_new[...] = row_back(cols)
    lin_low[...] = new.astype(BF)
    for k in range(3):
        grad = factor * main_ref[:, AT_MATS + k * D : AT_MATS + (k + 1) * D]
        new, rows, cols = factored(
            mats_ref[k],
            grad,
            mats_rows[k : k + 1],
            column_of(mats_cols[k : k + 1]),
            row_sums[21 + k],
            scales[:, 2:3],
            3 * D * D,
        )
        mats_new[k] = new
        mats_grad[k] = grad
        mats_rows_new[k : k + 1] = rows
        mats_cols_new[k : k + 1] = row_back(cols)


def fused_device(
    frames,
    options,
    legal,
    games,
    valid,
    rewards,
    returns,
    conv_kernels,
    enc_linear,
    plan_mats,
    option_emb,
    heads,
    biases,
    conv_moment,
    lin_rows,
    lin_cols,
    mats_rows,
    mats_cols,
    emb_moment,
    head_moment,
    bias_moment,
):
    width = enc_linear.shape[1]
    peers = D // width
    shards = (
        conv_kernels,
        enc_linear.T,
        plan_mats.transpose(0, 2, 1),
        option_emb.T,
        heads.reshape(3 * GAMES, width),
    )
    summed = fused_step(
        peers,
        frames,
        shards,
        biases,
        (
            options.transpose(2, 0, 1),
            legal.transpose(2, 0, 1),
            games,
            valid.transpose(2, 0, 1),
            rewards.transpose(2, 0, 1),
            returns.transpose(0, 2, 1),
        ),
    )
    shapes = [(16, 48)] * 3 + [(8, FEAT)] * 2 + [(FEAT,), (1, 8)] + [(3, 8, D)] * 2 + [(3, D), (3, 8)]
    shapes += [(8, OPTS)] * 3 + [(24, 8)] * 3 + [(BIAS,)] * 3 + [(1, 1)] * 2
    outs = [jax.ShapeDtypeStruct(shape, F32) for shape in shapes]
    outs += [jax.ShapeDtypeStruct((16, 48), BF), jax.ShapeDtypeStruct((8, FEAT), BF)]
    operands = [
        *summed,
        *shards,
        biases,
        conv_moment,
        lin_rows,
        lin_cols.reshape(1, width),
        mats_rows,
        mats_cols,
        emb_moment.T,
        head_moment.reshape(3 * GAMES, width),
        bias_moment,
    ]
    o = pl.pallas_call(
        update_kernel,
        out_shape=outs,
        in_specs=[VMEM_SPEC] * len(operands),
        out_specs=[VMEM_SPEC] * len(outs),
    )(*operands)
    flat_heads = [h.reshape(3, GAMES, width) for h in o[14:17]]
    return (
        *o[0:3],
        o[3].T,
        o[4].T,
        o[5],
        o[6].reshape(width),
        o[7].transpose(0, 2, 1),
        o[8].transpose(0, 2, 1),
        o[9],
        o[10],
        o[11].T,
        o[12].T,
        o[13].T,
        *flat_heads,
        *o[17:20],
        o[20].reshape(()),
        o[21].reshape(()),
        o[22],
        o[23].T,
    )


def gather_rows(shard):
    return lax.all_gather(shard, "dp", axis=0, tiled=True)


def relative(square_total, entries):
    return jnp.maximum(FLOOR_TWO, jnp.sqrt(square_total / entries))


def unfactored(weight, grad, moment, scale):
    moment_new = DECAY_RATE * moment + (1.0 - DECAY_RATE) * (grad * grad + FLOOR_ONE)
    return (weight - STEP_RATE * scale * grad * lax.rsqrt(moment_new), moment_new)


def per_device(
    frames,
    options,
    legal,
    games,
    valid,
    rewards,
    returns,
    conv_kernels,
    enc_linear,
    plan_mats,
    option_emb,
    heads,
    biases,
    conv_moment,
    lin_rows,
    lin_cols,
    mats_rows,
    mats_cols,
    emb_moment,
    head_moment,
    bias_moment,
):
    weight_squares = lax.psum(
        (
            jnp.sum(conv_kernels * conv_kernels),
            jnp.sum(enc_linear * enc_linear),
            jnp.sum(plan_mats * plan_mats),
            jnp.sum(option_emb * option_emb),
            jnp.sum(heads * heads),
        ),
        "dp",
    )
    width = enc_linear.shape[1]
    kernels = gather_rows(conv_kernels.astype(BF))
    linear_t = gather_rows(enc_linear.astype(BF).T)
    mats_t = gather_rows(plan_mats.astype(BF).transpose(2, 0, 1)).transpose(1, 0, 2)
    emb_t = gather_rows(option_emb.astype(BF).T)
    heads_t = gather_rows(heads.astype(BF).reshape(3 * GAMES, width).T)
    table = jnp.pad(
        jnp.concatenate([emb_t, heads_t], axis=1),
        ((0, 0), (EMB_LANE, 128 - HEAD_LANE - 3 * GAMES)),
    )
    lin, mats, table_grad, conv, small = local_step(
        frames,
        kernels,
        linear_t,
        mats_t,
        table,
        biases,
        options,
        legal,
        games,
        valid,
        rewards,
        returns,
    )
    rows = jnp.concatenate(
        [lin, mats[0], mats[1], mats[2], table_grad[:, EMB_LANE : HEAD_LANE + 3 * GAMES]], axis=1
    )
    rows = lax.psum(lax.psum_scatter(rows, "dp", scatter_dimension=0, tiled=True), "section")
    conv = lax.psum(
        lax.psum_scatter(conv[:, : C1 + C2], "dp", scatter_dimension=0, tiled=True), "section"
    )
    small = lax.psum(small, ("section", "dp"))
    inverse_count = 1.0 / jnp.sum(small[4])
    loss_value = jnp.sum(small[3]) * inverse_count
    bias_raw = (
        jnp.concatenate([small[0, : C1 + C2], small[1], small[2]]) * inverse_count
    )
    rows = rows * inverse_count
    g_conv = conv * inverse_count
    g_lin = rows[:, :FEAT].T
    g_mats = rows[:, FEAT : FEAT + 3 * D].reshape(width, 3, D).transpose(1, 2, 0)
    g_emb = rows[:, FEAT + 3 * D : FEAT + 3 * D + OPTS].T
    g_heads = rows[:, FEAT + 3 * D + OPTS :].T.reshape(3, GAMES, width)
    partial_squares = (
        jnp.sum(g_conv * g_conv)
        + jnp.sum(g_lin * g_lin)
        + jnp.sum(g_mats * g_mats)
        + jnp.sum(g_emb * g_emb)
        + jnp.sum(g_heads * g_heads)
    )
    reduced = lax.psum(
        (partial_squares, jnp.sum(g_lin * g_lin, axis=1), jnp.sum(g_mats * g_mats, axis=2)), "dp"
    )
    grad_norm = jnp.sqrt(reduced[0] + jnp.sum(bias_raw * bias_raw))
    factor = jnp.minimum(1.0, CLIP_LIMIT / grad_norm)
    conv_grad = factor * g_conv
    lin_grad = factor * g_lin
    mats_grad = factor * g_mats
    emb_grad = factor * g_emb
    heads_grad = factor * g_heads
    bias_grad = factor * bias_raw
    conv_new, conv_moment_new = unfactored(
        conv_kernels, conv_grad, conv_moment, relative(weight_squares[0], KERN * (C1 + C2))
    )
    emb_new, emb_moment_new = unfactored(
        option_emb, emb_grad, emb_moment, relative(weight_squares[3], OPTS * D)
    )
    heads_new, head_moment_new = unfactored(
        heads, heads_grad, head_moment, relative(weight_squares[4], 3 * GAMES * D)
    )
    bias_new, bias_moment_new = unfactored(
        biases, bias_grad, bias_moment, relative(jnp.sum(biases * biases), BIAS)
    )
    lin_rows_new = DECAY_RATE * lin_rows + (1.0 - DECAY_RATE) * (
        factor * factor * reduced[1] / D + FLOOR_ONE
    )
    lin_cols_new = DECAY_RATE * lin_cols + (1.0 - DECAY_RATE) * jnp.mean(
        lin_grad * lin_grad + FLOOR_ONE, axis=0
    )
    lin_second = lin_rows_new[:, None] * lin_cols_new[None, :] / jnp.mean(lin_rows_new)
    lin_new = enc_linear - STEP_RATE * relative(weight_squares[1], FEAT * D) * lin_grad * lax.rsqrt(
        lin_second
    )
    mats_rows_new = DECAY_RATE * mats_rows + (1.0 - DECAY_RATE) * (
        factor * factor * reduced[2] / D + FLOOR_ONE
    )
    mats_cols_new = DECAY_RATE * mats_cols + (1.0 - DECAY_RATE) * jnp.mean(
        mats_grad * mats_grad + FLOOR_ONE, axis=1
    )
    mats_second = (
        mats_rows_new[:, :, None]
        * mats_cols_new[:, None, :]
        / jnp.mean(mats_rows_new, axis=1)[:, None, None]
    )
    mats_new = plan_mats - STEP_RATE * relative(weight_squares[2], 3 * D * D) * mats_grad * lax.rsqrt(
        mats_second
    )
    return (
        conv_new,
        conv_grad,
        conv_moment_new,
        lin_new,
        lin_grad,
        lin_rows_new,
        lin_cols_new,
        mats_new,
        mats_grad,
        mats_rows_new,
        mats_cols_new,
        emb_new,
        emb_grad,
        emb_moment_new,
        heads_new,
        heads_grad,
        head_moment_new,
        bias_new,
        bias_grad,
        bias_moment_new,
        grad_norm,
        loss_value,
        conv_new.astype(BF),
        lin_new.astype(BF),
    )


def solution(mesh):
    return jax.shard_map(
        fused_device if mesh.shape["dp"] * 8 == D else per_device,
        mesh=mesh,
        in_specs=(
            P(None, "dp", None, None),
            P(None, "dp", None),
            P(None, "dp", None),
            P(None, "dp"),
            P(None, "dp", None),
            P(None, "dp", None),
            P(None, "dp", None),
            P("dp", None),
            P(None, "dp"),
            P(None, None, "dp"),
            P(None, "dp"),
            P(None, None, "dp"),
            P(),
            P("dp", None),
            P(),
            P("dp"),
            P(),
            P(None, "dp"),
            P(None, "dp"),
            P(None, None, "dp"),
            P(),
        ),
        out_specs=(
            P("dp", None),
            P("dp", None),
            P("dp", None),
            P(None, "dp"),
            P(None, "dp"),
            P(),
            P("dp"),
            P(None, None, "dp"),
            P(None, None, "dp"),
            P(),
            P(None, "dp"),
            P(None, "dp"),
            P(None, "dp"),
            P(None, "dp"),
            P(None, None, "dp"),
            P(None, None, "dp"),
            P(None, None, "dp"),
            P(),
            P(),
            P(),
            P(),
            P(),
            P("dp", None),
            P(None, "dp"),
        ),
        check_vma=False,
    )
```

```python
import functools

import jax
import jax.numpy as jnp
from jax import lax
from jax.experimental import pallas as pl
from jax.experimental.pallas import tpu as pltpu
from jax.sharding import PartitionSpec as P

D = 128
C1 = 16
C2 = 32
OPTS = 18
KERN = 256
GAMES = 8
FEAT = 2592
BIAS = 304

OUT1 = 20
OUT2 = 9
WIDE = 384
LIN_PAD = 2688
EMB_LANE = FEAT % 128
HEAD_LANE = EMB_LANE + OPTS
CHUNK = 12
LATE_POSITIONS = 12
FEATS_ROW = OUT2 * C2

CLIP_LIMIT = 0.05
DECAY_RATE = 0.8
STEP_RATE = 0.5
FLOOR_ONE = 1e-30
FLOOR_TWO = 0.001

HIGH = lax.Precision.HIGHEST
BF = jnp.bfloat16
F32 = jnp.float32


def dot(left, right, over_left=1, over_right=0, precision=None):
    return lax.dot_general(
        left,
        right,
        (((over_left,), (over_right,)), ((), ())),
        precision=precision,
        preferred_element_type=F32,
    )


def sigmoid(value):
    return 0.5 * jnp.tanh(0.5 * value) + 0.5


def slope(active, sigma):
    return sigma + active * (1.0 - sigma)


def iota(shape, axis):
    return lax.broadcasted_iota(jnp.int32, shape, axis)


def turn(value, steps):
    return pltpu.roll(value, steps, 1)


def fold(value, width):
    step = 64
    while step >= width:
        value = value + turn(value, step)
        step //= 2
    return value


def row_of(column):
    square = jnp.broadcast_to(column, (128, 128))
    return jnp.sum(jnp.where(iota((128, 128), 0) == iota((128, 128), 1), square, 0.0), axis=0, keepdims=True)


def load_frames(frames_hbm, section, frame_buf, sems, chunk):
    copies = []
    for which in range(frame_buf.shape[0] // chunk):
        rows = pl.ds(which * chunk, chunk)
        copies.append(
            pltpu.make_async_copy(
                frames_hbm.at[section, rows], frame_buf.at[rows], sems.at[which]
            )
        )
    return copies


def place_frames(frame_buf, pixels, first, chunk, frames):
    for row in range(first, first + chunk):
        block, part = row // 4, row % 4
        pixels[block * frames : (block + 1) * frames, part * WIDE : part * WIDE + 336] = frame_buf[row]


def fill_band(wide, put, width, taps, blocks):
    for tap in taps:
        fill_tap(wide, put, width, tap, blocks)


def fill_tap(wide, put, width, tap, blocks):
    per_tile = 128 // width
    group = iota((width, 128), 1) // width
    base = 2 * tap * width
    for block in range(blocks + 1):
        tile, spot = divmod(block, per_tile)
        lanes = slice(tile * 128, (tile + 1) * 128)
        left = jnp.where(group == spot, wide[base : base + width, lanes], 0.0)
        right = wide[base + width : base + 2 * width]
        if spot > 0:
            left = jnp.where(group == spot - 1, right[:, lanes], left)
        elif block > 0:
            before = slice((tile - 1) * 128, tile * 128)
            put(tap, block, before, jnp.where(group == per_tile - 1, right[:, before], 0.0).astype(BF))
        put(tap, block, lanes, left.astype(BF))


def repeat_kernels(kernels, first, width, positions, lanes):
    held = kernels.shape[1]
    rows = iota((held, lanes), 0)
    cols = iota((held, lanes), 1)
    pick = jnp.where((cols % width + first == rows) & (cols < positions * width), 1.0, 0.0)
    return dot(kernels, pick.astype(BF))


def build_one(kernels, band):
    wide = repeat_kernels(kernels, 0, C1, LATE_POSITIONS, 256)

    def put(tap, block, lanes, value):
        rows = tap * 256 + block * C1
        band[rows : rows + C1, lanes] = value

    fill_band(wide, put, C1, range(4), LATE_POSITIONS)


def build_two(kernels, band):
    wide = repeat_kernels(kernels, C1, C2, OUT2, WIDE)

    def put(tap, block, lanes, value):
        rows = tap * WIDE + block * C2
        band[rows : rows + C2, lanes] = value

    return [lambda tap=tap: fill_tap(wide, put, C2, tap, OUT2) for tap in range(4)]


def clear_bands(band_one, band_two):
    band_one[...] = jnp.zeros(band_one.shape, BF)
    band_two[...] = jnp.zeros(band_two.shape, BF)


def wide_biases(bias_row):
    bias8 = jnp.broadcast_to(bias_row, (8, BIAS))
    rows = iota((BIAS, WIDE), 0)
    lanes = iota((BIAS, WIDE), 1)
    one = jnp.where((lanes % C1 == rows) & (lanes < OUT1 * C1), 1.0, 0.0)
    two = jnp.where((lanes % C2 + C1 == rows) & (lanes < OUT2 * C2), 1.0, 0.0)
    rows = iota((D, BIAS), 0)
    lanes = iota((D, BIAS), 1)
    three = jnp.where(lanes == rows + C1 + C2, 1.0, 0.0)
    four = jnp.where(lanes == rows + C1 + C2 + D, 1.0, 0.0)
    return (
        dot(bias8, one, precision=HIGH)[0:1],
        dot(bias8, two, precision=HIGH)[0:1],
        dot(three, bias8, 1, 1, precision=HIGH)[:, 0:1],
        dot(four, bias8, 1, 1, precision=HIGH)[:, 0:1],
    )


def encode_one(
    pixels, band_one, half, more, bias, slope_one, act_one, frames, chunk, beside=()
):
    rows = chunk * frames
    band = band_one[half]
    for first in range(0, OUT1, chunk):
        block = pixels[pl.ds(pl.multiple_of((half + first) * frames, frames), rows), :]
        parts = []
        for low, wide in ((0, 128), (128, 256)):
            window = jnp.concatenate(
                [block[:, tap * WIDE + low : tap * WIDE + low + 256] for tap in range(4)], axis=1
            )
            parts.append(dot(window, band[:, 0:wide]))
        if first // chunk < len(beside):
            beside[first // chunk]()
        z = jnp.concatenate(parts, axis=1)
        for step in range(chunk):
            at, part = divmod(first + step, 2)
            spot = (slice(at * frames, (at + 1) * frames), slice(part * WIDE, (part + 1) * WIDE))
            z_step = z[step * frames : (step + 1) * frames]
            if more:
                slope_one[spot] = z_step
            else:
                z_step = z_step + slope_one[spot] + bias
                sigma = sigmoid(z_step)
                active = z_step * sigma
                slope_one[spot] = slope(active, sigma)
                act_one[spot] = active.astype(BF)


def encode_two(act_one, band_two, bias, slope_two, act_two, frames, chunk):
    rows = chunk * frames
    bands = []
    for low, high in ((0, 128), (128, WIDE)):
        bands.append(
            jnp.concatenate(
                [band_two[tap * WIDE + low : tap * WIDE + low + 256, low:high] for tap in range(4)],
                axis=0,
            )
        )
    for first in range(0, OUT2, chunk):
        at = first * frames
        parts = []
        for low, band in zip((0, 128), bands):
            window = jnp.concatenate(
                [
                    act_one[
                        at + tap // 2 * frames : at + tap // 2 * frames + rows,
                        tap % 2 * WIDE + low : tap % 2 * WIDE + low + 256,
                    ]
                    for tap in range(4)
                ],
                axis=1,
            )
            parts.append(dot(window, band))
        z = jnp.concatenate(parts, axis=1) + bias
        sigma = sigmoid(z)
        active = z * sigma
        slope_two[at : at + rows] = slope(active, sigma)
        act = active.astype(BF)
        for step in range(chunk):
            lane = (first + step) * FEATS_ROW
            act_two[:, lane : lane + FEATS_ROW] = act[step * frames : (step + 1) * frames, :FEATS_ROW]


def back_two(dstate_t, linear_t, slope_two, dz_two, frames):
    dact = dot(dstate_t, linear_t, 0, 0)
    dz_two[0:frames] = jnp.zeros((frames, WIDE), BF)
    dz_two[(OUT2 + 1) * frames : (OUT2 + 2) * frames] = jnp.zeros((frames, WIDE), BF)
    blank = jnp.zeros((frames, WIDE - FEATS_ROW), F32)
    for at in range(OUT2):
        part = jnp.concatenate([dact[:, at * FEATS_ROW : (at + 1) * FEATS_ROW], blank], axis=1)
        dz_two[(at + 1) * frames : (at + 2) * frames] = (
            part * slope_two[at * frames : (at + 1) * frames]
        ).astype(BF)


def back_one(dz_two, band_two, slope_one, dz_one, frames, chunk):
    rows = chunk * frames

    def rows_of(tap, low, high):
        return slice(tap * WIDE + low, tap * WIDE + high)

    for first in range(0, OUT1 // 2, chunk):
        low = first * frames
        sides = [dz_two[low + frames : low + frames + rows], dz_two[low : low + rows]]
        left = [
            sum(
                dot(sides[at][:, 0:256], band_two[rows_of(2 * at + part, 0, 256), 0:256], 1, 1)
                for at in range(2)
            )
            for part in range(2)
        ]
        right = sum(
            dot(
                sides[at][:, 128:WIDE],
                jnp.concatenate(
                    [band_two[rows_of(2 * at + part, 256, WIDE), 128:WIDE] for part in range(2)],
                    axis=0,
                ),
                1,
                1,
            )
            for at in range(2)
        )
        dact = jnp.concatenate([left[0], right[:, 0:128], left[1], right[:, 128:256]], axis=1)
        dz = (dact * slope_one[low : low + rows]).astype(BF)
        for step in range(chunk):
            for part in range(2):
                at = (2 * (first + step) + part) * frames
                dz_one[at : at + frames] = dz[
                    step * frames : (step + 1) * frames, part * WIDE : (part + 1) * WIDE
                ]


def band_sums(term, outputs, width):
    per_tile = 128 // width
    lane = iota((width, 128), 1) // width
    sums = []
    for shift in range(2):
        total = None
        for spot in range(per_tile):
            part = None
            for position in range(outputs):
                tile, inside = divmod(position + shift, per_tile)
                if inside != spot:
                    continue
                one = term(position, tile)
                part = one if part is None else part + one
            if part is None:
                continue
            part = jnp.where(lane == spot, part, 0.0)
            total = part if total is None else total + part
        sums.append(fold(total, width))
    return sums


def kernel_grad(terms, outputs, width):
    tiles = []
    lane = iota((width, 128), 1) // width
    pieces = []
    for term in terms:
        pieces.extend(band_sums(term, outputs, width))
    per_tile = 128 // width
    for tile in range(2):
        total = jnp.zeros((width, 128), F32)
        for spot in range(per_tile):
            total = jnp.where(lane == spot, pieces[tile * per_tile + spot], total)
        tiles.append(total)
    return jnp.concatenate(tiles, axis=1)


def tiled(tile, count):
    return jnp.concatenate([tile] * count, axis=1)


def twice(row):
    return jnp.concatenate([row, row], axis=1)


def plan(states, mats_t, table, bias_col, options, legal, games, valid, rewards, returns, scale):
    frames = states.shape[1]
    pairs = OPTS // 2
    lanes = OPTS * frames
    trans_in, trans_out, value_in = mats_t
    low_half = iota((1, 128), 1) < frames
    upper = iota((1, 128), 1) // frames

    valid_f = [twice(v.astype(F32)) for v in valid]
    rewards = [twice(r) for r in rewards]
    returns = [twice(r) for r in returns]
    chosen = [twice(o) for o in options]
    game = twice(games)

    game_rows = iota((128, WIDE), 0) - HEAD_LANE
    game_pick = jnp.where(
        game_rows == tiled(game, 3) + GAMES * (iota((128, WIDE), 1) // 128), 1.0, 0.0
    )
    head_rows = dot(table, game_pick.astype(BF))
    hr, hd, hv = (head_rows[:, k * 128 : (k + 1) * 128] for k in range(3))

    option_rows = jnp.where(
        iota((128, lanes), 0) - EMB_LANE == iota((128, lanes), 1) // frames, 1.0, 0.0
    ).astype(BF)
    s_low = twice(states)
    s_f = s_low.astype(F32)
    base = dot(trans_in, s_low)
    pre = tiled(base, pairs) + dot(table, option_rows)
    sig_h = sigmoid(pre)
    hid = pre * sig_h
    hid_low = hid.astype(BF)
    after = tiled(s_f, pairs) + dot(trans_out, hid_low)
    after_low = after.astype(BF)
    judge_pre = dot(value_in, after_low) + bias_col
    sig_j = sigmoid(judge_pre)
    judged = judge_pre * sig_j

    def tile_of(value, k):
        return value[:, k * 128 : (k + 1) * 128]

    def over(value):
        return jnp.sum(value, axis=0, keepdims=True)

    reward = [over(tile_of(hid, k) * hr) for k in range(pairs)]
    gamma = [sigmoid(over(tile_of(hid, k) * hd)) for k in range(pairs)]
    value = [over(tile_of(judged, k) * hv) for k in range(pairs)]
    backed = [reward[k] + gamma[k] * value[k] for k in range(pairs)]
    allowed = [
        jnp.concatenate([legal[2 * k], legal[2 * k + 1]], axis=1) > 0 for k in range(pairs)
    ]
    highest = functools.reduce(
        jnp.maximum, [jnp.where(allowed[k], backed[k], -1e30) for k in range(pairs)]
    )
    highest = jnp.maximum(highest, turn(highest, frames))
    shares = [
        jnp.where(allowed[k], jnp.exp(jnp.where(allowed[k], backed[k] - highest, -60.0)), 0.0)
        for k in range(pairs)
    ]

    def halves(total):
        return total + turn(total, frames)

    share_sum = halves(sum(shares))
    planned = halves(sum(shares[k] * backed[k] for k in range(pairs))) / share_sum
    choose = [chosen[0] == 2 * k + upper for k in range(pairs)]

    def chosen_of(parts):
        return halves(sum(jnp.where(choose[k], parts[k], 0.0) for k in range(pairs)))

    roll_f = [chosen_of([tile_of(after, k) for k in range(pairs)])]
    roll_low = [roll_f[0].astype(BF)]
    plan_miss = planned - returns[0]
    reward_miss = [chosen_of(reward) - rewards[0]]
    value_miss = [chosen_of(value) - returns[1]]
    steps = len(options)
    picks, pre_k, sig_k, hid_k, hid_k_low, judge_k, sig_jk, judged_k = ([None] for _ in range(8))
    for k in range(1, steps):
        picks.append(jnp.where(iota((128, 128), 0) - EMB_LANE == chosen[k], 1.0, 0.0).astype(BF))
        pre_k.append(dot(trans_in, roll_low[k - 1]) + dot(table, picks[k]))
        sig_k.append(sigmoid(pre_k[k]))
        hid_k.append(pre_k[k] * sig_k[k])
        hid_k_low.append(hid_k[k].astype(BF))
        roll_f.append(roll_f[k - 1] + dot(trans_out, hid_k_low[k]))
        roll_low.append(roll_f[k].astype(BF))
        judge_k.append(dot(value_in, roll_low[k]) + bias_col)
        sig_jk.append(sigmoid(judge_k[k]))
        judged_k.append(judge_k[k] * sig_jk[k])
        reward_miss.append(over(hid_k[k] * hr) - rewards[k])
        value_miss.append(over(judged_k[k] * hv) - returns[k + 1])
    errors = valid_f[0] * plan_miss * plan_miss
    for k in range(steps):
        errors = errors + valid_f[k] * (
            reward_miss[k] * reward_miss[k] + value_miss[k] * value_miss[k]
        )
    errors = jnp.where(low_half, errors * scale, 0.0)

    half = jnp.where(low_half, 1.0, 0.0)
    double = 2.0 * scale
    d_plan = double * valid_f[0] * plan_miss / share_sum
    d_reward_k = [double * valid_f[k] * reward_miss[k] for k in range(steps)]
    d_value_k = [double * valid_f[k] * value_miss[k] for k in range(steps)]

    def through(matrix_t, grad):
        return dot(matrix_t, grad, 0, 0)

    d_roll = None
    d_judge_low, d_step_low, d_pre_low = ([None] * steps for _ in range(3))
    d_hr = jnp.zeros((D, 128), F32)
    d_hd = jnp.zeros((D, 128), F32)
    d_hv = jnp.zeros((D, 128), F32)
    for k in range(steps - 1, 0, -1):
        d_judge_low[k] = (d_value_k[k] * hv * slope(judged_k[k], sig_jk[k])).astype(BF)
        term = through(value_in, d_judge_low[k])
        d_roll = term if d_roll is None else d_roll + term
        d_step_low[k] = d_roll.astype(BF)
        d_hid = through(trans_out, d_step_low[k]) + d_reward_k[k] * hr
        d_pre_low[k] = (d_hid * slope(hid_k[k], sig_k[k])).astype(BF)
        d_roll = d_roll + through(trans_in, d_pre_low[k])
        d_hr = d_hr + (half * d_reward_k[k]) * hid_k[k]
        d_hv = d_hv + (half * d_value_k[k]) * judged_k[k]

    d_backed = [d_plan * shares[k] * (1.0 + backed[k] - planned) for k in range(pairs)]
    d_reward = [
        d_backed[k] + jnp.where(choose[k], d_reward_k[0], 0.0) for k in range(pairs)
    ]
    d_value = [
        d_backed[k] * gamma[k] + jnp.where(choose[k], d_value_k[0], 0.0) for k in range(pairs)
    ]
    d_gamma = [d_backed[k] * value[k] * gamma[k] * (1.0 - gamma[k]) for k in range(pairs)]
    d_judge = [
        (d_value[k] * hv * slope(tile_of(judged, k), tile_of(sig_j, k))).astype(BF)
        for k in range(pairs)
    ]
    d_judge_all = jnp.concatenate(d_judge, axis=1)
    d_after = through(value_in, d_judge_all)
    d_after = [
        tile_of(d_after, k) + jnp.where(choose[k], d_roll, 0.0) for k in range(pairs)
    ]
    d_after_low = jnp.concatenate([d.astype(BF) for d in d_after], axis=1)
    d_hid_all = through(trans_out, d_after_low)
    d_pre = [
        (
            (tile_of(d_hid_all, k) + d_reward[k] * hr + d_gamma[k] * hd)
            * slope(tile_of(hid, k), tile_of(sig_h, k))
        ).astype(BF)
        for k in range(pairs)
    ]
    d_pre_all = jnp.concatenate(d_pre, axis=1)
    d_base = through(trans_in, d_pre_all)
    d_state = halves(sum(d_after[k] + tile_of(d_base, k) for k in range(pairs)))
    for k in range(pairs):
        d_hr = d_hr + d_reward[k] * tile_of(hid, k)
        d_hd = d_hd + d_gamma[k] * tile_of(hid, k)
        d_hv = d_hv + d_value[k] * tile_of(judged, k)

    def both(parts):
        joined = [jnp.where(low_half, parts[k].astype(F32), parts[k + 1].astype(F32)) for k in range(1, steps, 2)]
        return [part.astype(BF) for part in joined]

    def with_steps(wide, parts):
        return jnp.concatenate([wide] + both(parts), axis=1)

    before_low = [None] + roll_low[:-1]
    d_pre_cat = with_steps(d_pre_all, d_pre_low)
    d_judge_cat = with_steps(d_judge_all, d_judge_low)
    grad_in = dot(d_pre_cat, with_steps(tiled(s_low, pairs), before_low), 1, 1)
    grad_out = dot(
        with_steps(d_after_low, d_step_low), with_steps(hid_low, hid_k_low), 1, 1
    )
    grad_value = dot(d_judge_cat, with_steps(after_low, roll_low), 1, 1)
    grad_table = dot(d_pre_cat, with_steps(option_rows, picks), 1, 1) + dot(
        jnp.concatenate([d_hr, d_hd, d_hv], axis=1), game_pick, 1, 1, precision=HIGH
    )
    grad_bias = jnp.sum(d_judge_cat.astype(F32), axis=1, keepdims=True)
    return (
        d_state[:, :frames],
        (grad_in, grad_out, grad_value),
        grad_table,
        grad_bias,
        errors,
    )


def frame_rows(section, refs):
    options_ref, legal_ref, games_ref, valid_ref, rewards_ref, returns_ref = refs

    def row(ref, k):
        return ref[k, pl.ds(section, 1), :]

    depth = options_ref.shape[0]
    return (
        [row(options_ref, k) for k in range(depth)],
        [row(legal_ref, k) for k in range(OPTS)],
        games_ref[pl.ds(section, 1), :],
        [row(valid_ref, k) for k in range(depth)],
        [row(rewards_ref, k) for k in range(depth)],
        [returns_ref[section, k : k + 1, :] for k in range(depth + 1)],
    )


def clear_tails(pixels):
    tail = jnp.zeros((pixels.shape[0], WIDE - 336), BF)
    for part in range(4):
        pixels[:, part * WIDE + 336 : (part + 1) * WIDE] = tail


def grad_kernel_two(act_one, dz_two, frames):
    rows = OUT2 * frames
    d_two = dz_two[frames : frames + rows]
    turned = d_two.T

    def term_of(tap):
        first, base = (tap // 2) * frames, (tap % 2) * WIDE
        blocks = []
        for low, high in ((0, 128), (128, OUT2 * C2)):
            blocks.append(
                dot(turned[low:high], act_one[first : first + rows, base + low : base + low + 256])
            )

        def term(position, tile):
            group = min(position // 4, 1)
            inside, lane = position - 4 * group, (tile - group) * 128
            return blocks[group][inside * C2 : (inside + 1) * C2, lane : lane + 128]

        return term

    grad = kernel_grad([term_of(tap) for tap in range(4)], OUT2, C2)
    return grad, fold(tiles_sum(dot(jnp.ones((8, rows), BF), d_two)), C2)


def grad_kernel_one(pixels, dz_one, frames):
    rows = OUT1 * frames
    d_one = dz_one[...]
    turned = d_one.T

    def term_of(tap):
        first = (tap // 4) * frames
        base = (tap % 4) * WIDE
        blocks = []
        for low, high in ((0, 128), (128, OUT1 * C1)):
            blocks.append(
                dot(turned[low:high], pixels[first : first + rows, base + low : base + low + 256])
            )

        def term(position, tile):
            group = min(position // 8, 1)
            inside, lane = position - 8 * group, (tile - group) * 128
            return blocks[group][inside * C1 : (inside + 1) * C1, lane : lane + 128]

        return term

    grad = kernel_grad([term_of(tap) for tap in range(8)], OUT1, C1)
    return grad, fold(tiles_sum(dot(jnp.ones((8, rows), BF), d_one)), C1)


def local_kernel(
    frames_hbm,
    kernels_ref,
    linear_ref,
    mats_ref,
    table_ref,
    bias_ref,
    options_ref,
    legal_ref,
    games_ref,
    valid_ref,
    rewards_ref,
    returns_ref,
    lin_out,
    mats_out,
    table_out,
    conv_out,
    small_out,
    frame_buf,
    pixels,
    band_one,
    band_two,
    slope_one,
    act_one,
    slope_two,
    act_two,
    dz_two,
    dz_one,
    sems,
):
    section = lax.axis_index("section")
    frames = frame_buf.shape[1]
    copies = load_frames(frames_hbm, section, frame_buf, sems, CHUNK)
    for copy in copies:
        copy.start()
    clear_bands(band_one, band_two)
    kernels = kernels_ref[...]
    build_one(kernels[0 : KERN // 2], band_one.at[0])
    build_one(kernels[KERN // 2 : KERN], band_one.at[1])
    for fill in build_two(kernels, band_two):
        fill()
    bias_one, bias_two, bias_three, bias_four = wide_biases(bias_ref[...])
    clear_tails(pixels)
    for which, copy in enumerate(copies):
        copy.wait()
        place_frames(frame_buf, pixels, which * CHUNK, CHUNK, frames)
    encode_one(pixels, band_one, 0, True, bias_one, slope_one, act_one, frames, 4)
    encode_one(pixels, band_one, 1, False, bias_one, slope_one, act_one, frames, 4)
    encode_two(act_one, band_two, bias_two, slope_two, act_two, frames, 3)
    linear_t = linear_ref[...]
    states = (dot(linear_t, act_two[...], 1, 1) + bias_three).astype(BF)
    d_state, grad_mats, grad_table, grad_bias, errors = plan(
        states,
        tuple(mats_ref[k] for k in range(3)),
        table_ref[...],
        bias_four,
        *frame_rows(
            section, (options_ref, legal_ref, games_ref, valid_ref, rewards_ref, returns_ref)
        ),
        1.0,
    )
    for k in range(3):
        mats_out[k] = grad_mats[k]
    table_out[...] = grad_table
    d_state_low = d_state.astype(BF)
    lin_out[...] = dot(d_state_low, act_two[...])
    back_two(d_state_low, linear_t, slope_two, dz_two, frames)
    grad_two, bias_two_grad = grad_kernel_two(act_one, dz_two, frames)
    back_one(dz_two, band_two, slope_one, dz_one, frames, 5)
    grad_one, bias_one_grad = grad_kernel_one(pixels, dz_one, frames)
    conv_out[...] = stack_kernels(grad_one, grad_two)
    lane = iota((8, 128), 1)
    line = iota((8, 128), 0)
    row_zero = jnp.where(
        lane < C1, bias_one_grad, jnp.where(lane < C1 + C2, turn(bias_two_grad, C1), 0.0)
    )
    count = sum(
        valid_ref[k, pl.ds(section, 1), :].astype(F32) for k in range(valid_ref.shape[0])
    )
    count = jnp.where(iota((1, 128), 1) < frames, twice(count), 0.0)
    small = jnp.where(line == 0, row_zero, 0.0)
    small = jnp.where(line == 1, row_of(lane_sum(d_state_low)), small)
    small = jnp.where(line == 2, row_of(grad_bias), small)
    small = jnp.where(line == 3, errors, small)
    small = jnp.where(line == 4, count, small)
    small_out[...] = small


def lane_sum(value):
    return jnp.sum(value.astype(F32), axis=1, keepdims=True)


def stack_kernels(grad_one, grad_two):
    rows = jnp.concatenate([grad_one, grad_two, jnp.zeros((128 - C1 - C2, KERN), F32)], axis=0)
    return rows.T


def tiles_sum(value):
    return sum(value[:, k * 128 : (k + 1) * 128] for k in range(value.shape[1] // 128))


VMEM_SPEC = pl.BlockSpec(memory_space=pltpu.VMEM)
ANY_SPEC = pl.BlockSpec(memory_space=pl.ANY)


def local_scratch(frames, side):
    return [
        pltpu.VMEM((side, frames, 336), BF),
        pltpu.VMEM(((OUT1 + 1) * frames, 4 * WIDE), BF),
        pltpu.VMEM((2, 4 * 256, 256), BF),
        pltpu.VMEM((4 * WIDE, WIDE), BF),
        pltpu.VMEM((OUT1 // 2 * frames, 2 * WIDE), F32),
        pltpu.VMEM((OUT1 // 2 * frames, 2 * WIDE), BF),
        pltpu.VMEM((OUT2 * frames, WIDE), F32),
        pltpu.VMEM((frames, FEAT), BF),
        pltpu.VMEM(((OUT2 + 2) * frames, WIDE), BF),
        pltpu.VMEM((OUT1 * frames, WIDE), BF),
        pltpu.SemaphoreType.DMA((side // CHUNK,)),
    ]


def local_step(frames, kernels, linear_t, mats_t, table, biases, options, legal, games, valid, rewards, returns):
    count = frames.shape[1]
    side = frames.shape[2]
    shapes = [(D, FEAT), (3, D, D), (D, 128), (KERN, 128), (8, 128)]
    return pl.pallas_call(
        local_kernel,
        out_shape=[jax.ShapeDtypeStruct(shape, F32) for shape in shapes],
        in_specs=[ANY_SPEC] + [VMEM_SPEC] * 11,
        out_specs=[VMEM_SPEC] * len(shapes),
        scratch_shapes=local_scratch(count, side),
        compiler_params=pltpu.CompilerParams(vmem_limit_bytes=56 * 1024 * 1024),
    )(
        frames.transpose(0, 2, 1, 3),
        kernels,
        linear_t,
        mats_t,
        table,
        biases.reshape(1, BIAS),
        options.transpose(2, 0, 1),
        legal.transpose(2, 0, 1),
        games,
        valid.transpose(2, 0, 1),
        rewards.transpose(2, 0, 1),
        returns.transpose(0, 2, 1),
    )


MESH = pl.DeviceIdType.MESH


QUARTER = 768
HALF = 2 * QUARTER
AT_EMB = FEAT
AT_HEADS = AT_EMB + OPTS
AT_MATS = LIN_PAD
TILES = HALF // 128
SCALE_LANE = C1 + C2
NEAR = 8
FOUR = 4


def fused_kernel(
    peers,
    frames_hbm,
    conv_hbm,
    lin_hbm,
    mats_hbm,
    emb_hbm,
    heads_hbm,
    bias_hbm,
    options_hbm,
    legal_hbm,
    games_hbm,
    valid_hbm,
    rewards_hbm,
    returns_hbm,
    main_out,
    conv_out,
    stats_out,
    frame_buf,
    pixels,
    band_one,
    band_two,
    slope_one,
    act_one,
    slope_two,
    act_two,
    dz_two,
    dz_one,
    frame_sems,
    stage,
    kernel_msg,
    weight_msg,
    weights,
    grad_own,
    mate_in,
    grad_msg,
    near_in,
    cross_in,
    cross_msg,
    far_in,
    taps_msg,
    row_in,
    rows_in,
    taps_turned,
    stats_in,
    final,
    stats_base,
    half_in,
    send_sems,
    recv_sems,
    mate_send,
    mate_recv,
    conv_ref,
    lin_ref,
    mats_ref,
    emb_ref,
    heads_ref,
    bias_ref,
    options_ref,
    legal_ref,
    games_ref,
    valid_ref,
    rewards_ref,
    returns_ref,
    operand_sems,
):
    section = lax.axis_index("section")
    place = lax.axis_index("dp")
    mate = 1 - section
    frames = frame_buf.shape[1]

    barrier = pltpu.get_barrier_semaphore()

    def greet(step, carry):
        peer = lax.rem(place + step, peers)
        pl.semaphore_signal(barrier, inc=1, device_id=(section, peer), device_id_type=MESH)
        return carry

    def greet_row(step, carry):
        peer = place - lax.rem(place, FOUR) + lax.rem(place + step, FOUR)
        pl.semaphore_signal(barrier, inc=1, device_id=(mate, peer), device_id_type=MESH)
        return carry

    lax.fori_loop(1, peers, greet, 0)
    lax.fori_loop(0, FOUR, greet_row, 0)
    loads = [
        pltpu.make_async_copy(source, target, operand_sems.at[which])
        for which, (source, target) in enumerate(
            (
                (conv_hbm, conv_ref),
                (lin_hbm, lin_ref),
                (mats_hbm, mats_ref),
                (emb_hbm, emb_ref),
                (heads_hbm, heads_ref),
                (bias_hbm, bias_ref),
                (options_hbm, options_ref),
                (legal_hbm, legal_ref),
                (games_hbm, games_ref),
                (valid_hbm, valid_ref),
                (rewards_hbm, rewards_ref),
                (returns_hbm, returns_ref),
            )
        )
    ]
    for load in loads:
        load.start()
    copies = load_frames(frames_hbm, section, frame_buf, frame_sems, CHUNK)
    wait_frames = lambda: [copy.wait() for copy in copies]
    for copy in copies:
        copy.start()

    sends = []

    side, spot = place // NEAR, lax.rem(place, NEAR)
    row, column = spot // FOUR, lax.rem(spot, FOUR)

    def near(step):
        return side * NEAR + lax.rem(spot + step, NEAR)

    def beyond(step):
        return (1 - side) * NEAR + lax.rem(spot + step, NEAR)

    def beside(step):
        return place - column + lax.rem(column + step, FOUR)

    def across(step, where):
        return (1 - side) * NEAR + lax.rem(row + step, 2) * FOUR + where

    def send(sems, peer, source, target, core=section):
        pltpu.make_async_remote_copy(
            src_ref=source,
            dst_ref=target,
            send_sem=send_sems.at[sems],
            recv_sem=recv_sems.at[sems],
            device_id=(core, peer),
            device_id_type=MESH,
        ).start()

    def loop(low, high, act):
        def body(step, carry):
            act(step)
            return carry

        lax.fori_loop(low, high, body, 0)

    def settle(sems, blocks):
        whole = pltpu.make_async_remote_copy(
            src_ref=blocks,
            dst_ref=blocks,
            send_sem=send_sems.at[sems],
            recv_sem=recv_sems.at[sems],
            device_id=(mate, place),
            device_id_type=MESH,
        )
        sends.append(whole.wait_send)
        return whole.wait_recv

    def send_peers(sems, source, target):
        loop(0, NEAR, lambda step: send(sems, beyond(step), source, target.at[place]))
        loop(1, NEAR, lambda step: send(sems, near(step), source, target.at[place]))
        return settle(sems, target.at[pl.ds(0, peers - 1)])

    def send_mate(which, source, target, landing):
        def copy(into):
            return pltpu.make_async_remote_copy(
                src_ref=source,
                dst_ref=into,
                send_sem=mate_send.at[which],
                recv_sem=mate_recv.at[which],
                device_id=(mate, place),
                device_id_type=MESH,
            )

        copy(target).start()
        sends.append(lambda: copy(target).wait_send())
        return lambda: copy(landing).wait_recv()

    for load in loads:
        load.wait()
    upper_lanes = iota((16, 128), 1) >= 64
    counts = sum(
        valid_ref[k, m : m + 1, :].astype(F32)
        for k in range(valid_ref.shape[0])
        for m in range(valid_ref.shape[1])
    )
    conv_pad = jnp.concatenate([conv_ref[...], jnp.zeros((16, 80), F32)], axis=1)
    kernel_msg[place] = jnp.where(
        upper_lanes & (iota((16, 128), 0) == 0), jnp.broadcast_to(twice(counts), (16, 128)), conv_pad
    ).astype(BF)
    heads_pad = jnp.concatenate([heads_ref[...], jnp.zeros((24, 120), F32)], axis=1)
    heads_pad = jnp.concatenate([heads_pad, jnp.zeros((104, 128), F32)], axis=0).T
    last = FEAT - EMB_LANE
    stage[:, 0:last] = lin_ref[:, 0:last]
    stage[:, last:LIN_PAD] = jnp.concatenate(
        [
            lin_ref[:, last:FEAT],
            emb_ref[...],
            heads_pad[0:8, 0 : 3 * GAMES],
            jnp.zeros((8, 128 - HEAD_LANE - 3 * GAMES), F32),
        ],
        axis=1,
    )
    for k in range(3):
        stage[:, AT_MATS + k * D : AT_MATS + (k + 1) * D] = mats_ref[k]
    first = stage[:, pl.ds(pl.multiple_of(section * HALF, 128), QUARTER)]
    second = stage[:, pl.ds(pl.multiple_of(section * HALF + QUARTER, 128), QUARTER)]
    weight_msg[section, place] = jnp.concatenate([first, second], axis=0).astype(BF)

    def square_sum(value):
        return jnp.sum(jnp.sum(value * value, axis=0, keepdims=True), axis=1, keepdims=True)

    weight_squares = [
        square_sum(conv_pad),
        square_sum(lin_ref[...]),
        square_sum(mats_ref[...].reshape(24, D)),
        square_sum(emb_ref[...]),
        square_sum(heads_ref[...]),
    ]
    stat_line = iota((16, 128), 0)
    stat = jnp.zeros((16, 128), F32)
    for which, value in enumerate(weight_squares):
        at = iota((16, 128), 1) - SCALE_LANE
        rough = value.astype(BF).astype(F32)
        mixed = stat_line == TILES + 2
        stat = jnp.where(mixed & (at == which), rough, stat)
        stat = jnp.where(mixed & (at == which + 5), value - rough, stat)
    stats_base[...] = stat
    pl.semaphore_wait(barrier, peers - 1 + FOUR)
    half_msg = weight_msg.at[section]

    def spread_own(sems, blocks):
        own = blocks.at[place]
        loop(0, 2, lambda step: send(sems, across(step, column), own, own))
        wait_across = settle(sems, blocks.at[pl.ds(0, 2)])
        loop(1, NEAR, lambda step: send(sems + 1, near(step), own, own))
        return wait_across, settle(sems + 1, blocks.at[pl.ds(0, NEAR - 1)])

    def pass_on(sems, blocks):
        for which in range(2):
            block = blocks.at[across(which, column)]
            loop(1, FOUR, lambda step: send(sems, beside(step), block, block))
        return settle(sems, blocks.at[pl.ds(0, 2 * (FOUR - 1))])

    wait_kernel_across, wait_kernel_near = spread_own(0, kernel_msg)
    wait_across, wait_near = spread_own(3, half_msg)

    clear_bands(band_one, band_two)
    bias_one, bias_two, bias_three, bias_four = wide_biases(bias_ref[...].reshape(1, BIAS))
    clear_tails(pixels)
    act_two[:, FEAT:LIN_PAD] = jnp.zeros((frames, LIN_PAD - FEAT), BF)
    for which, copy in enumerate(copies):
        copy.wait()
        place_frames(frame_buf, pixels, which * CHUNK, CHUNK, frames)
    wait_kernel_across()
    wait_kernel_beside = pass_on(2, kernel_msg)
    wait_kernel_near()

    def side_kernels(which):
        return kernel_msg[pl.ds(which * NEAR, NEAR)].reshape(KERN // 2, 128)

    build_one(side_kernels(side), band_one.at[side])
    wait_across()
    wait_beside = pass_on(5, half_msg)
    encode_one(pixels, band_one, side, True, bias_one, slope_one, act_one, frames, 4)
    wait_kernel_beside()
    build_one(side_kernels(1 - side), band_one.at[1 - side])
    kernels = kernel_msg[...].reshape(KERN, 128)
    fills = build_two(kernels, band_two)
    counted = jnp.where(iota((KERN, 128), 1) >= 64, kernels.astype(F32), 0.0)
    count = jnp.sum(jnp.sum(counted, axis=0, keepdims=True), axis=1, keepdims=True)
    scale = 1.0 / count
    encode_one(pixels, band_one, 1 - side, False, bias_one, slope_one, act_one, frames, 4, fills)
    wait_near()
    own_side, far_side = pl.ds(side * NEAR, NEAR), pl.ds((1 - side) * NEAR, NEAR)
    wait_own_side = send_mate(
        0, half_msg.at[own_side], half_msg.at[own_side], weight_msg.at[mate, own_side]
    )
    wait_beside()
    wait_far_side = send_mate(
        5, half_msg.at[far_side], half_msg.at[far_side], weight_msg.at[mate, far_side]
    )
    encode_two(act_one, band_two, bias_two, slope_two, act_two, frames, 3)
    wait_own_side()
    wait_far_side()
    for half in range(2):
        block = weight_msg[half].astype(F32)
        for part in range(2):
            lane = (2 * half + part) * QUARTER
            weights[:, lane : lane + QUARTER] = (
                block[:, part * 8 : (part + 1) * 8].reshape(D, QUARTER).astype(BF)
            )
    linear_t = weights[:, 0:LIN_PAD]
    states = (dot(linear_t, act_two[...], 1, 1) + bias_three).astype(BF)
    d_state, grad_mats, grad_table, grad_bias, errors = plan(
        states,
        tuple(weights[:, AT_MATS + k * D : AT_MATS + (k + 1) * D] for k in range(3)),
        weights[:, LIN_PAD - 128 : LIN_PAD],
        bias_four,
        *frame_rows(
            section, (options_ref, legal_ref, games_ref, valid_ref, rewards_ref, returns_ref)
        ),
        scale,
    )

    d_state_low = d_state.astype(BF)
    grad_linear = dot(d_state_low, act_two[...])
    parts = [grad_linear[:, at * QUARTER : (at + 1) * QUARTER] for at in range(3)]
    parts.append(
        jnp.concatenate(
            [
                grad_linear[:, 3 * QUARTER : LIN_PAD - 128],
                grad_linear[:, LIN_PAD - 128 : LIN_PAD] + grad_table,
                *grad_mats,
            ],
            axis=1,
        )
    )
    parts = [part.reshape(peers, 8, QUARTER) for part in parts]
    for half in range(2):
        grad_own[half] = jnp.concatenate(parts[2 * half : 2 * half + 2], axis=1).astype(BF)
    wait_mate = send_mate(1, grad_own.at[mate], mate_in, mate_in)
    back_two(d_state_low, linear_t, slope_two, dz_two, frames)
    wait_mate()
    grad_msg[...] = (grad_own[section].astype(F32) + mate_in[...].astype(F32)).astype(BF)
    for which in range(2):

        def collect(step):
            peer = beside(step)
            owner = across(which, lax.rem(peer, FOUR))
            send(6, peer, grad_msg.at[owner], cross_in.at[which, column])

        loop(1, FOUR, collect)
        cross_in[which, column] = grad_msg[across(which, column)]
    wait_cross = settle(6, grad_msg.at[pl.ds(0, 2 * (FOUR - 1))])
    loop(1, NEAR, lambda step: send(7, near(step), grad_msg.at[near(step)], near_in.at[spot]))
    wait_grads = settle(7, near_in.at[pl.ds(0, NEAR - 1)])
    near_in[spot] = grad_msg[place]
    row_three = row_of(lane_sum(d_state_low))
    row_four = row_of(grad_bias)
    grad_two, bias_two_grad = grad_kernel_two(act_one, dz_two, frames)
    back_one(dz_two, band_two, slope_one, dz_one, frames, 5)
    grad_one, bias_one_grad = grad_kernel_one(pixels, dz_one, frames)

    kernel_grads = jnp.concatenate([grad_one, grad_two], axis=0).astype(BF)
    for half in range(2):
        taps_msg[half] = kernel_grads[:, half * 128 : (half + 1) * 128]
    own = section * FOUR + column
    loop(1, FOUR, lambda step: send(9, beside(step), taps_msg.at[section], row_in.at[own]))
    loop(0, FOUR, lambda step: send(9, beside(step), taps_msg.at[mate], row_in.at[own], mate))
    wait_row = settle(9, row_in.at[pl.ds(0, 2 * FOUR - 1)])
    row_in[own] = taps_msg[section]
    wait_cross()
    cross_msg[...] = jnp.sum(cross_in[...].astype(F32), axis=1).astype(BF)
    loop(0, 2, lambda step: send(8, across(step, column), cross_msg.at[step], far_in.at[row]))
    wait_far = settle(8, far_in)
    wait_row()
    level = place // FOUR
    rows_in[level] = jnp.sum(row_in[...].astype(F32), axis=0).astype(BF)
    loop(
        1,
        peers // FOUR,
        lambda step: send(
            11, lax.rem(place + step * FOUR, peers), rows_in.at[level], rows_in.at[level]
        ),
    )
    wait_rows = settle(11, rows_in.at[pl.ds(0, peers // FOUR - 1)])
    wait_grads()
    wait_far()
    total = jnp.sum(near_in[...].astype(F32), axis=0) + jnp.sum(far_in[...].astype(F32), axis=0)
    squares = total * total
    stat = stats_base[...]
    for part in range(2):
        sums = jnp.sum(squares[part * 8 : (part + 1) * 8], axis=0, keepdims=True)
        for tile in range(TILES // 2):
            stat = jnp.where(
                stat_line == part * (TILES // 2) + tile, sums[:, tile * 128 : (tile + 1) * 128], stat
            )
    lane = iota((1, 128), 1)
    row_first = jnp.where(
        lane < C1, bias_one_grad[0:1], jnp.where(lane < C1 + C2, turn(bias_two_grad, C1)[0:1], 0.0)
    )
    row_first = row_first + turn(errors, 64)
    stat = jnp.where(stat_line == TILES, row_three, stat)
    stat = jnp.where(stat_line == TILES + 1, row_four, stat)
    stat = stat + jnp.where(stat_line == TILES + 2, row_first, 0.0)
    stats_in[place] = stat.astype(BF)
    wait_stats = send_peers(10, stats_in.at[place], stats_in)
    half_in[section, :, 0:QUARTER] = total[0:8]
    half_in[section, :, QUARTER:HALF] = total[8:16]
    wait_half_grads = send_mate(3, half_in.at[section], half_in.at[section], half_in.at[mate])
    wait_rows()
    taps = jnp.sum(rows_in[...].astype(F32), axis=0)
    taps = jnp.concatenate([taps, jnp.zeros((128 - C1 - C2, 128), F32)], axis=0)
    taps_turned[...] = taps.T
    final[section, 16:32] = taps_turned[pl.ds(pl.multiple_of(spot * 16, 16), 16)]
    final[section, 32:40] = jnp.broadcast_to(
        jnp.sum(taps * taps, axis=0, keepdims=True), (8, 128)
    )
    wait_half_grads()
    for half in range(2):
        main_out[:, half * HALF : (half + 1) * HALF] = half_in[half]
    wait_stats()
    final[section, 0:16] = jnp.sum(stats_in[...].astype(F32), axis=0)
    wait_final = send_mate(4, final.at[section], final.at[section], final.at[mate])
    wait_final()
    conv_out[...] = final[side, 16:32]
    stats_out[...] = final[...]

    for wait in sends:
        wait()


def fused_step(peers, frames, shards, biases, rows):
    count = frames.shape[1]
    side = frames.shape[2]
    scratch = local_scratch(count, side)
    scratch[7] = pltpu.VMEM((count, LIN_PAD), BF)
    scratch += [
        pltpu.VMEM((8, 2 * HALF), F32),
        pltpu.VMEM((peers, 16, 128), BF),
        pltpu.VMEM((2, peers, 16, QUARTER), BF),
        pltpu.VMEM((D, 2 * HALF), BF),
        pltpu.VMEM((2, peers, 16, QUARTER), BF),
        pltpu.VMEM((peers, 16, QUARTER), BF),
        pltpu.VMEM((peers, 16, QUARTER), BF),
        pltpu.VMEM((NEAR, 16, QUARTER), BF),
        pltpu.VMEM((2, FOUR, 16, QUARTER), BF),
        pltpu.VMEM((2, 16, QUARTER), BF),
        pltpu.VMEM((2, 16, QUARTER), BF),
        pltpu.VMEM((2, C1 + C2, 128), BF),
        pltpu.VMEM((2 * FOUR, C1 + C2, 128), BF),
        pltpu.VMEM((peers // FOUR, C1 + C2, 128), BF),
        pltpu.VMEM((128, 128), F32),
        pltpu.VMEM((peers, 16, 128), BF),
        pltpu.VMEM((2, 40, 128), F32),
        pltpu.VMEM((16, 128), F32),
        pltpu.VMEM((2, 8, HALF), F32),
        pltpu.SemaphoreType.DMA((12,)),
        pltpu.SemaphoreType.DMA((12,)),
        pltpu.SemaphoreType.DMA((6,)),
        pltpu.SemaphoreType.DMA((6,)),
    ]
    shapes = [(8, 2 * HALF), (16, 128), (2, 40, 128)]
    operands = [frames.transpose(0, 2, 1, 3), *shards, biases, *rows]
    scratch += [pltpu.VMEM(operand.shape, operand.dtype) for operand in operands[1:]]
    scratch += [pltpu.SemaphoreType.DMA((len(operands) - 1,))]
    return pl.pallas_call(
        functools.partial(fused_kernel, peers),
        out_shape=[jax.ShapeDtypeStruct(shape, F32) for shape in shapes],
        in_specs=[ANY_SPEC] * len(operands),
        out_specs=[VMEM_SPEC] * len(shapes),
        scratch_shapes=scratch,
        compiler_params=pltpu.CompilerParams(
            vmem_limit_bytes=56 * 1024 * 1024, collective_id=0, has_side_effects=True
        ),
    )(*operands)


def column_of(row):
    square = jnp.broadcast_to(row, (8, 8))
    return jnp.sum(jnp.where(iota((8, 8), 0) == iota((8, 8), 1), square, 0.0), axis=1, keepdims=True)


def row_back(column):
    square = jnp.broadcast_to(column, (8, 8))
    return jnp.sum(jnp.where(iota((8, 8), 0) == iota((8, 8), 1), square, 0.0), axis=0, keepdims=True)


def total_of(value):
    return jnp.sum(jnp.sum(value, axis=0, keepdims=True), axis=1, keepdims=True)


def update_kernel(
    main_ref,
    convg_ref,
    stats_ref,
    conv_ref,
    lin_ref,
    mats_ref,
    emb_ref,
    heads_ref,
    bias_ref,
    conv_moment,
    lin_rows,
    lin_cols,
    mats_rows,
    mats_cols,
    emb_moment,
    head_moment,
    bias_moment,
    conv_new,
    conv_grad,
    conv_moment_new,
    lin_new,
    lin_grad,
    lin_rows_new,
    lin_cols_new,
    mats_new,
    mats_grad,
    mats_rows_new,
    mats_cols_new,
    emb_new,
    emb_grad,
    emb_moment_new,
    heads_new,
    heads_grad,
    head_moment_new,
    bias_new,
    bias_grad,
    bias_moment_new,
    norm_out,
    loss_out,
    conv_low,
    lin_low,
):
    stats = stats_ref[...]
    both = stats[0] + stats[1]
    squares = total_of(both[0:TILES]) + total_of(both[32:33])
    scales = stats[0, TILES + 2 : TILES + 3]
    scales = [
        scales[:, SCALE_LANE + k : SCALE_LANE + k + 1]
        + scales[:, SCALE_LANE + k + 5 : SCALE_LANE + k + 6]
        for k in range(5)
    ]
    bias_raw = jnp.concatenate(
        [both[TILES + 2 : TILES + 3, 0 : C1 + C2], both[TILES : TILES + 1], both[TILES + 1 : TILES + 2]],
        axis=1,
    )
    norm = jnp.sqrt(squares + total_of(bias_raw * bias_raw))
    factor = jnp.minimum(1.0, CLIP_LIMIT / norm)
    norm_out[...] = norm
    loss_out[...] = total_of(both[TILES + 2 : TILES + 3, 64:128])

    def simple(weight, grad, moment, square_total, outs):
        new, moment_new = unfactored(
            weight, grad, moment, relative(square_total, weight.size * outs[3])
        )
        for out, value in zip(outs, (new, grad, moment_new)):
            out[...] = value.reshape(out.shape)
        return new

    peers = D // lin_ref.shape[0]
    conv = simple(
        conv_ref[...],
        factor * convg_ref[:, 0 : C1 + C2],
        conv_moment[...],
        scales[0],
        (conv_new, conv_grad, conv_moment_new, peers),
    )
    conv_low[...] = conv.astype(BF)
    simple(
        emb_ref[...],
        factor * main_ref[:, AT_EMB:AT_HEADS],
        emb_moment[...],
        scales[3],
        (emb_new, emb_grad, emb_moment_new, peers),
    )
    heads_t = jnp.concatenate(
        [main_ref[:, LIN_PAD - 128 : LIN_PAD], jnp.zeros((120, 128), F32)], axis=0
    ).T
    simple(
        heads_ref[...],
        factor * heads_t[HEAD_LANE : HEAD_LANE + 3 * GAMES, 0:8],
        head_moment[...],
        scales[4],
        (heads_new, heads_grad, head_moment_new, peers),
    )
    bias = bias_ref[...].reshape(1, BIAS)
    simple(
        bias,
        factor * bias_raw,
        bias_moment[...].reshape(1, BIAS),
        total_of(bias * bias),
        (bias_new, bias_grad, bias_moment_new, 1),
    )
    row_sums = [stats[t // TILES, t % TILES : t % TILES + 1] for t in range(24)]

    def factored(weight, grad, rows_old, cols_old, row_sum, square_total, entries):
        rows = DECAY_RATE * rows_old + (1.0 - DECAY_RATE) * (
            factor * factor * row_sum / D + FLOOR_ONE
        )
        wide = grad.shape[1]
        cols = DECAY_RATE * cols_old + (1.0 - DECAY_RATE) * (
            jnp.sum(grad * grad + FLOOR_ONE, axis=1, keepdims=True) / wide
        )
        mean = jnp.sum(rows, axis=1, keepdims=True) / wide
        second = rows * cols / mean
        new = weight - STEP_RATE * relative(square_total, entries) * grad * lax.rsqrt(second)
        return new, rows, cols

    grad = factor * main_ref[:, 0:FEAT]
    new, rows, cols = factored(
        lin_ref[...],
        grad,
        lin_rows[...].reshape(1, FEAT),
        column_of(lin_cols[...]),
        jnp.concatenate(row_sums[:21], axis=1)[:, 0:FEAT],
        scales[1],
        FEAT * D,
    )
    lin_new[...] = new
    lin_grad[...] = grad
    lin_rows_new[...] = rows.reshape(FEAT)
    lin_cols_new[...] = row_back(cols)
    lin_low[...] = new.astype(BF)
    for k in range(3):
        grad = factor * main_ref[:, AT_MATS + k * D : AT_MATS + (k + 1) * D]
        new, rows, cols = factored(
            mats_ref[k],
            grad,
            mats_rows[k : k + 1],
            column_of(mats_cols[k : k + 1]),
            row_sums[21 + k],
            scales[2],
            3 * D * D,
        )
        mats_new[k] = new
        mats_grad[k] = grad
        mats_rows_new[k : k + 1] = rows
        mats_cols_new[k : k + 1] = row_back(cols)


def fused_device(
    frames,
    options,
    legal,
    games,
    valid,
    rewards,
    returns,
    conv_kernels,
    enc_linear,
    plan_mats,
    option_emb,
    heads,
    biases,
    conv_moment,
    lin_rows,
    lin_cols,
    mats_rows,
    mats_cols,
    emb_moment,
    head_moment,
    bias_moment,
):
    width = enc_linear.shape[1]
    peers = D // width
    shards = (
        conv_kernels,
        enc_linear.T,
        plan_mats.transpose(0, 2, 1),
        option_emb.T,
        heads.reshape(3 * GAMES, width),
    )
    summed = fused_step(
        peers,
        frames,
        shards,
        biases,
        (
            options.transpose(2, 0, 1),
            legal.transpose(2, 0, 1),
            games,
            valid.transpose(2, 0, 1),
            rewards.transpose(2, 0, 1),
            returns.transpose(0, 2, 1),
        ),
    )
    shapes = [(16, 48)] * 3 + [(8, FEAT)] * 2 + [(FEAT,), (1, 8)] + [(3, 8, D)] * 2 + [(3, D), (3, 8)]
    shapes += [(8, OPTS)] * 3 + [(24, 8)] * 3 + [(BIAS,)] * 3 + [(1, 1)] * 2
    outs = [jax.ShapeDtypeStruct(shape, F32) for shape in shapes]
    outs += [jax.ShapeDtypeStruct((16, 48), BF), jax.ShapeDtypeStruct((8, FEAT), BF)]
    operands = [
        *summed,
        *shards,
        biases,
        conv_moment,
        lin_rows,
        lin_cols.reshape(1, width),
        mats_rows,
        mats_cols,
        emb_moment.T,
        head_moment.reshape(3 * GAMES, width),
        bias_moment,
    ]
    o = pl.pallas_call(
        update_kernel,
        out_shape=outs,
        in_specs=[VMEM_SPEC] * len(operands),
        out_specs=[VMEM_SPEC] * len(outs),
    )(*operands)
    flat_heads = [h.reshape(3, GAMES, width) for h in o[14:17]]
    return (
        *o[0:3],
        o[3].T,
        o[4].T,
        o[5],
        o[6].reshape(width),
        o[7].transpose(0, 2, 1),
        o[8].transpose(0, 2, 1),
        o[9],
        o[10],
        o[11].T,
        o[12].T,
        o[13].T,
        *flat_heads,
        *o[17:20],
        o[20].reshape(()),
        o[21].reshape(()),
        o[22],
        o[23].T,
    )


def gather_rows(shard):
    return lax.all_gather(shard, "dp", axis=0, tiled=True)


def relative(square_total, entries):
    return jnp.maximum(FLOOR_TWO, jnp.sqrt(square_total / entries))


def unfactored(weight, grad, moment, scale):
    moment_new = DECAY_RATE * moment + (1.0 - DECAY_RATE) * (grad * grad + FLOOR_ONE)
    return (weight - STEP_RATE * scale * grad * lax.rsqrt(moment_new), moment_new)


def per_device(
    frames,
    options,
    legal,
    games,
    valid,
    rewards,
    returns,
    conv_kernels,
    enc_linear,
    plan_mats,
    option_emb,
    heads,
    biases,
    conv_moment,
    lin_rows,
    lin_cols,
    mats_rows,
    mats_cols,
    emb_moment,
    head_moment,
    bias_moment,
):
    weight_squares = lax.psum(
        (
            jnp.sum(conv_kernels * conv_kernels),
            jnp.sum(enc_linear * enc_linear),
            jnp.sum(plan_mats * plan_mats),
            jnp.sum(option_emb * option_emb),
            jnp.sum(heads * heads),
        ),
        "dp",
    )
    width = enc_linear.shape[1]
    kernels = gather_rows(conv_kernels.astype(BF))
    linear_t = gather_rows(enc_linear.astype(BF).T)
    mats_t = gather_rows(plan_mats.astype(BF).transpose(2, 0, 1)).transpose(1, 0, 2)
    emb_t = gather_rows(option_emb.astype(BF).T)
    heads_t = gather_rows(heads.astype(BF).reshape(3 * GAMES, width).T)
    table = jnp.pad(
        jnp.concatenate([emb_t, heads_t], axis=1),
        ((0, 0), (EMB_LANE, 128 - HEAD_LANE - 3 * GAMES)),
    )
    lin, mats, table_grad, conv, small = local_step(
        frames,
        kernels,
        linear_t,
        mats_t,
        table,
        biases,
        options,
        legal,
        games,
        valid,
        rewards,
        returns,
    )
    rows = jnp.concatenate(
        [lin, mats[0], mats[1], mats[2], table_grad[:, EMB_LANE : HEAD_LANE + 3 * GAMES]], axis=1
    )
    rows = lax.psum(lax.psum_scatter(rows, "dp", scatter_dimension=0, tiled=True), "section")
    conv = lax.psum(
        lax.psum_scatter(conv[:, : C1 + C2], "dp", scatter_dimension=0, tiled=True), "section"
    )
    small = lax.psum(small, ("section", "dp"))
    inverse_count = 1.0 / jnp.sum(small[4])
    loss_value = jnp.sum(small[3]) * inverse_count
    bias_raw = (
        jnp.concatenate([small[0, : C1 + C2], small[1], small[2]]) * inverse_count
    )
    rows = rows * inverse_count
    g_conv = conv * inverse_count
    g_lin = rows[:, :FEAT].T
    g_mats = rows[:, FEAT : FEAT + 3 * D].reshape(width, 3, D).transpose(1, 2, 0)
    g_emb = rows[:, FEAT + 3 * D : FEAT + 3 * D + OPTS].T
    g_heads = rows[:, FEAT + 3 * D + OPTS :].T.reshape(3, GAMES, width)
    partial_squares = (
        jnp.sum(g_conv * g_conv)
        + jnp.sum(g_lin * g_lin)
        + jnp.sum(g_mats * g_mats)
        + jnp.sum(g_emb * g_emb)
        + jnp.sum(g_heads * g_heads)
    )
    reduced = lax.psum(
        (partial_squares, jnp.sum(g_lin * g_lin, axis=1), jnp.sum(g_mats * g_mats, axis=2)), "dp"
    )
    grad_norm = jnp.sqrt(reduced[0] + jnp.sum(bias_raw * bias_raw))
    factor = jnp.minimum(1.0, CLIP_LIMIT / grad_norm)
    conv_grad = factor * g_conv
    lin_grad = factor * g_lin
    mats_grad = factor * g_mats
    emb_grad = factor * g_emb
    heads_grad = factor * g_heads
    bias_grad = factor * bias_raw
    conv_new, conv_moment_new = unfactored(
        conv_kernels, conv_grad, conv_moment, relative(weight_squares[0], KERN * (C1 + C2))
    )
    emb_new, emb_moment_new = unfactored(
        option_emb, emb_grad, emb_moment, relative(weight_squares[3], OPTS * D)
    )
    heads_new, head_moment_new = unfactored(
        heads, heads_grad, head_moment, relative(weight_squares[4], 3 * GAMES * D)
    )
    bias_new, bias_moment_new = unfactored(
        biases, bias_grad, bias_moment, relative(jnp.sum(biases * biases), BIAS)
    )
    lin_rows_new = DECAY_RATE * lin_rows + (1.0 - DECAY_RATE) * (
        factor * factor * reduced[1] / D + FLOOR_ONE
    )
    lin_cols_new = DECAY_RATE * lin_cols + (1.0 - DECAY_RATE) * jnp.mean(
        lin_grad * lin_grad + FLOOR_ONE, axis=0
    )
    lin_second = lin_rows_new[:, None] * lin_cols_new[None, :] / jnp.mean(lin_rows_new)
    lin_new = enc_linear - STEP_RATE * relative(weight_squares[1], FEAT * D) * lin_grad * lax.rsqrt(
        lin_second
    )
    mats_rows_new = DECAY_RATE * mats_rows + (1.0 - DECAY_RATE) * (
        factor * factor * reduced[2] / D + FLOOR_ONE
    )
    mats_cols_new = DECAY_RATE * mats_cols + (1.0 - DECAY_RATE) * jnp.mean(
        mats_grad * mats_grad + FLOOR_ONE, axis=1
    )
    mats_second = (
        mats_rows_new[:, :, None]
        * mats_cols_new[:, None, :]
        / jnp.mean(mats_rows_new, axis=1)[:, None, None]
    )
    mats_new = plan_mats - STEP_RATE * relative(weight_squares[2], 3 * D * D) * mats_grad * lax.rsqrt(
        mats_second
    )
    return (
        conv_new,
        conv_grad,
        conv_moment_new,
        lin_new,
        lin_grad,
        lin_rows_new,
        lin_cols_new,
        mats_new,
        mats_grad,
        mats_rows_new,
        mats_cols_new,
        emb_new,
        emb_grad,
        emb_moment_new,
        heads_new,
        heads_grad,
        head_moment_new,
        bias_new,
        bias_grad,
        bias_moment_new,
        grad_norm,
        loss_value,
        conv_new.astype(BF),
        lin_new.astype(BF),
    )


def solution(mesh):
    return jax.shard_map(
        fused_device if mesh.shape["dp"] * 8 == D else per_device,
        mesh=mesh,
        in_specs=(
            P(None, "dp", None, None),
            P(None, "dp", None),
            P(None, "dp", None),
            P(None, "dp"),
            P(None, "dp", None),
            P(None, "dp", None),
            P(None, "dp", None),
            P("dp", None),
            P(None, "dp"),
            P(None, None, "dp"),
            P(None, "dp"),
            P(None, None, "dp"),
            P(),
            P("dp", None),
            P(),
            P("dp"),
            P(),
            P(None, "dp"),
            P(None, "dp"),
            P(None, None, "dp"),
            P(),
        ),
        out_specs=(
            P("dp", None),
            P("dp", None),
            P("dp", None),
            P(None, "dp"),
            P(None, "dp"),
            P(),
            P("dp"),
            P(None, None, "dp"),
            P(None, None, "dp"),
            P(),
            P(None, "dp"),
            P(None, "dp"),
            P(None, "dp"),
            P(None, "dp"),
            P(None, None, "dp"),
            P(None, None, "dp"),
            P(None, None, "dp"),
            P(),
            P(),
            P(),
            P(),
            P(),
            P("dp", None),
            P(None, "dp"),
        ),
        check_vma=False,
    )
```

```python
import functools

import jax
import jax.numpy as jnp
from jax import lax
from jax.experimental import pallas as pl
from jax.experimental.pallas import tpu as pltpu
from jax.sharding import PartitionSpec as P

D = 128
C1 = 16
C2 = 32
OPTS = 18
KERN = 256
GAMES = 8
FEAT = 2592
BIAS = 304

OUT1 = 20
OUT2 = 9
WIDE = 384
LIN_PAD = 2688
EMB_LANE = FEAT % 128
HEAD_LANE = EMB_LANE + OPTS
CHUNK = 12
LATE_POSITIONS = 12
FEATS_ROW = OUT2 * C2

CLIP_LIMIT = 0.05
DECAY_RATE = 0.8
STEP_RATE = 0.5
FLOOR_ONE = 1e-30
FLOOR_TWO = 0.001

HIGH = lax.Precision.HIGHEST
BF = jnp.bfloat16
F32 = jnp.float32


def dot(left, right, over_left=1, over_right=0, precision=None):
    return lax.dot_general(
        left,
        right,
        (((over_left,), (over_right,)), ((), ())),
        precision=precision,
        preferred_element_type=F32,
    )


def sigmoid(value):
    return 0.5 * jnp.tanh(0.5 * value) + 0.5


def slope(active, sigma):
    return sigma + active * (1.0 - sigma)


def iota(shape, axis):
    return lax.broadcasted_iota(jnp.int32, shape, axis)


def turn(value, steps):
    return pltpu.roll(value, steps, 1)


def fold(value, width):
    step = 64
    while step >= width:
        value = value + turn(value, step)
        step //= 2
    return value


def row_of(column):
    square = jnp.broadcast_to(column, (128, 128))
    return jnp.sum(jnp.where(iota((128, 128), 0) == iota((128, 128), 1), square, 0.0), axis=0, keepdims=True)


def load_frames(frames_hbm, section, frame_buf, sems, chunk):
    copies = []
    for which in range(frame_buf.shape[0] // chunk):
        rows = pl.ds(which * chunk, chunk)
        copies.append(
            pltpu.make_async_copy(
                frames_hbm.at[section, rows], frame_buf.at[rows], sems.at[which]
            )
        )
    return copies


def place_frames(frame_buf, pixels, first, chunk, frames):
    for row in range(first, first + chunk):
        block, part = row // 4, row % 4
        pixels[block * frames : (block + 1) * frames, part * WIDE : part * WIDE + 336] = frame_buf[row]


def fill_band(wide, put, width, taps, blocks):
    for tap in taps:
        fill_tap(wide, put, width, tap, blocks)


def fill_tap(wide, put, width, tap, blocks):
    per_tile = 128 // width
    group = iota((width, 128), 1) // width
    base = 2 * tap * width
    for block in range(blocks + 1):
        tile, spot = divmod(block, per_tile)
        lanes = slice(tile * 128, (tile + 1) * 128)
        left = jnp.where(group == spot, wide[base : base + width, lanes], 0.0)
        right = wide[base + width : base + 2 * width]
        if spot > 0:
            left = jnp.where(group == spot - 1, right[:, lanes], left)
        elif block > 0:
            before = slice((tile - 1) * 128, tile * 128)
            put(tap, block, before, jnp.where(group == per_tile - 1, right[:, before], 0.0).astype(BF))
        put(tap, block, lanes, left.astype(BF))


def repeat_kernels(kernels, first, width, positions, lanes):
    held = kernels.shape[1]
    rows = iota((held, lanes), 0)
    cols = iota((held, lanes), 1)
    pick = jnp.where((cols % width + first == rows) & (cols < positions * width), 1.0, 0.0)
    return dot(kernels, pick.astype(BF))


def build_one(kernels, band):
    wide = repeat_kernels(kernels, 0, C1, LATE_POSITIONS, 256)

    def put(tap, block, lanes, value):
        rows = tap * 256 + block * C1
        band[rows : rows + C1, lanes] = value

    fill_band(wide, put, C1, range(4), LATE_POSITIONS)


def build_two(kernels, band):
    wide = repeat_kernels(kernels, C1, C2, OUT2, WIDE)

    def put(tap, block, lanes, value):
        rows = tap * WIDE + block * C2
        band[rows : rows + C2, lanes] = value

    return [lambda tap=tap: fill_tap(wide, put, C2, tap, OUT2) for tap in range(4)]


def clear_bands(band_one, band_two):
    band_one[...] = jnp.zeros(band_one.shape, BF)
    band_two[...] = jnp.zeros(band_two.shape, BF)


def wide_biases(bias_row):
    bias8 = jnp.broadcast_to(bias_row, (8, BIAS))
    rows = iota((BIAS, WIDE), 0)
    lanes = iota((BIAS, WIDE), 1)
    one = jnp.where((lanes % C1 == rows) & (lanes < OUT1 * C1), 1.0, 0.0)
    two = jnp.where((lanes % C2 + C1 == rows) & (lanes < OUT2 * C2), 1.0, 0.0)
    rows = iota((D, BIAS), 0)
    lanes = iota((D, BIAS), 1)
    three = jnp.where(lanes == rows + C1 + C2, 1.0, 0.0)
    four = jnp.where(lanes == rows + C1 + C2 + D, 1.0, 0.0)
    return (
        dot(bias8, one, precision=HIGH)[0:1],
        dot(bias8, two, precision=HIGH)[0:1],
        dot(three, bias8, 1, 1, precision=HIGH)[:, 0:1],
        dot(four, bias8, 1, 1, precision=HIGH)[:, 0:1],
    )


def encode_one(
    pixels, band_one, half, more, bias, slope_one, act_one, frames, chunk, beside=()
):
    rows = chunk * frames
    band = band_one[half]
    for first in range(0, OUT1, chunk):
        block = pixels[pl.ds(pl.multiple_of((half + first) * frames, frames), rows), :]
        parts = []
        for low, wide in ((0, 128), (128, 256)):
            window = jnp.concatenate(
                [block[:, tap * WIDE + low : tap * WIDE + low + 256] for tap in range(4)], axis=1
            )
            parts.append(dot(window, band[:, 0:wide]))
        if first // chunk < len(beside):
            beside[first // chunk]()
        z = jnp.concatenate(parts, axis=1)
        for step in range(chunk):
            at, part = divmod(first + step, 2)
            spot = (slice(at * frames, (at + 1) * frames), slice(part * WIDE, (part + 1) * WIDE))
            z_step = z[step * frames : (step + 1) * frames]
            if more:
                slope_one[spot] = z_step
            else:
                z_step = z_step + slope_one[spot] + bias
                sigma = sigmoid(z_step)
                active = z_step * sigma
                slope_one[spot] = slope(active, sigma)
                act_one[spot] = active.astype(BF)


def encode_two(act_one, band_two, bias, slope_two, act_two, frames, chunk):
    rows = chunk * frames
    bands = []
    for low, high in ((0, 128), (128, WIDE)):
        bands.append(
            jnp.concatenate(
                [band_two[tap * WIDE + low : tap * WIDE + low + 256, low:high] for tap in range(4)],
                axis=0,
            )
        )
    for first in range(0, OUT2, chunk):
        at = first * frames
        parts = []
        for low, band in zip((0, 128), bands):
            window = jnp.concatenate(
                [
                    act_one[
                        at + tap // 2 * frames : at + tap // 2 * frames + rows,
                        tap % 2 * WIDE + low : tap % 2 * WIDE + low + 256,
                    ]
                    for tap in range(4)
                ],
                axis=1,
            )
            parts.append(dot(window, band))
        z = jnp.concatenate(parts, axis=1) + bias
        sigma = sigmoid(z)
        active = z * sigma
        slope_two[at : at + rows] = slope(active, sigma)
        act = active.astype(BF)
        for step in range(chunk):
            lane = (first + step) * FEATS_ROW
            act_two[:, lane : lane + FEATS_ROW] = act[step * frames : (step + 1) * frames, :FEATS_ROW]


def back_two(dstate_t, linear_t, slope_two, dz_two, frames):
    dact = dot(dstate_t, linear_t, 0, 0)
    dz_two[0:frames] = jnp.zeros((frames, WIDE), BF)
    dz_two[(OUT2 + 1) * frames : (OUT2 + 2) * frames] = jnp.zeros((frames, WIDE), BF)
    blank = jnp.zeros((frames, WIDE - FEATS_ROW), F32)
    for at in range(OUT2):
        part = jnp.concatenate([dact[:, at * FEATS_ROW : (at + 1) * FEATS_ROW], blank], axis=1)
        dz_two[(at + 1) * frames : (at + 2) * frames] = (
            part * slope_two[at * frames : (at + 1) * frames]
        ).astype(BF)


def back_one(dz_two, band_two, slope_one, dz_one, frames, chunk):
    rows = chunk * frames

    def rows_of(tap, low, high):
        return slice(tap * WIDE + low, tap * WIDE + high)

    for first in range(0, OUT1 // 2, chunk):
        low = first * frames
        sides = [dz_two[low + frames : low + frames + rows], dz_two[low : low + rows]]
        left = [
            sum(
                dot(sides[at][:, 0:256], band_two[rows_of(2 * at + part, 0, 256), 0:256], 1, 1)
                for at in range(2)
            )
            for part in range(2)
        ]
        right = sum(
            dot(
                sides[at][:, 128:WIDE],
                jnp.concatenate(
                    [band_two[rows_of(2 * at + part, 256, WIDE), 128:WIDE] for part in range(2)],
                    axis=0,
                ),
                1,
                1,
            )
            for at in range(2)
        )
        dact = jnp.concatenate([left[0], right[:, 0:128], left[1], right[:, 128:256]], axis=1)
        dz = (dact * slope_one[low : low + rows]).astype(BF)
        for step in range(chunk):
            for part in range(2):
                at = (2 * (first + step) + part) * frames
                dz_one[at : at + frames] = dz[
                    step * frames : (step + 1) * frames, part * WIDE : (part + 1) * WIDE
                ]


def band_sums(term, outputs, width):
    per_tile = 128 // width
    lane = iota((width, 128), 1) // width
    sums = []
    for shift in range(2):
        total = None
        for spot in range(per_tile):
            part = None
            for position in range(outputs):
                tile, inside = divmod(position + shift, per_tile)
                if inside != spot:
                    continue
                one = term(position, tile)
                part = one if part is None else part + one
            if part is None:
                continue
            part = jnp.where(lane == spot, part, 0.0)
            total = part if total is None else total + part
        sums.append(fold(total, width))
    return sums


def kernel_grad(terms, outputs, width):
    tiles = []
    lane = iota((width, 128), 1) // width
    pieces = []
    for term in terms:
        pieces.extend(band_sums(term, outputs, width))
    per_tile = 128 // width
    for tile in range(2):
        total = jnp.zeros((width, 128), F32)
        for spot in range(per_tile):
            total = jnp.where(lane == spot, pieces[tile * per_tile + spot], total)
        tiles.append(total)
    return jnp.concatenate(tiles, axis=1)


def tiled(tile, count):
    return jnp.concatenate([tile] * count, axis=1)


def twice(row):
    return jnp.concatenate([row, row], axis=1)


def plan(states, mats_t, table, bias_col, options, legal, games, valid, rewards, returns, scale):
    frames = states.shape[1]
    pairs = OPTS // 2
    lanes = OPTS * frames
    trans_in, trans_out, value_in = mats_t
    low_half = iota((1, 128), 1) < frames
    upper = iota((1, 128), 1) // frames

    valid_f = [twice(v.astype(F32)) for v in valid]
    rewards = [twice(r) for r in rewards]
    returns = [twice(r) for r in returns]
    chosen = [twice(o) for o in options]
    game = twice(games)

    game_rows = iota((128, WIDE), 0) - HEAD_LANE
    game_pick = jnp.where(
        game_rows == tiled(game, 3) + GAMES * (iota((128, WIDE), 1) // 128), 1.0, 0.0
    )
    head_rows = dot(table, game_pick.astype(BF))
    hr, hd, hv = (head_rows[:, k * 128 : (k + 1) * 128] for k in range(3))

    option_rows = jnp.where(
        iota((128, lanes), 0) - EMB_LANE == iota((128, lanes), 1) // frames, 1.0, 0.0
    ).astype(BF)
    s_low = twice(states)
    s_f = s_low.astype(F32)
    base = dot(trans_in, s_low)
    pre = tiled(base, pairs) + dot(table, option_rows)
    sig_h = sigmoid(pre)
    hid = pre * sig_h
    hid_low = hid.astype(BF)
    after = tiled(s_f, pairs) + dot(trans_out, hid_low)
    after_low = after.astype(BF)
    judge_pre = dot(value_in, after_low) + bias_col
    sig_j = sigmoid(judge_pre)
    judged = judge_pre * sig_j

    def tile_of(value, k):
        return value[:, k * 128 : (k + 1) * 128]

    def over(value):
        return jnp.sum(value, axis=0, keepdims=True)

    reward = [over(tile_of(hid, k) * hr) for k in range(pairs)]
    gamma = [sigmoid(over(tile_of(hid, k) * hd)) for k in range(pairs)]
    value = [over(tile_of(judged, k) * hv) for k in range(pairs)]
    backed = [reward[k] + gamma[k] * value[k] for k in range(pairs)]
    allowed = [
        jnp.concatenate([legal[2 * k], legal[2 * k + 1]], axis=1) > 0 for k in range(pairs)
    ]
    highest = functools.reduce(
        jnp.maximum, [jnp.where(allowed[k], backed[k], -1e30) for k in range(pairs)]
    )
    highest = jnp.maximum(highest, turn(highest, frames))
    shares = [
        jnp.where(allowed[k], jnp.exp(jnp.where(allowed[k], backed[k] - highest, -60.0)), 0.0)
        for k in range(pairs)
    ]

    def halves(total):
        return total + turn(total, frames)

    share_sum = halves(sum(shares))
    planned = halves(sum(shares[k] * backed[k] for k in range(pairs))) / share_sum
    choose = [chosen[0] == 2 * k + upper for k in range(pairs)]

    def chosen_of(parts):
        return halves(sum(jnp.where(choose[k], parts[k], 0.0) for k in range(pairs)))

    roll_f = [chosen_of([tile_of(after, k) for k in range(pairs)])]
    roll_low = [roll_f[0].astype(BF)]
    plan_miss = planned - returns[0]
    reward_miss = [chosen_of(reward) - rewards[0]]
    value_miss = [chosen_of(value) - returns[1]]
    steps = len(options)
    picks, pre_k, sig_k, hid_k, hid_k_low, judge_k, sig_jk, judged_k = ([None] for _ in range(8))
    for k in range(1, steps):
        picks.append(jnp.where(iota((128, 128), 0) - EMB_LANE == chosen[k], 1.0, 0.0).astype(BF))
        pre_k.append(dot(trans_in, roll_low[k - 1]) + dot(table, picks[k]))
        sig_k.append(sigmoid(pre_k[k]))
        hid_k.append(pre_k[k] * sig_k[k])
        hid_k_low.append(hid_k[k].astype(BF))
        roll_f.append(roll_f[k - 1] + dot(trans_out, hid_k_low[k]))
        roll_low.append(roll_f[k].astype(BF))
        judge_k.append(dot(value_in, roll_low[k]) + bias_col)
        sig_jk.append(sigmoid(judge_k[k]))
        judged_k.append(judge_k[k] * sig_jk[k])
        reward_miss.append(over(hid_k[k] * hr) - rewards[k])
        value_miss.append(over(judged_k[k] * hv) - returns[k + 1])
    errors = valid_f[0] * plan_miss * plan_miss
    for k in range(steps):
        errors = errors + valid_f[k] * (
            reward_miss[k] * reward_miss[k] + value_miss[k] * value_miss[k]
        )
    errors = jnp.where(low_half, errors * scale, 0.0)

    half = jnp.where(low_half, 1.0, 0.0)
    double = 2.0 * scale
    d_plan = double * valid_f[0] * plan_miss / share_sum
    d_reward_k = [double * valid_f[k] * reward_miss[k] for k in range(steps)]
    d_value_k = [double * valid_f[k] * value_miss[k] for k in range(steps)]

    def through(matrix_t, grad):
        return dot(matrix_t, grad, 0, 0)

    d_roll = None
    d_judge_low, d_step_low, d_pre_low = ([None] * steps for _ in range(3))
    d_hr = jnp.zeros((D, 128), F32)
    d_hd = jnp.zeros((D, 128), F32)
    d_hv = jnp.zeros((D, 128), F32)
    for k in range(steps - 1, 0, -1):
        d_judge_low[k] = (d_value_k[k] * hv * slope(judged_k[k], sig_jk[k])).astype(BF)
        term = through(value_in, d_judge_low[k])
        d_roll = term if d_roll is None else d_roll + term
        d_step_low[k] = d_roll.astype(BF)
        d_hid = through(trans_out, d_step_low[k]) + d_reward_k[k] * hr
        d_pre_low[k] = (d_hid * slope(hid_k[k], sig_k[k])).astype(BF)
        d_roll = d_roll + through(trans_in, d_pre_low[k])
        d_hr = d_hr + (half * d_reward_k[k]) * hid_k[k]
        d_hv = d_hv + (half * d_value_k[k]) * judged_k[k]

    d_backed = [d_plan * shares[k] * (1.0 + backed[k] - planned) for k in range(pairs)]
    d_reward = [
        d_backed[k] + jnp.where(choose[k], d_reward_k[0], 0.0) for k in range(pairs)
    ]
    d_value = [
        d_backed[k] * gamma[k] + jnp.where(choose[k], d_value_k[0], 0.0) for k in range(pairs)
    ]
    d_gamma = [d_backed[k] * value[k] * gamma[k] * (1.0 - gamma[k]) for k in range(pairs)]
    d_judge = [
        (d_value[k] * hv * slope(tile_of(judged, k), tile_of(sig_j, k))).astype(BF)
        for k in range(pairs)
    ]
    d_judge_all = jnp.concatenate(d_judge, axis=1)
    d_after = through(value_in, d_judge_all)
    d_after = [
        tile_of(d_after, k) + jnp.where(choose[k], d_roll, 0.0) for k in range(pairs)
    ]
    d_after_low = jnp.concatenate([d.astype(BF) for d in d_after], axis=1)
    d_hid_all = through(trans_out, d_after_low)
    d_pre = [
        (
            (tile_of(d_hid_all, k) + d_reward[k] * hr + d_gamma[k] * hd)
            * slope(tile_of(hid, k), tile_of(sig_h, k))
        ).astype(BF)
        for k in range(pairs)
    ]
    d_pre_all = jnp.concatenate(d_pre, axis=1)
    d_base = through(trans_in, d_pre_all)
    d_state = halves(sum(d_after[k] + tile_of(d_base, k) for k in range(pairs)))
    for k in range(pairs):
        d_hr = d_hr + d_reward[k] * tile_of(hid, k)
        d_hd = d_hd + d_gamma[k] * tile_of(hid, k)
        d_hv = d_hv + d_value[k] * tile_of(judged, k)

    def both(parts):
        joined = [jnp.where(low_half, parts[k].astype(F32), parts[k + 1].astype(F32)) for k in range(1, steps, 2)]
        return [part.astype(BF) for part in joined]

    def with_steps(wide, parts):
        return jnp.concatenate([wide] + both(parts), axis=1)

    before_low = [None] + roll_low[:-1]
    d_pre_cat = with_steps(d_pre_all, d_pre_low)
    d_judge_cat = with_steps(d_judge_all, d_judge_low)
    grad_in = dot(d_pre_cat, with_steps(tiled(s_low, pairs), before_low), 1, 1)
    grad_out = dot(
        with_steps(d_after_low, d_step_low), with_steps(hid_low, hid_k_low), 1, 1
    )
    grad_value = dot(d_judge_cat, with_steps(after_low, roll_low), 1, 1)
    grad_table = dot(d_pre_cat, with_steps(option_rows, picks), 1, 1) + dot(
        jnp.concatenate([d_hr, d_hd, d_hv], axis=1), game_pick, 1, 1, precision=HIGH
    )
    grad_bias = jnp.sum(d_judge_cat.astype(F32), axis=1, keepdims=True)
    return (
        d_state[:, :frames],
        (grad_in, grad_out, grad_value),
        grad_table,
        grad_bias,
        errors,
    )


def frame_rows(section, refs):
    options_ref, legal_ref, games_ref, valid_ref, rewards_ref, returns_ref = refs

    def row(ref, k):
        return ref[k, pl.ds(section, 1), :]

    depth = options_ref.shape[0]
    return (
        [row(options_ref, k) for k in range(depth)],
        [row(legal_ref, k) for k in range(OPTS)],
        games_ref[pl.ds(section, 1), :],
        [row(valid_ref, k) for k in range(depth)],
        [row(rewards_ref, k) for k in range(depth)],
        [returns_ref[section, k : k + 1, :] for k in range(depth + 1)],
    )


def clear_tails(pixels):
    tail = jnp.zeros((pixels.shape[0], WIDE - 336), BF)
    for part in range(4):
        pixels[:, part * WIDE + 336 : (part + 1) * WIDE] = tail


def grad_kernel_two(act_one, dz_two, frames):
    rows = OUT2 * frames
    d_two = dz_two[frames : frames + rows]
    turned = d_two.T

    def term_of(tap):
        first, base = (tap // 2) * frames, (tap % 2) * WIDE
        blocks = []
        for low, high in ((0, 128), (128, OUT2 * C2)):
            blocks.append(
                dot(turned[low:high], act_one[first : first + rows, base + low : base + low + 256])
            )

        def term(position, tile):
            group = min(position // 4, 1)
            inside, lane = position - 4 * group, (tile - group) * 128
            return blocks[group][inside * C2 : (inside + 1) * C2, lane : lane + 128]

        return term

    grad = kernel_grad([term_of(tap) for tap in range(4)], OUT2, C2)
    return grad, fold(tiles_sum(dot(jnp.ones((8, rows), BF), d_two)), C2)


def grad_kernel_one(pixels, dz_one, frames):
    rows = OUT1 * frames
    d_one = dz_one[...]
    turned = d_one.T

    def term_of(tap):
        first = (tap // 4) * frames
        base = (tap % 4) * WIDE
        blocks = []
        for low, high in ((0, 128), (128, OUT1 * C1)):
            blocks.append(
                dot(turned[low:high], pixels[first : first + rows, base + low : base + low + 256])
            )

        def term(position, tile):
            group = min(position // 8, 1)
            inside, lane = position - 8 * group, (tile - group) * 128
            return blocks[group][inside * C1 : (inside + 1) * C1, lane : lane + 128]

        return term

    grad = kernel_grad([term_of(tap) for tap in range(8)], OUT1, C1)
    return grad, fold(tiles_sum(dot(jnp.ones((8, rows), BF), d_one)), C1)


def local_kernel(
    frames_hbm,
    kernels_ref,
    linear_ref,
    mats_ref,
    table_ref,
    bias_ref,
    options_ref,
    legal_ref,
    games_ref,
    valid_ref,
    rewards_ref,
    returns_ref,
    lin_out,
    mats_out,
    table_out,
    conv_out,
    small_out,
    frame_buf,
    pixels,
    band_one,
    band_two,
    slope_one,
    act_one,
    slope_two,
    act_two,
    dz_two,
    dz_one,
    sems,
):
    section = lax.axis_index("section")
    frames = frame_buf.shape[1]
    copies = load_frames(frames_hbm, section, frame_buf, sems, CHUNK)
    for copy in copies:
        copy.start()
    clear_bands(band_one, band_two)
    kernels = kernels_ref[...]
    build_one(kernels[0 : KERN // 2], band_one.at[0])
    build_one(kernels[KERN // 2 : KERN], band_one.at[1])
    for fill in build_two(kernels, band_two):
        fill()
    bias_one, bias_two, bias_three, bias_four = wide_biases(bias_ref[...])
    clear_tails(pixels)
    for which, copy in enumerate(copies):
        copy.wait()
        place_frames(frame_buf, pixels, which * CHUNK, CHUNK, frames)
    encode_one(pixels, band_one, 0, True, bias_one, slope_one, act_one, frames, 4)
    encode_one(pixels, band_one, 1, False, bias_one, slope_one, act_one, frames, 4)
    encode_two(act_one, band_two, bias_two, slope_two, act_two, frames, 3)
    linear_t = linear_ref[...]
    states = (dot(linear_t, act_two[...], 1, 1) + bias_three).astype(BF)
    d_state, grad_mats, grad_table, grad_bias, errors = plan(
        states,
        tuple(mats_ref[k] for k in range(3)),
        table_ref[...],
        bias_four,
        *frame_rows(
            section, (options_ref, legal_ref, games_ref, valid_ref, rewards_ref, returns_ref)
        ),
        1.0,
    )
    for k in range(3):
        mats_out[k] = grad_mats[k]
    table_out[...] = grad_table
    d_state_low = d_state.astype(BF)
    lin_out[...] = dot(d_state_low, act_two[...])
    back_two(d_state_low, linear_t, slope_two, dz_two, frames)
    grad_two, bias_two_grad = grad_kernel_two(act_one, dz_two, frames)
    back_one(dz_two, band_two, slope_one, dz_one, frames, 5)
    grad_one, bias_one_grad = grad_kernel_one(pixels, dz_one, frames)
    conv_out[...] = stack_kernels(grad_one, grad_two)
    lane = iota((8, 128), 1)
    line = iota((8, 128), 0)
    row_zero = jnp.where(
        lane < C1, bias_one_grad, jnp.where(lane < C1 + C2, turn(bias_two_grad, C1), 0.0)
    )
    count = sum(
        valid_ref[k, pl.ds(section, 1), :].astype(F32) for k in range(valid_ref.shape[0])
    )
    count = jnp.where(iota((1, 128), 1) < frames, twice(count), 0.0)
    small = jnp.where(line == 0, row_zero, 0.0)
    small = jnp.where(line == 1, row_of(lane_sum(d_state_low)), small)
    small = jnp.where(line == 2, row_of(grad_bias), small)
    small = jnp.where(line == 3, errors, small)
    small = jnp.where(line == 4, count, small)
    small_out[...] = small


def lane_sum(value):
    return jnp.sum(value.astype(F32), axis=1, keepdims=True)


def stack_kernels(grad_one, grad_two):
    rows = jnp.concatenate([grad_one, grad_two, jnp.zeros((128 - C1 - C2, KERN), F32)], axis=0)
    return rows.T


def tiles_sum(value):
    return sum(value[:, k * 128 : (k + 1) * 128] for k in range(value.shape[1] // 128))


VMEM_SPEC = pl.BlockSpec(memory_space=pltpu.VMEM)
ANY_SPEC = pl.BlockSpec(memory_space=pl.ANY)


def local_scratch(frames, side):
    return [
        pltpu.VMEM((side, frames, 336), BF),
        pltpu.VMEM(((OUT1 + 1) * frames, 4 * WIDE), BF),
        pltpu.VMEM((2, 4 * 256, 256), BF),
        pltpu.VMEM((4 * WIDE, WIDE), BF),
        pltpu.VMEM((OUT1 // 2 * frames, 2 * WIDE), F32),
        pltpu.VMEM((OUT1 // 2 * frames, 2 * WIDE), BF),
        pltpu.VMEM((OUT2 * frames, WIDE), F32),
        pltpu.VMEM((frames, FEAT), BF),
        pltpu.VMEM(((OUT2 + 2) * frames, WIDE), BF),
        pltpu.VMEM((OUT1 * frames, WIDE), BF),
        pltpu.SemaphoreType.DMA((side // CHUNK,)),
    ]


def local_step(frames, kernels, linear_t, mats_t, table, biases, options, legal, games, valid, rewards, returns):
    count = frames.shape[1]
    side = frames.shape[2]
    shapes = [(D, FEAT), (3, D, D), (D, 128), (KERN, 128), (8, 128)]
    return pl.pallas_call(
        local_kernel,
        out_shape=[jax.ShapeDtypeStruct(shape, F32) for shape in shapes],
        in_specs=[ANY_SPEC] + [VMEM_SPEC] * 11,
        out_specs=[VMEM_SPEC] * len(shapes),
        scratch_shapes=local_scratch(count, side),
        compiler_params=pltpu.CompilerParams(vmem_limit_bytes=56 * 1024 * 1024),
    )(
        frames.transpose(0, 2, 1, 3),
        kernels,
        linear_t,
        mats_t,
        table,
        biases.reshape(1, BIAS),
        options.transpose(2, 0, 1),
        legal.transpose(2, 0, 1),
        games,
        valid.transpose(2, 0, 1),
        rewards.transpose(2, 0, 1),
        returns.transpose(0, 2, 1),
    )


MESH = pl.DeviceIdType.MESH


QUARTER = 768
HALF = 2 * QUARTER
AT_EMB = FEAT
AT_HEADS = AT_EMB + OPTS
AT_MATS = LIN_PAD
TILES = HALF // 128
SCALE_LANE = C1 + C2
NEAR = 8
FOUR = 4


def fused_kernel(
    peers,
    frames_hbm,
    conv_hbm,
    lin_hbm,
    mats_hbm,
    emb_hbm,
    heads_hbm,
    bias_hbm,
    options_hbm,
    legal_hbm,
    games_hbm,
    valid_hbm,
    rewards_hbm,
    returns_hbm,
    main_out,
    conv_out,
    stats_out,
    frame_buf,
    pixels,
    band_one,
    band_two,
    slope_one,
    act_one,
    slope_two,
    act_two,
    dz_two,
    dz_one,
    frame_sems,
    stage,
    kernel_msg,
    weight_msg,
    weights,
    grad_own,
    mate_in,
    grad_msg,
    near_in,
    cross_in,
    cross_msg,
    far_in,
    taps_msg,
    row_in,
    rows_in,
    taps_turned,
    stats_in,
    final,
    stats_base,
    half_in,
    send_sems,
    recv_sems,
    mate_send,
    mate_recv,
    conv_ref,
    lin_ref,
    mats_ref,
    emb_ref,
    heads_ref,
    bias_ref,
    options_ref,
    legal_ref,
    games_ref,
    valid_ref,
    rewards_ref,
    returns_ref,
    operand_sems,
):
    section = lax.axis_index("section")
    place = lax.axis_index("dp")
    mate = 1 - section
    frames = frame_buf.shape[1]

    barrier = pltpu.get_barrier_semaphore()

    def greet(step, carry):
        peer = lax.rem(place + step, peers)
        pl.semaphore_signal(barrier, inc=1, device_id=(section, peer), device_id_type=MESH)
        return carry

    def greet_row(step, carry):
        peer = place - lax.rem(place, FOUR) + lax.rem(place + step, FOUR)
        pl.semaphore_signal(barrier, inc=1, device_id=(mate, peer), device_id_type=MESH)
        return carry

    lax.fori_loop(1, peers, greet, 0)
    lax.fori_loop(0, FOUR, greet_row, 0)
    loads = [
        pltpu.make_async_copy(source, target, operand_sems.at[which])
        for which, (source, target) in enumerate(
            (
                (conv_hbm, conv_ref),
                (lin_hbm, lin_ref),
                (mats_hbm, mats_ref),
                (emb_hbm, emb_ref),
                (heads_hbm, heads_ref),
                (bias_hbm, bias_ref),
                (options_hbm, options_ref),
                (legal_hbm, legal_ref),
                (games_hbm, games_ref),
                (valid_hbm, valid_ref),
                (rewards_hbm, rewards_ref),
                (returns_hbm, returns_ref),
            )
        )
    ]
    for load in loads:
        load.start()
    copies = load_frames(frames_hbm, section, frame_buf, frame_sems, CHUNK)
    wait_frames = lambda: [copy.wait() for copy in copies]
    for copy in copies:
        copy.start()

    sends = []

    side, spot = place // NEAR, lax.rem(place, NEAR)
    row, column = spot // FOUR, lax.rem(spot, FOUR)

    def near(step):
        return side * NEAR + lax.rem(spot + step, NEAR)

    def beyond(step):
        return (1 - side) * NEAR + lax.rem(spot + step, NEAR)

    def beside(step):
        return place - column + lax.rem(column + step, FOUR)

    def across(step, where):
        return (1 - side) * NEAR + lax.rem(row + step, 2) * FOUR + where

    def send(sems, peer, source, target, core=section):
        pltpu.make_async_remote_copy(
            src_ref=source,
            dst_ref=target,
            send_sem=send_sems.at[sems],
            recv_sem=recv_sems.at[sems],
            device_id=(core, peer),
            device_id_type=MESH,
        ).start()

    def loop(low, high, act):
        def body(step, carry):
            act(step)
            return carry

        lax.fori_loop(low, high, body, 0)

    def settle(sems, blocks):
        whole = pltpu.make_async_remote_copy(
            src_ref=blocks,
            dst_ref=blocks,
            send_sem=send_sems.at[sems],
            recv_sem=recv_sems.at[sems],
            device_id=(mate, place),
            device_id_type=MESH,
        )
        sends.append(whole.wait_send)
        return whole.wait_recv

    def send_peers(sems, source, target):
        loop(0, NEAR, lambda step: send(sems, beyond(step), source, target.at[place]))
        loop(1, NEAR, lambda step: send(sems, near(step), source, target.at[place]))
        return settle(sems, target.at[pl.ds(0, peers - 1)])

    def send_mate(which, source, target, landing):
        def copy(into):
            return pltpu.make_async_remote_copy(
                src_ref=source,
                dst_ref=into,
                send_sem=mate_send.at[which],
                recv_sem=mate_recv.at[which],
                device_id=(mate, place),
                device_id_type=MESH,
            )

        copy(target).start()
        sends.append(lambda: copy(target).wait_send())
        return lambda: copy(landing).wait_recv()

    for load in loads:
        load.wait()
    upper_lanes = iota((16, 128), 1) >= 64
    counts = sum(
        valid_ref[k, m : m + 1, :].astype(F32)
        for k in range(valid_ref.shape[0])
        for m in range(valid_ref.shape[1])
    )
    conv_pad = jnp.concatenate([conv_ref[...], jnp.zeros((16, 80), F32)], axis=1)
    kernel_msg[place] = jnp.where(
        upper_lanes & (iota((16, 128), 0) == 0), jnp.broadcast_to(twice(counts), (16, 128)), conv_pad
    ).astype(BF)
    heads_pad = jnp.concatenate([heads_ref[...], jnp.zeros((24, 120), F32)], axis=1)
    heads_pad = jnp.concatenate([heads_pad, jnp.zeros((104, 128), F32)], axis=0).T
    last = FEAT - EMB_LANE
    stage[:, 0:last] = lin_ref[:, 0:last]
    stage[:, last:LIN_PAD] = jnp.concatenate(
        [
            lin_ref[:, last:FEAT],
            emb_ref[...],
            heads_pad[0:8, 0 : 3 * GAMES],
            jnp.zeros((8, 128 - HEAD_LANE - 3 * GAMES), F32),
        ],
        axis=1,
    )
    for k in range(3):
        stage[:, AT_MATS + k * D : AT_MATS + (k + 1) * D] = mats_ref[k]
    first = stage[:, pl.ds(pl.multiple_of(section * HALF, 128), QUARTER)]
    second = stage[:, pl.ds(pl.multiple_of(section * HALF + QUARTER, 128), QUARTER)]
    weight_msg[section, place] = jnp.concatenate([first, second], axis=0).astype(BF)

    def square_sum(value):
        return jnp.sum(jnp.sum(value * value, axis=0, keepdims=True), axis=1, keepdims=True)

    weight_squares = [
        square_sum(conv_pad),
        square_sum(lin_ref[...]),
        square_sum(mats_ref[...].reshape(24, D)),
        square_sum(emb_ref[...]),
        square_sum(heads_ref[...]),
    ]
    stat_line = iota((16, 128), 0)
    stat = jnp.zeros((16, 128), F32)
    for which, value in enumerate(weight_squares):
        at = iota((16, 128), 1) - SCALE_LANE
        rough = value.astype(BF).astype(F32)
        mixed = stat_line == TILES + 2
        stat = jnp.where(mixed & (at == which), rough, stat)
        stat = jnp.where(mixed & (at == which + 5), value - rough, stat)
    stats_base[...] = stat
    pl.semaphore_wait(barrier, peers - 1 + FOUR)
    half_msg = weight_msg.at[section]

    def spread_own(sems, blocks):
        own = blocks.at[place]
        loop(0, 2, lambda step: send(sems, across(step, column), own, own))
        wait_across = settle(sems, blocks.at[pl.ds(0, 2)])
        loop(1, NEAR, lambda step: send(sems + 1, near(step), own, own))
        return wait_across, settle(sems + 1, blocks.at[pl.ds(0, NEAR - 1)])

    def pass_on(sems, blocks):
        for which in range(2):
            block = blocks.at[across(which, column)]
            loop(1, FOUR, lambda step: send(sems, beside(step), block, block))
        return settle(sems, blocks.at[pl.ds(0, 2 * (FOUR - 1))])

    wait_kernel_across, wait_kernel_near = spread_own(0, kernel_msg)
    wait_across, wait_near = spread_own(3, half_msg)

    clear_bands(band_one, band_two)
    bias_one, bias_two, bias_three, bias_four = wide_biases(bias_ref[...].reshape(1, BIAS))
    clear_tails(pixels)
    act_two[:, FEAT:LIN_PAD] = jnp.zeros((frames, LIN_PAD - FEAT), BF)
    for which, copy in enumerate(copies):
        copy.wait()
        place_frames(frame_buf, pixels, which * CHUNK, CHUNK, frames)
    wait_kernel_across()
    wait_kernel_beside = pass_on(2, kernel_msg)
    wait_kernel_near()

    def side_kernels(which):
        return kernel_msg[pl.ds(which * NEAR, NEAR)].reshape(KERN // 2, 128)

    build_one(side_kernels(side), band_one.at[side])
    wait_across()
    wait_beside = pass_on(5, half_msg)
    encode_one(pixels, band_one, side, True, bias_one, slope_one, act_one, frames, 4)
    wait_kernel_beside()
    build_one(side_kernels(1 - side), band_one.at[1 - side])
    kernels = kernel_msg[...].reshape(KERN, 128)
    fills = build_two(kernels, band_two)
    counted = jnp.where(iota((KERN, 128), 1) >= 64, kernels.astype(F32), 0.0)
    count = jnp.sum(jnp.sum(counted, axis=0, keepdims=True), axis=1, keepdims=True)
    scale = 1.0 / count
    encode_one(pixels, band_one, 1 - side, False, bias_one, slope_one, act_one, frames, 4, fills)
    wait_near()
    own_side, far_side = pl.ds(side * NEAR, NEAR), pl.ds((1 - side) * NEAR, NEAR)
    wait_own_side = send_mate(
        0, half_msg.at[own_side], half_msg.at[own_side], weight_msg.at[mate, own_side]
    )
    wait_beside()
    wait_far_side = send_mate(
        5, half_msg.at[far_side], half_msg.at[far_side], weight_msg.at[mate, far_side]
    )
    encode_two(act_one, band_two, bias_two, slope_two, act_two, frames, 3)
    wait_own_side()
    wait_far_side()
    for half in range(2):
        block = weight_msg[half].astype(F32)
        for part in range(2):
            lane = (2 * half + part) * QUARTER
            weights[:, lane : lane + QUARTER] = (
                block[:, part * 8 : (part + 1) * 8].reshape(D, QUARTER).astype(BF)
            )
    linear_t = weights[:, 0:LIN_PAD]
    states = (dot(linear_t, act_two[...], 1, 1) + bias_three).astype(BF)
    d_state, grad_mats, grad_table, grad_bias, errors = plan(
        states,
        tuple(weights[:, AT_MATS + k * D : AT_MATS + (k + 1) * D] for k in range(3)),
        weights[:, LIN_PAD - 128 : LIN_PAD],
        bias_four,
        *frame_rows(
            section, (options_ref, legal_ref, games_ref, valid_ref, rewards_ref, returns_ref)
        ),
        scale,
    )

    d_state_low = d_state.astype(BF)
    grad_linear = dot(d_state_low, act_two[...])
    parts = [grad_linear[:, at * QUARTER : (at + 1) * QUARTER] for at in range(3)]
    parts.append(
        jnp.concatenate(
            [
                grad_linear[:, 3 * QUARTER : LIN_PAD - 128],
                grad_linear[:, LIN_PAD - 128 : LIN_PAD] + grad_table,
                *grad_mats,
            ],
            axis=1,
        )
    )
    parts = [part.reshape(peers, 8, QUARTER) for part in parts]
    for half in range(2):
        grad_own[half] = jnp.concatenate(parts[2 * half : 2 * half + 2], axis=1).astype(BF)
    wait_mate = send_mate(1, grad_own.at[mate], mate_in, mate_in)
    back_two(d_state_low, linear_t, slope_two, dz_two, frames)
    wait_mate()
    grad_msg[...] = (grad_own[section].astype(F32) + mate_in[...].astype(F32)).astype(BF)
    twin = beyond(0)

    def collect(step):
        peer = near(step)
        send(6, peer, grad_msg.at[lax.rem(peer + NEAR, peers)], cross_in.at[spot])

    loop(1, NEAR, collect)
    cross_in[spot] = grad_msg[twin]
    wait_cross = settle(6, cross_in.at[pl.ds(0, NEAR - 1)])
    loop(1, NEAR, lambda step: send(7, near(step), grad_msg.at[near(step)], near_in.at[spot]))
    wait_grads = settle(7, near_in.at[pl.ds(0, NEAR - 1)])
    near_in[spot] = grad_msg[place]
    row_three = row_of(lane_sum(d_state_low))
    row_four = row_of(grad_bias)
    grad_two, bias_two_grad = grad_kernel_two(act_one, dz_two, frames)
    back_one(dz_two, band_two, slope_one, dz_one, frames, 5)
    grad_one, bias_one_grad = grad_kernel_one(pixels, dz_one, frames)

    kernel_grads = jnp.concatenate([grad_one, grad_two], axis=0).astype(BF)
    for half in range(2):
        taps_msg[half] = kernel_grads[:, half * 128 : (half + 1) * 128]
    own = section * FOUR + column
    loop(1, FOUR, lambda step: send(9, beside(step), taps_msg.at[section], row_in.at[own]))
    loop(0, FOUR, lambda step: send(9, beside(step), taps_msg.at[mate], row_in.at[own], mate))
    wait_row = settle(9, row_in.at[pl.ds(0, 2 * FOUR - 1)])
    row_in[own] = taps_msg[section]
    wait_cross()
    cross_msg[...] = jnp.sum(cross_in[...].astype(F32), axis=0).astype(BF)
    send(8, twin, cross_msg, far_in)
    wait_far = settle(8, far_in)
    wait_row()
    level = place // FOUR
    rows_in[level] = jnp.sum(row_in[...].astype(F32), axis=0).astype(BF)
    loop(
        1,
        peers // FOUR,
        lambda step: send(
            11, lax.rem(place + step * FOUR, peers), rows_in.at[level], rows_in.at[level]
        ),
    )
    wait_rows = settle(11, rows_in.at[pl.ds(0, peers // FOUR - 1)])
    wait_grads()
    wait_far()
    total = jnp.sum(near_in[...].astype(F32), axis=0) + far_in[...].astype(F32)
    squares = total * total
    stat = stats_base[...]
    for part in range(2):
        sums = jnp.sum(squares[part * 8 : (part + 1) * 8], axis=0, keepdims=True)
        for tile in range(TILES // 2):
            stat = jnp.where(
                stat_line == part * (TILES // 2) + tile, sums[:, tile * 128 : (tile + 1) * 128], stat
            )
    lane = iota((1, 128), 1)
    row_first = jnp.where(
        lane < C1, bias_one_grad[0:1], jnp.where(lane < C1 + C2, turn(bias_two_grad, C1)[0:1], 0.0)
    )
    row_first = row_first + turn(errors, 64)
    stat = jnp.where(stat_line == TILES, row_three, stat)
    stat = jnp.where(stat_line == TILES + 1, row_four, stat)
    stat = stat + jnp.where(stat_line == TILES + 2, row_first, 0.0)
    stats_in[place] = stat.astype(BF)
    wait_stats = send_peers(10, stats_in.at[place], stats_in)
    half_in[section, :, 0:QUARTER] = total[0:8]
    half_in[section, :, QUARTER:HALF] = total[8:16]
    wait_half_grads = send_mate(3, half_in.at[section], half_in.at[section], half_in.at[mate])
    wait_rows()
    taps = jnp.sum(rows_in[...].astype(F32), axis=0)
    taps = jnp.concatenate([taps, jnp.zeros((128 - C1 - C2, 128), F32)], axis=0)
    taps_turned[...] = taps.T
    final[section, 16:32] = taps_turned[pl.ds(pl.multiple_of(spot * 16, 16), 16)]
    final[section, 32:40] = jnp.broadcast_to(
        jnp.sum(taps * taps, axis=0, keepdims=True), (8, 128)
    )
    wait_half_grads()
    for half in range(2):
        main_out[:, half * HALF : (half + 1) * HALF] = half_in[half]
    wait_stats()
    final[section, 0:16] = jnp.sum(stats_in[...].astype(F32), axis=0)
    wait_final = send_mate(4, final.at[section], final.at[section], final.at[mate])
    wait_final()
    conv_out[...] = final[side, 16:32]
    stats_out[...] = final[...]

    for wait in sends:
        wait()


def fused_step(peers, frames, shards, biases, rows):
    count = frames.shape[1]
    side = frames.shape[2]
    scratch = local_scratch(count, side)
    scratch[7] = pltpu.VMEM((count, LIN_PAD), BF)
    scratch += [
        pltpu.VMEM((8, 2 * HALF), F32),
        pltpu.VMEM((peers, 16, 128), BF),
        pltpu.VMEM((2, peers, 16, QUARTER), BF),
        pltpu.VMEM((D, 2 * HALF), BF),
        pltpu.VMEM((2, peers, 16, QUARTER), BF),
        pltpu.VMEM((peers, 16, QUARTER), BF),
        pltpu.VMEM((peers, 16, QUARTER), BF),
        pltpu.VMEM((NEAR, 16, QUARTER), BF),
        pltpu.VMEM((NEAR, 16, QUARTER), BF),
        pltpu.VMEM((16, QUARTER), BF),
        pltpu.VMEM((16, QUARTER), BF),
        pltpu.VMEM((2, C1 + C2, 128), BF),
        pltpu.VMEM((2 * FOUR, C1 + C2, 128), BF),
        pltpu.VMEM((peers // FOUR, C1 + C2, 128), BF),
        pltpu.VMEM((128, 128), F32),
        pltpu.VMEM((peers, 16, 128), BF),
        pltpu.VMEM((2, 40, 128), F32),
        pltpu.VMEM((16, 128), F32),
        pltpu.VMEM((2, 8, HALF), F32),
        pltpu.SemaphoreType.DMA((12,)),
        pltpu.SemaphoreType.DMA((12,)),
        pltpu.SemaphoreType.DMA((6,)),
        pltpu.SemaphoreType.DMA((6,)),
    ]
    shapes = [(8, 2 * HALF), (16, 128), (2, 40, 128)]
    operands = [frames.transpose(0, 2, 1, 3), *shards, biases, *rows]
    scratch += [pltpu.VMEM(operand.shape, operand.dtype) for operand in operands[1:]]
    scratch += [pltpu.SemaphoreType.DMA((len(operands) - 1,))]
    return pl.pallas_call(
        functools.partial(fused_kernel, peers),
        out_shape=[jax.ShapeDtypeStruct(shape, F32) for shape in shapes],
        in_specs=[ANY_SPEC] * len(operands),
        out_specs=[VMEM_SPEC] * len(shapes),
        scratch_shapes=scratch,
        compiler_params=pltpu.CompilerParams(
            vmem_limit_bytes=56 * 1024 * 1024, collective_id=0, has_side_effects=True
        ),
    )(*operands)


def column_of(row):
    square = jnp.broadcast_to(row, (8, 8))
    return jnp.sum(jnp.where(iota((8, 8), 0) == iota((8, 8), 1), square, 0.0), axis=1, keepdims=True)


def row_back(column):
    square = jnp.broadcast_to(column, (8, 8))
    return jnp.sum(jnp.where(iota((8, 8), 0) == iota((8, 8), 1), square, 0.0), axis=0, keepdims=True)


def total_of(value):
    return jnp.sum(jnp.sum(value, axis=0, keepdims=True), axis=1, keepdims=True)


def update_kernel(
    main_ref,
    convg_ref,
    stats_ref,
    conv_ref,
    lin_ref,
    mats_ref,
    emb_ref,
    heads_ref,
    bias_ref,
    conv_moment,
    lin_rows,
    lin_cols,
    mats_rows,
    mats_cols,
    emb_moment,
    head_moment,
    bias_moment,
    conv_new,
    conv_grad,
    conv_moment_new,
    lin_new,
    lin_grad,
    lin_rows_new,
    lin_cols_new,
    mats_new,
    mats_grad,
    mats_rows_new,
    mats_cols_new,
    emb_new,
    emb_grad,
    emb_moment_new,
    heads_new,
    heads_grad,
    head_moment_new,
    bias_new,
    bias_grad,
    bias_moment_new,
    norm_out,
    loss_out,
    conv_low,
    lin_low,
):
    stats = stats_ref[...]
    both = stats[0] + stats[1]
    squares = total_of(both[0:TILES]) + total_of(both[32:33])
    scales = stats[0, TILES + 2 : TILES + 3]
    scales = [
        scales[:, SCALE_LANE + k : SCALE_LANE + k + 1]
        + scales[:, SCALE_LANE + k + 5 : SCALE_LANE + k + 6]
        for k in range(5)
    ]
    bias_raw = jnp.concatenate(
        [both[TILES + 2 : TILES + 3, 0 : C1 + C2], both[TILES : TILES + 1], both[TILES + 1 : TILES + 2]],
        axis=1,
    )
    norm = jnp.sqrt(squares + total_of(bias_raw * bias_raw))
    factor = jnp.minimum(1.0, CLIP_LIMIT / norm)
    norm_out[...] = norm
    loss_out[...] = total_of(both[TILES + 2 : TILES + 3, 64:128])

    def simple(weight, grad, moment, square_total, outs):
        new, moment_new = unfactored(
            weight, grad, moment, relative(square_total, weight.size * outs[3])
        )
        for out, value in zip(outs, (new, grad, moment_new)):
            out[...] = value.reshape(out.shape)
        return new

    peers = D // lin_ref.shape[0]
    conv = simple(
        conv_ref[...],
        factor * convg_ref[:, 0 : C1 + C2],
        conv_moment[...],
        scales[0],
        (conv_new, conv_grad, conv_moment_new, peers),
    )
    conv_low[...] = conv.astype(BF)
    simple(
        emb_ref[...],
        factor * main_ref[:, AT_EMB:AT_HEADS],
        emb_moment[...],
        scales[3],
        (emb_new, emb_grad, emb_moment_new, peers),
    )
    heads_t = jnp.concatenate(
        [main_ref[:, LIN_PAD - 128 : LIN_PAD], jnp.zeros((120, 128), F32)], axis=0
    ).T
    simple(
        heads_ref[...],
        factor * heads_t[HEAD_LANE : HEAD_LANE + 3 * GAMES, 0:8],
        head_moment[...],
        scales[4],
        (heads_new, heads_grad, head_moment_new, peers),
    )
    bias = bias_ref[...].reshape(1, BIAS)
    simple(
        bias,
        factor * bias_raw,
        bias_moment[...].reshape(1, BIAS),
        total_of(bias * bias),
        (bias_new, bias_grad, bias_moment_new, 1),
    )
    row_sums = [stats[t // TILES, t % TILES : t % TILES + 1] for t in range(24)]

    def factored(weight, grad, rows_old, cols_old, row_sum, square_total, entries):
        rows = DECAY_RATE * rows_old + (1.0 - DECAY_RATE) * (
            factor * factor * row_sum / D + FLOOR_ONE
        )
        wide = grad.shape[1]
        cols = DECAY_RATE * cols_old + (1.0 - DECAY_RATE) * (
            jnp.sum(grad * grad + FLOOR_ONE, axis=1, keepdims=True) / wide
        )
        mean = jnp.sum(rows, axis=1, keepdims=True) / wide
        second = rows * cols / mean
        new = weight - STEP_RATE * relative(square_total, entries) * grad * lax.rsqrt(second)
        return new, rows, cols

    grad = factor * main_ref[:, 0:FEAT]
    new, rows, cols = factored(
        lin_ref[...],
        grad,
        lin_rows[...].reshape(1, FEAT),
        column_of(lin_cols[...]),
        jnp.concatenate(row_sums[:21], axis=1)[:, 0:FEAT],
        scales[1],
        FEAT * D,
    )
    lin_new[...] = new
    lin_grad[...] = grad
    lin_rows_new[...] = rows.reshape(FEAT)
    lin_cols_new[...] = row_back(cols)
    lin_low[...] = new.astype(BF)
    for k in range(3):
        grad = factor * main_ref[:, AT_MATS + k * D : AT_MATS + (k + 1) * D]
        new, rows, cols = factored(
            mats_ref[k],
            grad,
            mats_rows[k : k + 1],
            column_of(mats_cols[k : k + 1]),
            row_sums[21 + k],
            scales[2],
            3 * D * D,
        )
        mats_new[k] = new
        mats_grad[k] = grad
        mats_rows_new[k : k + 1] = rows
        mats_cols_new[k : k + 1] = row_back(cols)


def fused_device(
    frames,
    options,
    legal,
    games,
    valid,
    rewards,
    returns,
    conv_kernels,
    enc_linear,
    plan_mats,
    option_emb,
    heads,
    biases,
    conv_moment,
    lin_rows,
    lin_cols,
    mats_rows,
    mats_cols,
    emb_moment,
    head_moment,
    bias_moment,
):
    width = enc_linear.shape[1]
    peers = D // width
    shards = (
        conv_kernels,
        enc_linear.T,
        plan_mats.transpose(0, 2, 1),
        option_emb.T,
        heads.reshape(3 * GAMES, width),
    )
    summed = fused_step(
        peers,
        frames,
        shards,
        biases,
        (
            options.transpose(2, 0, 1),
            legal.transpose(2, 0, 1),
            games,
            valid.transpose(2, 0, 1),
            rewards.transpose(2, 0, 1),
            returns.transpose(0, 2, 1),
        ),
    )
    shapes = [(16, 48)] * 3 + [(8, FEAT)] * 2 + [(FEAT,), (1, 8)] + [(3, 8, D)] * 2 + [(3, D), (3, 8)]
    shapes += [(8, OPTS)] * 3 + [(24, 8)] * 3 + [(BIAS,)] * 3 + [(1, 1)] * 2
    outs = [jax.ShapeDtypeStruct(shape, F32) for shape in shapes]
    outs += [jax.ShapeDtypeStruct((16, 48), BF), jax.ShapeDtypeStruct((8, FEAT), BF)]
    operands = [
        *summed,
        *shards,
        biases,
        conv_moment,
        lin_rows,
        lin_cols.reshape(1, width),
        mats_rows,
        mats_cols,
        emb_moment.T,
        head_moment.reshape(3 * GAMES, width),
        bias_moment,
    ]
    o = pl.pallas_call(
        update_kernel,
        out_shape=outs,
        in_specs=[VMEM_SPEC] * len(operands),
        out_specs=[VMEM_SPEC] * len(outs),
    )(*operands)
    flat_heads = [h.reshape(3, GAMES, width) for h in o[14:17]]
    return (
        *o[0:3],
        o[3].T,
        o[4].T,
        o[5],
        o[6].reshape(width),
        o[7].transpose(0, 2, 1),
        o[8].transpose(0, 2, 1),
        o[9],
        o[10],
        o[11].T,
        o[12].T,
        o[13].T,
        *flat_heads,
        *o[17:20],
        o[20].reshape(()),
        o[21].reshape(()),
        o[22],
        o[23].T,
    )


def gather_rows(shard):
    return lax.all_gather(shard, "dp", axis=0, tiled=True)


def relative(square_total, entries):
    return jnp.maximum(FLOOR_TWO, jnp.sqrt(square_total / entries))


def unfactored(weight, grad, moment, scale):
    moment_new = DECAY_RATE * moment + (1.0 - DECAY_RATE) * (grad * grad + FLOOR_ONE)
    return (weight - STEP_RATE * scale * grad * lax.rsqrt(moment_new), moment_new)


def per_device(
    frames,
    options,
    legal,
    games,
    valid,
    rewards,
    returns,
    conv_kernels,
    enc_linear,
    plan_mats,
    option_emb,
    heads,
    biases,
    conv_moment,
    lin_rows,
    lin_cols,
    mats_rows,
    mats_cols,
    emb_moment,
    head_moment,
    bias_moment,
):
    weight_squares = lax.psum(
        (
            jnp.sum(conv_kernels * conv_kernels),
            jnp.sum(enc_linear * enc_linear),
            jnp.sum(plan_mats * plan_mats),
            jnp.sum(option_emb * option_emb),
            jnp.sum(heads * heads),
        ),
        "dp",
    )
    width = enc_linear.shape[1]
    kernels = gather_rows(conv_kernels.astype(BF))
    linear_t = gather_rows(enc_linear.astype(BF).T)
    mats_t = gather_rows(plan_mats.astype(BF).transpose(2, 0, 1)).transpose(1, 0, 2)
    emb_t = gather_rows(option_emb.astype(BF).T)
    heads_t = gather_rows(heads.astype(BF).reshape(3 * GAMES, width).T)
    table = jnp.pad(
        jnp.concatenate([emb_t, heads_t], axis=1),
        ((0, 0), (EMB_LANE, 128 - HEAD_LANE - 3 * GAMES)),
    )
    lin, mats, table_grad, conv, small = local_step(
        frames,
        kernels,
        linear_t,
        mats_t,
        table,
        biases,
        options,
        legal,
        games,
        valid,
        rewards,
        returns,
    )
    rows = jnp.concatenate(
        [lin, mats[0], mats[1], mats[2], table_grad[:, EMB_LANE : HEAD_LANE + 3 * GAMES]], axis=1
    )
    rows = lax.psum(lax.psum_scatter(rows, "dp", scatter_dimension=0, tiled=True), "section")
    conv = lax.psum(
        lax.psum_scatter(conv[:, : C1 + C2], "dp", scatter_dimension=0, tiled=True), "section"
    )
    small = lax.psum(small, ("section", "dp"))
    inverse_count = 1.0 / jnp.sum(small[4])
    loss_value = jnp.sum(small[3]) * inverse_count
    bias_raw = (
        jnp.concatenate([small[0, : C1 + C2], small[1], small[2]]) * inverse_count
    )
    rows = rows * inverse_count
    g_conv = conv * inverse_count
    g_lin = rows[:, :FEAT].T
    g_mats = rows[:, FEAT : FEAT + 3 * D].reshape(width, 3, D).transpose(1, 2, 0)
    g_emb = rows[:, FEAT + 3 * D : FEAT + 3 * D + OPTS].T
    g_heads = rows[:, FEAT + 3 * D + OPTS :].T.reshape(3, GAMES, width)
    partial_squares = (
        jnp.sum(g_conv * g_conv)
        + jnp.sum(g_lin * g_lin)
        + jnp.sum(g_mats * g_mats)
        + jnp.sum(g_emb * g_emb)
        + jnp.sum(g_heads * g_heads)
    )
    reduced = lax.psum(
        (partial_squares, jnp.sum(g_lin * g_lin, axis=1), jnp.sum(g_mats * g_mats, axis=2)), "dp"
    )
    grad_norm = jnp.sqrt(reduced[0] + jnp.sum(bias_raw * bias_raw))
    factor = jnp.minimum(1.0, CLIP_LIMIT / grad_norm)
    conv_grad = factor * g_conv
    lin_grad = factor * g_lin
    mats_grad = factor * g_mats
    emb_grad = factor * g_emb
    heads_grad = factor * g_heads
    bias_grad = factor * bias_raw
    conv_new, conv_moment_new = unfactored(
        conv_kernels, conv_grad, conv_moment, relative(weight_squares[0], KERN * (C1 + C2))
    )
    emb_new, emb_moment_new = unfactored(
        option_emb, emb_grad, emb_moment, relative(weight_squares[3], OPTS * D)
    )
    heads_new, head_moment_new = unfactored(
        heads, heads_grad, head_moment, relative(weight_squares[4], 3 * GAMES * D)
    )
    bias_new, bias_moment_new = unfactored(
        biases, bias_grad, bias_moment, relative(jnp.sum(biases * biases), BIAS)
    )
    lin_rows_new = DECAY_RATE * lin_rows + (1.0 - DECAY_RATE) * (
        factor * factor * reduced[1] / D + FLOOR_ONE
    )
    lin_cols_new = DECAY_RATE * lin_cols + (1.0 - DECAY_RATE) * jnp.mean(
        lin_grad * lin_grad + FLOOR_ONE, axis=0
    )
    lin_second = lin_rows_new[:, None] * lin_cols_new[None, :] / jnp.mean(lin_rows_new)
    lin_new = enc_linear - STEP_RATE * relative(weight_squares[1], FEAT * D) * lin_grad * lax.rsqrt(
        lin_second
    )
    mats_rows_new = DECAY_RATE * mats_rows + (1.0 - DECAY_RATE) * (
        factor * factor * reduced[2] / D + FLOOR_ONE
    )
    mats_cols_new = DECAY_RATE * mats_cols + (1.0 - DECAY_RATE) * jnp.mean(
        mats_grad * mats_grad + FLOOR_ONE, axis=1
    )
    mats_second = (
        mats_rows_new[:, :, None]
        * mats_cols_new[:, None, :]
        / jnp.mean(mats_rows_new, axis=1)[:, None, None]
    )
    mats_new = plan_mats - STEP_RATE * relative(weight_squares[2], 3 * D * D) * mats_grad * lax.rsqrt(
        mats_second
    )
    return (
        conv_new,
        conv_grad,
        conv_moment_new,
        lin_new,
        lin_grad,
        lin_rows_new,
        lin_cols_new,
        mats_new,
        mats_grad,
        mats_rows_new,
        mats_cols_new,
        emb_new,
        emb_grad,
        emb_moment_new,
        heads_new,
        heads_grad,
        head_moment_new,
        bias_new,
        bias_grad,
        bias_moment_new,
        grad_norm,
        loss_value,
        conv_new.astype(BF),
        lin_new.astype(BF),
    )


def solution(mesh):
    return jax.shard_map(
        fused_device if mesh.shape["dp"] * 8 == D else per_device,
        mesh=mesh,
        in_specs=(
            P(None, "dp", None, None),
            P(None, "dp", None),
            P(None, "dp", None),
            P(None, "dp"),
            P(None, "dp", None),
            P(None, "dp", None),
            P(None, "dp", None),
            P("dp", None),
            P(None, "dp"),
            P(None, None, "dp"),
            P(None, "dp"),
            P(None, None, "dp"),
            P(),
            P("dp", None),
            P(),
            P("dp"),
            P(),
            P(None, "dp"),
            P(None, "dp"),
            P(None, None, "dp"),
            P(),
        ),
        out_specs=(
            P("dp", None),
            P("dp", None),
            P("dp", None),
            P(None, "dp"),
            P(None, "dp"),
            P(),
            P("dp"),
            P(None, None, "dp"),
            P(None, None, "dp"),
            P(),
            P(None, "dp"),
            P(None, "dp"),
            P(None, "dp"),
            P(None, "dp"),
            P(None, None, "dp"),
            P(None, None, "dp"),
            P(None, None, "dp"),
            P(),
            P(),
            P(),
            P(),
            P(),
            P("dp", None),
            P(None, "dp"),
        ),
        check_vma=False,
    )
```

```python
import functools

import jax
import jax.numpy as jnp
from jax import lax
from jax.experimental import pallas as pl
from jax.experimental.pallas import tpu as pltpu
from jax.sharding import PartitionSpec as P

D = 128
C1 = 16
C2 = 32
OPTS = 18
KERN = 256
GAMES = 8
FEAT = 2592
BIAS = 304

OUT1 = 20
OUT2 = 9
WIDE = 384
LIN_PAD = 2688
EMB_LANE = FEAT % 128
HEAD_LANE = EMB_LANE + OPTS
CHUNK = 12
LATE_POSITIONS = 12
FEATS_ROW = OUT2 * C2

CLIP_LIMIT = 0.05
DECAY_RATE = 0.8
STEP_RATE = 0.5
FLOOR_ONE = 1e-30
FLOOR_TWO = 0.001

HIGH = lax.Precision.HIGHEST
BF = jnp.bfloat16
F32 = jnp.float32


def dot(left, right, over_left=1, over_right=0, precision=None):
    return lax.dot_general(
        left,
        right,
        (((over_left,), (over_right,)), ((), ())),
        precision=precision,
        preferred_element_type=F32,
    )


def sigmoid(value):
    return 0.5 * jnp.tanh(0.5 * value) + 0.5


def slope(active, sigma):
    return sigma + active * (1.0 - sigma)


def iota(shape, axis):
    return lax.broadcasted_iota(jnp.int32, shape, axis)


def turn(value, steps):
    return pltpu.roll(value, steps, 1)


def fold(value, width):
    step = 64
    while step >= width:
        value = value + turn(value, step)
        step //= 2
    return value


def row_of(column):
    square = jnp.broadcast_to(column, (128, 128))
    return jnp.sum(jnp.where(iota((128, 128), 0) == iota((128, 128), 1), square, 0.0), axis=0, keepdims=True)


def load_frames(frames_hbm, section, frame_buf, sems, chunk):
    copies = []
    for which in range(frame_buf.shape[0] // chunk):
        rows = pl.ds(which * chunk, chunk)
        copies.append(
            pltpu.make_async_copy(
                frames_hbm.at[section, rows], frame_buf.at[rows], sems.at[which]
            )
        )
    return copies


def place_frames(frame_buf, pixels, first, chunk, frames):
    for row in range(first, first + chunk):
        block, part = row // 4, row % 4
        pixels[block * frames : (block + 1) * frames, part * WIDE : part * WIDE + 336] = frame_buf[row]


def fill_band(wide, put, width, taps, blocks):
    for tap in taps:
        fill_tap(wide, put, width, tap, blocks)


def fill_tap(wide, put, width, tap, blocks):
    per_tile = 128 // width
    group = iota((width, 128), 1) // width
    base = 2 * tap * width
    for block in range(blocks + 1):
        tile, spot = divmod(block, per_tile)
        lanes = slice(tile * 128, (tile + 1) * 128)
        left = jnp.where(group == spot, wide[base : base + width, lanes], 0.0)
        right = wide[base + width : base + 2 * width]
        if spot > 0:
            left = jnp.where(group == spot - 1, right[:, lanes], left)
        elif block > 0:
            before = slice((tile - 1) * 128, tile * 128)
            put(tap, block, before, jnp.where(group == per_tile - 1, right[:, before], 0.0).astype(BF))
        put(tap, block, lanes, left.astype(BF))


def repeat_kernels(kernels, first, width, positions, lanes):
    held = kernels.shape[1]
    rows = iota((held, lanes), 0)
    cols = iota((held, lanes), 1)
    pick = jnp.where((cols % width + first == rows) & (cols < positions * width), 1.0, 0.0)
    return dot(kernels, pick.astype(BF))


def build_one(kernels, band):
    wide = repeat_kernels(kernels, 0, C1, LATE_POSITIONS, 256)

    def put(tap, block, lanes, value):
        rows = tap * 256 + block * C1
        band[rows : rows + C1, lanes] = value

    fill_band(wide, put, C1, range(4), LATE_POSITIONS)


def build_two(kernels, band):
    wide = repeat_kernels(kernels, C1, C2, OUT2, WIDE)

    def put(tap, block, lanes, value):
        rows = tap * WIDE + block * C2
        band[rows : rows + C2, lanes] = value

    return [lambda tap=tap: fill_tap(wide, put, C2, tap, OUT2) for tap in range(4)]


def clear_bands(band_one, band_two):
    band_one[...] = jnp.zeros(band_one.shape, BF)
    band_two[...] = jnp.zeros(band_two.shape, BF)


def wide_biases(bias_row):
    bias8 = jnp.broadcast_to(bias_row, (8, BIAS))
    rows = iota((BIAS, WIDE), 0)
    lanes = iota((BIAS, WIDE), 1)
    one = jnp.where((lanes % C1 == rows) & (lanes < OUT1 * C1), 1.0, 0.0)
    two = jnp.where((lanes % C2 + C1 == rows) & (lanes < OUT2 * C2), 1.0, 0.0)
    rows = iota((D, BIAS), 0)
    lanes = iota((D, BIAS), 1)
    three = jnp.where(lanes == rows + C1 + C2, 1.0, 0.0)
    four = jnp.where(lanes == rows + C1 + C2 + D, 1.0, 0.0)
    return (
        dot(bias8, one, precision=HIGH)[0:1],
        dot(bias8, two, precision=HIGH)[0:1],
        dot(three, bias8, 1, 1, precision=HIGH)[:, 0:1],
        dot(four, bias8, 1, 1, precision=HIGH)[:, 0:1],
    )


def encode_one(
    pixels, band_one, half, more, bias, slope_one, act_one, frames, chunk, beside=()
):
    rows = chunk * frames
    band = band_one[half]
    for first in range(0, OUT1, chunk):
        block = pixels[pl.ds(pl.multiple_of((half + first) * frames, frames), rows), :]
        parts = []
        for low, wide in ((0, 128), (128, 256)):
            window = jnp.concatenate(
                [block[:, tap * WIDE + low : tap * WIDE + low + 256] for tap in range(4)], axis=1
            )
            parts.append(dot(window, band[:, 0:wide]))
        if first // chunk < len(beside):
            beside[first // chunk]()
        z = jnp.concatenate(parts, axis=1)
        for step in range(chunk):
            at, part = divmod(first + step, 2)
            spot = (slice(at * frames, (at + 1) * frames), slice(part * WIDE, (part + 1) * WIDE))
            z_step = z[step * frames : (step + 1) * frames]
            if more:
                slope_one[spot] = z_step
            else:
                z_step = z_step + slope_one[spot] + bias
                sigma = sigmoid(z_step)
                active = z_step * sigma
                slope_one[spot] = slope(active, sigma)
                act_one[spot] = active.astype(BF)


def encode_two(act_one, band_two, bias, slope_two, act_two, frames, chunk):
    rows = chunk * frames
    bands = []
    for low, high in ((0, 128), (128, WIDE)):
        bands.append(
            jnp.concatenate(
                [band_two[tap * WIDE + low : tap * WIDE + low + 256, low:high] for tap in range(4)],
                axis=0,
            )
        )
    for first in range(0, OUT2, chunk):
        at = first * frames
        parts = []
        for low, band in zip((0, 128), bands):
            window = jnp.concatenate(
                [
                    act_one[
                        at + tap // 2 * frames : at + tap // 2 * frames + rows,
                        tap % 2 * WIDE + low : tap % 2 * WIDE + low + 256,
                    ]
                    for tap in range(4)
                ],
                axis=1,
            )
            parts.append(dot(window, band))
        z = jnp.concatenate(parts, axis=1) + bias
        sigma = sigmoid(z)
        active = z * sigma
        slope_two[at : at + rows] = slope(active, sigma)
        act = active.astype(BF)
        for step in range(chunk):
            lane = (first + step) * FEATS_ROW
            act_two[:, lane : lane + FEATS_ROW] = act[step * frames : (step + 1) * frames, :FEATS_ROW]


def back_two(dstate_t, linear_t, slope_two, dz_two, frames):
    dact = dot(dstate_t, linear_t, 0, 0)
    dz_two[0:frames] = jnp.zeros((frames, WIDE), BF)
    dz_two[(OUT2 + 1) * frames : (OUT2 + 2) * frames] = jnp.zeros((frames, WIDE), BF)
    blank = jnp.zeros((frames, WIDE - FEATS_ROW), F32)
    for at in range(OUT2):
        part = jnp.concatenate([dact[:, at * FEATS_ROW : (at + 1) * FEATS_ROW], blank], axis=1)
        dz_two[(at + 1) * frames : (at + 2) * frames] = (
            part * slope_two[at * frames : (at + 1) * frames]
        ).astype(BF)


def back_one(dz_two, band_two, slope_one, dz_one, frames, chunk):
    rows = chunk * frames

    def rows_of(tap, low, high):
        return slice(tap * WIDE + low, tap * WIDE + high)

    for first in range(0, OUT1 // 2, chunk):
        low = first * frames
        sides = [dz_two[low + frames : low + frames + rows], dz_two[low : low + rows]]
        left = [
            sum(
                dot(sides[at][:, 0:256], band_two[rows_of(2 * at + part, 0, 256), 0:256], 1, 1)
                for at in range(2)
            )
            for part in range(2)
        ]
        right = sum(
            dot(
                sides[at][:, 128:WIDE],
                jnp.concatenate(
                    [band_two[rows_of(2 * at + part, 256, WIDE), 128:WIDE] for part in range(2)],
                    axis=0,
                ),
                1,
                1,
            )
            for at in range(2)
        )
        dact = jnp.concatenate([left[0], right[:, 0:128], left[1], right[:, 128:256]], axis=1)
        dz = (dact * slope_one[low : low + rows]).astype(BF)
        for step in range(chunk):
            for part in range(2):
                at = (2 * (first + step) + part) * frames
                dz_one[at : at + frames] = dz[
                    step * frames : (step + 1) * frames, part * WIDE : (part + 1) * WIDE
                ]


def band_sums(term, outputs, width):
    per_tile = 128 // width
    lane = iota((width, 128), 1) // width
    sums = []
    for shift in range(2):
        total = None
        for spot in range(per_tile):
            part = None
            for position in range(outputs):
                tile, inside = divmod(position + shift, per_tile)
                if inside != spot:
                    continue
                one = term(position, tile)
                part = one if part is None else part + one
            if part is None:
                continue
            part = jnp.where(lane == spot, part, 0.0)
            total = part if total is None else total + part
        sums.append(fold(total, width))
    return sums


def kernel_grad(terms, outputs, width):
    tiles = []
    lane = iota((width, 128), 1) // width
    pieces = []
    for term in terms:
        pieces.extend(band_sums(term, outputs, width))
    per_tile = 128 // width
    for tile in range(2):
        total = jnp.zeros((width, 128), F32)
        for spot in range(per_tile):
            total = jnp.where(lane == spot, pieces[tile * per_tile + spot], total)
        tiles.append(total)
    return jnp.concatenate(tiles, axis=1)


def tiled(tile, count):
    return jnp.concatenate([tile] * count, axis=1)


def twice(row):
    return jnp.concatenate([row, row], axis=1)


def plan(states, mats_t, table, bias_col, options, legal, games, valid, rewards, returns, scale):
    frames = states.shape[1]
    pairs = OPTS // 2
    lanes = OPTS * frames
    trans_in, trans_out, value_in = mats_t
    low_half = iota((1, 128), 1) < frames
    upper = iota((1, 128), 1) // frames

    valid_f = [twice(v.astype(F32)) for v in valid]
    rewards = [twice(r) for r in rewards]
    returns = [twice(r) for r in returns]
    chosen = [twice(o) for o in options]
    game = twice(games)

    game_rows = iota((128, WIDE), 0) - HEAD_LANE
    game_pick = jnp.where(
        game_rows == tiled(game, 3) + GAMES * (iota((128, WIDE), 1) // 128), 1.0, 0.0
    )
    head_rows = dot(table, game_pick.astype(BF))
    hr, hd, hv = (head_rows[:, k * 128 : (k + 1) * 128] for k in range(3))

    option_rows = jnp.where(
        iota((128, lanes), 0) - EMB_LANE == iota((128, lanes), 1) // frames, 1.0, 0.0
    ).astype(BF)
    s_low = twice(states)
    s_f = s_low.astype(F32)
    base = dot(trans_in, s_low)
    pre = tiled(base, pairs) + dot(table, option_rows)
    sig_h = sigmoid(pre)
    hid = pre * sig_h
    hid_low = hid.astype(BF)
    after = tiled(s_f, pairs) + dot(trans_out, hid_low)
    after_low = after.astype(BF)
    judge_pre = dot(value_in, after_low) + bias_col
    sig_j = sigmoid(judge_pre)
    judged = judge_pre * sig_j

    def tile_of(value, k):
        return value[:, k * 128 : (k + 1) * 128]

    def over(value):
        return jnp.sum(value, axis=0, keepdims=True)

    reward = [over(tile_of(hid, k) * hr) for k in range(pairs)]
    gamma = [sigmoid(over(tile_of(hid, k) * hd)) for k in range(pairs)]
    value = [over(tile_of(judged, k) * hv) for k in range(pairs)]
    backed = [reward[k] + gamma[k] * value[k] for k in range(pairs)]
    allowed = [
        jnp.concatenate([legal[2 * k], legal[2 * k + 1]], axis=1) > 0 for k in range(pairs)
    ]
    highest = functools.reduce(
        jnp.maximum, [jnp.where(allowed[k], backed[k], -1e30) for k in range(pairs)]
    )
    highest = jnp.maximum(highest, turn(highest, frames))
    shares = [
        jnp.where(allowed[k], jnp.exp(jnp.where(allowed[k], backed[k] - highest, -60.0)), 0.0)
        for k in range(pairs)
    ]

    def halves(total):
        return total + turn(total, frames)

    share_sum = halves(sum(shares))
    planned = halves(sum(shares[k] * backed[k] for k in range(pairs))) / share_sum
    choose = [chosen[0] == 2 * k + upper for k in range(pairs)]

    def chosen_of(parts):
        return halves(sum(jnp.where(choose[k], parts[k], 0.0) for k in range(pairs)))

    roll_f = [chosen_of([tile_of(after, k) for k in range(pairs)])]
    roll_low = [roll_f[0].astype(BF)]
    plan_miss = planned - returns[0]
    reward_miss = [chosen_of(reward) - rewards[0]]
    value_miss = [chosen_of(value) - returns[1]]
    steps = len(options)
    picks, pre_k, sig_k, hid_k, hid_k_low, judge_k, sig_jk, judged_k = ([None] for _ in range(8))
    for k in range(1, steps):
        picks.append(jnp.where(iota((128, 128), 0) - EMB_LANE == chosen[k], 1.0, 0.0).astype(BF))
        pre_k.append(dot(trans_in, roll_low[k - 1]) + dot(table, picks[k]))
        sig_k.append(sigmoid(pre_k[k]))
        hid_k.append(pre_k[k] * sig_k[k])
        hid_k_low.append(hid_k[k].astype(BF))
        roll_f.append(roll_f[k - 1] + dot(trans_out, hid_k_low[k]))
        roll_low.append(roll_f[k].astype(BF))
        judge_k.append(dot(value_in, roll_low[k]) + bias_col)
        sig_jk.append(sigmoid(judge_k[k]))
        judged_k.append(judge_k[k] * sig_jk[k])
        reward_miss.append(over(hid_k[k] * hr) - rewards[k])
        value_miss.append(over(judged_k[k] * hv) - returns[k + 1])
    errors = valid_f[0] * plan_miss * plan_miss
    for k in range(steps):
        errors = errors + valid_f[k] * (
            reward_miss[k] * reward_miss[k] + value_miss[k] * value_miss[k]
        )
    errors = jnp.where(low_half, errors * scale, 0.0)

    half = jnp.where(low_half, 1.0, 0.0)
    double = 2.0 * scale
    d_plan = double * valid_f[0] * plan_miss / share_sum
    d_reward_k = [double * valid_f[k] * reward_miss[k] for k in range(steps)]
    d_value_k = [double * valid_f[k] * value_miss[k] for k in range(steps)]

    def through(matrix_t, grad):
        return dot(matrix_t, grad, 0, 0)

    d_roll = None
    d_judge_low, d_step_low, d_pre_low = ([None] * steps for _ in range(3))
    d_hr = jnp.zeros((D, 128), F32)
    d_hd = jnp.zeros((D, 128), F32)
    d_hv = jnp.zeros((D, 128), F32)
    for k in range(steps - 1, 0, -1):
        d_judge_low[k] = (d_value_k[k] * hv * slope(judged_k[k], sig_jk[k])).astype(BF)
        term = through(value_in, d_judge_low[k])
        d_roll = term if d_roll is None else d_roll + term
        d_step_low[k] = d_roll.astype(BF)
        d_hid = through(trans_out, d_step_low[k]) + d_reward_k[k] * hr
        d_pre_low[k] = (d_hid * slope(hid_k[k], sig_k[k])).astype(BF)
        d_roll = d_roll + through(trans_in, d_pre_low[k])
        d_hr = d_hr + (half * d_reward_k[k]) * hid_k[k]
        d_hv = d_hv + (half * d_value_k[k]) * judged_k[k]

    d_backed = [d_plan * shares[k] * (1.0 + backed[k] - planned) for k in range(pairs)]
    d_reward = [
        d_backed[k] + jnp.where(choose[k], d_reward_k[0], 0.0) for k in range(pairs)
    ]
    d_value = [
        d_backed[k] * gamma[k] + jnp.where(choose[k], d_value_k[0], 0.0) for k in range(pairs)
    ]
    d_gamma = [d_backed[k] * value[k] * gamma[k] * (1.0 - gamma[k]) for k in range(pairs)]
    d_judge = [
        (d_value[k] * hv * slope(tile_of(judged, k), tile_of(sig_j, k))).astype(BF)
        for k in range(pairs)
    ]
    d_judge_all = jnp.concatenate(d_judge, axis=1)
    d_after = through(value_in, d_judge_all)
    d_after = [
        tile_of(d_after, k) + jnp.where(choose[k], d_roll, 0.0) for k in range(pairs)
    ]
    d_after_low = jnp.concatenate([d.astype(BF) for d in d_after], axis=1)
    d_hid_all = through(trans_out, d_after_low)
    d_pre = [
        (
            (tile_of(d_hid_all, k) + d_reward[k] * hr + d_gamma[k] * hd)
            * slope(tile_of(hid, k), tile_of(sig_h, k))
        ).astype(BF)
        for k in range(pairs)
    ]
    d_pre_all = jnp.concatenate(d_pre, axis=1)
    d_base = through(trans_in, d_pre_all)
    d_state = halves(sum(d_after[k] + tile_of(d_base, k) for k in range(pairs)))
    for k in range(pairs):
        d_hr = d_hr + d_reward[k] * tile_of(hid, k)
        d_hd = d_hd + d_gamma[k] * tile_of(hid, k)
        d_hv = d_hv + d_value[k] * tile_of(judged, k)

    def both(parts):
        joined = [jnp.where(low_half, parts[k].astype(F32), parts[k + 1].astype(F32)) for k in range(1, steps, 2)]
        return [part.astype(BF) for part in joined]

    def with_steps(wide, parts):
        return jnp.concatenate([wide] + both(parts), axis=1)

    before_low = [None] + roll_low[:-1]
    d_pre_cat = with_steps(d_pre_all, d_pre_low)
    d_judge_cat = with_steps(d_judge_all, d_judge_low)
    grad_in = dot(d_pre_cat, with_steps(tiled(s_low, pairs), before_low), 1, 1)
    grad_out = dot(
        with_steps(d_after_low, d_step_low), with_steps(hid_low, hid_k_low), 1, 1
    )
    grad_value = dot(d_judge_cat, with_steps(after_low, roll_low), 1, 1)
    grad_table = dot(d_pre_cat, with_steps(option_rows, picks), 1, 1) + dot(
        jnp.concatenate([d_hr, d_hd, d_hv], axis=1), game_pick, 1, 1, precision=HIGH
    )
    grad_bias = jnp.sum(d_judge_cat.astype(F32), axis=1, keepdims=True)
    return (
        d_state[:, :frames],
        (grad_in, grad_out, grad_value),
        grad_table,
        grad_bias,
        errors,
    )


def frame_rows(section, refs):
    options_ref, legal_ref, games_ref, valid_ref, rewards_ref, returns_ref = refs

    def row(ref, k):
        return ref[k, pl.ds(section, 1), :]

    depth = options_ref.shape[0]
    return (
        [row(options_ref, k) for k in range(depth)],
        [row(legal_ref, k) for k in range(OPTS)],
        games_ref[pl.ds(section, 1), :],
        [row(valid_ref, k) for k in range(depth)],
        [row(rewards_ref, k) for k in range(depth)],
        [returns_ref[section, k : k + 1, :] for k in range(depth + 1)],
    )


def clear_tails(pixels):
    tail = jnp.zeros((pixels.shape[0], WIDE - 336), BF)
    for part in range(4):
        pixels[:, part * WIDE + 336 : (part + 1) * WIDE] = tail


def grad_kernel_two(act_one, dz_two, frames):
    rows = OUT2 * frames
    d_two = dz_two[frames : frames + rows]
    turned = d_two.T

    def term_of(tap):
        first, base = (tap // 2) * frames, (tap % 2) * WIDE
        blocks = []
        for low, high in ((0, 128), (128, OUT2 * C2)):
            blocks.append(
                dot(turned[low:high], act_one[first : first + rows, base + low : base + low + 256])
            )

        def term(position, tile):
            group = min(position // 4, 1)
            inside, lane = position - 4 * group, (tile - group) * 128
            return blocks[group][inside * C2 : (inside + 1) * C2, lane : lane + 128]

        return term

    grad = kernel_grad([term_of(tap) for tap in range(4)], OUT2, C2)
    return grad, fold(tiles_sum(dot(jnp.ones((8, rows), BF), d_two)), C2)


def grad_kernel_one(pixels, dz_one, frames):
    rows = OUT1 * frames
    d_one = dz_one[...]
    turned = d_one.T

    def term_of(tap):
        first = (tap // 4) * frames
        base = (tap % 4) * WIDE
        blocks = []
        for low, high in ((0, 128), (128, OUT1 * C1)):
            blocks.append(
                dot(turned[low:high], pixels[first : first + rows, base + low : base + low + 256])
            )

        def term(position, tile):
            group = min(position // 8, 1)
            inside, lane = position - 8 * group, (tile - group) * 128
            return blocks[group][inside * C1 : (inside + 1) * C1, lane : lane + 128]

        return term

    grad = kernel_grad([term_of(tap) for tap in range(8)], OUT1, C1)
    return grad, fold(tiles_sum(dot(jnp.ones((8, rows), BF), d_one)), C1)


def local_kernel(
    frames_hbm,
    kernels_ref,
    linear_ref,
    mats_ref,
    table_ref,
    bias_ref,
    options_ref,
    legal_ref,
    games_ref,
    valid_ref,
    rewards_ref,
    returns_ref,
    lin_out,
    mats_out,
    table_out,
    conv_out,
    small_out,
    frame_buf,
    pixels,
    band_one,
    band_two,
    slope_one,
    act_one,
    slope_two,
    act_two,
    dz_two,
    dz_one,
    sems,
):
    section = lax.axis_index("section")
    frames = frame_buf.shape[1]
    copies = load_frames(frames_hbm, section, frame_buf, sems, CHUNK)
    for copy in copies:
        copy.start()
    clear_bands(band_one, band_two)
    kernels = kernels_ref[...]
    build_one(kernels[0 : KERN // 2], band_one.at[0])
    build_one(kernels[KERN // 2 : KERN], band_one.at[1])
    for fill in build_two(kernels, band_two):
        fill()
    bias_one, bias_two, bias_three, bias_four = wide_biases(bias_ref[...])
    clear_tails(pixels)
    for which, copy in enumerate(copies):
        copy.wait()
        place_frames(frame_buf, pixels, which * CHUNK, CHUNK, frames)
    encode_one(pixels, band_one, 0, True, bias_one, slope_one, act_one, frames, 4)
    encode_one(pixels, band_one, 1, False, bias_one, slope_one, act_one, frames, 4)
    encode_two(act_one, band_two, bias_two, slope_two, act_two, frames, 3)
    linear_t = linear_ref[...]
    states = (dot(linear_t, act_two[...], 1, 1) + bias_three).astype(BF)
    d_state, grad_mats, grad_table, grad_bias, errors = plan(
        states,
        tuple(mats_ref[k] for k in range(3)),
        table_ref[...],
        bias_four,
        *frame_rows(
            section, (options_ref, legal_ref, games_ref, valid_ref, rewards_ref, returns_ref)
        ),
        1.0,
    )
    for k in range(3):
        mats_out[k] = grad_mats[k]
    table_out[...] = grad_table
    d_state_low = d_state.astype(BF)
    lin_out[...] = dot(d_state_low, act_two[...])
    back_two(d_state_low, linear_t, slope_two, dz_two, frames)
    grad_two, bias_two_grad = grad_kernel_two(act_one, dz_two, frames)
    back_one(dz_two, band_two, slope_one, dz_one, frames, 5)
    grad_one, bias_one_grad = grad_kernel_one(pixels, dz_one, frames)
    conv_out[...] = stack_kernels(grad_one, grad_two)
    lane = iota((8, 128), 1)
    line = iota((8, 128), 0)
    row_zero = jnp.where(
        lane < C1, bias_one_grad, jnp.where(lane < C1 + C2, turn(bias_two_grad, C1), 0.0)
    )
    count = sum(
        valid_ref[k, pl.ds(section, 1), :].astype(F32) for k in range(valid_ref.shape[0])
    )
    count = jnp.where(iota((1, 128), 1) < frames, twice(count), 0.0)
    small = jnp.where(line == 0, row_zero, 0.0)
    small = jnp.where(line == 1, row_of(lane_sum(d_state_low)), small)
    small = jnp.where(line == 2, row_of(grad_bias), small)
    small = jnp.where(line == 3, errors, small)
    small = jnp.where(line == 4, count, small)
    small_out[...] = small


def lane_sum(value):
    return jnp.sum(value.astype(F32), axis=1, keepdims=True)


def stack_kernels(grad_one, grad_two):
    rows = jnp.concatenate([grad_one, grad_two, jnp.zeros((128 - C1 - C2, KERN), F32)], axis=0)
    return rows.T


def tiles_sum(value):
    return sum(value[:, k * 128 : (k + 1) * 128] for k in range(value.shape[1] // 128))


VMEM_SPEC = pl.BlockSpec(memory_space=pltpu.VMEM)
ANY_SPEC = pl.BlockSpec(memory_space=pl.ANY)


def local_scratch(frames, side):
    return [
        pltpu.VMEM((side, frames, 336), BF),
        pltpu.VMEM(((OUT1 + 1) * frames, 4 * WIDE), BF),
        pltpu.VMEM((2, 4 * 256, 256), BF),
        pltpu.VMEM((4 * WIDE, WIDE), BF),
        pltpu.VMEM((OUT1 // 2 * frames, 2 * WIDE), F32),
        pltpu.VMEM((OUT1 // 2 * frames, 2 * WIDE), BF),
        pltpu.VMEM((OUT2 * frames, WIDE), F32),
        pltpu.VMEM((frames, FEAT), BF),
        pltpu.VMEM(((OUT2 + 2) * frames, WIDE), BF),
        pltpu.VMEM((OUT1 * frames, WIDE), BF),
        pltpu.SemaphoreType.DMA((side // CHUNK,)),
    ]


def local_step(frames, kernels, linear_t, mats_t, table, biases, options, legal, games, valid, rewards, returns):
    count = frames.shape[1]
    side = frames.shape[2]
    shapes = [(D, FEAT), (3, D, D), (D, 128), (KERN, 128), (8, 128)]
    return pl.pallas_call(
        local_kernel,
        out_shape=[jax.ShapeDtypeStruct(shape, F32) for shape in shapes],
        in_specs=[ANY_SPEC] + [VMEM_SPEC] * 11,
        out_specs=[VMEM_SPEC] * len(shapes),
        scratch_shapes=local_scratch(count, side),
        compiler_params=pltpu.CompilerParams(vmem_limit_bytes=56 * 1024 * 1024),
    )(
        frames.transpose(0, 2, 1, 3),
        kernels,
        linear_t,
        mats_t,
        table,
        biases.reshape(1, BIAS),
        options.transpose(2, 0, 1),
        legal.transpose(2, 0, 1),
        games,
        valid.transpose(2, 0, 1),
        rewards.transpose(2, 0, 1),
        returns.transpose(0, 2, 1),
    )


MESH = pl.DeviceIdType.MESH


QUARTER = 768
HALF = 2 * QUARTER
AT_EMB = FEAT
AT_HEADS = AT_EMB + OPTS
AT_MATS = LIN_PAD
TILES = HALF // 128
SCALE_LANE = C1 + C2
NEAR = 8
FOUR = 4


def fused_kernel(
    peers,
    frames_hbm,
    conv_hbm,
    lin_hbm,
    mats_hbm,
    emb_hbm,
    heads_hbm,
    bias_hbm,
    options_hbm,
    legal_hbm,
    games_hbm,
    valid_hbm,
    rewards_hbm,
    returns_hbm,
    main_out,
    conv_out,
    stats_out,
    frame_buf,
    pixels,
    band_one,
    band_two,
    slope_one,
    act_one,
    slope_two,
    act_two,
    dz_two,
    dz_one,
    frame_sems,
    stage,
    kernel_msg,
    weight_msg,
    weights,
    grad_own,
    mate_in,
    grad_msg,
    near_in,
    cross_in,
    cross_msg,
    far_in,
    taps_msg,
    row_in,
    rows_in,
    taps_turned,
    stats_in,
    final,
    stats_base,
    half_in,
    send_sems,
    recv_sems,
    mate_send,
    mate_recv,
    conv_ref,
    lin_ref,
    mats_ref,
    emb_ref,
    heads_ref,
    bias_ref,
    options_ref,
    legal_ref,
    games_ref,
    valid_ref,
    rewards_ref,
    returns_ref,
    operand_sems,
):
    section = lax.axis_index("section")
    place = lax.axis_index("dp")
    mate = 1 - section
    frames = frame_buf.shape[1]

    barrier = pltpu.get_barrier_semaphore()

    def greet(step, carry):
        peer = lax.rem(place + step, peers)
        pl.semaphore_signal(barrier, inc=1, device_id=(section, peer), device_id_type=MESH)
        return carry

    def greet_row(step, carry):
        peer = place - lax.rem(place, FOUR) + lax.rem(place + step, FOUR)
        pl.semaphore_signal(barrier, inc=1, device_id=(mate, peer), device_id_type=MESH)
        return carry

    lax.fori_loop(1, peers, greet, 0)
    lax.fori_loop(0, FOUR, greet_row, 0)
    loads = [
        pltpu.make_async_copy(source, target, operand_sems.at[which])
        for which, (source, target) in enumerate(
            (
                (conv_hbm, conv_ref),
                (lin_hbm, lin_ref),
                (mats_hbm, mats_ref),
                (emb_hbm, emb_ref),
                (heads_hbm, heads_ref),
                (bias_hbm, bias_ref),
                (options_hbm, options_ref),
                (legal_hbm, legal_ref),
                (games_hbm, games_ref),
                (valid_hbm, valid_ref),
                (rewards_hbm, rewards_ref),
                (returns_hbm, returns_ref),
            )
        )
    ]
    for load in loads:
        load.start()
    copies = load_frames(frames_hbm, section, frame_buf, frame_sems, CHUNK)
    wait_frames = lambda: [copy.wait() for copy in copies]
    for copy in copies:
        copy.start()

    sends = []

    side, spot = place // NEAR, lax.rem(place, NEAR)
    row, column = spot // FOUR, lax.rem(spot, FOUR)

    def near(step):
        return side * NEAR + lax.rem(spot + step, NEAR)

    def beyond(step):
        return (1 - side) * NEAR + lax.rem(spot + step, NEAR)

    def beside(step):
        return place - column + lax.rem(column + step, FOUR)

    def across(step, where):
        return (1 - side) * NEAR + lax.rem(row + step, 2) * FOUR + where

    def send(sems, peer, source, target, core=section):
        pltpu.make_async_remote_copy(
            src_ref=source,
            dst_ref=target,
            send_sem=send_sems.at[sems],
            recv_sem=recv_sems.at[sems],
            device_id=(core, peer),
            device_id_type=MESH,
        ).start()

    def loop(low, high, act):
        def body(step, carry):
            act(step)
            return carry

        lax.fori_loop(low, high, body, 0)

    def settle(sems, blocks):
        whole = pltpu.make_async_remote_copy(
            src_ref=blocks,
            dst_ref=blocks,
            send_sem=send_sems.at[sems],
            recv_sem=recv_sems.at[sems],
            device_id=(mate, place),
            device_id_type=MESH,
        )
        sends.append(whole.wait_send)
        return whole.wait_recv

    def send_peers(sems, source, target):
        loop(0, NEAR, lambda step: send(sems, beyond(step), source, target.at[place]))
        loop(1, NEAR, lambda step: send(sems, near(step), source, target.at[place]))
        return settle(sems, target.at[pl.ds(0, peers - 1)])

    def send_mate(which, source, target, landing):
        def copy(into):
            return pltpu.make_async_remote_copy(
                src_ref=source,
                dst_ref=into,
                send_sem=mate_send.at[which],
                recv_sem=mate_recv.at[which],
                device_id=(mate, place),
                device_id_type=MESH,
            )

        copy(target).start()
        sends.append(lambda: copy(target).wait_send())
        return lambda: copy(landing).wait_recv()

    for load in loads:
        load.wait()
    upper_lanes = iota((16, 128), 1) >= 64
    counts = sum(
        valid_ref[k, m : m + 1, :].astype(F32)
        for k in range(valid_ref.shape[0])
        for m in range(valid_ref.shape[1])
    )
    conv_pad = jnp.concatenate([conv_ref[...], jnp.zeros((16, 80), F32)], axis=1)
    kernel_msg[place] = jnp.where(
        upper_lanes & (iota((16, 128), 0) == 0), jnp.broadcast_to(twice(counts), (16, 128)), conv_pad
    ).astype(BF)
    heads_pad = jnp.concatenate([heads_ref[...], jnp.zeros((24, 120), F32)], axis=1)
    heads_pad = jnp.concatenate([heads_pad, jnp.zeros((104, 128), F32)], axis=0).T
    last = FEAT - EMB_LANE
    stage[:, 0:last] = lin_ref[:, 0:last]
    stage[:, last:LIN_PAD] = jnp.concatenate(
        [
            lin_ref[:, last:FEAT],
            emb_ref[...],
            heads_pad[0:8, 0 : 3 * GAMES],
            jnp.zeros((8, 128 - HEAD_LANE - 3 * GAMES), F32),
        ],
        axis=1,
    )
    for k in range(3):
        stage[:, AT_MATS + k * D : AT_MATS + (k + 1) * D] = mats_ref[k]
    first = stage[:, pl.ds(pl.multiple_of(section * HALF, 128), QUARTER)]
    second = stage[:, pl.ds(pl.multiple_of(section * HALF + QUARTER, 128), QUARTER)]
    weight_msg[section, place] = jnp.concatenate([first, second], axis=0).astype(BF)

    def square_sum(value):
        return jnp.sum(jnp.sum(value * value, axis=0, keepdims=True), axis=1, keepdims=True)

    weight_squares = [
        square_sum(conv_pad),
        square_sum(lin_ref[...]),
        square_sum(mats_ref[...].reshape(24, D)),
        square_sum(emb_ref[...]),
        square_sum(heads_ref[...]),
    ]
    stat_line = iota((16, 128), 0)
    stat = jnp.zeros((16, 128), F32)
    for which, value in enumerate(weight_squares):
        at = iota((16, 128), 1) - SCALE_LANE
        rough = value.astype(BF).astype(F32)
        mixed = stat_line == TILES + 2
        stat = jnp.where(mixed & (at == which), rough, stat)
        stat = jnp.where(mixed & (at == which + 5), value - rough, stat)
    stats_base[...] = stat
    pl.semaphore_wait(barrier, peers - 1 + FOUR)
    half_msg = weight_msg.at[section]

    def spread_own(sems, blocks):
        own = blocks.at[place]
        loop(0, 2, lambda step: send(sems, across(step, column), own, own))
        wait_across = settle(sems, blocks.at[pl.ds(0, 2)])
        loop(1, NEAR, lambda step: send(sems + 1, near(step), own, own))
        return wait_across, settle(sems + 1, blocks.at[pl.ds(0, NEAR - 1)])

    def pass_on(sems, blocks):
        for which in range(2):
            block = blocks.at[across(which, column)]
            loop(1, FOUR, lambda step: send(sems, beside(step), block, block))
        return settle(sems, blocks.at[pl.ds(0, 2 * (FOUR - 1))])

    wait_kernel_across, wait_kernel_near = spread_own(0, kernel_msg)
    wait_across, wait_near = spread_own(3, half_msg)

    clear_bands(band_one, band_two)
    bias_one, bias_two, bias_three, bias_four = wide_biases(bias_ref[...].reshape(1, BIAS))
    clear_tails(pixels)
    act_two[:, FEAT:LIN_PAD] = jnp.zeros((frames, LIN_PAD - FEAT), BF)
    for which, copy in enumerate(copies):
        copy.wait()
        place_frames(frame_buf, pixels, which * CHUNK, CHUNK, frames)
    wait_kernel_across()
    wait_kernel_beside = pass_on(2, kernel_msg)
    wait_kernel_near()

    def side_kernels(which):
        return kernel_msg[pl.ds(which * NEAR, NEAR)].reshape(KERN // 2, 128)

    build_one(side_kernels(side), band_one.at[side])
    wait_across()
    wait_beside = pass_on(5, half_msg)
    encode_one(pixels, band_one, side, True, bias_one, slope_one, act_one, frames, 4)
    wait_kernel_beside()
    build_one(side_kernels(1 - side), band_one.at[1 - side])
    kernels = kernel_msg[...].reshape(KERN, 128)
    fills = build_two(kernels, band_two)
    counted = jnp.where(iota((KERN, 128), 1) >= 64, kernels.astype(F32), 0.0)
    count = jnp.sum(jnp.sum(counted, axis=0, keepdims=True), axis=1, keepdims=True)
    scale = 1.0 / count
    encode_one(pixels, band_one, 1 - side, False, bias_one, slope_one, act_one, frames, 4, fills)
    wait_near()
    own_side, far_side = pl.ds(side * NEAR, NEAR), pl.ds((1 - side) * NEAR, NEAR)
    wait_own_side = send_mate(
        0, half_msg.at[own_side], half_msg.at[own_side], weight_msg.at[mate, own_side]
    )
    wait_beside()
    wait_far_side = send_mate(
        5, half_msg.at[far_side], half_msg.at[far_side], weight_msg.at[mate, far_side]
    )
    encode_two(act_one, band_two, bias_two, slope_two, act_two, frames, 3)
    wait_own_side()
    wait_far_side()
    for half in range(2):
        block = weight_msg[half].astype(F32)
        for part in range(2):
            lane = (2 * half + part) * QUARTER
            weights[:, lane : lane + QUARTER] = (
                block[:, part * 8 : (part + 1) * 8].reshape(D, QUARTER).astype(BF)
            )
    linear_t = weights[:, 0:LIN_PAD]
    states = (dot(linear_t, act_two[...], 1, 1) + bias_three).astype(BF)
    d_state, grad_mats, grad_table, grad_bias, errors = plan(
        states,
        tuple(weights[:, AT_MATS + k * D : AT_MATS + (k + 1) * D] for k in range(3)),
        weights[:, LIN_PAD - 128 : LIN_PAD],
        bias_four,
        *frame_rows(
            section, (options_ref, legal_ref, games_ref, valid_ref, rewards_ref, returns_ref)
        ),
        scale,
    )

    d_state_low = d_state.astype(BF)
    grad_linear = dot(d_state_low, act_two[...])
    parts = [grad_linear[:, at * QUARTER : (at + 1) * QUARTER] for at in range(3)]
    parts.append(
        jnp.concatenate(
            [
                grad_linear[:, 3 * QUARTER : LIN_PAD - 128],
                grad_linear[:, LIN_PAD - 128 : LIN_PAD] + grad_table,
                *grad_mats,
            ],
            axis=1,
        )
    )
    parts = [part.reshape(peers, 8, QUARTER) for part in parts]
    for half in range(2):
        grad_own[half] = jnp.concatenate(parts[2 * half : 2 * half + 2], axis=1).astype(BF)
    wait_mate_far, wait_mate_near = (
        send_mate(which, grad_own.at[mate, part], mate_in.at[part], mate_in.at[part])
        for which, part in ((1, far_side), (2, own_side))
    )
    back_two(d_state_low, linear_t, slope_two, dz_two, frames)

    def pair_up(part):
        paired = grad_own[section, part].astype(F32) + mate_in[part].astype(F32)
        grad_msg[part] = paired.astype(BF)

    wait_mate_far()
    pair_up(far_side)
    twin = beyond(0)

    def collect(step):
        peer = near(step)
        send(6, peer, grad_msg.at[lax.rem(peer + NEAR, peers)], cross_in.at[spot])

    loop(1, NEAR, collect)
    cross_in[spot] = grad_msg[twin]
    wait_cross = settle(6, cross_in.at[pl.ds(0, NEAR - 1)])
    wait_mate_near()
    pair_up(own_side)
    loop(1, NEAR, lambda step: send(7, near(step), grad_msg.at[near(step)], near_in.at[spot]))
    wait_grads = settle(7, near_in.at[pl.ds(0, NEAR - 1)])
    near_in[spot] = grad_msg[place]
    row_three = row_of(lane_sum(d_state_low))
    row_four = row_of(grad_bias)
    grad_two, bias_two_grad = grad_kernel_two(act_one, dz_two, frames)
    back_one(dz_two, band_two, slope_one, dz_one, frames, 5)
    grad_one, bias_one_grad = grad_kernel_one(pixels, dz_one, frames)

    kernel_grads = jnp.concatenate([grad_one, grad_two], axis=0).astype(BF)
    for half in range(2):
        taps_msg[half] = kernel_grads[:, half * 128 : (half + 1) * 128]
    own = section * FOUR + column
    loop(1, FOUR, lambda step: send(9, beside(step), taps_msg.at[section], row_in.at[own]))
    loop(0, FOUR, lambda step: send(9, beside(step), taps_msg.at[mate], row_in.at[own], mate))
    wait_row = settle(9, row_in.at[pl.ds(0, 2 * FOUR - 1)])
    row_in[own] = taps_msg[section]
    wait_cross()
    cross_msg[...] = jnp.sum(cross_in[...].astype(F32), axis=0).astype(BF)
    send(8, twin, cross_msg, far_in)
    wait_far = settle(8, far_in)
    wait_row()
    level = place // FOUR
    rows_in[level] = jnp.sum(row_in[...].astype(F32), axis=0).astype(BF)
    loop(
        1,
        peers // FOUR,
        lambda step: send(
            11, lax.rem(place + step * FOUR, peers), rows_in.at[level], rows_in.at[level]
        ),
    )
    wait_rows = settle(11, rows_in.at[pl.ds(0, peers // FOUR - 1)])
    wait_grads()
    wait_far()
    total = jnp.sum(near_in[...].astype(F32), axis=0) + far_in[...].astype(F32)
    squares = total * total
    stat = stats_base[...]
    for part in range(2):
        sums = jnp.sum(squares[part * 8 : (part + 1) * 8], axis=0, keepdims=True)
        for tile in range(TILES // 2):
            stat = jnp.where(
                stat_line == part * (TILES // 2) + tile, sums[:, tile * 128 : (tile + 1) * 128], stat
            )
    lane = iota((1, 128), 1)
    row_first = jnp.where(
        lane < C1, bias_one_grad[0:1], jnp.where(lane < C1 + C2, turn(bias_two_grad, C1)[0:1], 0.0)
    )
    row_first = row_first + turn(errors, 64)
    stat = jnp.where(stat_line == TILES, row_three, stat)
    stat = jnp.where(stat_line == TILES + 1, row_four, stat)
    stat = stat + jnp.where(stat_line == TILES + 2, row_first, 0.0)
    stats_in[place] = stat.astype(BF)
    wait_stats = send_peers(10, stats_in.at[place], stats_in)
    half_in[section, :, 0:QUARTER] = total[0:8]
    half_in[section, :, QUARTER:HALF] = total[8:16]
    wait_half_grads = send_mate(3, half_in.at[section], half_in.at[section], half_in.at[mate])
    wait_rows()
    taps = jnp.sum(rows_in[...].astype(F32), axis=0)
    taps = jnp.concatenate([taps, jnp.zeros((128 - C1 - C2, 128), F32)], axis=0)
    taps_turned[...] = taps.T
    final[section, 16:32] = taps_turned[pl.ds(pl.multiple_of(spot * 16, 16), 16)]
    final[section, 32:40] = jnp.broadcast_to(
        jnp.sum(taps * taps, axis=0, keepdims=True), (8, 128)
    )
    wait_half_grads()
    for half in range(2):
        main_out[:, half * HALF : (half + 1) * HALF] = half_in[half]
    wait_stats()
    final[section, 0:16] = jnp.sum(stats_in[...].astype(F32), axis=0)
    wait_final = send_mate(4, final.at[section], final.at[section], final.at[mate])
    wait_final()
    conv_out[...] = final[side, 16:32]
    stats_out[...] = final[...]

    for wait in sends:
        wait()


def fused_step(peers, frames, shards, biases, rows):
    count = frames.shape[1]
    side = frames.shape[2]
    scratch = local_scratch(count, side)
    scratch[7] = pltpu.VMEM((count, LIN_PAD), BF)
    scratch += [
        pltpu.VMEM((8, 2 * HALF), F32),
        pltpu.VMEM((peers, 16, 128), BF),
        pltpu.VMEM((2, peers, 16, QUARTER), BF),
        pltpu.VMEM((D, 2 * HALF), BF),
        pltpu.VMEM((2, peers, 16, QUARTER), BF),
        pltpu.VMEM((peers, 16, QUARTER), BF),
        pltpu.VMEM((peers, 16, QUARTER), BF),
        pltpu.VMEM((NEAR, 16, QUARTER), BF),
        pltpu.VMEM((NEAR, 16, QUARTER), BF),
        pltpu.VMEM((16, QUARTER), BF),
        pltpu.VMEM((16, QUARTER), BF),
        pltpu.VMEM((2, C1 + C2, 128), BF),
        pltpu.VMEM((2 * FOUR, C1 + C2, 128), BF),
        pltpu.VMEM((peers // FOUR, C1 + C2, 128), BF),
        pltpu.VMEM((128, 128), F32),
        pltpu.VMEM((peers, 16, 128), BF),
        pltpu.VMEM((2, 40, 128), F32),
        pltpu.VMEM((16, 128), F32),
        pltpu.VMEM((2, 8, HALF), F32),
        pltpu.SemaphoreType.DMA((12,)),
        pltpu.SemaphoreType.DMA((12,)),
        pltpu.SemaphoreType.DMA((6,)),
        pltpu.SemaphoreType.DMA((6,)),
    ]
    shapes = [(8, 2 * HALF), (16, 128), (2, 40, 128)]
    operands = [frames.transpose(0, 2, 1, 3), *shards, biases, *rows]
    scratch += [pltpu.VMEM(operand.shape, operand.dtype) for operand in operands[1:]]
    scratch += [pltpu.SemaphoreType.DMA((len(operands) - 1,))]
    return pl.pallas_call(
        functools.partial(fused_kernel, peers),
        out_shape=[jax.ShapeDtypeStruct(shape, F32) for shape in shapes],
        in_specs=[ANY_SPEC] * len(operands),
        out_specs=[VMEM_SPEC] * len(shapes),
        scratch_shapes=scratch,
        compiler_params=pltpu.CompilerParams(
            vmem_limit_bytes=56 * 1024 * 1024, collective_id=0, has_side_effects=True
        ),
    )(*operands)


def column_of(row):
    square = jnp.broadcast_to(row, (8, 8))
    return jnp.sum(jnp.where(iota((8, 8), 0) == iota((8, 8), 1), square, 0.0), axis=1, keepdims=True)


def row_back(column):
    square = jnp.broadcast_to(column, (8, 8))
    return jnp.sum(jnp.where(iota((8, 8), 0) == iota((8, 8), 1), square, 0.0), axis=0, keepdims=True)


def total_of(value):
    return jnp.sum(jnp.sum(value, axis=0, keepdims=True), axis=1, keepdims=True)


def update_kernel(
    main_ref,
    convg_ref,
    stats_ref,
    conv_ref,
    lin_ref,
    mats_ref,
    emb_ref,
    heads_ref,
    bias_ref,
    conv_moment,
    lin_rows,
    lin_cols,
    mats_rows,
    mats_cols,
    emb_moment,
    head_moment,
    bias_moment,
    conv_new,
    conv_grad,
    conv_moment_new,
    lin_new,
    lin_grad,
    lin_rows_new,
    lin_cols_new,
    mats_new,
    mats_grad,
    mats_rows_new,
    mats_cols_new,
    emb_new,
    emb_grad,
    emb_moment_new,
    heads_new,
    heads_grad,
    head_moment_new,
    bias_new,
    bias_grad,
    bias_moment_new,
    norm_out,
    loss_out,
    conv_low,
    lin_low,
):
    stats = stats_ref[...]
    both = stats[0] + stats[1]
    squares = total_of(both[0:TILES]) + total_of(both[32:33])
    scales = stats[0, TILES + 2 : TILES + 3]
    scales = [
        scales[:, SCALE_LANE + k : SCALE_LANE + k + 1]
        + scales[:, SCALE_LANE + k + 5 : SCALE_LANE + k + 6]
        for k in range(5)
    ]
    bias_raw = jnp.concatenate(
        [both[TILES + 2 : TILES + 3, 0 : C1 + C2], both[TILES : TILES + 1], both[TILES + 1 : TILES + 2]],
        axis=1,
    )
    norm = jnp.sqrt(squares + total_of(bias_raw * bias_raw))
    factor = jnp.minimum(1.0, CLIP_LIMIT / norm)
    norm_out[...] = norm
    loss_out[...] = total_of(both[TILES + 2 : TILES + 3, 64:128])

    def simple(weight, grad, moment, square_total, outs):
        new, moment_new = unfactored(
            weight, grad, moment, relative(square_total, weight.size * outs[3])
        )
        for out, value in zip(outs, (new, grad, moment_new)):
            out[...] = value.reshape(out.shape)
        return new

    peers = D // lin_ref.shape[0]
    conv = simple(
        conv_ref[...],
        factor * convg_ref[:, 0 : C1 + C2],
        conv_moment[...],
        scales[0],
        (conv_new, conv_grad, conv_moment_new, peers),
    )
    conv_low[...] = conv.astype(BF)
    simple(
        emb_ref[...],
        factor * main_ref[:, AT_EMB:AT_HEADS],
        emb_moment[...],
        scales[3],
        (emb_new, emb_grad, emb_moment_new, peers),
    )
    heads_t = jnp.concatenate(
        [main_ref[:, LIN_PAD - 128 : LIN_PAD], jnp.zeros((120, 128), F32)], axis=0
    ).T
    simple(
        heads_ref[...],
        factor * heads_t[HEAD_LANE : HEAD_LANE + 3 * GAMES, 0:8],
        head_moment[...],
        scales[4],
        (heads_new, heads_grad, head_moment_new, peers),
    )
    bias = bias_ref[...].reshape(1, BIAS)
    simple(
        bias,
        factor * bias_raw,
        bias_moment[...].reshape(1, BIAS),
        total_of(bias * bias),
        (bias_new, bias_grad, bias_moment_new, 1),
    )
    row_sums = [stats[t // TILES, t % TILES : t % TILES + 1] for t in range(24)]

    def factored(weight, grad, rows_old, cols_old, row_sum, square_total, entries):
        rows = DECAY_RATE * rows_old + (1.0 - DECAY_RATE) * (
            factor * factor * row_sum / D + FLOOR_ONE
        )
        wide = grad.shape[1]
        cols = DECAY_RATE * cols_old + (1.0 - DECAY_RATE) * (
            jnp.sum(grad * grad + FLOOR_ONE, axis=1, keepdims=True) / wide
        )
        mean = jnp.sum(rows, axis=1, keepdims=True) / wide
        second = rows * cols / mean
        new = weight - STEP_RATE * relative(square_total, entries) * grad * lax.rsqrt(second)
        return new, rows, cols

    grad = factor * main_ref[:, 0:FEAT]
    new, rows, cols = factored(
        lin_ref[...],
        grad,
        lin_rows[...].reshape(1, FEAT),
        column_of(lin_cols[...]),
        jnp.concatenate(row_sums[:21], axis=1)[:, 0:FEAT],
        scales[1],
        FEAT * D,
    )
    lin_new[...] = new
    lin_grad[...] = grad
    lin_rows_new[...] = rows.reshape(FEAT)
    lin_cols_new[...] = row_back(cols)
    lin_low[...] = new.astype(BF)
    for k in range(3):
        grad = factor * main_ref[:, AT_MATS + k * D : AT_MATS + (k + 1) * D]
        new, rows, cols = factored(
            mats_ref[k],
            grad,
            mats_rows[k : k + 1],
            column_of(mats_cols[k : k + 1]),
            row_sums[21 + k],
            scales[2],
            3 * D * D,
        )
        mats_new[k] = new
        mats_grad[k] = grad
        mats_rows_new[k : k + 1] = rows
        mats_cols_new[k : k + 1] = row_back(cols)


def fused_device(
    frames,
    options,
    legal,
    games,
    valid,
    rewards,
    returns,
    conv_kernels,
    enc_linear,
    plan_mats,
    option_emb,
    heads,
    biases,
    conv_moment,
    lin_rows,
    lin_cols,
    mats_rows,
    mats_cols,
    emb_moment,
    head_moment,
    bias_moment,
):
    width = enc_linear.shape[1]
    peers = D // width
    shards = (
        conv_kernels,
        enc_linear.T,
        plan_mats.transpose(0, 2, 1),
        option_emb.T,
        heads.reshape(3 * GAMES, width),
    )
    summed = fused_step(
        peers,
        frames,
        shards,
        biases,
        (
            options.transpose(2, 0, 1),
            legal.transpose(2, 0, 1),
            games,
            valid.transpose(2, 0, 1),
            rewards.transpose(2, 0, 1),
            returns.transpose(0, 2, 1),
        ),
    )
    shapes = [(16, 48)] * 3 + [(8, FEAT)] * 2 + [(FEAT,), (1, 8)] + [(3, 8, D)] * 2 + [(3, D), (3, 8)]
    shapes += [(8, OPTS)] * 3 + [(24, 8)] * 3 + [(BIAS,)] * 3 + [(1, 1)] * 2
    outs = [jax.ShapeDtypeStruct(shape, F32) for shape in shapes]
    outs += [jax.ShapeDtypeStruct((16, 48), BF), jax.ShapeDtypeStruct((8, FEAT), BF)]
    operands = [
        *summed,
        *shards,
        biases,
        conv_moment,
        lin_rows,
        lin_cols.reshape(1, width),
        mats_rows,
        mats_cols,
        emb_moment.T,
        head_moment.reshape(3 * GAMES, width),
        bias_moment,
    ]
    o = pl.pallas_call(
        update_kernel,
        out_shape=outs,
        in_specs=[VMEM_SPEC] * len(operands),
        out_specs=[VMEM_SPEC] * len(outs),
    )(*operands)
    flat_heads = [h.reshape(3, GAMES, width) for h in o[14:17]]
    return (
        *o[0:3],
        o[3].T,
        o[4].T,
        o[5],
        o[6].reshape(width),
        o[7].transpose(0, 2, 1),
        o[8].transpose(0, 2, 1),
        o[9],
        o[10],
        o[11].T,
        o[12].T,
        o[13].T,
        *flat_heads,
        *o[17:20],
        o[20].reshape(()),
        o[21].reshape(()),
        o[22],
        o[23].T,
    )


def gather_rows(shard):
    return lax.all_gather(shard, "dp", axis=0, tiled=True)


def relative(square_total, entries):
    return jnp.maximum(FLOOR_TWO, jnp.sqrt(square_total / entries))


def unfactored(weight, grad, moment, scale):
    moment_new = DECAY_RATE * moment + (1.0 - DECAY_RATE) * (grad * grad + FLOOR_ONE)
    return (weight - STEP_RATE * scale * grad * lax.rsqrt(moment_new), moment_new)


def per_device(
    frames,
    options,
    legal,
    games,
    valid,
    rewards,
    returns,
    conv_kernels,
    enc_linear,
    plan_mats,
    option_emb,
    heads,
    biases,
    conv_moment,
    lin_rows,
    lin_cols,
    mats_rows,
    mats_cols,
    emb_moment,
    head_moment,
    bias_moment,
):
    weight_squares = lax.psum(
        (
            jnp.sum(conv_kernels * conv_kernels),
            jnp.sum(enc_linear * enc_linear),
            jnp.sum(plan_mats * plan_mats),
            jnp.sum(option_emb * option_emb),
            jnp.sum(heads * heads),
        ),
        "dp",
    )
    width = enc_linear.shape[1]
    kernels = gather_rows(conv_kernels.astype(BF))
    linear_t = gather_rows(enc_linear.astype(BF).T)
    mats_t = gather_rows(plan_mats.astype(BF).transpose(2, 0, 1)).transpose(1, 0, 2)
    emb_t = gather_rows(option_emb.astype(BF).T)
    heads_t = gather_rows(heads.astype(BF).reshape(3 * GAMES, width).T)
    table = jnp.pad(
        jnp.concatenate([emb_t, heads_t], axis=1),
        ((0, 0), (EMB_LANE, 128 - HEAD_LANE - 3 * GAMES)),
    )
    lin, mats, table_grad, conv, small = local_step(
        frames,
        kernels,
        linear_t,
        mats_t,
        table,
        biases,
        options,
        legal,
        games,
        valid,
        rewards,
        returns,
    )
    rows = jnp.concatenate(
        [lin, mats[0], mats[1], mats[2], table_grad[:, EMB_LANE : HEAD_LANE + 3 * GAMES]], axis=1
    )
    rows = lax.psum(lax.psum_scatter(rows, "dp", scatter_dimension=0, tiled=True), "section")
    conv = lax.psum(
        lax.psum_scatter(conv[:, : C1 + C2], "dp", scatter_dimension=0, tiled=True), "section"
    )
    small = lax.psum(small, ("section", "dp"))
    inverse_count = 1.0 / jnp.sum(small[4])
    loss_value = jnp.sum(small[3]) * inverse_count
    bias_raw = (
        jnp.concatenate([small[0, : C1 + C2], small[1], small[2]]) * inverse_count
    )
    rows = rows * inverse_count
    g_conv = conv * inverse_count
    g_lin = rows[:, :FEAT].T
    g_mats = rows[:, FEAT : FEAT + 3 * D].reshape(width, 3, D).transpose(1, 2, 0)
    g_emb = rows[:, FEAT + 3 * D : FEAT + 3 * D + OPTS].T
    g_heads = rows[:, FEAT + 3 * D + OPTS :].T.reshape(3, GAMES, width)
    partial_squares = (
        jnp.sum(g_conv * g_conv)
        + jnp.sum(g_lin * g_lin)
        + jnp.sum(g_mats * g_mats)
        + jnp.sum(g_emb * g_emb)
        + jnp.sum(g_heads * g_heads)
    )
    reduced = lax.psum(
        (partial_squares, jnp.sum(g_lin * g_lin, axis=1), jnp.sum(g_mats * g_mats, axis=2)), "dp"
    )
    grad_norm = jnp.sqrt(reduced[0] + jnp.sum(bias_raw * bias_raw))
    factor = jnp.minimum(1.0, CLIP_LIMIT / grad_norm)
    conv_grad = factor * g_conv
    lin_grad = factor * g_lin
    mats_grad = factor * g_mats
    emb_grad = factor * g_emb
    heads_grad = factor * g_heads
    bias_grad = factor * bias_raw
    conv_new, conv_moment_new = unfactored(
        conv_kernels, conv_grad, conv_moment, relative(weight_squares[0], KERN * (C1 + C2))
    )
    emb_new, emb_moment_new = unfactored(
        option_emb, emb_grad, emb_moment, relative(weight_squares[3], OPTS * D)
    )
    heads_new, head_moment_new = unfactored(
        heads, heads_grad, head_moment, relative(weight_squares[4], 3 * GAMES * D)
    )
    bias_new, bias_moment_new = unfactored(
        biases, bias_grad, bias_moment, relative(jnp.sum(biases * biases), BIAS)
    )
    lin_rows_new = DECAY_RATE * lin_rows + (1.0 - DECAY_RATE) * (
        factor * factor * reduced[1] / D + FLOOR_ONE
    )
    lin_cols_new = DECAY_RATE * lin_cols + (1.0 - DECAY_RATE) * jnp.mean(
        lin_grad * lin_grad + FLOOR_ONE, axis=0
    )
    lin_second = lin_rows_new[:, None] * lin_cols_new[None, :] / jnp.mean(lin_rows_new)
    lin_new = enc_linear - STEP_RATE * relative(weight_squares[1], FEAT * D) * lin_grad * lax.rsqrt(
        lin_second
    )
    mats_rows_new = DECAY_RATE * mats_rows + (1.0 - DECAY_RATE) * (
        factor * factor * reduced[2] / D + FLOOR_ONE
    )
    mats_cols_new = DECAY_RATE * mats_cols + (1.0 - DECAY_RATE) * jnp.mean(
        mats_grad * mats_grad + FLOOR_ONE, axis=1
    )
    mats_second = (
        mats_rows_new[:, :, None]
        * mats_cols_new[:, None, :]
        / jnp.mean(mats_rows_new, axis=1)[:, None, None]
    )
    mats_new = plan_mats - STEP_RATE * relative(weight_squares[2], 3 * D * D) * mats_grad * lax.rsqrt(
        mats_second
    )
    return (
        conv_new,
        conv_grad,
        conv_moment_new,
        lin_new,
        lin_grad,
        lin_rows_new,
        lin_cols_new,
        mats_new,
        mats_grad,
        mats_rows_new,
        mats_cols_new,
        emb_new,
        emb_grad,
        emb_moment_new,
        heads_new,
        heads_grad,
        head_moment_new,
        bias_new,
        bias_grad,
        bias_moment_new,
        grad_norm,
        loss_value,
        conv_new.astype(BF),
        lin_new.astype(BF),
    )


def solution(mesh):
    return jax.shard_map(
        fused_device if mesh.shape["dp"] * 8 == D else per_device,
        mesh=mesh,
        in_specs=(
            P(None, "dp", None, None),
            P(None, "dp", None),
            P(None, "dp", None),
            P(None, "dp"),
            P(None, "dp", None),
            P(None, "dp", None),
            P(None, "dp", None),
            P("dp", None),
            P(None, "dp"),
            P(None, None, "dp"),
            P(None, "dp"),
            P(None, None, "dp"),
            P(),
            P("dp", None),
            P(),
            P("dp"),
            P(),
            P(None, "dp"),
            P(None, "dp"),
            P(None, None, "dp"),
            P(),
        ),
        out_specs=(
            P("dp", None),
            P("dp", None),
            P("dp", None),
            P(None, "dp"),
            P(None, "dp"),
            P(),
            P("dp"),
            P(None, None, "dp"),
            P(None, None, "dp"),
            P(),
            P(None, "dp"),
            P(None, "dp"),
            P(None, "dp"),
            P(None, "dp"),
            P(None, None, "dp"),
            P(None, None, "dp"),
            P(None, None, "dp"),
            P(),
            P(),
            P(),
            P(),
            P(),
            P("dp", None),
            P(None, "dp"),
        ),
        check_vma=False,
    )
```
